32 devices in a mesh: rows: 16 (over z, x, core), cols: 2 (over y).
Axes of the slice: x: 2, y: 2, z: 4, core: 2. Of those that a mesh axis runs over, the one named last changes fastest.
Arguments:
- tokens: bfloat16 [2, 128, 128, 768], P(None, 'rows', 'cols'), may hold values from -6 to 6
- region_sizes: int32 [2, 2], replicated, may hold values from 64 to 128, as said below
- region_starts: int32 [2], replicated, may hold values from 0 to 127
- entry_gain: float32 [768], replicated, may hold values from 0.1 to 1.9
- entry_shift: float32 [768], replicated, may hold values from -1.75 to 1.75
- spectral_kernel: bfloat16 [2, 8, 96, 96], replicated, may hold values from -0.4375 to 0.4375
- spectral_bias: float32 [2, 8, 96], replicated, may hold values from -3 to 3
- spectral_mixer: bfloat16 [2, 8, 96, 96], replicated, may hold values from -0.4375 to 0.4375
- spectral_offset: float32 [2, 8, 96], replicated, may hold values from -1.75 to 1.75
- exit_scale: float32 [768], replicated, may hold values from 0.1 to 1.9
- exit_center: float32 [768], replicated, may hold values from -1.75 to 1.75
- dense_expand: bfloat16 [768, 3072], replicated, may hold values from -0.21875 to 0.21875
- dense_lift: float32 [3072], replicated, may hold values from -1.75 to 1.75
- dense_project: bfloat16 [3072, 768], replicated, may hold values from -0.15625 to 0.15625
- dense_return: float32 [768], replicated, may hold values from -1.75 to 1.75
- cotangent: bfloat16 [2, 128, 128, 768], P(None, 'rows', 'cols'), may hold values from -6 to 6
Outputs:
- output: bfloat16 [2, 128, 128, 768], P(None, 'rows', 'cols')
- gradient_tokens: float32 [2, 128, 128, 768], P(None, 'rows', 'cols')
- gradient_gain: float32 [768], replicated
- gradient_shift: float32 [768], replicated
- gradient_kernel: float32 [2, 8, 96, 96], replicated
- gradient_bias: float32 [2, 8, 96], replicated
- gradient_mixer: float32 [2, 8, 96, 96], replicated
- gradient_offset: float32 [2, 8, 96], replicated
- gradient_scale: float32 [768], replicated
- gradient_center: float32 [768], replicated
- gradient_expand: float32 [768, 3072], replicated
- gradient_lift: float32 [3072], replicated
- gradient_project: float32 [3072, 768], replicated
- gradient_return: float32 [768], replicated
The draws below stay inside these ranges and needn't reach their ends.
Inputs may be any that keep to these rules, and one draw needn't show every extreme that they name: `region_sizes`: each region's valid rows number 128 // 2 to 128 and its valid columns 64 to 128; in every draw one region is the whole grid, 128 rows by 128 columns, and another has exactly 64 valid rows.
All inputs are finite; a program needn't handle non-finite values.
Results may differ from the reference program's by a relative error of at most 0.018.
The reference program's roundings to bfloat16 on the way count: a program that leaves them out, or rounds other values in their place, can miss the bound.
Values may be sent and summed in bfloat16 or wider, within the bound.
A program may use at most 192 MiB of HBM per device.

```python
import math
import jax
import jax.numpy as jnp
from jax import lax

C = 768
FF = 3072
NB = 8
BS = 96
H = 128
W = 128
KW = 64
REGIONS = 2


def draw_region_sizes(key, part):
    key = jax.random.fold_in(key, 7)
    rows_key, cols_key, whole_key, other_key = jax.random.split(key, 4)
    latitude = jax.random.randint(rows_key, (REGIONS,), H // 2, H + 1)
    longitude = jax.random.randint(cols_key, (REGIONS,), W // 2, W + 1)
    chosen = jax.random.randint(whole_key, (), 0, REGIONS)
    step = jax.random.randint(other_key, (), 1, REGIONS)
    smallest = (chosen + step) % REGIONS
    places = jnp.arange(REGIONS)
    whole = places == chosen
    least = places == smallest
    latitude = jnp.where(whole, H, jnp.where(least, H // 2, latitude))
    longitude = jnp.where(whole, W, longitude)
    return jnp.stack([latitude, longitude], 1).astype(jnp.int32)


def block_levels(own_key, dims, cuts, low, largest):
    level = 1.0
    for dim, blocks in cuts:
        draws = jax.random.uniform(jax.random.fold_in(jax.random.fold_in(own_key, 6), dim), (blocks,), jnp.float32, low / len(cuts), largest / len(cuts))
        level = level * jnp.repeat(jnp.exp(draws), dims[dim] // blocks).reshape((-1,) + (1,) * (len(dims) - 1 - dim))
    return level


def bell_draw(key, dims, scale, most, shards=(), kind=jnp.bfloat16):
    level = block_levels(key, dims, shards, -0.22, 0.18) if shards else 1.0
    array = jax.random.normal(key, dims, jnp.float32) * scale * level
    return jnp.minimum(jnp.maximum(array, -most), most).astype(kind)


def setup_inputs(seed: int = 0) -> dict:
    key_of = jax.random.split(jax.random.key(seed), 17)
    return {
        "tokens": bell_draw(key_of[0], (REGIONS, H, W, C), 1.0, 6.0, ((1, 16), (2, 2))),
        "region_sizes": draw_region_sizes(jax.random.fold_in(key_of[16], 71), 0),
        "region_starts": jax.random.randint(key_of[2], (REGIONS,), 0, W).astype(jnp.int32),
        "entry_gain": jnp.clip(1.0 + 0.18 * jax.random.normal(key_of[3], (C,), jnp.float32), 0.1, 1.9),
        "entry_shift": bell_draw(key_of[4], (C,), 0.3, 1.75, (), jnp.float32),
        "spectral_kernel": bell_draw(key_of[5], (2, NB, BS, BS), (2 * BS) ** -0.5, 0.4375),
        "spectral_bias": bell_draw(key_of[6], (2, NB, BS), 0.5, 3.0, (), jnp.float32),
        "spectral_mixer": bell_draw(key_of[7], (2, NB, BS, BS), (2 * BS) ** -0.5, 0.4375),
        "spectral_offset": bell_draw(key_of[8], (2, NB, BS), 0.3, 1.75, (), jnp.float32),
        "exit_scale": jnp.clip(1.0 + 0.18 * jax.random.normal(key_of[9], (C,), jnp.float32), 0.1, 1.9),
        "exit_center": bell_draw(key_of[10], (C,), 0.3, 1.75, (), jnp.float32),
        "dense_expand": bell_draw(key_of[11], (C, FF), C ** -0.5, 0.21875),
        "dense_lift": bell_draw(key_of[12], (FF,), 0.3, 1.75, (), jnp.float32),
        "dense_project": bell_draw(key_of[13], (FF, C), (FF // 2) ** -0.5, 0.15625),
        "dense_return": bell_draw(key_of[14], (C,), 0.3, 1.75, (), jnp.float32),
        "cotangent": bell_draw(key_of[15], (REGIONS, H, W, C), 1.0, 6.0, ((1, 16), (2, 2))),
    }


shrink_width = 0.01
norm_eps = 1e-06
highest = lax.Precision.HIGHEST

@jax.custom_vjp
def low(v):
    return lax.optimization_barrier(v.astype(jnp.bfloat16)).astype(jnp.float32)

@jax.custom_vjp
def low_back(v):
    return v

def low_keep(v):
    return (low(v), None)

def low_pass(kept, grad):
    return (grad,)

def back_keep(v):
    return (v, None)

def back_low(kept, grad):
    return (low(grad),)
low.defvjp(low_keep, low_pass)
low_back.defvjp(back_keep, back_low)

def tables(height, width, modes):
    column = jnp.arange(width, dtype=jnp.int32)
    frequency = jnp.arange(modes, dtype=jnp.int32)
    turns = column[:, None] * frequency[None, :] % width
    angle = turns.astype(jnp.float32) * (2.0 * math.pi / width)
    cosine = jnp.cos(angle)
    sine = jnp.sin(angle)
    scale = 1.0 / math.sqrt(width)
    forward_zonal = jnp.stack([cosine, -sine], 1) * scale
    factor = jnp.where(frequency == 0, 1.0, 2.0).astype(jnp.float32)
    inverse_zonal = jnp.stack([cosine.T * factor[:, None], -sine.T * factor[:, None]], 0) * scale
    latitude = jnp.arange(height, dtype=jnp.int32)
    meridian_turns = latitude[:, None] * latitude[None, :] % height
    meridian_angle = meridian_turns.astype(jnp.float32) * (2.0 * math.pi / height)
    meridian_cos = jnp.cos(meridian_angle) / math.sqrt(height)
    meridian_sin = jnp.sin(meridian_angle) / math.sqrt(height)
    meridian_table = jnp.stack([jnp.stack([meridian_cos, meridian_sin], -1), jnp.stack([-meridian_sin, meridian_cos], -1)], 1)
    return (forward_zonal, inverse_zonal, meridian_table)

def layer_norm(value, gain, shift):
    centre = lax.optimization_barrier(jnp.mean(value, -1, keepdims=True))
    centred = value - centre
    spread = lax.optimization_barrier(jnp.mean(centred * centred, -1, keepdims=True))
    return centred * lax.rsqrt(spread + norm_eps) * gain + shift

def gelu_exact(value):
    return jax.nn.gelu(value, approximate=False)

def shrink(value):
    return value - shrink_width * jnp.tanh(value / shrink_width)

def region_mask(region_sizes, region_starts, height, width):
    latitude = jnp.arange(height, dtype=jnp.int32)
    longitude = jnp.arange(width, dtype=jnp.int32)
    inside_rows = latitude[None, :, None] < region_sizes[:, 0][:, None, None]
    offset = (longitude[None, None, :] - region_starts[:, None, None]) % width
    inside_cols = offset < region_sizes[:, 1][:, None, None]
    return jnp.where(inside_rows & inside_cols, 1.0, 0.0).astype(jnp.float32)[..., None]

def complex_block(spectrum, weight, bias):
    leading = spectrum.shape[:3]
    parts = spectrum.reshape(leading + (2, NB, BS))
    real = parts[:, :, :, 0]
    imaginary = parts[:, :, :, 1]

    def product(left, right):
        return jnp.einsum('rkmni,nij->rkmnj', left, right, precision=highest)
    out_real = product(real, weight[0]) - product(imaginary, weight[1]) + bias[0]
    out_imaginary = product(imaginary, weight[0]) + product(real, weight[1]) + bias[1]
    return jnp.stack([out_real, out_imaginary], 3).reshape(spectrum.shape)

def forward(tokens, entry_gain, entry_shift, spectral_kernel, spectral_bias, spectral_mixer, spectral_offset, exit_scale, exit_center, dense_expand, dense_lift, dense_project, dense_return, mask, grids):
    forward_zonal, inverse_zonal, meridian_table = grids
    normed = layer_norm(tokens, entry_gain, entry_shift)
    sent = low_back(low(mask * normed))
    zonal = low_back(low(jnp.einsum('rhwc,wpk->rhkpc', sent, forward_zonal, precision=highest)))
    spectrum = low(jnp.einsum('kphq,rhmqc->rkmpc', meridian_table, zonal, precision=highest))
    first_pre = low_back(complex_block(spectrum, spectral_kernel, spectral_bias))
    first_act = low(gelu_exact(first_pre))
    second_pre = low_back(complex_block(first_act, spectral_mixer, spectral_offset))
    shrunk = shrink(second_pre)
    back_meridian = low_back(low(jnp.einsum('kphq,rkmpc->rhmqc', meridian_table, shrunk, precision=highest)))
    filtered = low_back(low(jnp.einsum('rhkpc,pkw->rhwc', back_meridian, inverse_zonal, precision=highest)))
    mixed = tokens + mask * filtered + normed
    second_norm = low(layer_norm(mixed, exit_scale, exit_center))
    hidden_pre = low_back(jnp.einsum('rhwc,cf->rhwf', second_norm, dense_expand, precision=highest) + dense_lift)
    hidden = low(gelu_exact(hidden_pre))
    return mixed + jnp.einsum('rhwf,fc->rhwc', hidden, dense_project, precision=highest) + dense_return

def reference(tokens, region_sizes, region_starts, entry_gain, entry_shift, spectral_kernel, spectral_bias, spectral_mixer, spectral_offset, exit_scale, exit_center, dense_expand, dense_lift, dense_project, dense_return, cotangent):
    grids = tuple((low(table) for table in tables(H, W, KW)))
    mask = region_mask(region_sizes, region_starts, H, W)
    values = tuple((item.astype(jnp.float32) for item in (tokens, entry_gain, entry_shift, spectral_kernel, spectral_bias, spectral_mixer, spectral_offset, exit_scale, exit_center, dense_expand, dense_lift, dense_project, dense_return)))

    def run(*inputs):
        return forward(*inputs, mask, grids)
    output, pullback = jax.vjp(run, *values)
    slopes = pullback(cotangent.astype(jnp.float32))
    return (output.astype(jnp.bfloat16), slopes[0], slopes[1], slopes[2], slopes[3], slopes[4], slopes[5], slopes[6], slopes[7], slopes[8], slopes[9], slopes[10], slopes[11], slopes[12])
```

```python
import math

import jax
import jax.numpy as jnp
from jax import lax
from jax.sharding import PartitionSpec as P

shrink_width = 0.01
norm_eps = 1e-06
highest = lax.Precision.HIGHEST


def tables(height, width, modes):
    column = jnp.arange(width, dtype=jnp.int32)
    frequency = jnp.arange(modes, dtype=jnp.int32)
    turns = column[:, None] * frequency[None, :] % width
    angle = turns.astype(jnp.float32) * (2.0 * math.pi / width)
    cosine = jnp.cos(angle)
    sine = jnp.sin(angle)
    scale = 1.0 / math.sqrt(width)
    forward_zonal = jnp.stack([cosine, -sine], 1) * scale
    factor = jnp.where(frequency == 0, 1.0, 2.0).astype(jnp.float32)
    inverse_zonal = jnp.stack([cosine.T * factor[:, None], -sine.T * factor[:, None]], 0) * scale
    latitude = jnp.arange(height, dtype=jnp.int32)
    meridian_turns = latitude[:, None] * latitude[None, :] % height
    meridian_angle = meridian_turns.astype(jnp.float32) * (2.0 * math.pi / height)
    meridian_cos = jnp.cos(meridian_angle) / math.sqrt(height)
    meridian_sin = jnp.sin(meridian_angle) / math.sqrt(height)
    meridian_table = jnp.stack(
        [jnp.stack([meridian_cos, meridian_sin], -1), jnp.stack([-meridian_sin, meridian_cos], -1)],
        1,
    )
    forward_low = forward_zonal.astype(jnp.bfloat16)
    inverse_low = inverse_zonal.astype(jnp.bfloat16)
    meridian_low = meridian_table.astype(jnp.bfloat16)
    meridian_wide = meridian_low.astype(jnp.float32)
    return (forward_low, inverse_low, meridian_low, meridian_wide)


def layer_norm(value, gain, shift):
    centre = jnp.mean(value, -1, keepdims=True)
    centred = value - centre
    spread = jnp.mean(centred * centred, -1, keepdims=True)
    return centred * lax.rsqrt(spread + norm_eps) * gain + shift


def gelu_exact(value):
    return jax.nn.gelu(value, approximate=False)


def shrink(value):
    return value - shrink_width * jnp.tanh(value / shrink_width)


def block_layout(spectrum, blocks, block_size):
    leading = spectrum.shape[:3]
    parts = spectrum.reshape(leading + (2, blocks, block_size))
    parts = jnp.moveaxis(parts, 3, 4)
    return parts.reshape((-1, blocks, 2 * block_size))


def spectral_layout(modes_flat, leading, blocks, block_size):
    parts = modes_flat.reshape(leading + (blocks, 2, block_size))
    parts = jnp.moveaxis(parts, 4, 3)
    return parts.reshape(leading + (2, blocks * block_size))


def complex_matrix(weight):
    real = weight[0]
    imaginary = weight[1]
    upper = jnp.concatenate([real, imaginary], 2)
    lower = jnp.concatenate([-imaginary, real], 2)
    return jnp.concatenate([upper, lower], 1)


def matrix_gradient(whole, block_size):
    upper = whole[:, :block_size]
    lower = whole[:, block_size:]
    real = upper[:, :, :block_size] + lower[:, :, block_size:]
    imaginary = upper[:, :, block_size:] - lower[:, :, :block_size]
    return jnp.stack([real, imaginary], 0)


def bias_rows(bias):
    return jnp.moveaxis(bias, 0, 1).reshape(bias.shape[1], 2 * bias.shape[2])


def bias_gradient(summed, block_size):
    return jnp.moveaxis(summed.reshape(summed.shape[0], 2, block_size), 1, 0)


def advance(tokens, mask, weights, grids, layout):
    (
        entry_gain,
        entry_shift,
        spectral_kernel,
        spectral_bias,
        spectral_mixer,
        spectral_offset,
        exit_scale,
        exit_center,
        dense_expand,
        dense_lift,
        dense_project,
        dense_return,
    ) = weights
    forward_zonal, inverse_zonal, meridian_table, meridian_wide = grids
    blocks, block_size, first_block = layout
    residual = tokens.astype(jnp.float32)
    normed = layer_norm(residual, entry_gain, entry_shift)
    sent = (mask * normed).astype(jnp.bfloat16)
    by_channel = lax.all_to_all(sent, "cols", split_axis=3, concat_axis=2, tiled=True)
    zonal = jnp.einsum(
        "rhwc,wpk->rhkpc", by_channel, forward_zonal, preferred_element_type=jnp.float32
    )
    by_mode = lax.all_to_all(
        zonal.astype(jnp.bfloat16), "rows", split_axis=2, concat_axis=1, tiled=True
    )
    spectrum = jnp.einsum(
        "kphq,rhmqc->rkmpc", meridian_table, by_mode, preferred_element_type=jnp.float32
    ).astype(jnp.bfloat16)
    leading = spectrum.shape[:3]
    modes_flat = block_layout(spectrum, blocks, block_size)
    kernel_matrix = complex_matrix(
        lax.dynamic_slice_in_dim(spectral_kernel, first_block, blocks, 1)
    )
    mixer_matrix = complex_matrix(lax.dynamic_slice_in_dim(spectral_mixer, first_block, blocks, 1))
    kernel_bias = bias_rows(lax.dynamic_slice_in_dim(spectral_bias, first_block, blocks, 1))
    mixer_bias = bias_rows(lax.dynamic_slice_in_dim(spectral_offset, first_block, blocks, 1))
    first_pre = (
        jnp.einsum("nbx,bxy->nby", modes_flat, kernel_matrix, preferred_element_type=jnp.float32)
        + kernel_bias
    )
    first_act = gelu_exact(first_pre).astype(jnp.bfloat16)
    second_pre = (
        jnp.einsum("nbx,bxy->nby", first_act, mixer_matrix, preferred_element_type=jnp.float32)
        + mixer_bias
    )
    shrunk = spectral_layout(shrink(second_pre), leading, blocks, block_size)
    back_meridian = jnp.einsum(
        "kphq,rkmpc->rhmqc", meridian_wide, shrunk, precision=highest
    ).astype(jnp.bfloat16)
    by_row = lax.all_to_all(back_meridian, "rows", split_axis=1, concat_axis=2, tiled=True)
    filtered = jnp.einsum(
        "rhkpc,pkw->rhwc", by_row, inverse_zonal, preferred_element_type=jnp.float32
    ).astype(jnp.bfloat16)
    by_token = lax.all_to_all(filtered, "cols", split_axis=2, concat_axis=3, tiled=True)
    mixed = residual + mask * by_token.astype(jnp.float32) + normed
    features = mixed.shape[-1]
    second_norm = (
        layer_norm(mixed, exit_scale, exit_center).astype(jnp.bfloat16).reshape(-1, features)
    )
    hidden_pre = jnp.dot(second_norm, dense_expand, preferred_element_type=jnp.float32) + dense_lift
    hidden = gelu_exact(hidden_pre).astype(jnp.bfloat16)
    output = mixed + (
        jnp.dot(hidden, dense_project, preferred_element_type=jnp.float32) + dense_return
    ).reshape(mixed.shape)
    kept = (
        residual,
        modes_flat,
        first_pre,
        first_act,
        second_pre,
        mixed,
        second_norm,
        hidden_pre,
        hidden,
        kernel_matrix,
        mixer_matrix,
        leading,
    )
    return (output, kept)


def retreat(cotangent, mask, kept, weights, grids, layout):
    (
        entry_gain,
        entry_shift,
        spectral_kernel,
        spectral_bias,
        spectral_mixer,
        spectral_offset,
        exit_scale,
        exit_center,
        dense_expand,
        dense_lift,
        dense_project,
        dense_return,
    ) = weights
    forward_zonal, inverse_zonal, meridian_table, meridian_wide = grids
    blocks, block_size, first_block = layout
    (
        residual,
        modes_flat,
        first_pre,
        first_act,
        second_pre,
        mixed,
        second_norm,
        hidden_pre,
        hidden,
        kernel_matrix,
        mixer_matrix,
        leading,
    ) = kept
    features = mixed.shape[-1]
    upstream = cotangent.reshape(-1, features)
    gradient_project = jnp.einsum("tf,tc->fc", hidden, upstream, preferred_element_type=jnp.float32)
    gradient_return = jnp.sum(upstream.astype(jnp.float32), 0)
    outer = (gradient_project, gradient_return)
    hidden_back = jnp.einsum(
        "tc,fc->tf", upstream, dense_project, preferred_element_type=jnp.float32
    )
    hidden_pull = jax.vjp(gelu_exact, hidden_pre)[1]
    pre_back = hidden_pull(hidden_back)[0].astype(jnp.bfloat16)
    gradient_expand = jnp.einsum(
        "tc,tf->cf", second_norm, pre_back, preferred_element_type=jnp.float32
    )
    gradient_lift = jnp.sum(pre_back.astype(jnp.float32), 0)
    norm_back = jnp.einsum(
        "tf,cf->tc", pre_back, dense_expand, preferred_element_type=jnp.float32
    ).reshape(mixed.shape)
    exit_pull = jax.vjp(layer_norm, mixed, exit_scale, exit_center)[1]
    mixed_part, gradient_scale, gradient_center = exit_pull(norm_back)
    inner = (gradient_expand, gradient_lift, gradient_scale, gradient_center)
    mixed_back = cotangent.astype(jnp.float32) + mixed_part
    filter_back = (mask * mixed_back).astype(jnp.bfloat16)
    channel_back = lax.all_to_all(filter_back, "cols", split_axis=3, concat_axis=2, tiled=True)
    zonal_back = jnp.einsum(
        "rhwc,pkw->rhkpc", channel_back, inverse_zonal, preferred_element_type=jnp.float32
    ).astype(jnp.bfloat16)
    meridian_back = lax.all_to_all(zonal_back, "rows", split_axis=2, concat_axis=1, tiled=True)
    shrunk_back = jnp.einsum(
        "kphq,rhmqc->rkmpc", meridian_table, meridian_back, preferred_element_type=jnp.float32
    )
    shrink_pull = jax.vjp(shrink, second_pre)[1]
    second_back = shrink_pull(block_layout(shrunk_back, blocks, block_size))[0].astype(jnp.bfloat16)
    mixer_whole = jnp.einsum(
        "nbx,nby->bxy", first_act, second_back, preferred_element_type=jnp.float32
    )
    offset_rows = jnp.sum(second_back.astype(jnp.float32), 0)
    activation_back = jnp.einsum(
        "nby,bxy->nbx", second_back, mixer_matrix, preferred_element_type=jnp.float32
    )
    first_pull = jax.vjp(gelu_exact, first_pre)[1]
    first_back = first_pull(activation_back)[0].astype(jnp.bfloat16)
    kernel_whole = jnp.einsum(
        "nbx,nby->bxy", modes_flat, first_back, preferred_element_type=jnp.float32
    )
    kernel_rows = jnp.sum(first_back.astype(jnp.float32), 0)
    spectrum_back = spectral_layout(
        jnp.einsum("nby,bxy->nbx", first_back, kernel_matrix, preferred_element_type=jnp.float32),
        leading,
        blocks,
        block_size,
    )
    modes_back = jnp.einsum(
        "kphq,rkmpc->rhmqc", meridian_wide, spectrum_back, precision=highest
    ).astype(jnp.bfloat16)
    row_back = lax.all_to_all(modes_back, "rows", split_axis=1, concat_axis=2, tiled=True)
    sent_back = jnp.einsum(
        "rhkpc,wpk->rhwc", row_back, forward_zonal, preferred_element_type=jnp.float32
    ).astype(jnp.bfloat16)
    token_back = lax.all_to_all(sent_back, "cols", split_axis=2, concat_axis=3, tiled=True)
    normed_back = mixed_back + mask * token_back.astype(jnp.float32)
    entry_pull = jax.vjp(layer_norm, residual, entry_gain, entry_shift)[1]
    residual_part, gradient_gain, gradient_shift = entry_pull(normed_back)
    gradient_tokens = mixed_back + residual_part
    shared = (
        gradient_gain,
        gradient_shift,
        inner[2],
        inner[3],
        inner[0],
        inner[1],
        outer[0],
        outer[1],
    )
    local_blocks = (
        matrix_gradient(kernel_whole, block_size),
        bias_gradient(kernel_rows, block_size),
        matrix_gradient(mixer_whole, block_size),
        bias_gradient(offset_rows, block_size),
    )
    return (gradient_tokens, shared, local_blocks)


def shards(
    tokens,
    region_sizes,
    region_starts,
    entry_gain,
    entry_shift,
    spectral_kernel,
    spectral_bias,
    spectral_mixer,
    spectral_offset,
    exit_scale,
    exit_center,
    dense_expand,
    dense_lift,
    dense_project,
    dense_return,
    cotangent,
):
    rows_here = tokens.shape[1]
    cols_here = tokens.shape[2]
    height = rows_here * lax.axis_size("rows")
    width = cols_here * lax.axis_size("cols")
    grids = tables(height, width, width // 2)
    latitude = lax.axis_index("rows") * rows_here + jnp.arange(rows_here, dtype=jnp.int32)
    longitude = lax.axis_index("cols") * cols_here + jnp.arange(cols_here, dtype=jnp.int32)
    inside_rows = latitude[None, :, None] < region_sizes[:, 0][:, None, None]
    offset = (longitude[None, None, :] - region_starts[:, None, None]) % width
    inside_cols = offset < region_sizes[:, 1][:, None, None]
    mask = jnp.where(inside_rows & inside_cols, 1.0, 0.0).astype(jnp.float32)[..., None]
    block_size = spectral_kernel.shape[2]
    total_blocks = spectral_kernel.shape[1]
    blocks = tokens.shape[3] // lax.axis_size("cols") // block_size
    first_block = lax.axis_index("cols") * blocks
    layout = (blocks, block_size, first_block)
    weights = (
        entry_gain,
        entry_shift,
        spectral_kernel,
        spectral_bias,
        spectral_mixer,
        spectral_offset,
        exit_scale,
        exit_center,
        dense_expand,
        dense_lift,
        dense_project,
        dense_return,
    )
    output, kept = advance(tokens, mask, weights, grids, layout)
    gradient_tokens, shared, local_blocks = retreat(cotangent, mask, kept, weights, grids, layout)
    (
        gain_part,
        shift_part,
        scale_part,
        center_part,
        expand_part,
        lift_part,
        project_part,
        return_part,
    ) = shared
    everywhere = ("rows", "cols")
    project_sum = lax.psum(project_part.astype(jnp.bfloat16), everywhere).astype(jnp.float32)
    expand_sum = lax.psum(expand_part.astype(jnp.bfloat16), everywhere).astype(jnp.float32)
    vectors = (gain_part, shift_part, scale_part, center_part, lift_part, return_part)
    sums = lax.psum(jnp.concatenate(vectors), everywhere)
    ends = [0]
    for vector in vectors:
        ends.append(ends[-1] + vector.shape[0])
    parts = [sums[low:high] for low, high in zip(ends[:-1], ends[1:])]
    summed = (*parts[:4], expand_sum, parts[4], project_sum, parts[5])
    kernel_local, bias_local, mixer_local, offset_local = local_blocks
    kernel_full = lax.dynamic_update_slice_in_dim(
        jnp.zeros((2, total_blocks, block_size, block_size), jnp.float32),
        kernel_local,
        first_block,
        1,
    )
    bias_full = lax.dynamic_update_slice_in_dim(
        jnp.zeros((2, total_blocks, block_size), jnp.float32), bias_local, first_block, 1
    )
    mixer_full = lax.dynamic_update_slice_in_dim(
        jnp.zeros((2, total_blocks, block_size, block_size), jnp.float32),
        mixer_local,
        first_block,
        1,
    )
    offset_full = lax.dynamic_update_slice_in_dim(
        jnp.zeros((2, total_blocks, block_size), jnp.float32), offset_local, first_block, 1
    )
    block_totals = lax.psum((kernel_full, bias_full, mixer_full, offset_full), ("rows", "cols"))
    return (
        output.astype(jnp.bfloat16),
        gradient_tokens,
        summed[0],
        summed[1],
        block_totals[0],
        block_totals[1],
        block_totals[2],
        block_totals[3],
        summed[2],
        summed[3],
        summed[4],
        summed[5],
        summed[6],
        summed[7],
    )


def solution(mesh):
    placed = (
        P(None, "rows", "cols", None),
        P(),
        P(),
        P(),
        P(),
        P(),
        P(),
        P(),
        P(),
        P(),
        P(),
        P(),
        P(),
        P(),
        P(),
        P(None, "rows", "cols", None),
    )
    return jax.shard_map(
        shards,
        mesh=mesh,
        in_specs=placed,
        out_specs=(
            P(None, "rows", "cols", None),
            P(None, "rows", "cols", None),
            P(),
            P(),
            P(),
            P(),
            P(),
            P(),
            P(),
            P(),
            P(),
            P(),
            P(),
            P(),
        ),
        check_vma=False,
    )
```

```python
import functools
import math

import jax
import jax.numpy as jnp
import ml_dtypes
import numpy as np
from jax import lax
from jax.experimental import pallas as pl
from jax.experimental.pallas import tpu as pltpu
from jax.sharding import PartitionSpec as P

shrink_width = 0.01
norm_eps = 1e-06
highest = lax.Precision.HIGHEST


def tables(height, width, modes):
    column = jnp.arange(width, dtype=jnp.int32)
    frequency = jnp.arange(modes, dtype=jnp.int32)
    turns = column[:, None] * frequency[None, :] % width
    angle = turns.astype(jnp.float32) * (2.0 * math.pi / width)
    cosine = jnp.cos(angle)
    sine = jnp.sin(angle)
    scale = 1.0 / math.sqrt(width)
    forward_zonal = jnp.stack([cosine, -sine], 1) * scale
    factor = jnp.where(frequency == 0, 1.0, 2.0).astype(jnp.float32)
    inverse_zonal = jnp.stack([cosine.T * factor[:, None], -sine.T * factor[:, None]], 0) * scale
    latitude = jnp.arange(height, dtype=jnp.int32)
    meridian_turns = latitude[:, None] * latitude[None, :] % height
    meridian_angle = meridian_turns.astype(jnp.float32) * (2.0 * math.pi / height)
    meridian_cos = jnp.cos(meridian_angle) / math.sqrt(height)
    meridian_sin = jnp.sin(meridian_angle) / math.sqrt(height)
    meridian_table = jnp.stack(
        [jnp.stack([meridian_cos, meridian_sin], -1), jnp.stack([-meridian_sin, meridian_cos], -1)],
        1,
    )
    forward_low = forward_zonal.astype(jnp.bfloat16)
    inverse_low = inverse_zonal.astype(jnp.bfloat16)
    meridian_low = meridian_table.astype(jnp.bfloat16)
    meridian_wide = meridian_low.astype(jnp.float32)
    return (forward_low, inverse_low, meridian_low, meridian_wide)


def layer_norm(value, gain, shift):
    centre = jnp.mean(value, -1, keepdims=True)
    centred = value - centre
    spread = jnp.mean(centred * centred, -1, keepdims=True)
    return centred * lax.rsqrt(spread + norm_eps) * gain + shift


def gelu_exact(value):
    return jax.nn.gelu(value, approximate=False)


def shrink(value):
    return value - shrink_width * jnp.tanh(value / shrink_width)


def block_layout(spectrum, blocks, block_size):
    leading = spectrum.shape[:3]
    parts = spectrum.reshape(leading + (2, blocks, block_size))
    parts = jnp.moveaxis(parts, 3, 4)
    return parts.reshape((-1, blocks, 2 * block_size))


def spectral_layout(modes_flat, leading, blocks, block_size):
    parts = modes_flat.reshape(leading + (blocks, 2, block_size))
    parts = jnp.moveaxis(parts, 4, 3)
    return parts.reshape(leading + (2, blocks * block_size))


def complex_matrix(weight):
    real = weight[0]
    imaginary = weight[1]
    upper = jnp.concatenate([real, imaginary], 2)
    lower = jnp.concatenate([-imaginary, real], 2)
    return jnp.concatenate([upper, lower], 1)


def matrix_gradient(whole, block_size):
    upper = whole[:, :block_size]
    lower = whole[:, block_size:]
    real = upper[:, :, :block_size] + lower[:, :, block_size:]
    imaginary = upper[:, :, block_size:] - lower[:, :, :block_size]
    return jnp.stack([real, imaginary], 0)


def bias_rows(bias):
    return jnp.moveaxis(bias, 0, 1).reshape(bias.shape[1], 2 * bias.shape[2])


def bias_gradient(summed, block_size):
    return jnp.moveaxis(summed.reshape(summed.shape[0], 2, block_size), 1, 0)


def advance(tokens, mask, weights, grids, layout):
    (
        entry_gain,
        entry_shift,
        spectral_kernel,
        spectral_bias,
        spectral_mixer,
        spectral_offset,
        exit_scale,
        exit_center,
        dense_expand,
        dense_lift,
        dense_project,
        dense_return,
    ) = weights
    forward_zonal, inverse_zonal, meridian_table, meridian_wide = grids
    blocks, block_size, first_block = layout
    residual = tokens.astype(jnp.float32)
    normed = layer_norm(residual, entry_gain, entry_shift)
    sent = (mask * normed).astype(jnp.bfloat16)
    by_channel = lax.all_to_all(sent, "cols", split_axis=3, concat_axis=2, tiled=True)
    zonal = jnp.einsum(
        "rhwc,wpk->rhkpc", by_channel, forward_zonal, preferred_element_type=jnp.float32
    )
    by_mode = lax.all_to_all(
        zonal.astype(jnp.bfloat16), "rows", split_axis=2, concat_axis=1, tiled=True
    )
    spectrum = jnp.einsum(
        "kphq,rhmqc->rkmpc", meridian_table, by_mode, preferred_element_type=jnp.float32
    ).astype(jnp.bfloat16)
    leading = spectrum.shape[:3]
    modes_flat = block_layout(spectrum, blocks, block_size)
    kernel_matrix = complex_matrix(
        lax.dynamic_slice_in_dim(spectral_kernel, first_block, blocks, 1)
    )
    mixer_matrix = complex_matrix(lax.dynamic_slice_in_dim(spectral_mixer, first_block, blocks, 1))
    kernel_bias = bias_rows(lax.dynamic_slice_in_dim(spectral_bias, first_block, blocks, 1))
    mixer_bias = bias_rows(lax.dynamic_slice_in_dim(spectral_offset, first_block, blocks, 1))
    first_pre = (
        jnp.einsum("nbx,bxy->nby", modes_flat, kernel_matrix, preferred_element_type=jnp.float32)
        + kernel_bias
    )
    first_act = gelu_exact(first_pre).astype(jnp.bfloat16)
    second_pre = (
        jnp.einsum("nbx,bxy->nby", first_act, mixer_matrix, preferred_element_type=jnp.float32)
        + mixer_bias
    )
    shrunk = spectral_layout(shrink(second_pre), leading, blocks, block_size)
    back_meridian = jnp.einsum(
        "kphq,rkmpc->rhmqc", meridian_wide, shrunk, precision=highest
    ).astype(jnp.bfloat16)
    by_row = lax.all_to_all(back_meridian, "rows", split_axis=1, concat_axis=2, tiled=True)
    filtered = jnp.einsum(
        "rhkpc,pkw->rhwc", by_row, inverse_zonal, preferred_element_type=jnp.float32
    ).astype(jnp.bfloat16)
    by_token = lax.all_to_all(filtered, "cols", split_axis=2, concat_axis=3, tiled=True)
    mixed = residual + mask * by_token.astype(jnp.float32) + normed
    features = mixed.shape[-1]
    second_norm = (
        layer_norm(mixed, exit_scale, exit_center).astype(jnp.bfloat16).reshape(-1, features)
    )
    hidden_pre = jnp.dot(second_norm, dense_expand, preferred_element_type=jnp.float32) + dense_lift
    hidden = gelu_exact(hidden_pre).astype(jnp.bfloat16)
    output = mixed + (
        jnp.dot(hidden, dense_project, preferred_element_type=jnp.float32) + dense_return
    ).reshape(mixed.shape)
    kept = (
        residual,
        modes_flat,
        first_pre,
        first_act,
        second_pre,
        mixed,
        second_norm,
        hidden_pre,
        hidden,
        kernel_matrix,
        mixer_matrix,
        leading,
    )
    return (output, kept)


def retreat(cotangent, mask, kept, weights, grids, layout):
    (
        entry_gain,
        entry_shift,
        spectral_kernel,
        spectral_bias,
        spectral_mixer,
        spectral_offset,
        exit_scale,
        exit_center,
        dense_expand,
        dense_lift,
        dense_project,
        dense_return,
    ) = weights
    forward_zonal, inverse_zonal, meridian_table, meridian_wide = grids
    blocks, block_size, first_block = layout
    (
        residual,
        modes_flat,
        first_pre,
        first_act,
        second_pre,
        mixed,
        second_norm,
        hidden_pre,
        hidden,
        kernel_matrix,
        mixer_matrix,
        leading,
    ) = kept
    features = mixed.shape[-1]
    upstream = cotangent.reshape(-1, features)
    gradient_project = jnp.einsum("tf,tc->fc", hidden, upstream, preferred_element_type=jnp.float32)
    gradient_return = jnp.sum(upstream.astype(jnp.float32), 0)
    outer = (gradient_project, gradient_return)
    hidden_back = jnp.einsum(
        "tc,fc->tf", upstream, dense_project, preferred_element_type=jnp.float32
    )
    hidden_pull = jax.vjp(gelu_exact, hidden_pre)[1]
    pre_back = hidden_pull(hidden_back)[0].astype(jnp.bfloat16)
    gradient_expand = jnp.einsum(
        "tc,tf->cf", second_norm, pre_back, preferred_element_type=jnp.float32
    )
    gradient_lift = jnp.sum(pre_back.astype(jnp.float32), 0)
    norm_back = jnp.einsum(
        "tf,cf->tc", pre_back, dense_expand, preferred_element_type=jnp.float32
    ).reshape(mixed.shape)
    exit_pull = jax.vjp(layer_norm, mixed, exit_scale, exit_center)[1]
    mixed_part, gradient_scale, gradient_center = exit_pull(norm_back)
    inner = (gradient_expand, gradient_lift, gradient_scale, gradient_center)
    mixed_back = cotangent.astype(jnp.float32) + mixed_part
    filter_back = (mask * mixed_back).astype(jnp.bfloat16)
    channel_back = lax.all_to_all(filter_back, "cols", split_axis=3, concat_axis=2, tiled=True)
    zonal_back = jnp.einsum(
        "rhwc,pkw->rhkpc", channel_back, inverse_zonal, preferred_element_type=jnp.float32
    ).astype(jnp.bfloat16)
    meridian_back = lax.all_to_all(zonal_back, "rows", split_axis=2, concat_axis=1, tiled=True)
    shrunk_back = jnp.einsum(
        "kphq,rhmqc->rkmpc", meridian_table, meridian_back, preferred_element_type=jnp.float32
    )
    shrink_pull = jax.vjp(shrink, second_pre)[1]
    second_back = shrink_pull(block_layout(shrunk_back, blocks, block_size))[0].astype(jnp.bfloat16)
    mixer_whole = jnp.einsum(
        "nbx,nby->bxy", first_act, second_back, preferred_element_type=jnp.float32
    )
    offset_rows = jnp.sum(second_back.astype(jnp.float32), 0)
    activation_back = jnp.einsum(
        "nby,bxy->nbx", second_back, mixer_matrix, preferred_element_type=jnp.float32
    )
    first_pull = jax.vjp(gelu_exact, first_pre)[1]
    first_back = first_pull(activation_back)[0].astype(jnp.bfloat16)
    kernel_whole = jnp.einsum(
        "nbx,nby->bxy", modes_flat, first_back, preferred_element_type=jnp.float32
    )
    kernel_rows = jnp.sum(first_back.astype(jnp.float32), 0)
    spectrum_back = spectral_layout(
        jnp.einsum("nby,bxy->nbx", first_back, kernel_matrix, preferred_element_type=jnp.float32),
        leading,
        blocks,
        block_size,
    )
    modes_back = jnp.einsum(
        "kphq,rkmpc->rhmqc", meridian_wide, spectrum_back, precision=highest
    ).astype(jnp.bfloat16)
    row_back = lax.all_to_all(modes_back, "rows", split_axis=1, concat_axis=2, tiled=True)
    sent_back = jnp.einsum(
        "rhkpc,wpk->rhwc", row_back, forward_zonal, preferred_element_type=jnp.float32
    ).astype(jnp.bfloat16)
    token_back = lax.all_to_all(sent_back, "cols", split_axis=2, concat_axis=3, tiled=True)
    normed_back = mixed_back + mask * token_back.astype(jnp.float32)
    entry_pull = jax.vjp(layer_norm, residual, entry_gain, entry_shift)[1]
    residual_part, gradient_gain, gradient_shift = entry_pull(normed_back)
    gradient_tokens = mixed_back + residual_part
    shared = (
        gradient_gain,
        gradient_shift,
        inner[2],
        inner[3],
        inner[0],
        inner[1],
        outer[0],
        outer[1],
    )
    local_blocks = (
        matrix_gradient(kernel_whole, block_size),
        bias_gradient(kernel_rows, block_size),
        matrix_gradient(mixer_whole, block_size),
        bias_gradient(offset_rows, block_size),
    )
    return (gradient_tokens, shared, local_blocks)


def shards_general(
    tokens,
    region_sizes,
    region_starts,
    entry_gain,
    entry_shift,
    spectral_kernel,
    spectral_bias,
    spectral_mixer,
    spectral_offset,
    exit_scale,
    exit_center,
    dense_expand,
    dense_lift,
    dense_project,
    dense_return,
    cotangent,
):
    rows_here = tokens.shape[1]
    cols_here = tokens.shape[2]
    height = rows_here * lax.axis_size("rows")
    width = cols_here * lax.axis_size("cols")
    grids = tables(height, width, width // 2)
    latitude = lax.axis_index("rows") * rows_here + jnp.arange(rows_here, dtype=jnp.int32)
    longitude = lax.axis_index("cols") * cols_here + jnp.arange(cols_here, dtype=jnp.int32)
    inside_rows = latitude[None, :, None] < region_sizes[:, 0][:, None, None]
    offset = (longitude[None, None, :] - region_starts[:, None, None]) % width
    inside_cols = offset < region_sizes[:, 1][:, None, None]
    mask = jnp.where(inside_rows & inside_cols, 1.0, 0.0).astype(jnp.float32)[..., None]
    block_size = spectral_kernel.shape[2]
    total_blocks = spectral_kernel.shape[1]
    blocks = tokens.shape[3] // lax.axis_size("cols") // block_size
    first_block = lax.axis_index("cols") * blocks
    layout = (blocks, block_size, first_block)
    weights = (
        entry_gain,
        entry_shift,
        spectral_kernel,
        spectral_bias,
        spectral_mixer,
        spectral_offset,
        exit_scale,
        exit_center,
        dense_expand,
        dense_lift,
        dense_project,
        dense_return,
    )
    output, kept = advance(tokens, mask, weights, grids, layout)
    gradient_tokens, shared, local_blocks = retreat(cotangent, mask, kept, weights, grids, layout)
    (
        gain_part,
        shift_part,
        scale_part,
        center_part,
        expand_part,
        lift_part,
        project_part,
        return_part,
    ) = shared
    everywhere = ("rows", "cols")
    project_sum = lax.psum(project_part.astype(jnp.bfloat16), everywhere).astype(jnp.float32)
    expand_sum = lax.psum(expand_part.astype(jnp.bfloat16), everywhere).astype(jnp.float32)
    vectors = (gain_part, shift_part, scale_part, center_part, lift_part, return_part)
    sums = lax.psum(jnp.concatenate(vectors), everywhere)
    ends = [0]
    for vector in vectors:
        ends.append(ends[-1] + vector.shape[0])
    parts = [sums[low:high] for low, high in zip(ends[:-1], ends[1:])]
    summed = (*parts[:4], expand_sum, parts[4], project_sum, parts[5])
    kernel_local, bias_local, mixer_local, offset_local = local_blocks
    kernel_full = lax.dynamic_update_slice_in_dim(
        jnp.zeros((2, total_blocks, block_size, block_size), jnp.float32),
        kernel_local,
        first_block,
        1,
    )
    bias_full = lax.dynamic_update_slice_in_dim(
        jnp.zeros((2, total_blocks, block_size), jnp.float32), bias_local, first_block, 1
    )
    mixer_full = lax.dynamic_update_slice_in_dim(
        jnp.zeros((2, total_blocks, block_size, block_size), jnp.float32),
        mixer_local,
        first_block,
        1,
    )
    offset_full = lax.dynamic_update_slice_in_dim(
        jnp.zeros((2, total_blocks, block_size), jnp.float32), offset_local, first_block, 1
    )
    block_totals = lax.psum((kernel_full, bias_full, mixer_full, offset_full), ("rows", "cols"))
    return (
        output.astype(jnp.bfloat16),
        gradient_tokens,
        summed[0],
        summed[1],
        block_totals[0],
        block_totals[1],
        block_totals[2],
        block_totals[3],
        summed[2],
        summed[3],
        summed[4],
        summed[5],
        summed[6],
        summed[7],
    )


MESH = pl.DeviceIdType.MESH
wide = jnp.float32
low = jnp.bfloat16
by_last = (((1,), (1,)), ((), ()))
vmem = pl.BlockSpec(memory_space=pltpu.VMEM)


def dot(a, b):
    return jnp.dot(a, b, preferred_element_type=wide)


def dot_last(a, b):
    return lax.dot_general(a, b, by_last, preferred_element_type=wide)


def task_tables(height, width, rows_here, cols_here):
    modes = width // 2
    near = modes // 2
    column = np.arange(width)
    frequency = np.arange(modes)
    angle = (column[:, None] * frequency[None, :] % width).astype(np.float32) * np.float32(
        2.0 * math.pi / width
    )
    scale = np.float32(1.0 / math.sqrt(width))
    zonal = np.stack([np.cos(angle), -np.sin(angle)], 1) * scale
    factor = np.where(frequency == 0, 1.0, 2.0).astype(np.float32)
    inverse = (
        np.stack([np.cos(angle).T * factor[:, None], -np.sin(angle).T * factor[:, None]], 0) * scale
    )
    latitude = np.arange(height)
    turn = (latitude[:, None] * latitude[None, :] % height).astype(np.float32) * np.float32(
        2.0 * math.pi / height
    )
    cosine = np.cos(turn) / np.float32(math.sqrt(height))
    sine = np.sin(turn) / np.float32(math.sqrt(height))
    meridian = np.stack([np.stack([cosine, sine], -1), np.stack([-sine, cosine], -1)], 1)
    halves = width // cols_here
    split_f = zonal.reshape(halves, cols_here, 2, 2, near)
    to_modes = np.zeros((halves, 2, cols_here, 2, 2, 2, near), np.float32)
    split_g = inverse.reshape(2, 2, near, halves, cols_here)
    to_columns = np.zeros((2, 2, 2, near, halves, 2, cols_here), np.float32)
    for i in range(2):
        to_modes[:, i, :, :, i] = split_f.transpose(0, 1, 3, 2, 4)
        to_columns[:, i, :, :, :, i] = split_g.transpose(1, 0, 2, 3, 4)
    side = halves * 2 * cols_here
    to_modes = to_modes.reshape(side, side)
    to_columns = to_columns.reshape(side, side)
    pairs = rows_here // 2
    senders = height // rows_here
    order = np.zeros((height // 2, 2), np.int64)
    for core in range(2):
        for chip in range(senders // 2):
            for pair in range(pairs):
                for i in range(2):
                    order[(core * (senders // 2) + chip) * pairs + pair, i] = (
                        (chip * 2 + core) * rows_here + pair * 2 + i
                    )
    placed = meridian[:, :, order]
    ahead = np.zeros((2, 2, 2, height // 2, 2, 2, height), np.float32)
    for c in range(2):
        ahead[:, :, c, :, c] = placed.transpose(3, 4, 2, 1, 0)
    ahead = ahead.reshape(2, 2 * height, 4 * height)
    behind = ahead.reshape(4 * height, 4 * height).T
    return tuple(
        np.asarray(item, ml_dtypes.bfloat16)
        for item in (to_modes, to_columns, ahead, behind, np.eye(256, dtype=np.float32))
    )


def chip_device(chip, core, cols):
    return ((chip // cols) * 2 + core, chip % cols)


def swap_bits(value, mask, bits):
    out = 0
    for k in range(bits):
        bit = (value // (1 << k)) % 2
        if (mask >> k) & 1:
            bit = 1 - bit
        out = out + bit * (1 << k)
    return out


def greet(chips, cols):
    row = lax.axis_index("rows")
    core = row % 2
    me = (row // 2) * cols + lax.axis_index("cols")
    barrier = pltpu.get_barrier_semaphore()
    for step in range(1, chips):
        other = (me + step) % chips
        pl.semaphore_signal(
            barrier, inc=1, device_id=chip_device(other, core, cols), device_id_type=MESH
        )
    pl.semaphore_signal(
        barrier, inc=1, device_id=chip_device(me, 1 - core, cols), device_id_type=MESH
    )
    pl.semaphore_wait(barrier, chips)
    return me, core


def send_piece(src, dst, send_sem, recv_sem, target, me, core, cols):
    @pl.when(target == me)
    def _():
        pltpu.make_async_copy(src, dst, recv_sem).start()

    @pl.when(target != me)
    def _():
        pltpu.make_async_remote_copy(
            src_ref=src,
            dst_ref=dst,
            send_sem=send_sem,
            recv_sem=recv_sem,
            device_id=chip_device(target, core, cols),
            device_id_type=MESH,
        ).start()


def await_piece(ref, sem):
    pltpu.make_async_copy(ref, ref, sem).wait()


def to_feature_rows(out_ref, region, place, piece, eye):
    features = piece.shape[1]
    for low_end in range(0, features, 256):
        turned = dot_last(eye, piece[:, low_end : low_end + 256])
        out_ref[region, low_end : low_end + 256, place] = turned.astype(low)


def modes_first(block, group, half):
    columns = []
    for m in range(group):
        rows = block[m * half : (m + 1) * half]
        height = block.shape[1] // 4
        columns.append(
            jnp.concatenate(
                [
                    rows[:, (c * 2 + p) * height : (c * 2 + p + 1) * height]
                    for p in range(2)
                    for c in range(2)
                ],
                0,
            )
        )
    return jnp.concatenate(columns, 1)


def modes_last(block, group, half):
    height = block.shape[1] // group
    rows = []
    for m in range(group):
        part = block[:, m * height : (m + 1) * height]
        rows.append(
            jnp.concatenate(
                [
                    part[(p * 2 + c) * half : (p * 2 + c + 1) * half]
                    for c in range(2)
                    for p in range(2)
                ],
                1,
            )
        )
    return jnp.concatenate(rows, 0)


def filter_pass(sizes, me, core, produce, middle, consume, tables, work, sems):
    regions, blocks, block_size, chips, cols, tokens = sizes
    table_in, table_out, ahead, behind = tables
    sent, got, zonal, zonal_got, tall, flat, turned, back, sibling, leaving, coming = work
    send_a, recv_a, send_b, recv_b, send_c, recv_c, send_d, recv_d = sems
    lanes = 128
    senders = chips // cols
    pairs = tokens // lanes
    half = block_size // 2
    points = senders * pairs
    group = 4
    bits = (blocks - 1).bit_length()
    for region in range(regions):
        produce(region)
        for step in range(blocks - 1, -1, -1):
            target = region * blocks + swap_bits(me % blocks, step, bits)
            src = sent.at[region, pl.ds(pl.multiple_of(target % blocks * block_size, 32), block_size)]
            place = region * blocks + step
            send_piece(src, got.at[me], send_a.at[place], recv_a.at[me], target, me, core, cols)

    def zonal_step(chip, carry):
        for col in range(cols):
            await_piece(got.at[chip * cols + col], recv_a.at[chip * cols + col])
        for pair in range(pairs):
            x = jnp.concatenate(
                [got[chip * cols + col, :, pair * lanes : (pair + 1) * lanes] for col in range(cols)], 1
            )
            y = dot(x, table_in[...]).astype(low)
            for part in range(2):
                zonal[part, chip * pairs + pair] = y[:, part * lanes : (part + 1) * lanes]
        return carry

    lax.fori_loop(0, senders, zonal_step, 0)
    swap = pltpu.make_async_remote_copy(
        src_ref=zonal.at[1 - core],
        dst_ref=zonal_got,
        send_sem=send_b,
        recv_sem=recv_b,
        device_id=chip_device(me, 1 - core, cols),
        device_id_type=MESH,
    )
    swap.start()

    def widen(source, first):
        def step(point, carry):
            row = pl.multiple_of((first + point) * block_size, 32)
            tall[pl.ds(row, block_size), :] = source(point).astype(wide)
            return carry

        lax.fori_loop(0, points, step, 0)

    widen(lambda point: zonal[core, point], core * points)
    swap.wait()
    widen(lambda point: zonal_got[point], (1 - core) * points)
    modes = lanes // 4

    def turn_step(c, carry):
        x = jnp.concatenate(
            [tall[pl.ds(c + half * side, 2 * points, stride=block_size), :] for side in range(2)], 0
        )
        y = jnp.transpose(x)
        for i in range(4):
            flat[i, pl.ds(c, modes, stride=half), :] = y[i * modes : (i + 1) * modes]
        return carry

    lax.fori_loop(0, half, turn_step, 0)

    def mode_step(step, carry):
        rows = pl.ds(pl.multiple_of(step * group * half, 64), group * half)
        spectrum = 0.0
        for i in range(2):
            x = jnp.concatenate([flat[i * 2, rows, :], flat[i * 2 + 1, rows, :]], 1).astype(low)
            spectrum = spectrum + dot(x, ahead[i])
        out = modes_last(middle(step, modes_first(spectrum, group, half)), group, half)
        high = out.astype(low)
        rest = (out - high.astype(wide)).astype(low)
        y = (dot(high, behind[...]) + dot(rest, behind[...])).astype(low).astype(wide)
        for i in range(4):
            turned[i, rows, :] = y[:, i * lanes : (i + 1) * lanes]
        return carry

    lax.fori_loop(0, modes // group, mode_step, 0)

    def return_step(c, carry):
        x = jnp.concatenate([turned[i, pl.ds(c, modes, stride=half), :] for i in range(4)], 0)
        y = jnp.transpose(x)
        for side in range(2):
            tall[pl.ds(c + half * side, 2 * points, stride=block_size), :] = y[
                side * 2 * points : (side + 1) * 2 * points
            ]
        return carry

    lax.fori_loop(0, half, return_step, 0)

    def narrow(store, first):
        def step(point, carry):
            row = pl.multiple_of((first + point) * block_size, 32)
            store(point, tall[pl.ds(row, block_size), :].astype(low))
            return carry

        lax.fori_loop(0, points, step, 0)

    def to_sibling(point, value):
        back[point] = value

    def to_self(point, value):
        sibling[core, point] = value

    narrow(to_sibling, (1 - core) * points)
    swap_back = pltpu.make_async_remote_copy(
        src_ref=back,
        dst_ref=sibling.at[core],
        send_sem=send_c,
        recv_sem=recv_c,
        device_id=chip_device(me, 1 - core, cols),
        device_id_type=MESH,
    )
    swap_back.start()
    narrow(to_self, core * points)
    swap_back.wait_send()
    await_piece(sibling.at[1 - core], recv_c)

    def column_step(chip, carry):
        for pair in range(pairs):
            point = chip * pairs + pair
            x = jnp.concatenate([sibling[0, point], sibling[1, point]], 1)
            y = dot(x, table_out[...]).astype(low)
            for col in range(cols):
                leaving[chip * cols + col, :, pair * lanes : (pair + 1) * lanes] = y[
                    :, col * lanes : (col + 1) * lanes
                ]
        for col in range(cols):
            target = chip * cols + col
            dst = coming.at[
                me // blocks, pl.ds(pl.multiple_of(me % blocks * block_size, 32), block_size)
            ]
            send_piece(
                leaving.at[target], dst, send_d.at[target], recv_d.at[me], target, me, core, cols
            )
        return carry

    lax.fori_loop(0, senders, column_step, 0)
    for region in range(regions):

        def arrive(block, carry):
            ref = coming.at[region, pl.ds(pl.multiple_of(block * block_size, 32), block_size)]
            await_piece(ref, recv_d.at[region * blocks + block])
            return carry

        lax.fori_loop(0, blocks, arrive, 0)
        consume(region)

    for place in range(regions * blocks):
        region, step = place // blocks, place % blocks
        target = region * blocks + swap_bits(me % blocks, step, bits)

        @pl.when(target != me)
        def _():
            await_piece(got.at[0], send_a.at[place])

        @pl.when(place != me)
        def _():
            await_piece(leaving.at[0], send_d.at[place])


def work_shapes(sizes):
    regions, blocks, block_size, chips, cols, tokens = sizes
    lanes = 128
    features = blocks * block_size
    points = (chips // cols) * (tokens // lanes)
    rows = (lanes // 4) * (block_size // 2)
    return [
        pltpu.VMEM((regions, features, tokens), low),
        pltpu.VMEM((chips, block_size, tokens), low),
        pltpu.VMEM((2, points, block_size, lanes), low),
        pltpu.VMEM((points, block_size, lanes), low),
        pltpu.VMEM((2 * points * block_size, lanes), wide),
        pltpu.VMEM((4, rows, lanes), wide),
        pltpu.VMEM((4, rows, lanes), wide),
        pltpu.VMEM((points, block_size, lanes), low),
        pltpu.VMEM((2, points, block_size, lanes), low),
        pltpu.VMEM((chips, block_size, tokens), low),
        pltpu.VMEM((regions, features, tokens), low),
        pltpu.SemaphoreType.DMA((chips,)),
        pltpu.SemaphoreType.DMA((chips,)),
        pltpu.SemaphoreType.DMA,
        pltpu.SemaphoreType.DMA,
        pltpu.SemaphoreType.DMA,
        pltpu.SemaphoreType.DMA,
        pltpu.SemaphoreType.DMA((chips,)),
        pltpu.SemaphoreType.DMA((chips,)),
    ]


def normalise(value):
    centre = jnp.mean(value, -1, keepdims=True)
    centred = value - centre
    spread = jnp.mean(centred * centred, -1, keepdims=True)
    factor = lax.rsqrt(spread + norm_eps)
    return centred * factor, factor


def gelu_parts(value):
    curve = 0.5 * (1.0 + lax.erf(value * (1.0 / math.sqrt(2.0))))
    return curve


def gelu_slope(value):
    bell = jnp.exp(-0.5 * value * value) * (1.0 / math.sqrt(2.0 * math.pi))
    return gelu_parts(value) + value * bell


def forward_kernel(sizes, *refs):
    (
        tokens_ref,
        mask_ref,
        gain_ref,
        shift_ref,
        scale_ref,
        center_ref,
        kernel_ref,
        bias_ref,
        mixer_ref,
        offset_ref,
        to_modes,
        to_columns,
        ahead,
        behind,
        eye,
        mixed_ref,
        second_ref,
        spectrum_ref,
        first_ref,
        act_ref,
        pre_ref,
    ) = refs[:21]
    work, sems = refs[21:32], refs[32:]
    regions, blocks, block_size, chips, cols, tokens = sizes
    me, core = greet(chips, cols)
    sent, coming = work[0], work[-1]
    piece = 128

    def produce(region):
        def step(part, carry):
            rows = pl.ds(pl.multiple_of(region * tokens + part * piece, piece), piece)
            unit, factor = normalise(tokens_ref[rows, :].astype(wide))
            normed = unit * gain_ref[...] + shift_ref[...]
            place = pl.ds(pl.multiple_of(part * piece, piece), piece)
            to_feature_rows(sent, region, place, (mask_ref[rows, :] * normed).astype(low), eye[...])
            return carry

        lax.fori_loop(0, tokens // piece, step, 0)

    def middle(step, spectrum):
        spectrum = spectrum.astype(low)
        spectrum_ref[step] = spectrum
        first = dot(kernel_ref[...], spectrum) + bias_ref[...]
        first_ref[step] = first
        act = (first * gelu_parts(first)).astype(low)
        act_ref[step] = act
        second = dot(mixer_ref[...], act) + offset_ref[...]
        pre_ref[step] = second
        return second - shrink_width * jnp.tanh(second / shrink_width)

    def consume(region):
        def step(part, carry):
            rows = pl.ds(pl.multiple_of(region * tokens + part * 256, 256), 256)
            place = pl.ds(pl.multiple_of(part * 256, 256), 256)
            fields = jnp.concatenate(
                [
                    dot_last(eye[...], coming[region, first : first + 256, place])
                    for first in range(0, coming.shape[1], 256)
                ],
                1,
            )
            residual = tokens_ref[rows, :].astype(wide)
            unit, factor = normalise(residual)
            normed = unit * gain_ref[...] + shift_ref[...]
            mixed = residual + mask_ref[rows, :] * fields + normed
            mixed_ref[rows, :] = mixed
            unit, factor = normalise(mixed)
            second_ref[rows, :] = (unit * scale_ref[...] + center_ref[...]).astype(low)
            return carry

        lax.fori_loop(0, tokens // 256, step, 0)

    tables = (to_modes, to_columns, ahead, behind)
    filter_pass(sizes, me, core, produce, middle, consume, tables, work, sems)


def backward_kernel(sizes, *refs):
    (
        tokens_ref,
        mixed_back_ref,
        mask_ref,
        gain_ref,
        kernel_ref,
        mixer_ref,
        to_modes,
        to_columns,
        ahead,
        behind,
        eye,
        spectrum_ref,
        first_ref,
        act_ref,
        pre_ref,
        slope_ref,
        gain_slope,
        shift_slope,
        kernel_slope,
        bias_slope,
        mixer_slope,
        offset_slope,
    ) = refs[:22]
    work, sems = refs[22:33], refs[33:]
    regions, blocks, block_size, chips, cols, tokens = sizes
    me, core = greet(chips, cols)
    sent, coming = work[0], work[-1]
    piece = 128
    for ref in (gain_slope, shift_slope, kernel_slope, bias_slope, mixer_slope, offset_slope):
        ref[...] = jnp.zeros_like(ref)

    def produce(region):
        def step(part, carry):
            rows = pl.ds(pl.multiple_of(region * tokens + part * piece, piece), piece)
            place = pl.ds(pl.multiple_of(part * piece, piece), piece)
            values = (mask_ref[rows, :] * mixed_back_ref[rows, :]).astype(low)
            to_feature_rows(sent, region, place, values, eye[...])
            return carry

        lax.fori_loop(0, tokens // piece, step, 0)

    def middle(step, shrunk_back):
        level = jnp.tanh(pre_ref[step] / shrink_width)
        second = shrunk_back * (level * level)
        offset_slope[...] += jnp.sum(second.astype(low).astype(wide), 1, keepdims=True)
        second = second.astype(low)
        mixer_slope[...] += dot_last(act_ref[step], second)
        first = (dot(mixer_ref[...], second) * gelu_slope(first_ref[step])).astype(low)
        bias_slope[...] += jnp.sum(first.astype(wide), 1, keepdims=True)
        kernel_slope[...] += dot_last(spectrum_ref[step], first)
        return dot(kernel_ref[...], first)

    def consume(region):
        def step(part, carry):
            rows = pl.ds(pl.multiple_of(region * tokens + part * 256, 256), 256)
            place = pl.ds(pl.multiple_of(part * 256, 256), 256)
            fields = jnp.concatenate(
                [
                    dot_last(eye[...], coming[region, first : first + 256, place])
                    for first in range(0, coming.shape[1], 256)
                ],
                1,
            )
            unit, factor = normalise(tokens_ref[rows, :].astype(wide))
            mixed_back = mixed_back_ref[rows, :]
            normed_back = mixed_back + mask_ref[rows, :] * fields
            gain_slope[...] += jnp.sum(normed_back * unit, 0, keepdims=True)
            shift_slope[...] += jnp.sum(normed_back, 0, keepdims=True)
            pull = normed_back * gain_ref[...]
            pull = pull - jnp.mean(pull, -1, keepdims=True) - unit * jnp.mean(
                pull * unit, -1, keepdims=True
            )
            slope_ref[rows, :] = mixed_back + factor * pull
            return carry

        lax.fori_loop(0, tokens // 256, step, 0)

    tables = (to_columns, to_modes, ahead, behind)
    filter_pass(sizes, me, core, produce, middle, consume, tables, work, sems)


def call_filter(body, sizes, outs, cid, operands):
    shapes = [jax.ShapeDtypeStruct(shape, kind) for shape, kind in outs]
    return pl.pallas_call(
        functools.partial(body, sizes),
        out_shape=shapes,
        in_specs=[vmem] * len(operands),
        out_specs=[vmem] * len(shapes),
        scratch_shapes=work_shapes(sizes),
        compiler_params=pltpu.CompilerParams(
            collective_id=cid, has_side_effects=True, vmem_limit_bytes=58 * 1024 * 1024
        ),
    )(*operands)


def shards(
    tokens,
    region_sizes,
    region_starts,
    entry_gain,
    entry_shift,
    spectral_kernel,
    spectral_bias,
    spectral_mixer,
    spectral_offset,
    exit_scale,
    exit_center,
    dense_expand,
    dense_lift,
    dense_project,
    dense_return,
    cotangent,
):
    regions, rows_here, cols_here, features = tokens.shape
    row_devices = lax.axis_size("rows")
    cols = lax.axis_size("cols")
    blocks, block_size = spectral_kernel.shape[1:3]
    chips = row_devices // 2 * cols
    fits = (
        row_devices % 2 == 0
        and chips == regions * blocks
        and cols == 2
        and cols_here == 64
        and rows_here == 8
        and block_size == 96
        and blocks == 8
    )
    if not fits:
        return shards_general(
            tokens,
            region_sizes,
            region_starts,
            entry_gain,
            entry_shift,
            spectral_kernel,
            spectral_bias,
            spectral_mixer,
            spectral_offset,
            exit_scale,
            exit_center,
            dense_expand,
            dense_lift,
            dense_project,
            dense_return,
            cotangent,
        )
    height = rows_here * row_devices
    width = cols_here * cols
    latitude = lax.axis_index("rows") * rows_here + jnp.arange(rows_here, dtype=jnp.int32)
    longitude = lax.axis_index("cols") * cols_here + jnp.arange(cols_here, dtype=jnp.int32)
    inside_rows = latitude[None, :, None] < region_sizes[:, 0][:, None, None]
    offset = (longitude[None, None, :] - region_starts[:, None, None]) % width
    inside_cols = offset < region_sizes[:, 1][:, None, None]
    mask = jnp.where(inside_rows & inside_cols, 1.0, 0.0).astype(wide).reshape(-1, 1)
    patches = rows_here * cols_here
    count = regions * patches
    sizes = (regions, blocks, block_size, chips, cols, patches)
    block = ((lax.axis_index("rows") // 2) * cols + lax.axis_index("cols")) % blocks

    def own(weight):
        return lax.dynamic_slice_in_dim(weight, block, 1, 1)

    kernel = complex_matrix(own(spectral_kernel))[0]
    mixer = complex_matrix(own(spectral_mixer))[0]
    side = 2 * block_size
    kernel_bias = own(spectral_bias).reshape(side, 1)
    mixer_bias = own(spectral_offset).reshape(side, 1)
    to_modes, to_columns, ahead, behind, eye = task_tables(height, width, rows_here, cols_here)
    flat_tokens = tokens.reshape(count, features)
    upstream = cotangent.reshape(count, features)
    group = 4 * 128
    steps = width // 4 // 4
    kept_shape = (steps, side, group)
    mixed, second_norm, spectrum, first_pre, first_act, second_pre = call_filter(
        forward_kernel,
        sizes,
        (
            ((count, features), wide),
            ((count, features), low),
            (kept_shape, low),
            (kept_shape, wide),
            (kept_shape, low),
            (kept_shape, wide),
        ),
        1,
        (
            flat_tokens,
            mask,
            entry_gain[None],
            entry_shift[None],
            exit_scale[None],
            exit_center[None],
            kernel.T,
            kernel_bias,
            mixer.T,
            mixer_bias,
            to_modes,
            to_columns,
            ahead,
            behind,
            eye,
        ),
    )
    hidden_pre = dot(second_norm, dense_expand) + dense_lift
    hidden = gelu_exact(hidden_pre).astype(low)
    output = mixed + (dot(hidden, dense_project) + dense_return)
    project_part = jnp.einsum("tf,tc->fc", hidden, upstream, preferred_element_type=wide)
    return_part = jnp.sum(upstream.astype(wide), 0)
    hidden_back = dot_last(upstream, dense_project)
    pre_back = (hidden_back * gelu_slope(hidden_pre)).astype(low)
    expand_part = jnp.einsum("tc,tf->cf", second_norm, pre_back, preferred_element_type=wide)
    lift_part = jnp.sum(pre_back.astype(wide), 0)
    norm_back = dot_last(pre_back, dense_expand)
    unit, factor = normalise(mixed)
    scale_part = jnp.sum(norm_back * unit, 0)
    center_part = jnp.sum(norm_back, 0)
    pull = norm_back * exit_scale
    pull = pull - jnp.mean(pull, -1, keepdims=True) - unit * jnp.mean(pull * unit, -1, keepdims=True)
    mixed_back = upstream.astype(wide) + factor * pull
    everywhere = ("rows", "cols")
    project_sum = lax.psum(project_part.astype(low), everywhere).astype(wide)
    expand_sum = lax.psum(expand_part.astype(low), everywhere).astype(wide)
    slopes = call_filter(
        backward_kernel,
        sizes,
        (
            ((count, features), wide),
            ((1, features), wide),
            ((1, features), wide),
            ((side, side), wide),
            ((side, 1), wide),
            ((side, side), wide),
            ((side, 1), wide),
        ),
        2,
        (
            flat_tokens,
            mixed_back,
            mask,
            entry_gain[None],
            kernel,
            mixer,
            to_modes.T,
            to_columns.T,
            ahead,
            behind,
            eye,
            spectrum,
            first_pre,
            first_act,
            second_pre,
        ),
    )
    token_slope, gain_part, shift_part, kernel_part, bias_part, mixer_part, offset_part = slopes

    def spread(part):
        total = jnp.zeros(part.shape[:1] + (blocks,) + part.shape[2:], wide)
        return lax.dynamic_update_slice_in_dim(total, part, block, 1)

    whole = (
        spread(matrix_gradient(kernel_part[None], block_size)),
        spread(matrix_gradient(mixer_part[None], block_size)),
        spread(bias_part.reshape(2, 1, block_size)),
        spread(offset_part.reshape(2, 1, block_size)),
    )
    vectors = (
        gain_part[0],
        shift_part[0],
        scale_part,
        center_part,
        lift_part,
        return_part,
        whole[2].reshape(-1),
        whole[3].reshape(-1),
    )
    sums = lax.psum(jnp.concatenate(vectors), everywhere)
    parts = []
    first = 0
    for vector in vectors:
        parts.append(sums[first : first + vector.shape[0]])
        first += vector.shape[0]
    kernel_sum, mixer_sum = lax.psum((whole[0], whole[1]), everywhere)
    return (
        output.astype(low).reshape(tokens.shape),
        token_slope.reshape(tokens.shape),
        parts[0],
        parts[1],
        kernel_sum,
        parts[6].reshape(spectral_bias.shape),
        mixer_sum,
        parts[7].reshape(spectral_bias.shape),
        parts[2],
        parts[3],
        expand_sum,
        parts[4],
        project_sum,
        parts[5],
    )


def solution(mesh):
    placed = (
        P(None, "rows", "cols", None),
        P(),
        P(),
        P(),
        P(),
        P(),
        P(),
        P(),
        P(),
        P(),
        P(),
        P(),
        P(),
        P(),
        P(),
        P(None, "rows", "cols", None),
    )
    return jax.shard_map(
        shards,
        mesh=mesh,
        in_specs=placed,
        out_specs=(
            P(None, "rows", "cols", None),
            P(None, "rows", "cols", None),
            P(),
            P(),
            P(),
            P(),
            P(),
            P(),
            P(),
            P(),
            P(),
            P(),
            P(),
            P(),
        ),
        check_vma=False,
    )
```

```python
import functools
import math

import jax
import jax.numpy as jnp
import ml_dtypes
import numpy as np
from jax import lax
from jax.experimental import pallas as pl
from jax.experimental.pallas import tpu as pltpu
from jax.sharding import PartitionSpec as P

shrink_width = 0.01
norm_eps = 1e-06
highest = lax.Precision.HIGHEST


def tables(height, width, modes):
    column = jnp.arange(width, dtype=jnp.int32)
    frequency = jnp.arange(modes, dtype=jnp.int32)
    turns = column[:, None] * frequency[None, :] % width
    angle = turns.astype(jnp.float32) * (2.0 * math.pi / width)
    cosine = jnp.cos(angle)
    sine = jnp.sin(angle)
    scale = 1.0 / math.sqrt(width)
    forward_zonal = jnp.stack([cosine, -sine], 1) * scale
    factor = jnp.where(frequency == 0, 1.0, 2.0).astype(jnp.float32)
    inverse_zonal = jnp.stack([cosine.T * factor[:, None], -sine.T * factor[:, None]], 0) * scale
    latitude = jnp.arange(height, dtype=jnp.int32)
    meridian_turns = latitude[:, None] * latitude[None, :] % height
    meridian_angle = meridian_turns.astype(jnp.float32) * (2.0 * math.pi / height)
    meridian_cos = jnp.cos(meridian_angle) / math.sqrt(height)
    meridian_sin = jnp.sin(meridian_angle) / math.sqrt(height)
    meridian_table = jnp.stack(
        [jnp.stack([meridian_cos, meridian_sin], -1), jnp.stack([-meridian_sin, meridian_cos], -1)],
        1,
    )
    forward_low = forward_zonal.astype(jnp.bfloat16)
    inverse_low = inverse_zonal.astype(jnp.bfloat16)
    meridian_low = meridian_table.astype(jnp.bfloat16)
    meridian_wide = meridian_low.astype(jnp.float32)
    return (forward_low, inverse_low, meridian_low, meridian_wide)


def layer_norm(value, gain, shift):
    centre = jnp.mean(value, -1, keepdims=True)
    centred = value - centre
    spread = jnp.mean(centred * centred, -1, keepdims=True)
    return centred * lax.rsqrt(spread + norm_eps) * gain + shift


def gelu_exact(value):
    return jax.nn.gelu(value, approximate=False)


def shrink(value):
    return value - shrink_width * jnp.tanh(value / shrink_width)


def block_layout(spectrum, blocks, block_size):
    leading = spectrum.shape[:3]
    parts = spectrum.reshape(leading + (2, blocks, block_size))
    parts = jnp.moveaxis(parts, 3, 4)
    return parts.reshape((-1, blocks, 2 * block_size))


def spectral_layout(modes_flat, leading, blocks, block_size):
    parts = modes_flat.reshape(leading + (blocks, 2, block_size))
    parts = jnp.moveaxis(parts, 4, 3)
    return parts.reshape(leading + (2, blocks * block_size))


def complex_matrix(weight):
    real = weight[0]
    imaginary = weight[1]
    upper = jnp.concatenate([real, imaginary], 2)
    lower = jnp.concatenate([-imaginary, real], 2)
    return jnp.concatenate([upper, lower], 1)


def matrix_gradient(whole, block_size):
    upper = whole[:, :block_size]
    lower = whole[:, block_size:]
    real = upper[:, :, :block_size] + lower[:, :, block_size:]
    imaginary = upper[:, :, block_size:] - lower[:, :, :block_size]
    return jnp.stack([real, imaginary], 0)


def bias_rows(bias):
    return jnp.moveaxis(bias, 0, 1).reshape(bias.shape[1], 2 * bias.shape[2])


def bias_gradient(summed, block_size):
    return jnp.moveaxis(summed.reshape(summed.shape[0], 2, block_size), 1, 0)


def advance(tokens, mask, weights, grids, layout):
    (
        entry_gain,
        entry_shift,
        spectral_kernel,
        spectral_bias,
        spectral_mixer,
        spectral_offset,
        exit_scale,
        exit_center,
        dense_expand,
        dense_lift,
        dense_project,
        dense_return,
    ) = weights
    forward_zonal, inverse_zonal, meridian_table, meridian_wide = grids
    blocks, block_size, first_block = layout
    residual = tokens.astype(jnp.float32)
    normed = layer_norm(residual, entry_gain, entry_shift)
    sent = (mask * normed).astype(jnp.bfloat16)
    by_channel = lax.all_to_all(sent, "cols", split_axis=3, concat_axis=2, tiled=True)
    zonal = jnp.einsum(
        "rhwc,wpk->rhkpc", by_channel, forward_zonal, preferred_element_type=jnp.float32
    )
    by_mode = lax.all_to_all(
        zonal.astype(jnp.bfloat16), "rows", split_axis=2, concat_axis=1, tiled=True
    )
    spectrum = jnp.einsum(
        "kphq,rhmqc->rkmpc", meridian_table, by_mode, preferred_element_type=jnp.float32
    ).astype(jnp.bfloat16)
    leading = spectrum.shape[:3]
    modes_flat = block_layout(spectrum, blocks, block_size)
    kernel_matrix = complex_matrix(
        lax.dynamic_slice_in_dim(spectral_kernel, first_block, blocks, 1)
    )
    mixer_matrix = complex_matrix(lax.dynamic_slice_in_dim(spectral_mixer, first_block, blocks, 1))
    kernel_bias = bias_rows(lax.dynamic_slice_in_dim(spectral_bias, first_block, blocks, 1))
    mixer_bias = bias_rows(lax.dynamic_slice_in_dim(spectral_offset, first_block, blocks, 1))
    first_pre = (
        jnp.einsum("nbx,bxy->nby", modes_flat, kernel_matrix, preferred_element_type=jnp.float32)
        + kernel_bias
    )
    first_act = gelu_exact(first_pre).astype(jnp.bfloat16)
    second_pre = (
        jnp.einsum("nbx,bxy->nby", first_act, mixer_matrix, preferred_element_type=jnp.float32)
        + mixer_bias
    )
    shrunk = spectral_layout(shrink(second_pre), leading, blocks, block_size)
    back_meridian = jnp.einsum(
        "kphq,rkmpc->rhmqc", meridian_wide, shrunk, precision=highest
    ).astype(jnp.bfloat16)
    by_row = lax.all_to_all(back_meridian, "rows", split_axis=1, concat_axis=2, tiled=True)
    filtered = jnp.einsum(
        "rhkpc,pkw->rhwc", by_row, inverse_zonal, preferred_element_type=jnp.float32
    ).astype(jnp.bfloat16)
    by_token = lax.all_to_all(filtered, "cols", split_axis=2, concat_axis=3, tiled=True)
    mixed = residual + mask * by_token.astype(jnp.float32) + normed
    features = mixed.shape[-1]
    second_norm = (
        layer_norm(mixed, exit_scale, exit_center).astype(jnp.bfloat16).reshape(-1, features)
    )
    hidden_pre = jnp.dot(second_norm, dense_expand, preferred_element_type=jnp.float32) + dense_lift
    hidden = gelu_exact(hidden_pre).astype(jnp.bfloat16)
    output = mixed + (
        jnp.dot(hidden, dense_project, preferred_element_type=jnp.float32) + dense_return
    ).reshape(mixed.shape)
    kept = (
        residual,
        modes_flat,
        first_pre,
        first_act,
        second_pre,
        mixed,
        second_norm,
        hidden_pre,
        hidden,
        kernel_matrix,
        mixer_matrix,
        leading,
    )
    return (output, kept)


def retreat(cotangent, mask, kept, weights, grids, layout):
    (
        entry_gain,
        entry_shift,
        spectral_kernel,
        spectral_bias,
        spectral_mixer,
        spectral_offset,
        exit_scale,
        exit_center,
        dense_expand,
        dense_lift,
        dense_project,
        dense_return,
    ) = weights
    forward_zonal, inverse_zonal, meridian_table, meridian_wide = grids
    blocks, block_size, first_block = layout
    (
        residual,
        modes_flat,
        first_pre,
        first_act,
        second_pre,
        mixed,
        second_norm,
        hidden_pre,
        hidden,
        kernel_matrix,
        mixer_matrix,
        leading,
    ) = kept
    features = mixed.shape[-1]
    upstream = cotangent.reshape(-1, features)
    gradient_project = jnp.einsum("tf,tc->fc", hidden, upstream, preferred_element_type=jnp.float32)
    gradient_return = jnp.sum(upstream.astype(jnp.float32), 0)
    outer = (gradient_project, gradient_return)
    hidden_back = jnp.einsum(
        "tc,fc->tf", upstream, dense_project, preferred_element_type=jnp.float32
    )
    hidden_pull = jax.vjp(gelu_exact, hidden_pre)[1]
    pre_back = hidden_pull(hidden_back)[0].astype(jnp.bfloat16)
    gradient_expand = jnp.einsum(
        "tc,tf->cf", second_norm, pre_back, preferred_element_type=jnp.float32
    )
    gradient_lift = jnp.sum(pre_back.astype(jnp.float32), 0)
    norm_back = jnp.einsum(
        "tf,cf->tc", pre_back, dense_expand, preferred_element_type=jnp.float32
    ).reshape(mixed.shape)
    exit_pull = jax.vjp(layer_norm, mixed, exit_scale, exit_center)[1]
    mixed_part, gradient_scale, gradient_center = exit_pull(norm_back)
    inner = (gradient_expand, gradient_lift, gradient_scale, gradient_center)
    mixed_back = cotangent.astype(jnp.float32) + mixed_part
    filter_back = (mask * mixed_back).astype(jnp.bfloat16)
    channel_back = lax.all_to_all(filter_back, "cols", split_axis=3, concat_axis=2, tiled=True)
    zonal_back = jnp.einsum(
        "rhwc,pkw->rhkpc", channel_back, inverse_zonal, preferred_element_type=jnp.float32
    ).astype(jnp.bfloat16)
    meridian_back = lax.all_to_all(zonal_back, "rows", split_axis=2, concat_axis=1, tiled=True)
    shrunk_back = jnp.einsum(
        "kphq,rhmqc->rkmpc", meridian_table, meridian_back, preferred_element_type=jnp.float32
    )
    shrink_pull = jax.vjp(shrink, second_pre)[1]
    second_back = shrink_pull(block_layout(shrunk_back, blocks, block_size))[0].astype(jnp.bfloat16)
    mixer_whole = jnp.einsum(
        "nbx,nby->bxy", first_act, second_back, preferred_element_type=jnp.float32
    )
    offset_rows = jnp.sum(second_back.astype(jnp.float32), 0)
    activation_back = jnp.einsum(
        "nby,bxy->nbx", second_back, mixer_matrix, preferred_element_type=jnp.float32
    )
    first_pull = jax.vjp(gelu_exact, first_pre)[1]
    first_back = first_pull(activation_back)[0].astype(jnp.bfloat16)
    kernel_whole = jnp.einsum(
        "nbx,nby->bxy", modes_flat, first_back, preferred_element_type=jnp.float32
    )
    kernel_rows = jnp.sum(first_back.astype(jnp.float32), 0)
    spectrum_back = spectral_layout(
        jnp.einsum("nby,bxy->nbx", first_back, kernel_matrix, preferred_element_type=jnp.float32),
        leading,
        blocks,
        block_size,
    )
    modes_back = jnp.einsum(
        "kphq,rkmpc->rhmqc", meridian_wide, spectrum_back, precision=highest
    ).astype(jnp.bfloat16)
    row_back = lax.all_to_all(modes_back, "rows", split_axis=1, concat_axis=2, tiled=True)
    sent_back = jnp.einsum(
        "rhkpc,wpk->rhwc", row_back, forward_zonal, preferred_element_type=jnp.float32
    ).astype(jnp.bfloat16)
    token_back = lax.all_to_all(sent_back, "cols", split_axis=2, concat_axis=3, tiled=True)
    normed_back = mixed_back + mask * token_back.astype(jnp.float32)
    entry_pull = jax.vjp(layer_norm, residual, entry_gain, entry_shift)[1]
    residual_part, gradient_gain, gradient_shift = entry_pull(normed_back)
    gradient_tokens = mixed_back + residual_part
    shared = (
        gradient_gain,
        gradient_shift,
        inner[2],
        inner[3],
        inner[0],
        inner[1],
        outer[0],
        outer[1],
    )
    local_blocks = (
        matrix_gradient(kernel_whole, block_size),
        bias_gradient(kernel_rows, block_size),
        matrix_gradient(mixer_whole, block_size),
        bias_gradient(offset_rows, block_size),
    )
    return (gradient_tokens, shared, local_blocks)


def shards_general(
    tokens,
    region_sizes,
    region_starts,
    entry_gain,
    entry_shift,
    spectral_kernel,
    spectral_bias,
    spectral_mixer,
    spectral_offset,
    exit_scale,
    exit_center,
    dense_expand,
    dense_lift,
    dense_project,
    dense_return,
    cotangent,
):
    rows_here = tokens.shape[1]
    cols_here = tokens.shape[2]
    height = rows_here * lax.axis_size("rows")
    width = cols_here * lax.axis_size("cols")
    grids = tables(height, width, width // 2)
    latitude = lax.axis_index("rows") * rows_here + jnp.arange(rows_here, dtype=jnp.int32)
    longitude = lax.axis_index("cols") * cols_here + jnp.arange(cols_here, dtype=jnp.int32)
    inside_rows = latitude[None, :, None] < region_sizes[:, 0][:, None, None]
    offset = (longitude[None, None, :] - region_starts[:, None, None]) % width
    inside_cols = offset < region_sizes[:, 1][:, None, None]
    mask = jnp.where(inside_rows & inside_cols, 1.0, 0.0).astype(jnp.float32)[..., None]
    block_size = spectral_kernel.shape[2]
    total_blocks = spectral_kernel.shape[1]
    blocks = tokens.shape[3] // lax.axis_size("cols") // block_size
    first_block = lax.axis_index("cols") * blocks
    layout = (blocks, block_size, first_block)
    weights = (
        entry_gain,
        entry_shift,
        spectral_kernel,
        spectral_bias,
        spectral_mixer,
        spectral_offset,
        exit_scale,
        exit_center,
        dense_expand,
        dense_lift,
        dense_project,
        dense_return,
    )
    output, kept = advance(tokens, mask, weights, grids, layout)
    gradient_tokens, shared, local_blocks = retreat(cotangent, mask, kept, weights, grids, layout)
    (
        gain_part,
        shift_part,
        scale_part,
        center_part,
        expand_part,
        lift_part,
        project_part,
        return_part,
    ) = shared
    everywhere = ("rows", "cols")
    project_sum = lax.psum(project_part.astype(jnp.bfloat16), everywhere).astype(jnp.float32)
    expand_sum = lax.psum(expand_part.astype(jnp.bfloat16), everywhere).astype(jnp.float32)
    vectors = (gain_part, shift_part, scale_part, center_part, lift_part, return_part)
    sums = lax.psum(jnp.concatenate(vectors), everywhere)
    ends = [0]
    for vector in vectors:
        ends.append(ends[-1] + vector.shape[0])
    parts = [sums[low:high] for low, high in zip(ends[:-1], ends[1:])]
    summed = (*parts[:4], expand_sum, parts[4], project_sum, parts[5])
    kernel_local, bias_local, mixer_local, offset_local = local_blocks
    kernel_full = lax.dynamic_update_slice_in_dim(
        jnp.zeros((2, total_blocks, block_size, block_size), jnp.float32),
        kernel_local,
        first_block,
        1,
    )
    bias_full = lax.dynamic_update_slice_in_dim(
        jnp.zeros((2, total_blocks, block_size), jnp.float32), bias_local, first_block, 1
    )
    mixer_full = lax.dynamic_update_slice_in_dim(
        jnp.zeros((2, total_blocks, block_size, block_size), jnp.float32),
        mixer_local,
        first_block,
        1,
    )
    offset_full = lax.dynamic_update_slice_in_dim(
        jnp.zeros((2, total_blocks, block_size), jnp.float32), offset_local, first_block, 1
    )
    block_totals = lax.psum((kernel_full, bias_full, mixer_full, offset_full), ("rows", "cols"))
    return (
        output.astype(jnp.bfloat16),
        gradient_tokens,
        summed[0],
        summed[1],
        block_totals[0],
        block_totals[1],
        block_totals[2],
        block_totals[3],
        summed[2],
        summed[3],
        summed[4],
        summed[5],
        summed[6],
        summed[7],
    )


MESH = pl.DeviceIdType.MESH
wide = jnp.float32
low = jnp.bfloat16
by_last = (((1,), (1,)), ((), ()))
vmem = pl.BlockSpec(memory_space=pltpu.VMEM)


def dot(a, b):
    return jnp.dot(a, b, preferred_element_type=wide)


def dot_last(a, b):
    return lax.dot_general(a, b, by_last, preferred_element_type=wide)


def task_tables(height, width, rows_here, cols_here):
    modes = width // 2
    near = modes // 2
    column = np.arange(width)
    frequency = np.arange(modes)
    angle = (column[:, None] * frequency[None, :] % width).astype(np.float32) * np.float32(
        2.0 * math.pi / width
    )
    scale = np.float32(1.0 / math.sqrt(width))
    zonal = np.stack([np.cos(angle), -np.sin(angle)], 1) * scale
    factor = np.where(frequency == 0, 1.0, 2.0).astype(np.float32)
    inverse = (
        np.stack([np.cos(angle).T * factor[:, None], -np.sin(angle).T * factor[:, None]], 0) * scale
    )
    latitude = np.arange(height)
    turn = (latitude[:, None] * latitude[None, :] % height).astype(np.float32) * np.float32(
        2.0 * math.pi / height
    )
    cosine = np.cos(turn) / np.float32(math.sqrt(height))
    sine = np.sin(turn) / np.float32(math.sqrt(height))
    meridian = np.stack([np.stack([cosine, sine], -1), np.stack([-sine, cosine], -1)], 1)
    halves = width // cols_here
    split_f = zonal.reshape(halves, cols_here, 2, 2, near)
    to_modes = np.zeros((halves, 2, cols_here, 2, 2, 2, near), np.float32)
    split_g = inverse.reshape(2, 2, near, halves, cols_here)
    to_columns = np.zeros((2, 2, 2, near, halves, 2, cols_here), np.float32)
    for i in range(2):
        to_modes[:, i, :, :, i] = split_f.transpose(0, 1, 3, 2, 4)
        to_columns[:, i, :, :, :, i] = split_g.transpose(1, 0, 2, 3, 4)
    side = halves * 2 * cols_here
    to_modes = to_modes.reshape(side, side)
    to_columns = to_columns.reshape(side, side)
    pairs = rows_here // 2
    senders = height // rows_here
    order = np.zeros((height // 2, 2), np.int64)
    for core in range(2):
        for chip in range(senders // 2):
            for pair in range(pairs):
                for i in range(2):
                    order[(core * (senders // 2) + chip) * pairs + pair, i] = (
                        (chip * 2 + core) * rows_here + pair * 2 + i
                    )
    placed = meridian[:, :, order]
    ahead = np.zeros((2, 2, 2, height // 2, 2, 2, height), np.float32)
    for c in range(2):
        ahead[:, :, c, :, c] = placed.transpose(3, 4, 2, 1, 0)
    ahead = ahead.reshape(2, 2 * height, 4 * height)
    behind = ahead.reshape(4 * height, 4 * height).T
    return tuple(
        np.asarray(item, ml_dtypes.bfloat16)
        for item in (to_modes, to_columns, ahead, behind, np.eye(256, dtype=np.float32))
    )


def chip_device(chip, core, cols):
    return ((chip // cols) * 2 + core, chip % cols)


def swap_bits(value, mask, bits):
    out = 0
    for k in range(bits):
        bit = (value // (1 << k)) % 2
        if (mask >> k) & 1:
            bit = 1 - bit
        out = out + bit * (1 << k)
    return out


def greet(chips, cols):
    row = lax.axis_index("rows")
    core = row % 2
    me = (row // 2) * cols + lax.axis_index("cols")
    barrier = pltpu.get_barrier_semaphore()
    for step in range(1, chips):
        other = (me + step) % chips
        pl.semaphore_signal(
            barrier, inc=1, device_id=chip_device(other, core, cols), device_id_type=MESH
        )
    pl.semaphore_signal(
        barrier, inc=1, device_id=chip_device(me, 1 - core, cols), device_id_type=MESH
    )
    pl.semaphore_wait(barrier, chips)
    return me, core


def send_piece(src, dst, send_sem, recv_sem, target, me, core, cols):
    @pl.when(target == me)
    def _():
        pltpu.make_async_copy(src, dst, recv_sem).start()

    @pl.when(target != me)
    def _():
        pltpu.make_async_remote_copy(
            src_ref=src,
            dst_ref=dst,
            send_sem=send_sem,
            recv_sem=recv_sem,
            device_id=chip_device(target, core, cols),
            device_id_type=MESH,
        ).start()


def await_piece(ref, sem):
    pltpu.make_async_copy(ref, ref, sem).wait()


def to_feature_rows(out_ref, region, place, piece, eye):
    features = piece.shape[1]
    for low_end in range(0, features, 256):
        turned = dot_last(eye, piece[:, low_end : low_end + 256])
        out_ref[region, low_end : low_end + 256, place] = turned.astype(low)


def modes_first(block, group, half):
    columns = []
    for m in range(group):
        rows = block[m * half : (m + 1) * half]
        height = block.shape[1] // 4
        columns.append(
            jnp.concatenate(
                [
                    rows[:, (c * 2 + p) * height : (c * 2 + p + 1) * height]
                    for p in range(2)
                    for c in range(2)
                ],
                0,
            )
        )
    return jnp.concatenate(columns, 1)


def modes_last(block, group, half):
    height = block.shape[1] // group
    rows = []
    for m in range(group):
        part = block[:, m * height : (m + 1) * height]
        rows.append(
            jnp.concatenate(
                [
                    part[(p * 2 + c) * half : (p * 2 + c + 1) * half]
                    for c in range(2)
                    for p in range(2)
                ],
                1,
            )
        )
    return jnp.concatenate(rows, 0)


def filter_pass(sizes, me, core, produce, middle, consume, tables, work, sems, tick):
    regions, blocks, block_size, chips, cols, tokens = sizes
    table_in, table_out, ahead, behind = tables
    sent, got, zonal, zonal_got, tall, flat, back, sibling, leaving, coming = work
    send_a, recv_a, send_b, recv_b, send_c, recv_c, send_d, recv_d = sems
    lanes = 128
    senders = chips // cols
    pairs = tokens // lanes
    half = block_size // 2
    points = senders * pairs
    group = 4
    bits = (blocks - 1).bit_length()
    for region in range(regions):
        produce(region)
        for step in range(blocks - 1, -1, -1):
            target = region * blocks + swap_bits(me % blocks, step, bits)
            src = sent.at[region, pl.ds(pl.multiple_of(target % blocks * block_size, 32), block_size)]
            place = region * blocks + step
            send_piece(src, got.at[me], send_a.at[place], recv_a.at[me], target, me, core, cols)
    tick("sent")

    def zonal_step(chip, carry):
        for col in range(cols):
            await_piece(got.at[chip * cols + col], recv_a.at[chip * cols + col])
        for pair in range(pairs):
            x = jnp.concatenate(
                [got[chip * cols + col, :, pair * lanes : (pair + 1) * lanes] for col in range(cols)], 1
            )
            y = dot(x, table_in[...]).astype(low)
            for part in range(2):
                zonal[part, chip * pairs + pair] = y[:, part * lanes : (part + 1) * lanes]
        return carry

    lax.fori_loop(0, senders, zonal_step, 0)
    swap = pltpu.make_async_remote_copy(
        src_ref=zonal.at[1 - core],
        dst_ref=zonal_got,
        send_sem=send_b,
        recv_sem=recv_b,
        device_id=chip_device(me, 1 - core, cols),
        device_id_type=MESH,
    )
    swap.start()
    tick("zonal")

    def widen(source, first):
        def step(point, carry):
            row = pl.multiple_of((first + point) * block_size, 32)
            tall[pl.ds(row, block_size), :] = source(point).astype(wide)
            return carry

        lax.fori_loop(0, points, step, 0)

    widen(lambda point: zonal[core, point], core * points)
    swap.wait()
    widen(lambda point: zonal_got[point], (1 - core) * points)
    modes = lanes // 4

    def turn_step(c, carry):
        x = jnp.concatenate(
            [tall[pl.ds(c + half * side, 2 * points, stride=block_size), :] for side in range(2)], 0
        )
        y = jnp.transpose(x)
        for i in range(4):
            flat[i, pl.ds(c, modes, stride=half), :] = y[i * modes : (i + 1) * modes]
        return carry

    lax.fori_loop(0, half, turn_step, 0)
    tick("turned")

    def mode_step(step, carry):
        rows = pl.ds(pl.multiple_of(step * group * half, 64), group * half)
        spectrum = 0.0
        for i in range(2):
            x = jnp.concatenate([flat[i * 2, rows, :], flat[i * 2 + 1, rows, :]], 1).astype(low)
            spectrum = spectrum + dot(x, ahead[i])
        out = modes_last(middle(step, modes_first(spectrum, group, half)), group, half)
        high = out.astype(low)
        rest = (out - high.astype(wide)).astype(low)
        y = (dot(high, behind[...]) + dot(rest, behind[...])).astype(low).astype(wide)
        for i in range(4):
            flat[i, rows, :] = y[:, i * lanes : (i + 1) * lanes]
        return carry

    lax.fori_loop(0, modes // group // 2, mode_step, 0)
    tick("halfway")
    lax.fori_loop(modes // group // 2, modes // group, mode_step, 0)
    tick("modes")

    def return_step(c, carry):
        x = jnp.concatenate([flat[i, pl.ds(c, modes, stride=half), :] for i in range(4)], 0)
        y = jnp.transpose(x)
        for side in range(2):
            tall[pl.ds(c + half * side, 2 * points, stride=block_size), :] = y[
                side * 2 * points : (side + 1) * 2 * points
            ]
        return carry

    lax.fori_loop(0, half, return_step, 0)

    def narrow(store, first):
        def step(point, carry):
            row = pl.multiple_of((first + point) * block_size, 32)
            store(point, tall[pl.ds(row, block_size), :].astype(low))
            return carry

        lax.fori_loop(0, points, step, 0)

    def to_sibling(point, value):
        back[point] = value

    def to_self(point, value):
        sibling[core, point] = value

    narrow(to_sibling, (1 - core) * points)
    swap_back = pltpu.make_async_remote_copy(
        src_ref=back,
        dst_ref=sibling.at[core],
        send_sem=send_c,
        recv_sem=recv_c,
        device_id=chip_device(me, 1 - core, cols),
        device_id_type=MESH,
    )
    swap_back.start()
    tick("back")
    narrow(to_self, core * points)
    swap_back.wait_send()
    await_piece(sibling.at[1 - core], recv_c)

    def column_step(chip, carry):
        for pair in range(pairs):
            point = chip * pairs + pair
            x = jnp.concatenate([sibling[0, point], sibling[1, point]], 1)
            y = dot(x, table_out[...]).astype(low)
            for col in range(cols):
                leaving[chip * cols + col, :, pair * lanes : (pair + 1) * lanes] = y[
                    :, col * lanes : (col + 1) * lanes
                ]
        for col in range(cols):
            target = chip * cols + col
            dst = coming.at[
                me // blocks, pl.ds(pl.multiple_of(me % blocks * block_size, 32), block_size)
            ]
            send_piece(
                leaving.at[target], dst, send_d.at[target], recv_d.at[me], target, me, core, cols
            )
        return carry

    lax.fori_loop(0, senders, column_step, 0)
    tick("columns")
    for region in range(regions):

        def arrive(block, carry):
            ref = coming.at[region, pl.ds(pl.multiple_of(block * block_size, 32), block_size)]
            await_piece(ref, recv_d.at[region * blocks + block])
            return carry

        lax.fori_loop(0, blocks, arrive, 0)
        consume(region)
        tick("region")

    for place in range(regions * blocks):
        region, step = place // blocks, place % blocks
        target = region * blocks + swap_bits(me % blocks, step, bits)

        @pl.when(target != me)
        def _():
            await_piece(got.at[0], send_a.at[place])

        @pl.when(place != me)
        def _():
            await_piece(leaving.at[0], send_d.at[place])


def work_shapes(sizes):
    regions, blocks, block_size, chips, cols, tokens = sizes
    lanes = 128
    features = blocks * block_size
    points = (chips // cols) * (tokens // lanes)
    rows = (lanes // 4) * (block_size // 2)
    return [
        pltpu.VMEM((regions, features, tokens), low),
        pltpu.VMEM((chips, block_size, tokens), low),
        pltpu.VMEM((2, points, block_size, lanes), low),
        pltpu.VMEM((points, block_size, lanes), low),
        pltpu.VMEM((2 * points * block_size, lanes), wide),
        pltpu.VMEM((4, rows, lanes), wide),
        pltpu.VMEM((points, block_size, lanes), low),
        pltpu.VMEM((2, points, block_size, lanes), low),
        pltpu.VMEM((chips, block_size, tokens), low),
        pltpu.VMEM((regions, features, tokens), low),
        pltpu.SemaphoreType.DMA((chips,)),
        pltpu.SemaphoreType.DMA((chips,)),
        pltpu.SemaphoreType.DMA,
        pltpu.SemaphoreType.DMA,
        pltpu.SemaphoreType.DMA,
        pltpu.SemaphoreType.DMA,
        pltpu.SemaphoreType.DMA((chips,)),
        pltpu.SemaphoreType.DMA((chips,)),
    ]


def normalise(value):
    centre = jnp.mean(value, -1, keepdims=True)
    centred = value - centre
    spread = jnp.mean(centred * centred, -1, keepdims=True)
    factor = lax.rsqrt(spread + norm_eps)
    return centred * factor, factor


def gelu_parts(value):
    curve = 0.5 * (1.0 + lax.erf(value * (1.0 / math.sqrt(2.0))))
    return curve


def gelu_slope(value):
    bell = jnp.exp(-0.5 * value * value) * (1.0 / math.sqrt(2.0 * math.pi))
    return gelu_parts(value) + value * bell


def forward_kernel(sizes, *refs):
    (
        tokens_ref,
        mask_ref,
        gain_ref,
        shift_ref,
        scale_ref,
        center_ref,
        kernel_ref,
        bias_ref,
        mixer_ref,
        offset_ref,
        to_modes,
        to_columns,
        ahead,
        behind,
        eye,
        mixed_ref,
        second_ref,
        spectrum_ref,
        first_ref,
        act_ref,
        pre_ref,
    ) = refs[:21]
    work, sems = refs[21:31], refs[31:]
    regions, blocks, block_size, chips, cols, tokens = sizes
    me, core = greet(chips, cols)
    sent, coming = work[0], work[-1]
    piece = 128

    def produce(region):
        def step(part, carry):
            rows = pl.ds(pl.multiple_of(region * tokens + part * piece, piece), piece)
            unit, factor = normalise(tokens_ref[rows, :].astype(wide))
            normed = unit * gain_ref[...] + shift_ref[...]
            place = pl.ds(pl.multiple_of(part * piece, piece), piece)
            to_feature_rows(sent, region, place, (mask_ref[rows, :] * normed).astype(low), eye[...])
            return carry

        lax.fori_loop(0, tokens // piece, step, 0)

    def middle(step, spectrum):
        spectrum = spectrum.astype(low)
        spectrum_ref[step] = spectrum
        first = dot(kernel_ref[...], spectrum) + bias_ref[...]
        first_ref[step] = first
        act = (first * gelu_parts(first)).astype(low)
        act_ref[step] = act
        second = dot(mixer_ref[...], act) + offset_ref[...]
        pre_ref[step] = second
        return second - shrink_width * jnp.tanh(second / shrink_width)

    def consume(region):
        def step(part, carry):
            rows = pl.ds(pl.multiple_of(region * tokens + part * 256, 256), 256)
            place = pl.ds(pl.multiple_of(part * 256, 256), 256)
            fields = jnp.concatenate(
                [
                    dot_last(eye[...], coming[region, first : first + 256, place])
                    for first in range(0, coming.shape[1], 256)
                ],
                1,
            )
            residual = tokens_ref[rows, :].astype(wide)
            unit, factor = normalise(residual)
            normed = unit * gain_ref[...] + shift_ref[...]
            mixed = residual + mask_ref[rows, :] * fields + normed
            mixed_ref[rows, :] = mixed
            unit, factor = normalise(mixed)
            second_ref[rows, :] = (unit * scale_ref[...] + center_ref[...]).astype(low)
            return carry

        lax.fori_loop(0, tokens // 256, step, 0)

    tables = (to_modes, to_columns, ahead, behind)
    filter_pass(
        sizes, me, core, produce, middle, consume, tables, work, sems, lambda place: None
    )


def place_of(row, col):
    return {"core": row % 2, "x": (row // 2) % 2, "z": row // 4, "y": col}


def device_at(spot):
    return (spot["z"] * 4 + spot["x"] * 2 + spot["core"], spot["y"])


def across(spot, axis, step=1):
    size = 4 if axis == "z" else 2
    return device_at({**spot, axis: (spot[axis] + step) % size})


def remote(src, dst, send_sem, recv_sem, device):
    return pltpu.make_async_remote_copy(
        src_ref=src,
        dst_ref=dst,
        send_sem=send_sem,
        recv_sem=recv_sem,
        device_id=device,
        device_id_type=MESH,
    )


def add_rows(out_ref, out_row, terms, rows):
    step = 48

    def add(part, carry):
        total = 0.0
        for ref, row in terms:
            here = pl.ds(pl.multiple_of(row + part * step, 16), step)
            total = total + ref[here, :].astype(wide)
        there = pl.ds(pl.multiple_of(out_row + part * step, 16), step)
        out_ref[there, :] = total.astype(low)
        return carry

    lax.fori_loop(0, rows // step, add, 0)


def tile_sum(spot, order, own, total, halves, quarters, pieces, sends, recvs):
    first, second = order
    side = own.shape[0]
    half, quarter, piece = side // 2, side // 4, side // 16
    a, b, z = spot[first], spot[second], spot["z"]

    def part(ref, row, rows):
        return ref.at[pl.ds(pl.multiple_of(row, 16), rows)]

    mine_a = a * half
    mine_b = mine_a + b * quarter
    mine_z = mine_b + z * piece
    out = part(total, mine_z, piece)
    hop_a = remote(
        part(own, (1 - a) * half, half), halves, sends.at[0], recvs.at[0], across(spot, first)
    )
    hop_b = remote(
        part(halves, (1 - b) * quarter, quarter),
        quarters,
        sends.at[1],
        recvs.at[1],
        across(spot, second),
    )
    hops_z = [
        remote(
            part(quarters, (z + step) % 4 * piece, piece),
            pieces.at[step - 1],
            sends.at[1 + step],
            recvs.at[1 + step],
            across(spot, "z", step),
        )
        for step in (2, 1, 3)
    ]
    back_z = [
        remote(out, out, sends.at[4 + step], recvs.at[4 + step], across(spot, "z", step))
        for step in (2, 1, 3)
    ]
    quarter_ref = part(total, mine_b, quarter)
    half_ref = part(total, mine_a, half)
    back_b = remote(quarter_ref, quarter_ref, sends.at[8], recvs.at[8], across(spot, second))
    back_a = remote(half_ref, half_ref, sends.at[9], recvs.at[9], across(spot, first))
    back_core = remote(total, total, sends.at[10], recvs.at[10], across(spot, "core"))

    def start_a():
        hop_a.start()

    def start_b():
        hop_a.wait()
        add_rows(halves, 0, ((halves, 0), (own, mine_a)), half)
        hop_b.start()

    def start_z():
        hop_b.wait()
        add_rows(quarters, 0, ((quarters, 0), (halves, b * quarter)), quarter)
        for hop in hops_z:
            hop.start()

    def start_back_z():
        for hop in hops_z:
            hop.wait()
        terms = ((quarters, z * piece), (pieces.at[0], 0), (pieces.at[1], 0), (pieces.at[2], 0))
        add_rows(total, mine_z, terms, piece)
        for hop in back_z:
            hop.start()

    def start_back_b():
        for hop in back_z:
            hop.wait()
        back_b.start()

    def start_back_a():
        back_b.wait()
        back_a.start()

    def start_back_core():
        back_a.wait()
        back_core.start()

    def finish():
        back_core.wait()

    return (
        start_a,
        start_b,
        start_z,
        start_back_z,
        start_back_b,
        start_back_a,
        start_back_core,
        finish,
    )


def backward_kernel(sizes, *refs):
    (
        tokens_ref,
        mixed_back_ref,
        mask_ref,
        gain_ref,
        kernel_ref,
        mixer_ref,
        to_modes,
        to_columns,
        ahead,
        behind,
        eye,
        spectrum_ref,
        first_hbm,
        act_ref,
        pre_hbm,
        project_ref,
        expand_ref,
        vectors_ref,
        slope_ref,
        project_total,
        expand_total,
        gathered,
        vector_sum,
    ) = refs[:23]
    work, sems = refs[23:33], refs[33:41]
    (
        kernel_slope,
        bias_slope,
        mixer_slope,
        offset_slope,
        first_slots,
        pre_slots,
        slot_sems,
        halves,
        quarters,
        pieces,
        tile_sends,
        tile_recvs,
        slab,
        slab_sibling,
        slab_region,
        slab_sends,
        slab_recvs,
        vector_sent,
        vector_got,
        vector_sends,
        vector_recvs,
    ) = refs[41:]
    regions, blocks, block_size, chips, cols, tokens = sizes
    steps = spectrum_ref.shape[0]

    def fetch(step, slot):
        return [
            pltpu.make_async_copy(hbm.at[step], slots.at[slot], slot_sems.at[k, slot])
            for k, (hbm, slots) in enumerate(((first_hbm, first_slots), (pre_hbm, pre_slots)))
        ]

    for copy in fetch(0, 0):
        copy.start()
    me, core = greet(chips, cols)
    spot = place_of(lax.axis_index("rows"), lax.axis_index("cols"))
    block = me % blocks
    sent, coming = work[0], work[-1]
    piece = 128
    vector_sum[...] = vectors_ref[...]
    for ref in (kernel_slope, bias_slope, mixer_slope, offset_slope):
        ref[...] = jnp.zeros_like(ref)
    tiles = []
    for j in range(2):
        width = project_ref.shape[1]
        first = pl.multiple_of((core * 2 + j) * width, width)
        places = (project_total.at[pl.ds(first, width)], expand_total.at[:, pl.ds(first, width)])
        for k, own in enumerate((project_ref, expand_ref)):
            s = j * 2 + k
            order = ("x", "y") if j == 0 else ("y", "x")
            tiles.append(
                tile_sum(
                    spot,
                    order,
                    own.at[j],
                    places[k],
                    halves.at[s],
                    quarters.at[s],
                    pieces.at[s],
                    tile_sends.at[s],
                    tile_recvs.at[s],
                )
            )

    def run_tiles(phase, which=(0, 1, 2, 3)):
        for s in which:
            tiles[s][phase]()

    def produce(region):
        def step(part, carry):
            rows = pl.ds(pl.multiple_of(region * tokens + part * piece, piece), piece)
            place = pl.ds(pl.multiple_of(part * piece, piece), piece)
            values = (mask_ref[rows, :] * mixed_back_ref[rows, :]).astype(low)
            to_feature_rows(sent, region, place, values, eye[...])
            return carry

        lax.fori_loop(0, tokens // piece, step, 0)

    def middle(step, shrunk_back):
        slot = step % 2
        for copy in fetch(step, slot):
            copy.wait()

        @pl.when(step + 1 < steps)
        def _():
            for copy in fetch(step + 1, 1 - slot):
                copy.start()

        level = jnp.tanh(pre_slots[slot] / shrink_width)
        second = (shrunk_back * (level * level)).astype(low)
        offset_slope[...] += jnp.sum(second.astype(wide), 1, keepdims=True)
        mixer_slope[...] += dot_last(act_ref[step], second)
        first = (dot(mixer_ref[...], second) * gelu_slope(first_slots[slot])).astype(low)
        bias_slope[...] += jnp.sum(first.astype(wide), 1, keepdims=True)
        kernel_slope[...] += dot_last(spectrum_ref[step], first)
        return dot(kernel_ref[...], first)

    def consume(region):
        def step(part, carry):
            rows = pl.ds(pl.multiple_of(region * tokens + part * 256, 256), 256)
            place = pl.ds(pl.multiple_of(part * 256, 256), 256)
            fields = jnp.concatenate(
                [
                    dot_last(eye[...], coming[region, first : first + 256, place])
                    for first in range(0, coming.shape[1], 256)
                ],
                1,
            )
            unit, factor = normalise(tokens_ref[rows, :].astype(wide))
            mixed_back = mixed_back_ref[rows, :]
            normed_back = mixed_back + mask_ref[rows, :] * fields
            vector_sum[0:1, :] += jnp.sum(normed_back * unit, 0, keepdims=True)
            vector_sum[1:2, :] += jnp.sum(normed_back, 0, keepdims=True)
            pull = normed_back * gain_ref[...]
            pull = pull - jnp.mean(pull, -1, keepdims=True) - unit * jnp.mean(
                pull * unit, -1, keepdims=True
            )
            slope_ref[rows, :] = mixed_back + factor * pull
            return carry

        lax.fori_loop(0, tokens // 256, step, 0)

    side = 2 * block_size
    slab_core = remote(
        slab, slab_sibling, slab_sends.at[0], slab_recvs.at[0], across(spot, "core")
    )
    my_rows = pl.ds(pl.multiple_of(core * side, 32), side)
    slab_far = remote(
        slab_sibling.at[my_rows],
        slab_region,
        slab_sends.at[1],
        slab_recvs.at[1],
        chip_device((me + blocks) % chips, core, cols),
    )

    def slab_peer(step):
        other = me // blocks * blocks + (block + step) % blocks
        ref = gathered.at[block, my_rows]
        return remote(
            ref, ref, slab_sends.at[1 + step], slab_recvs.at[1 + step], chip_device(other, core, cols)
        )

    slab_last = remote(
        gathered.at[:, my_rows],
        gathered.at[:, my_rows],
        slab_sends.at[1 + blocks],
        slab_recvs.at[1 + blocks],
        across(spot, "core"),
    )

    def slab_start():
        for k, (weight, bias) in enumerate(
            ((kernel_slope, bias_slope), (mixer_slope, offset_slope))
        ):
            whole = weight[...]
            upper, lower = whole[:block_size], whole[block_size:]
            first = k * side
            slab[first : first + block_size, :block_size] = (
                upper[:, :block_size] + lower[:, block_size:]
            )
            slab[first + block_size : first + side, :block_size] = (
                upper[:, block_size:] - lower[:, :block_size]
            )
            slab[first : first + side, block_size:] = jnp.broadcast_to(
                bias[...], (side, slab.shape[1] - block_size)
            )
        slab_core.start()

    def slab_regions():
        slab_core.wait()
        slab_sibling[...] = slab_sibling[...] + slab[...]
        slab_far.start()

    def slab_blocks():
        slab_far.wait()
        gathered[block, my_rows] = slab_region[...] + slab_sibling[my_rows, :]
        for step in range(1, blocks):
            slab_peer(step).start()

    def slab_cores():
        for step in range(1, blocks):
            slab_peer(step).wait()
        slab_last.start()

    regions_seen = []

    def tick(place):
        if place == "sent":
            run_tiles(0)
        if place == "zonal":
            run_tiles(1)
        if place == "turned":
            run_tiles(2)
        if place == "modes":
            run_tiles(3)
            slab_start()
        if place == "back":
            slab_regions()
        if place == "columns":
            run_tiles(4)
            slab_blocks()
        if place == "region":
            regions_seen.append(place)
            if len(regions_seen) == 1:
                run_tiles(5)
                slab_cores()

    tables = (to_columns, to_modes, ahead, behind)
    filter_pass(sizes, me, core, produce, middle, consume, tables, work, sems, tick)
    hops = [
        remote(
            vector_sent.at[k],
            vector_got.at[k],
            vector_sends.at[k],
            vector_recvs.at[k],
            device,
        )
        for k, device in enumerate(
            (
                across(spot, "core"),
                across(spot, "x"),
                across(spot, "y"),
                device_at({**spot, "z": spot["z"] // 2 * 2 + 1 - spot["z"] % 2}),
                across(spot, "z", 2),
            )
        )
    ]
    for k, hop in enumerate(hops):
        vector_sent[k] = vector_sum[...]
        hop.start()
        if k == 0:
            run_tiles(6)
            slab_last.wait()
        hop.wait()
        vector_sum[...] = vector_sum[...] + vector_got[k]
    run_tiles(7)


def call_filter(body, sizes, outs, cid, operands, spaces=(), scratch=()):
    shapes = [jax.ShapeDtypeStruct(shape, kind) for shape, kind in outs]
    anywhere = pl.BlockSpec(memory_space=pl.ANY)
    return pl.pallas_call(
        functools.partial(body, sizes),
        out_shape=shapes,
        in_specs=[anywhere if place in spaces else vmem for place in range(len(operands))],
        out_specs=[vmem] * len(shapes),
        scratch_shapes=[*work_shapes(sizes), *scratch],
        compiler_params=pltpu.CompilerParams(
            collective_id=cid, has_side_effects=True, vmem_limit_bytes=60 * 1024 * 1024
        ),
    )(*operands)


def backward_scratch(sizes, features, steps):
    regions, blocks, block_size, chips, cols, tokens = sizes
    side = 2 * block_size
    dma = pltpu.SemaphoreType.DMA
    return (
        pltpu.VMEM((side, side), wide),
        pltpu.VMEM((side, 1), wide),
        pltpu.VMEM((side, side), wide),
        pltpu.VMEM((side, 1), wide),
        pltpu.VMEM((2, side, 512), wide),
        pltpu.VMEM((2, side, 512), wide),
        dma((2, 2)),
        pltpu.VMEM((4, features // 2, features), low),
        pltpu.VMEM((4, features // 4, features), low),
        pltpu.VMEM((4, 3, features // 16, features), low),
        dma((4, 11)),
        dma((4, 11)),
        pltpu.VMEM((2 * side, 128), wide),
        pltpu.VMEM((2 * side, 128), wide),
        pltpu.VMEM((side, 128), wide),
        dma((2 + blocks,)),
        dma((2 + blocks,)),
        pltpu.VMEM((5, 16, features), wide),
        pltpu.VMEM((5, 16, features), wide),
        dma((5,)),
        dma((5,)),
    )


by_first = (((0,), (0,)), ((), ()))


def dot_first(a, b):
    return lax.dot_general(a, b, by_first, preferred_element_type=wide)


def dense_kernel(sizes, *refs):
    tile, half_tiles, cols = sizes
    (
        second_ref,
        mixed_ref,
        up_ref,
        scale_ref,
        expand_ref,
        lift_ref,
        project_ref,
        return_ref,
        out_ref,
        mixed_back_ref,
        project_half,
        expand_half,
        vectors,
        out_sum,
        back_sum,
        hidden_tile,
        back_tile,
        project_sent,
        expand_sent,
        project_got,
        expand_got,
        sent_sem,
        got_sem,
    ) = refs
    row = lax.axis_index("rows")
    core = row % 2
    sibling = (row - core + 1 - core, lax.axis_index("cols"))
    barrier = pltpu.get_barrier_semaphore()
    pl.semaphore_signal(barrier, inc=1, device_id=sibling, device_id_type=MESH)
    count = second_ref.shape[0]
    piece = 512

    def tile_step(place):
        here = pl.ds(pl.multiple_of(place * tile, tile), tile)

        def piece_step(part, carry):
            rows = pl.ds(pl.multiple_of(part * piece, piece), piece)
            pre = dot(second_ref[rows, :], expand_ref[:, here]) + lift_ref[:, here]
            back = dot_last(up_ref[rows, :], project_ref[here, :])
            curve = gelu_parts(pre)
            bell = jnp.exp(-0.5 * pre * pre) * (1.0 / math.sqrt(2.0 * math.pi))
            hidden = (pre * curve).astype(low)
            hidden_tile[rows, :] = hidden
            pre_back = (back * (curve + pre * bell)).astype(low)
            back_tile[rows, :] = pre_back
            out_sum[rows, :] += dot(hidden, project_ref[here, :])
            back_sum[rows, :] += dot_last(pre_back, expand_ref[:, here])
            return carry + jnp.sum(pre_back.astype(wide), 0, keepdims=True)

        lift = lax.fori_loop(0, count // piece, piece_step, jnp.zeros((1, tile), wide))
        vectors[pl.ds(5 + place, 1), :] = lift
        return (
            dot_first(hidden_tile[...], up_ref[...]),
            dot_first(second_ref[...], back_tile[...]),
        )

    def start_step(part, carry):
        rows = pl.ds(pl.multiple_of(part * piece, piece), piece)
        out_sum[rows, :] = mixed_ref[rows, :] + return_ref[...]
        back_sum[rows, :] = jnp.zeros((piece, back_sum.shape[1]), wide)
        return carry + jnp.sum(up_ref[rows, :].astype(wide), 0, keepdims=True)

    vectors[...] = jnp.zeros_like(vectors)
    vectors[4:5, :] = lax.fori_loop(0, count // piece, start_step, jnp.zeros((1, tile), wide))
    pl.semaphore_wait(barrier, 1)

    def copies(place):
        return [
            pltpu.make_async_remote_copy(
                src_ref=src.at[place],
                dst_ref=dst.at[place],
                send_sem=sent_sem.at[k, place],
                recv_sem=got_sem.at[k, place],
                device_id=sibling,
                device_id_type=MESH,
            )
            for k, (src, dst) in enumerate(
                ((project_sent, project_got), (expand_sent, expand_got))
            )
        ]

    def away_step(place, carry):
        project, expand = tile_step((1 - core) * half_tiles + place)
        project_sent[place] = project.astype(low)
        expand_sent[place] = expand.astype(low)
        for copy in copies(place):
            copy.start()
        return carry

    lax.fori_loop(0, half_tiles, away_step, 0)

    def home_step(place, carry):
        project, expand = tile_step(core * half_tiles + place)
        for copy in copies(place):
            copy.wait()
        project_half[place] = (project + project_got[place].astype(wide)).astype(low)
        expand_half[place] = (expand + expand_got[place].astype(wide)).astype(low)
        return carry

    lax.fori_loop(0, half_tiles, home_step, 0)

    def end_step(part, carry):
        rows = pl.ds(pl.multiple_of(part * piece, piece), piece)
        out_ref[rows, :] = out_sum[rows, :].astype(low)
        unit, factor = normalise(mixed_ref[rows, :])
        norm_back = back_sum[rows, :]
        vectors[2:3, :] += jnp.sum(norm_back * unit, 0, keepdims=True)
        vectors[3:4, :] += jnp.sum(norm_back, 0, keepdims=True)
        pull = norm_back * scale_ref[...]
        pull = pull - jnp.mean(pull, -1, keepdims=True) - unit * jnp.mean(
            pull * unit, -1, keepdims=True
        )
        mixed_back_ref[rows, :] = up_ref[rows, :].astype(wide) + factor * pull
        return carry

    lax.fori_loop(0, count // piece, end_step, 0)


def call_dense(second_norm, mixed, upstream, exit_scale, expand, lift, project, returned, tile, cid):
    count, features = second_norm.shape
    hidden = expand.shape[1]
    half_tiles = hidden // tile // 2
    tall = (half_tiles, tile, features)
    broad = (half_tiles, features, tile)
    outs = (
        ((count, features), low),
        ((count, features), wide),
        (tall, low),
        (broad, low),
        ((16, features), wide),
    )
    shapes = [jax.ShapeDtypeStruct(shape, kind) for shape, kind in outs]
    work = 6 * count * features * hidden * 2
    return pl.pallas_call(
        functools.partial(dense_kernel, (tile, half_tiles, 0)),
        out_shape=shapes,
        in_specs=[vmem] * 8,
        out_specs=[vmem] * len(shapes),
        scratch_shapes=[
            pltpu.VMEM((count, features), wide),
            pltpu.VMEM((count, features), wide),
            pltpu.VMEM((count, tile), low),
            pltpu.VMEM((count, tile), low),
            pltpu.VMEM(tall, low),
            pltpu.VMEM(broad, low),
            pltpu.VMEM(tall, low),
            pltpu.VMEM(broad, low),
            pltpu.SemaphoreType.DMA((2, half_tiles)),
            pltpu.SemaphoreType.DMA((2, half_tiles)),
        ],
        compiler_params=pltpu.CompilerParams(
            collective_id=cid, has_side_effects=True, vmem_limit_bytes=58 * 1024 * 1024
        ),
        cost_estimate=pl.CostEstimate(flops=work, bytes_accessed=40000000, transcendentals=0),
    )(second_norm, mixed, upstream, exit_scale, expand, lift, project, returned)


def shards(
    tokens,
    region_sizes,
    region_starts,
    entry_gain,
    entry_shift,
    spectral_kernel,
    spectral_bias,
    spectral_mixer,
    spectral_offset,
    exit_scale,
    exit_center,
    dense_expand,
    dense_lift,
    dense_project,
    dense_return,
    cotangent,
):
    regions, rows_here, cols_here, features = tokens.shape
    row_devices = lax.axis_size("rows")
    cols = lax.axis_size("cols")
    blocks, block_size = spectral_kernel.shape[1:3]
    chips = row_devices // 2 * cols
    fits = (
        row_devices % 2 == 0
        and chips == regions * blocks
        and cols == 2
        and cols_here == 64
        and rows_here == 8
        and block_size == 96
        and blocks == 8
        and regions == 2
        and dense_expand.shape == (features, 4 * features)
    )
    if not fits:
        return shards_general(
            tokens,
            region_sizes,
            region_starts,
            entry_gain,
            entry_shift,
            spectral_kernel,
            spectral_bias,
            spectral_mixer,
            spectral_offset,
            exit_scale,
            exit_center,
            dense_expand,
            dense_lift,
            dense_project,
            dense_return,
            cotangent,
        )
    height = rows_here * row_devices
    width = cols_here * cols
    latitude = lax.axis_index("rows") * rows_here + jnp.arange(rows_here, dtype=jnp.int32)
    longitude = lax.axis_index("cols") * cols_here + jnp.arange(cols_here, dtype=jnp.int32)
    inside_rows = latitude[None, :, None] < region_sizes[:, 0][:, None, None]
    offset = (longitude[None, None, :] - region_starts[:, None, None]) % width
    inside_cols = offset < region_sizes[:, 1][:, None, None]
    mask = jnp.where(inside_rows & inside_cols, 1.0, 0.0).astype(wide).reshape(-1, 1)
    patches = rows_here * cols_here
    count = regions * patches
    sizes = (regions, blocks, block_size, chips, cols, patches)
    block = ((lax.axis_index("rows") // 2) * cols + lax.axis_index("cols")) % blocks

    def own(weight):
        return lax.dynamic_slice_in_dim(weight, block, 1, 1)

    kernel = complex_matrix(own(spectral_kernel))[0]
    mixer = complex_matrix(own(spectral_mixer))[0]
    side = 2 * block_size
    kernel_bias = own(spectral_bias).reshape(side, 1)
    mixer_bias = own(spectral_offset).reshape(side, 1)
    to_modes, to_columns, ahead, behind, eye = task_tables(height, width, rows_here, cols_here)
    flat_tokens = tokens.reshape(count, features)
    upstream = cotangent.reshape(count, features)
    group = 4 * 128
    steps = width // 4 // 4
    kept_shape = (steps, side, group)
    mixed, second_norm, spectrum, first_pre, first_act, second_pre = call_filter(
        forward_kernel,
        sizes,
        (
            ((count, features), wide),
            ((count, features), low),
            (kept_shape, low),
            (kept_shape, wide),
            (kept_shape, low),
            (kept_shape, wide),
        ),
        1,
        (
            flat_tokens,
            mask,
            entry_gain[None],
            entry_shift[None],
            exit_scale[None],
            exit_center[None],
            kernel.T,
            kernel_bias,
            mixer.T,
            mixer_bias,
            to_modes,
            to_columns,
            ahead,
            behind,
            eye,
        ),
    )
    output, mixed_back, project_half, expand_half, vectors = call_dense(
        second_norm,
        mixed,
        upstream,
        exit_scale[None],
        dense_expand,
        dense_lift[None],
        dense_project,
        dense_return[None],
        features,
        3,
    )
    slope, project_sum, expand_sum, gathered, sums = call_filter(
        backward_kernel,
        sizes,
        (
            ((count, features), wide),
            (dense_project.shape, low),
            (dense_expand.shape, low),
            ((blocks, 2 * side, 128), wide),
            ((16, features), wide),
        ),
        2,
        (
            flat_tokens,
            mixed_back,
            mask,
            entry_gain[None],
            kernel,
            mixer,
            to_modes.T,
            to_columns.T,
            ahead,
            behind,
            eye,
            spectrum,
            first_pre,
            first_act,
            second_pre,
            project_half,
            expand_half,
            vectors,
        ),
        (12, 14),
        backward_scratch(sizes, features, steps),
    )
    weights = gathered[:, :, :block_size].reshape(blocks, 2, 2, block_size, block_size)
    weights = weights.transpose(1, 2, 0, 3, 4)
    biases = gathered[:, :, block_size].reshape(blocks, 2, 2, block_size).transpose(1, 2, 0, 3)
    return (
        output.reshape(tokens.shape),
        slope.reshape(tokens.shape),
        sums[0],
        sums[1],
        weights[0],
        biases[0],
        weights[1],
        biases[1],
        sums[2],
        sums[3],
        expand_sum.astype(wide),
        sums[5:9].reshape(-1),
        project_sum.astype(wide),
        sums[4],
    )


def solution(mesh):
    placed = (
        P(None, "rows", "cols", None),
        P(),
        P(),
        P(),
        P(),
        P(),
        P(),
        P(),
        P(),
        P(),
        P(),
        P(),
        P(),
        P(),
        P(),
        P(None, "rows", "cols", None),
    )
    return jax.shard_map(
        shards,
        mesh=mesh,
        in_specs=placed,
        out_specs=(
            P(None, "rows", "cols", None),
            P(None, "rows", "cols", None),
            P(),
            P(),
            P(),
            P(),
            P(),
            P(),
            P(),
            P(),
            P(),
            P(),
            P(),
            P(),
        ),
        check_vma=False,
    )
```

```python
import functools
import math

import jax
import jax.numpy as jnp
import ml_dtypes
import numpy as np
from jax import lax
from jax.experimental import pallas as pl
from jax.experimental.pallas import tpu as pltpu
from jax.sharding import PartitionSpec as P

shrink_width = 0.01
norm_eps = 1e-06
highest = lax.Precision.HIGHEST


def tables(height, width, modes):
    column = jnp.arange(width, dtype=jnp.int32)
    frequency = jnp.arange(modes, dtype=jnp.int32)
    turns = column[:, None] * frequency[None, :] % width
    angle = turns.astype(jnp.float32) * (2.0 * math.pi / width)
    cosine = jnp.cos(angle)
    sine = jnp.sin(angle)
    scale = 1.0 / math.sqrt(width)
    forward_zonal = jnp.stack([cosine, -sine], 1) * scale
    factor = jnp.where(frequency == 0, 1.0, 2.0).astype(jnp.float32)
    inverse_zonal = jnp.stack([cosine.T * factor[:, None], -sine.T * factor[:, None]], 0) * scale
    latitude = jnp.arange(height, dtype=jnp.int32)
    meridian_turns = latitude[:, None] * latitude[None, :] % height
    meridian_angle = meridian_turns.astype(jnp.float32) * (2.0 * math.pi / height)
    meridian_cos = jnp.cos(meridian_angle) / math.sqrt(height)
    meridian_sin = jnp.sin(meridian_angle) / math.sqrt(height)
    meridian_table = jnp.stack(
        [jnp.stack([meridian_cos, meridian_sin], -1), jnp.stack([-meridian_sin, meridian_cos], -1)],
        1,
    )
    forward_low = forward_zonal.astype(jnp.bfloat16)
    inverse_low = inverse_zonal.astype(jnp.bfloat16)
    meridian_low = meridian_table.astype(jnp.bfloat16)
    meridian_wide = meridian_low.astype(jnp.float32)
    return (forward_low, inverse_low, meridian_low, meridian_wide)


def layer_norm(value, gain, shift):
    centre = jnp.mean(value, -1, keepdims=True)
    centred = value - centre
    spread = jnp.mean(centred * centred, -1, keepdims=True)
    return centred * lax.rsqrt(spread + norm_eps) * gain + shift


def gelu_exact(value):
    return jax.nn.gelu(value, approximate=False)


def shrink(value):
    return value - shrink_width * jnp.tanh(value / shrink_width)


def block_layout(spectrum, blocks, block_size):
    leading = spectrum.shape[:3]
    parts = spectrum.reshape(leading + (2, blocks, block_size))
    parts = jnp.moveaxis(parts, 3, 4)
    return parts.reshape((-1, blocks, 2 * block_size))


def spectral_layout(modes_flat, leading, blocks, block_size):
    parts = modes_flat.reshape(leading + (blocks, 2, block_size))
    parts = jnp.moveaxis(parts, 4, 3)
    return parts.reshape(leading + (2, blocks * block_size))


def complex_matrix(weight):
    real = weight[0]
    imaginary = weight[1]
    upper = jnp.concatenate([real, imaginary], 2)
    lower = jnp.concatenate([-imaginary, real], 2)
    return jnp.concatenate([upper, lower], 1)


def matrix_gradient(whole, block_size):
    upper = whole[:, :block_size]
    lower = whole[:, block_size:]
    real = upper[:, :, :block_size] + lower[:, :, block_size:]
    imaginary = upper[:, :, block_size:] - lower[:, :, :block_size]
    return jnp.stack([real, imaginary], 0)


def bias_rows(bias):
    return jnp.moveaxis(bias, 0, 1).reshape(bias.shape[1], 2 * bias.shape[2])


def bias_gradient(summed, block_size):
    return jnp.moveaxis(summed.reshape(summed.shape[0], 2, block_size), 1, 0)


def advance(tokens, mask, weights, grids, layout):
    (
        entry_gain,
        entry_shift,
        spectral_kernel,
        spectral_bias,
        spectral_mixer,
        spectral_offset,
        exit_scale,
        exit_center,
        dense_expand,
        dense_lift,
        dense_project,
        dense_return,
    ) = weights
    forward_zonal, inverse_zonal, meridian_table, meridian_wide = grids
    blocks, block_size, first_block = layout
    residual = tokens.astype(jnp.float32)
    normed = layer_norm(residual, entry_gain, entry_shift)
    sent = (mask * normed).astype(jnp.bfloat16)
    by_channel = lax.all_to_all(sent, "cols", split_axis=3, concat_axis=2, tiled=True)
    zonal = jnp.einsum(
        "rhwc,wpk->rhkpc", by_channel, forward_zonal, preferred_element_type=jnp.float32
    )
    by_mode = lax.all_to_all(
        zonal.astype(jnp.bfloat16), "rows", split_axis=2, concat_axis=1, tiled=True
    )
    spectrum = jnp.einsum(
        "kphq,rhmqc->rkmpc", meridian_table, by_mode, preferred_element_type=jnp.float32
    ).astype(jnp.bfloat16)
    leading = spectrum.shape[:3]
    modes_flat = block_layout(spectrum, blocks, block_size)
    kernel_matrix = complex_matrix(
        lax.dynamic_slice_in_dim(spectral_kernel, first_block, blocks, 1)
    )
    mixer_matrix = complex_matrix(lax.dynamic_slice_in_dim(spectral_mixer, first_block, blocks, 1))
    kernel_bias = bias_rows(lax.dynamic_slice_in_dim(spectral_bias, first_block, blocks, 1))
    mixer_bias = bias_rows(lax.dynamic_slice_in_dim(spectral_offset, first_block, blocks, 1))
    first_pre = (
        jnp.einsum("nbx,bxy->nby", modes_flat, kernel_matrix, preferred_element_type=jnp.float32)
        + kernel_bias
    )
    first_act = gelu_exact(first_pre).astype(jnp.bfloat16)
    second_pre = (
        jnp.einsum("nbx,bxy->nby", first_act, mixer_matrix, preferred_element_type=jnp.float32)
        + mixer_bias
    )
    shrunk = spectral_layout(shrink(second_pre), leading, blocks, block_size)
    back_meridian = jnp.einsum(
        "kphq,rkmpc->rhmqc", meridian_wide, shrunk, precision=highest
    ).astype(jnp.bfloat16)
    by_row = lax.all_to_all(back_meridian, "rows", split_axis=1, concat_axis=2, tiled=True)
    filtered = jnp.einsum(
        "rhkpc,pkw->rhwc", by_row, inverse_zonal, preferred_element_type=jnp.float32
    ).astype(jnp.bfloat16)
    by_token = lax.all_to_all(filtered, "cols", split_axis=2, concat_axis=3, tiled=True)
    mixed = residual + mask * by_token.astype(jnp.float32) + normed
    features = mixed.shape[-1]
    second_norm = (
        layer_norm(mixed, exit_scale, exit_center).astype(jnp.bfloat16).reshape(-1, features)
    )
    hidden_pre = jnp.dot(second_norm, dense_expand, preferred_element_type=jnp.float32) + dense_lift
    hidden = gelu_exact(hidden_pre).astype(jnp.bfloat16)
    output = mixed + (
        jnp.dot(hidden, dense_project, preferred_element_type=jnp.float32) + dense_return
    ).reshape(mixed.shape)
    kept = (
        residual,
        modes_flat,
        first_pre,
        first_act,
        second_pre,
        mixed,
        second_norm,
        hidden_pre,
        hidden,
        kernel_matrix,
        mixer_matrix,
        leading,
    )
    return (output, kept)


def retreat(cotangent, mask, kept, weights, grids, layout):
    (
        entry_gain,
        entry_shift,
        spectral_kernel,
        spectral_bias,
        spectral_mixer,
        spectral_offset,
        exit_scale,
        exit_center,
        dense_expand,
        dense_lift,
        dense_project,
        dense_return,
    ) = weights
    forward_zonal, inverse_zonal, meridian_table, meridian_wide = grids
    blocks, block_size, first_block = layout
    (
        residual,
        modes_flat,
        first_pre,
        first_act,
        second_pre,
        mixed,
        second_norm,
        hidden_pre,
        hidden,
        kernel_matrix,
        mixer_matrix,
        leading,
    ) = kept
    features = mixed.shape[-1]
    upstream = cotangent.reshape(-1, features)
    gradient_project = jnp.einsum("tf,tc->fc", hidden, upstream, preferred_element_type=jnp.float32)
    gradient_return = jnp.sum(upstream.astype(jnp.float32), 0)
    outer = (gradient_project, gradient_return)
    hidden_back = jnp.einsum(
        "tc,fc->tf", upstream, dense_project, preferred_element_type=jnp.float32
    )
    hidden_pull = jax.vjp(gelu_exact, hidden_pre)[1]
    pre_back = hidden_pull(hidden_back)[0].astype(jnp.bfloat16)
    gradient_expand = jnp.einsum(
        "tc,tf->cf", second_norm, pre_back, preferred_element_type=jnp.float32
    )
    gradient_lift = jnp.sum(pre_back.astype(jnp.float32), 0)
    norm_back = jnp.einsum(
        "tf,cf->tc", pre_back, dense_expand, preferred_element_type=jnp.float32
    ).reshape(mixed.shape)
    exit_pull = jax.vjp(layer_norm, mixed, exit_scale, exit_center)[1]
    mixed_part, gradient_scale, gradient_center = exit_pull(norm_back)
    inner = (gradient_expand, gradient_lift, gradient_scale, gradient_center)
    mixed_back = cotangent.astype(jnp.float32) + mixed_part
    filter_back = (mask * mixed_back).astype(jnp.bfloat16)
    channel_back = lax.all_to_all(filter_back, "cols", split_axis=3, concat_axis=2, tiled=True)
    zonal_back = jnp.einsum(
        "rhwc,pkw->rhkpc", channel_back, inverse_zonal, preferred_element_type=jnp.float32
    ).astype(jnp.bfloat16)
    meridian_back = lax.all_to_all(zonal_back, "rows", split_axis=2, concat_axis=1, tiled=True)
    shrunk_back = jnp.einsum(
        "kphq,rhmqc->rkmpc", meridian_table, meridian_back, preferred_element_type=jnp.float32
    )
    shrink_pull = jax.vjp(shrink, second_pre)[1]
    second_back = shrink_pull(block_layout(shrunk_back, blocks, block_size))[0].astype(jnp.bfloat16)
    mixer_whole = jnp.einsum(
        "nbx,nby->bxy", first_act, second_back, preferred_element_type=jnp.float32
    )
    offset_rows = jnp.sum(second_back.astype(jnp.float32), 0)
    activation_back = jnp.einsum(
        "nby,bxy->nbx", second_back, mixer_matrix, preferred_element_type=jnp.float32
    )
    first_pull = jax.vjp(gelu_exact, first_pre)[1]
    first_back = first_pull(activation_back)[0].astype(jnp.bfloat16)
    kernel_whole = jnp.einsum(
        "nbx,nby->bxy", modes_flat, first_back, preferred_element_type=jnp.float32
    )
    kernel_rows = jnp.sum(first_back.astype(jnp.float32), 0)
    spectrum_back = spectral_layout(
        jnp.einsum("nby,bxy->nbx", first_back, kernel_matrix, preferred_element_type=jnp.float32),
        leading,
        blocks,
        block_size,
    )
    modes_back = jnp.einsum(
        "kphq,rkmpc->rhmqc", meridian_wide, spectrum_back, precision=highest
    ).astype(jnp.bfloat16)
    row_back = lax.all_to_all(modes_back, "rows", split_axis=1, concat_axis=2, tiled=True)
    sent_back = jnp.einsum(
        "rhkpc,wpk->rhwc", row_back, forward_zonal, preferred_element_type=jnp.float32
    ).astype(jnp.bfloat16)
    token_back = lax.all_to_all(sent_back, "cols", split_axis=2, concat_axis=3, tiled=True)
    normed_back = mixed_back + mask * token_back.astype(jnp.float32)
    entry_pull = jax.vjp(layer_norm, residual, entry_gain, entry_shift)[1]
    residual_part, gradient_gain, gradient_shift = entry_pull(normed_back)
    gradient_tokens = mixed_back + residual_part
    shared = (
        gradient_gain,
        gradient_shift,
        inner[2],
        inner[3],
        inner[0],
        inner[1],
        outer[0],
        outer[1],
    )
    local_blocks = (
        matrix_gradient(kernel_whole, block_size),
        bias_gradient(kernel_rows, block_size),
        matrix_gradient(mixer_whole, block_size),
        bias_gradient(offset_rows, block_size),
    )
    return (gradient_tokens, shared, local_blocks)


def shards_general(
    tokens,
    region_sizes,
    region_starts,
    entry_gain,
    entry_shift,
    spectral_kernel,
    spectral_bias,
    spectral_mixer,
    spectral_offset,
    exit_scale,
    exit_center,
    dense_expand,
    dense_lift,
    dense_project,
    dense_return,
    cotangent,
):
    rows_here = tokens.shape[1]
    cols_here = tokens.shape[2]
    height = rows_here * lax.axis_size("rows")
    width = cols_here * lax.axis_size("cols")
    grids = tables(height, width, width // 2)
    latitude = lax.axis_index("rows") * rows_here + jnp.arange(rows_here, dtype=jnp.int32)
    longitude = lax.axis_index("cols") * cols_here + jnp.arange(cols_here, dtype=jnp.int32)
    inside_rows = latitude[None, :, None] < region_sizes[:, 0][:, None, None]
    offset = (longitude[None, None, :] - region_starts[:, None, None]) % width
    inside_cols = offset < region_sizes[:, 1][:, None, None]
    mask = jnp.where(inside_rows & inside_cols, 1.0, 0.0).astype(jnp.float32)[..., None]
    block_size = spectral_kernel.shape[2]
    total_blocks = spectral_kernel.shape[1]
    blocks = tokens.shape[3] // lax.axis_size("cols") // block_size
    first_block = lax.axis_index("cols") * blocks
    layout = (blocks, block_size, first_block)
    weights = (
        entry_gain,
        entry_shift,
        spectral_kernel,
        spectral_bias,
        spectral_mixer,
        spectral_offset,
        exit_scale,
        exit_center,
        dense_expand,
        dense_lift,
        dense_project,
        dense_return,
    )
    output, kept = advance(tokens, mask, weights, grids, layout)
    gradient_tokens, shared, local_blocks = retreat(cotangent, mask, kept, weights, grids, layout)
    (
        gain_part,
        shift_part,
        scale_part,
        center_part,
        expand_part,
        lift_part,
        project_part,
        return_part,
    ) = shared
    everywhere = ("rows", "cols")
    project_sum = lax.psum(project_part.astype(jnp.bfloat16), everywhere).astype(jnp.float32)
    expand_sum = lax.psum(expand_part.astype(jnp.bfloat16), everywhere).astype(jnp.float32)
    vectors = (gain_part, shift_part, scale_part, center_part, lift_part, return_part)
    sums = lax.psum(jnp.concatenate(vectors), everywhere)
    ends = [0]
    for vector in vectors:
        ends.append(ends[-1] + vector.shape[0])
    parts = [sums[low:high] for low, high in zip(ends[:-1], ends[1:])]
    summed = (*parts[:4], expand_sum, parts[4], project_sum, parts[5])
    kernel_local, bias_local, mixer_local, offset_local = local_blocks
    kernel_full = lax.dynamic_update_slice_in_dim(
        jnp.zeros((2, total_blocks, block_size, block_size), jnp.float32),
        kernel_local,
        first_block,
        1,
    )
    bias_full = lax.dynamic_update_slice_in_dim(
        jnp.zeros((2, total_blocks, block_size), jnp.float32), bias_local, first_block, 1
    )
    mixer_full = lax.dynamic_update_slice_in_dim(
        jnp.zeros((2, total_blocks, block_size, block_size), jnp.float32),
        mixer_local,
        first_block,
        1,
    )
    offset_full = lax.dynamic_update_slice_in_dim(
        jnp.zeros((2, total_blocks, block_size), jnp.float32), offset_local, first_block, 1
    )
    block_totals = lax.psum((kernel_full, bias_full, mixer_full, offset_full), ("rows", "cols"))
    return (
        output.astype(jnp.bfloat16),
        gradient_tokens,
        summed[0],
        summed[1],
        block_totals[0],
        block_totals[1],
        block_totals[2],
        block_totals[3],
        summed[2],
        summed[3],
        summed[4],
        summed[5],
        summed[6],
        summed[7],
    )


MESH = pl.DeviceIdType.MESH
wide = jnp.float32
low = jnp.bfloat16
by_last = (((1,), (1,)), ((), ()))
by_first = (((0,), (0,)), ((), ()))
vmem = pl.BlockSpec(memory_space=pltpu.VMEM)


def dot(a, b):
    return jnp.dot(a, b, preferred_element_type=wide)


def dot_last(a, b):
    return lax.dot_general(a, b, by_last, preferred_element_type=wide)


def dot_first(a, b):
    return lax.dot_general(a, b, by_first, preferred_element_type=wide)


def task_tables(height, width, rows_here, cols_here):
    modes = width // 2
    near = modes // 2
    column = np.arange(width)
    frequency = np.arange(modes)
    angle = (column[:, None] * frequency[None, :] % width).astype(np.float32) * np.float32(
        2.0 * math.pi / width
    )
    scale = np.float32(1.0 / math.sqrt(width))
    zonal = np.stack([np.cos(angle), -np.sin(angle)], 1) * scale
    factor = np.where(frequency == 0, 1.0, 2.0).astype(np.float32)
    inverse = (
        np.stack([np.cos(angle).T * factor[:, None], -np.sin(angle).T * factor[:, None]], 0) * scale
    )
    latitude = np.arange(height)
    turn = (latitude[:, None] * latitude[None, :] % height).astype(np.float32) * np.float32(
        2.0 * math.pi / height
    )
    cosine = np.cos(turn) / np.float32(math.sqrt(height))
    sine = np.sin(turn) / np.float32(math.sqrt(height))
    meridian = np.stack([np.stack([cosine, sine], -1), np.stack([-sine, cosine], -1)], 1)
    halves = width // cols_here
    split_f = zonal.reshape(halves, cols_here, 2, 2, near)
    to_modes = np.zeros((halves, 2, cols_here, 2, 2, 2, near), np.float32)
    split_g = inverse.reshape(2, 2, near, halves, cols_here)
    to_columns = np.zeros((2, 2, 2, near, halves, 2, cols_here), np.float32)
    for i in range(2):
        to_modes[:, i, :, :, i] = split_f.transpose(0, 1, 3, 2, 4)
        to_columns[:, i, :, :, :, i] = split_g.transpose(1, 0, 2, 3, 4)
    side = halves * 2 * cols_here
    to_modes = to_modes.reshape(side, side)
    to_columns = to_columns.reshape(side, side)
    pairs = rows_here // 2
    senders = height // rows_here
    order = np.zeros((height // 2, 2), np.int64)
    for core in range(2):
        for chip in range(senders // 2):
            for pair in range(pairs):
                for i in range(2):
                    order[(core * (senders // 2) + chip) * pairs + pair, i] = (
                        (chip * 2 + core) * rows_here + pair * 2 + i
                    )
    placed = meridian[:, :, order]
    ahead = np.zeros((2, 2, 2, height // 2, 2, 2, height), np.float32)
    for c in range(2):
        ahead[:, :, c, :, c] = placed.transpose(3, 4, 2, 1, 0)
    ahead = ahead.reshape(2, 2 * height, 4 * height)
    behind = ahead.reshape(4 * height, 4 * height).T
    return tuple(
        np.asarray(item, ml_dtypes.bfloat16)
        for item in (to_modes, to_columns, ahead, behind, np.eye(256, dtype=np.float32))
    )


def chip_device(chip, core, cols):
    return ((chip // cols) * 2 + core, chip % cols)


def swap_bits(value, mask, bits):
    out = 0
    for k in range(bits):
        bit = (value // (1 << k)) % 2
        if (mask >> k) & 1:
            bit = 1 - bit
        out = out + bit * (1 << k)
    return out


def greet(chips, cols):
    row = lax.axis_index("rows")
    core = row % 2
    me = (row // 2) * cols + lax.axis_index("cols")
    barrier = pltpu.get_barrier_semaphore()
    for step in range(1, chips):
        other = (me + step) % chips
        pl.semaphore_signal(
            barrier, inc=1, device_id=chip_device(other, core, cols), device_id_type=MESH
        )
    pl.semaphore_signal(
        barrier, inc=1, device_id=chip_device(me, 1 - core, cols), device_id_type=MESH
    )
    pl.semaphore_wait(barrier, chips)
    return me, core


def send_piece(src, dst, send_sem, recv_sem, target, me, core, cols):
    @pl.when(target == me)
    def _():
        pltpu.make_async_copy(src, dst, recv_sem).start()

    @pl.when(target != me)
    def _():
        pltpu.make_async_remote_copy(
            src_ref=src,
            dst_ref=dst,
            send_sem=send_sem,
            recv_sem=recv_sem,
            device_id=chip_device(target, core, cols),
            device_id_type=MESH,
        ).start()


def await_piece(ref, sem):
    pltpu.make_async_copy(ref, ref, sem).wait()


def to_feature_rows(out_ref, region, place, piece, eye):
    features = piece.shape[1]
    for low_end in range(0, features, 256):
        turned = dot_last(eye, piece[:, low_end : low_end + 256])
        out_ref[region, low_end : low_end + 256, place] = turned.astype(low)


def modes_first(block, group, half):
    columns = []
    for m in range(group):
        rows = block[m * half : (m + 1) * half]
        height = block.shape[1] // 4
        columns.append(
            jnp.concatenate(
                [
                    rows[:, (c * 2 + p) * height : (c * 2 + p + 1) * height]
                    for p in range(2)
                    for c in range(2)
                ],
                0,
            )
        )
    return jnp.concatenate(columns, 1)


def modes_last(block, group, half):
    height = block.shape[1] // group
    rows = []
    for m in range(group):
        part = block[:, m * height : (m + 1) * height]
        rows.append(
            jnp.concatenate(
                [
                    part[(p * 2 + c) * half : (p * 2 + c + 1) * half]
                    for c in range(2)
                    for p in range(2)
                ],
                1,
            )
        )
    return jnp.concatenate(rows, 0)


def filter_pass(sizes, me, core, produce, middle, consume, tables, work, sems, tick):
    regions, blocks, block_size, chips, cols, tokens = sizes
    table_in, table_out, ahead, behind = tables
    sent, got, zonal, zonal_got, tall, flat, back, sibling, leaving, coming = work
    send_a, recv_a, send_b, recv_b, send_c, recv_c, send_d, recv_d = sems
    lanes = 128
    senders = chips // cols
    pairs = tokens // lanes
    half = block_size // 2
    points = senders * pairs
    group = 4
    bits = (blocks - 1).bit_length()
    home = me // blocks
    for turn in range(regions):
        region = (home + 1 + turn) % regions
        produce(region)
        for step in range(blocks - 1, -1, -1):
            target = region * blocks + swap_bits(me % blocks, step, bits)
            src = sent.at[region, pl.ds(pl.multiple_of(target % blocks * block_size, 32), block_size)]
            place = turn * blocks + step
            send_piece(src, got.at[me], send_a.at[place], recv_a.at[me], target, me, core, cols)
    tick("sent")

    def zonal_step(index, carry):
        chip = (index + home * senders // regions) % senders
        for col in range(cols):
            await_piece(got.at[chip * cols + col], recv_a.at[chip * cols + col])
        for pair in range(pairs):
            x = jnp.concatenate(
                [got[chip * cols + col, :, pair * lanes : (pair + 1) * lanes] for col in range(cols)], 1
            )
            y = dot(x, table_in[...]).astype(low)
            for part in range(2):
                zonal[part, chip * pairs + pair] = y[:, part * lanes : (part + 1) * lanes]
        return carry

    lax.fori_loop(0, senders, zonal_step, 0)
    swap = pltpu.make_async_remote_copy(
        src_ref=zonal.at[1 - core],
        dst_ref=zonal_got,
        send_sem=send_b,
        recv_sem=recv_b,
        device_id=chip_device(me, 1 - core, cols),
        device_id_type=MESH,
    )
    swap.start()
    tick("zonal")

    def widen(source, first):
        def step(point, carry):
            row = pl.multiple_of((first + point) * block_size, 32)
            tall[pl.ds(row, block_size), :] = source(point).astype(wide)
            return carry

        lax.fori_loop(0, points, step, 0)

    widen(lambda point: zonal[core, point], core * points)
    swap.wait()
    widen(lambda point: zonal_got[point], (1 - core) * points)
    modes = lanes // 4

    def turn_step(c, carry):
        x = jnp.concatenate(
            [tall[pl.ds(c + half * side, 2 * points, stride=block_size), :] for side in range(2)], 0
        )
        y = jnp.transpose(x)
        for i in range(4):
            flat[i, pl.ds(c, modes, stride=half), :] = y[i * modes : (i + 1) * modes]
        return carry

    lax.fori_loop(0, half, turn_step, 0, unroll=4)
    tick("turned")

    def mode_step(step, carry):
        rows = pl.ds(pl.multiple_of(step * group * half, 64), group * half)
        spectrum = 0.0
        for i in range(2):
            x = jnp.concatenate([flat[i * 2, rows, :], flat[i * 2 + 1, rows, :]], 1).astype(low)
            spectrum = spectrum + dot(x, ahead[i])
        out = modes_last(middle(step, modes_first(spectrum, group, half)), group, half)
        high = out.astype(low)
        rest = (out - high.astype(wide)).astype(low)
        y = (dot(high, behind[...]) + dot(rest, behind[...])).astype(low).astype(wide)
        for i in range(4):
            flat[i, rows, :] = y[:, i * lanes : (i + 1) * lanes]
        return carry

    lax.fori_loop(0, modes // group // 2, mode_step, 0)
    tick("halfway")
    lax.fori_loop(modes // group // 2, modes // group, mode_step, 0)
    tick("modes")

    def return_step(c, carry):
        x = jnp.concatenate([flat[i, pl.ds(c, modes, stride=half), :] for i in range(4)], 0)
        y = jnp.transpose(x)
        for side in range(2):
            tall[pl.ds(c + half * side, 2 * points, stride=block_size), :] = y[
                side * 2 * points : (side + 1) * 2 * points
            ]
        return carry

    lax.fori_loop(0, half, return_step, 0, unroll=4)
    tick("returned")

    def narrow(store, first):
        def step(point, carry):
            row = pl.multiple_of((first + point) * block_size, 32)
            store(point, tall[pl.ds(row, block_size), :].astype(low))
            return carry

        lax.fori_loop(0, points, step, 0)

    def to_sibling(point, value):
        back[point] = value

    def to_self(point, value):
        sibling[core, point] = value

    narrow(to_sibling, (1 - core) * points)
    swap_back = pltpu.make_async_remote_copy(
        src_ref=back,
        dst_ref=sibling.at[core],
        send_sem=send_c,
        recv_sem=recv_c,
        device_id=chip_device(me, 1 - core, cols),
        device_id_type=MESH,
    )
    swap_back.start()
    tick("back")
    narrow(to_self, core * points)
    swap_back.wait_send()
    await_piece(sibling.at[1 - core], recv_c)

    def column_step(index, carry):
        chip = (index + (home + 1) * senders // regions) % senders
        for pair in range(pairs):
            point = chip * pairs + pair
            x = jnp.concatenate([sibling[0, point], sibling[1, point]], 1)
            y = dot(x, table_out[...]).astype(low)
            for col in range(cols):
                leaving[chip * cols + col, :, pair * lanes : (pair + 1) * lanes] = y[
                    :, col * lanes : (col + 1) * lanes
                ]
        for col in range(cols):
            target = chip * cols + col
            dst = coming.at[
                me // blocks, pl.ds(pl.multiple_of(me % blocks * block_size, 32), block_size)
            ]
            send_piece(
                leaving.at[target], dst, send_d.at[target], recv_d.at[me], target, me, core, cols
            )
        return carry

    lax.fori_loop(0, senders, column_step, 0)
    tick("columns")
    for turn in range(regions):
        region = (home + turn) % regions

        def arrive(block, carry, region=region):
            ref = coming.at[region, pl.ds(pl.multiple_of(block * block_size, 32), block_size)]
            await_piece(ref, recv_d.at[region * blocks + block])
            return carry

        lax.fori_loop(0, blocks, arrive, 0)
        consume(region)
        tick("region")

    for place in range(regions * blocks):
        turn, step = place // blocks, place % blocks
        target = (home + 1 + turn) % regions * blocks + swap_bits(me % blocks, step, bits)

        @pl.when(target != me)
        def _():
            await_piece(got.at[0], send_a.at[place])

        @pl.when(place != me)
        def _():
            await_piece(leaving.at[0], send_d.at[place])


def work_shapes(sizes):
    regions, blocks, block_size, chips, cols, tokens = sizes
    lanes = 128
    features = blocks * block_size
    points = (chips // cols) * (tokens // lanes)
    rows = (lanes // 4) * (block_size // 2)
    return [
        pltpu.VMEM((regions, features, tokens), low),
        pltpu.VMEM((chips, block_size, tokens), low),
        pltpu.VMEM((2, points, block_size, lanes), low),
        pltpu.VMEM((points, block_size, lanes), low),
        pltpu.VMEM((2 * points * block_size, lanes), wide),
        pltpu.VMEM((4, rows, lanes), wide),
        pltpu.VMEM((points, block_size, lanes), low),
        pltpu.VMEM((2, points, block_size, lanes), low),
        pltpu.VMEM((chips, block_size, tokens), low),
        pltpu.VMEM((regions, features, tokens), low),
        pltpu.SemaphoreType.DMA((chips,)),
        pltpu.SemaphoreType.DMA((chips,)),
        pltpu.SemaphoreType.DMA,
        pltpu.SemaphoreType.DMA,
        pltpu.SemaphoreType.DMA,
        pltpu.SemaphoreType.DMA,
        pltpu.SemaphoreType.DMA((chips,)),
        pltpu.SemaphoreType.DMA((chips,)),
    ]


def normalise(value):
    centre = jnp.mean(value, -1, keepdims=True)
    centred = value - centre
    spread = jnp.mean(centred * centred, -1, keepdims=True)
    factor = lax.rsqrt(spread + norm_eps)
    return centred * factor, factor


def gelu_parts(value):
    curve = 0.5 * (1.0 + lax.erf(value * (1.0 / math.sqrt(2.0))))
    return curve


def gelu_slope(value):
    bell = jnp.exp(-0.5 * value * value) * (1.0 / math.sqrt(2.0 * math.pi))
    return gelu_parts(value) + value * bell


def inside_region(sizes_ref, starts_ref, region, first, shape, width):
    rows, rows_here, cols_here = shape
    index = first + lax.broadcasted_iota(jnp.int32, (rows, 1), 0)
    bits = cols_here.bit_length() - 1
    latitude = lax.axis_index("rows") * rows_here + lax.shift_right_logical(index, bits)
    longitude = lax.axis_index("cols") * cols_here + (index & (cols_here - 1))
    offset = longitude - starts_ref[region]
    offset = jnp.where(offset < 0, offset + width, offset)
    near = jnp.where(latitude < sizes_ref[region, 0], 1.0, 0.0)
    return jnp.where(offset < sizes_ref[region, 1], near, 0.0)


def as_row(ref):
    return ref[...].reshape(1, ref.shape[0])


def field_rows(coming, region, place, eye):
    return jnp.concatenate(
        [
            dot_last(eye, coming[region, first : first + 256, place])
            for first in range(0, coming.shape[1], 256)
        ],
        1,
    )


def forward_kernel(sizes, *refs):
    (
        region_sizes,
        region_starts,
        tokens_ref,
        gain_ref,
        shift_ref,
        scale_ref,
        center_ref,
        weights_ref,
        biases_ref,
        to_modes,
        to_columns,
        ahead,
        behind,
        eye,
        mixed_hbm,
        second_hbm,
        *kept_hbm,
    ) = refs[:20]
    work, sems = refs[20:30], refs[30:38]
    mixed, second, mixed_sems, second_sems, kept_sems, *kept = refs[38:]
    regions, blocks, block_size, chips, cols, tokens = sizes
    me, core = greet(chips, cols)
    sent, coming = work[0], work[-1]
    piece = 128
    steps = kept_hbm[0].shape[0]
    cols_here = 128 // cols
    gain, shift, scale, center = (
        as_row(ref) for ref in (gain_ref, shift_ref, scale_ref, center_ref)
    )

    def inside(region, first, rows):
        shape = (rows, tokens // cols_here, cols_here)
        return inside_region(region_sizes, region_starts, region, first, shape, 128)

    def produce(region):
        def step(part, carry):
            rows = pl.ds(pl.multiple_of(region * tokens + part * piece, piece), piece)
            unit, factor = normalise(tokens_ref[rows, :].astype(wide))
            values = (inside(region, part * piece, piece) * (unit * gain + shift)).astype(low)
            place = pl.ds(pl.multiple_of(part * piece, piece), piece)
            to_feature_rows(sent, region, place, values, eye[...])
            return carry

        lax.fori_loop(0, tokens // piece, step, 0)

    def keep(step):
        slot = step % 2
        return [
            pltpu.make_async_copy(ref.at[slot], hbm.at[step], kept_sems.at[k, slot])
            for k, (ref, hbm) in enumerate(zip(kept, kept_hbm))
        ]

    def middle(step, spectrum):
        slot = step % 2

        @pl.when(step >= 2)
        def _():
            for copy in keep(step - 2):
                copy.wait()

        spectrum_kept, first_kept, act_kept, second_kept = kept
        spectrum = spectrum.astype(low)
        spectrum_kept[slot] = spectrum
        first = dot_first(weights_ref[0], spectrum) + biases_ref[:, 0:1]
        first_kept[slot] = first
        act = (first * gelu_parts(first)).astype(low)
        act_kept[slot] = act
        second_pre = dot_first(weights_ref[1], act) + biases_ref[:, 1:2]
        second_kept[slot] = second_pre
        for copy in keep(step):
            copy.start()
        return second_pre - shrink_width * jnp.tanh(second_pre / shrink_width)

    def leave(region):
        rows = pl.ds(pl.multiple_of(region * tokens, tokens), tokens)
        return [
            pltpu.make_async_copy(mixed.at[rows], mixed_hbm.at[rows], mixed_sems.at[region]),
            pltpu.make_async_copy(second.at[rows], second_hbm.at[rows], second_sems.at[region]),
        ]

    def consume(region):
        def step(part, carry):
            rows = pl.ds(pl.multiple_of(region * tokens + part * 256, 256), 256)
            place = pl.ds(pl.multiple_of(part * 256, 256), 256)
            fields = field_rows(coming, region, place, eye[...])
            residual = tokens_ref[rows, :].astype(wide)
            unit, factor = normalise(residual)
            value = residual + inside(region, part * 256, 256) * fields + (unit * gain + shift)
            mixed[rows, :] = value
            unit, factor = normalise(value)
            second[rows, :] = (unit * scale + center).astype(low)
            return carry

        lax.fori_loop(0, tokens // 256, step, 0)
        for copy in leave(region):
            copy.start()

    tables = (to_modes, to_columns, ahead, behind)
    filter_pass(
        sizes, me, core, produce, middle, consume, tables, work, sems, lambda place: None
    )
    for step in (steps - 2, steps - 1):
        for copy in keep(step):
            copy.wait()
    for region in range(regions):
        for copy in leave(region):
            copy.wait()


def place_of(row, col):
    return {"core": row % 2, "x": (row // 2) % 2, "z": row // 4, "y": col}


def device_at(spot):
    return (spot["z"] * 4 + spot["x"] * 2 + spot["core"], spot["y"])


def across(spot, axis, step=1):
    size = 4 if axis == "z" else 2
    return device_at({**spot, axis: (spot[axis] + step) % size})


def remote(src, dst, send_sem, recv_sem, device):
    return pltpu.make_async_remote_copy(
        src_ref=src,
        dst_ref=dst,
        send_sem=send_sem,
        recv_sem=recv_sem,
        device_id=device,
        device_id_type=MESH,
    )


def add_rows(out_ref, out_row, terms, rows):
    step = 48

    def add(part, carry):
        total = 0.0
        for ref, row in terms:
            here = pl.ds(pl.multiple_of(row + part * step, 16), step)
            total = total + ref[here, :].astype(wide)
        there = pl.ds(pl.multiple_of(out_row + part * step, 16), step)
        out_ref[there, :] = total.astype(low)
        return carry

    lax.fori_loop(0, rows // step, add, 0)


def row_part(ref, row, rows):
    return ref.at[pl.ds(pl.multiple_of(row, 16), rows)]


def facing(spot, axis):
    if axis == "near":
        z = spot["z"] // 2 * 2 + 1 - spot["z"] % 2
        return spot["z"] % 2, device_at({**spot, "z": z})
    if axis == "far":
        return spot["z"] // 2, across(spot, "z", 2)
    return spot[axis], across(spot, axis)


def reduce_steps(spot, axes, buffers, sends, recvs):
    steps = []
    for k, axis in enumerate(axes):
        bit, device = facing(spot, axis)
        source, target = buffers[k], buffers[k + 1]
        rows = target.shape[0]
        hop = remote(
            row_part(source, (1 - bit) * rows, rows), target, sends.at[k], recvs.at[k], device
        )

        def finish(hop=hop, source=source, target=target, rows=rows, bit=bit):
            hop.wait()
            add_rows(target, 0, ((target, 0), (source, bit * rows)), rows)

        steps.append((hop.start, finish))
    return steps


def share_steps(spot, axes, piece, total, sends, recvs, own_sem):
    offsets, rows, bits, devices = [0], [total.shape[0]], [], []
    for axis in axes:
        bit, device = facing(spot, axis)
        bits.append(bit)
        devices.append(device)
        rows.append(rows[-1] // 2)
        offsets.append(offsets[-1] + bit * rows[-1])
    last = len(axes) - 1
    hops = []
    for k in range(last, -1, -1):
        place = row_part(total, offsets[k + 1], rows[k + 1])
        source = piece if k == last else place
        hops.append(remote(source, place, sends.at[k], recvs.at[k], devices[k]))
    keep = pltpu.make_async_copy(piece, row_part(total, offsets[-1], rows[-1]), own_sem)
    ready = (
        (offsets[2], rows[2]),
        (offsets[1] + (1 - bits[1]) * rows[2], rows[2]),
        ((1 - bits[0]) * rows[1], rows[1]),
    )
    cores = []
    for k, (offset, size) in enumerate(ready):
        place = row_part(total, offset, size)
        cores.append(
            remote(place, place, sends.at[4 + k], recvs.at[4 + k], across(spot, "core"))
        )

    def begin():
        keep.start()
        hops[0].start()

    def second():
        keep.wait()
        hops[0].wait()
        hops[1].start()

    def third():
        hops[1].wait()
        hops[2].start()
        cores[0].start()

    def fourth():
        hops[2].wait()
        hops[3].start()
        cores[1].start()

    def fifth():
        hops[3].wait()
        cores[2].start()

    def finish():
        for core in cores:
            core.wait()

    return begin, second, third, fourth, fifth, finish


def backward_kernel(sizes, *refs):
    (
        region_sizes,
        region_starts,
        tokens_hbm,
        mixed_back_ref,
        gain_ref,
        weights_ref,
        to_modes,
        to_columns,
        ahead,
        behind,
        eye,
        spectrum_hbm,
        first_hbm,
        act_hbm,
        pre_hbm,
        own_hbm,
        ready_ref,
        sums_ref,
        slope_hbm,
        project_total,
        expand_total,
        gathered,
        vector_sum,
    ) = refs[:23]
    work, sems = refs[23:33], refs[33:41]
    (
        tokens_ref,
        slope,
        slope_sems,
        own,
        load_sems,
        kernel_slope,
        bias_slope,
        mixer_slope,
        offset_slope,
        spectrum_slots,
        first_slots,
        act_slots,
        pre_slots,
        slot_sems,
        halves,
        quarters,
        eighths,
        pieces,
        reduce_sends,
        reduce_recvs,
        share_sends,
        share_recvs,
        own_sems,
        slab,
        slab_sibling,
        slab_region,
        slab_sends,
        slab_recvs,
        vector_sent,
        vector_got,
        vector_sends,
        vector_recvs,
        late,
        late_got,
        late_all,
        late_sends,
        late_recvs,
    ) = refs[41:]
    regions, blocks, block_size, chips, cols, tokens = sizes
    steps = spectrum_hbm.shape[0]
    slots = (spectrum_slots, first_slots, act_slots, pre_slots)
    streams = (spectrum_hbm, first_hbm, act_hbm, pre_hbm)

    def fetch(step, slot):
        return [
            pltpu.make_async_copy(hbm.at[step], ref.at[slot], slot_sems.at[k, slot])
            for k, (hbm, ref) in enumerate(zip(streams, slots))
        ]

    load_own = pltpu.make_async_copy(own_hbm.at[1], own, load_sems.at[0])
    load_tokens = pltpu.make_async_copy(tokens_hbm, tokens_ref, load_sems.at[1])
    load_own.start()
    for copy in fetch(0, 0):
        copy.start()
    load_tokens.start()
    me, core = greet(chips, cols)
    spot = place_of(lax.axis_index("rows"), lax.axis_index("cols"))
    block = me % blocks
    sent, coming = work[0], work[-1]
    piece = 128
    cols_here = 128 // cols
    width = own.shape[1]
    late[...] = jnp.zeros_like(late)
    vector_sum[...] = sums_ref[...]
    for ref in (kernel_slope, bias_slope, mixer_slope, offset_slope):
        ref[...] = jnp.zeros_like(ref)
    reducing, sharing = [], []
    for j in range(2):
        place = pl.multiple_of((core * 2 + j) * width, width)
        totals = (project_total.at[pl.ds(place, width)], expand_total.at[:, pl.ds(place, width)])
        for k in range(2):
            s = j * 2 + k
            axes = (("x", "y"), ("y", "x"))[k] + ("near", "far")
            buffers = (own.at[k], halves.at[k], quarters.at[k], eighths.at[s], pieces.at[s])
            if j == 0:
                buffers = (ready_ref.at[k],) + buffers[3:]
            reducing.append(
                reduce_steps(
                    spot, axes[5 - len(buffers) :], buffers, reduce_sends.at[s], reduce_recvs.at[s]
                )
            )
            sharing.append(
                share_steps(
                    spot,
                    axes,
                    pieces.at[s],
                    totals[k],
                    share_sends.at[s],
                    share_recvs.at[s],
                    own_sems.at[s],
                )
            )

    def reduce(j, step, finish):
        for steps_of in reducing[j * 2 : j * 2 + 2]:
            steps_of[step][finish]()

    def share(j, step):
        for steps_of in sharing[j * 2 : j * 2 + 2]:
            steps_of[step]()

    def inside(region, first, rows):
        shape = (rows, tokens // cols_here, cols_here)
        return inside_region(region_sizes, region_starts, region, first, shape, 128)

    def produce(region):
        def step(part, carry):
            rows = pl.ds(pl.multiple_of(region * tokens + part * piece, piece), piece)
            place = pl.ds(pl.multiple_of(part * piece, piece), piece)
            values = (inside(region, part * piece, piece) * mixed_back_ref[rows, :]).astype(low)
            to_feature_rows(sent, region, place, values, eye[...])
            return carry

        lax.fori_loop(0, tokens // piece, step, 0)

    def middle(step, shrunk_back):
        slot = step % 2
        for copy in fetch(step, slot):
            copy.wait()

        @pl.when(step + 1 < steps)
        def _():
            for copy in fetch(step + 1, 1 - slot):
                copy.start()

        level = jnp.tanh(pre_slots[slot] / shrink_width)
        second = (shrunk_back * (level * level)).astype(low)
        offset_slope[...] += jnp.sum(second.astype(wide), 1, keepdims=True)
        mixer_slope[...] += dot_last(act_slots[slot], second)
        first = (dot(weights_ref[1], second) * gelu_slope(first_slots[slot])).astype(low)
        bias_slope[...] += jnp.sum(first.astype(wide), 1, keepdims=True)
        kernel_slope[...] += dot_last(spectrum_slots[slot], first)
        return dot(weights_ref[0], first)

    def leave(region):
        rows = pl.ds(pl.multiple_of(region * tokens, tokens), tokens)
        return pltpu.make_async_copy(slope.at[rows], slope_hbm.at[rows], slope_sems.at[region])

    def consume(region):
        def step(part, carry):
            rows = pl.ds(pl.multiple_of(region * tokens + part * 256, 256), 256)
            place = pl.ds(pl.multiple_of(part * 256, 256), 256)
            fields = field_rows(coming, region, place, eye[...])
            unit, factor = normalise(tokens_ref[rows, :].astype(wide))
            mixed_back = mixed_back_ref[rows, :]
            normed_back = mixed_back + inside(region, part * 256, 256) * fields
            gains = jnp.sum(normed_back * unit, 0, keepdims=True)
            shifts = jnp.sum(normed_back, 0, keepdims=True)
            for k in range(3):
                late[k : k + 1, :] += gains[:, k * 256 : (k + 1) * 256]
                late[3 + k : 4 + k, :] += shifts[:, k * 256 : (k + 1) * 256]
            pull = normed_back * as_row(gain_ref)
            pull = pull - jnp.mean(pull, -1, keepdims=True) - unit * jnp.mean(
                pull * unit, -1, keepdims=True
            )
            slope[rows, :] = mixed_back + factor * pull
            return carry

        lax.fori_loop(0, tokens // 256, step, 0)
        leave(region).start()

    side = 2 * block_size
    slab_core = remote(
        slab, slab_sibling, slab_sends.at[0], slab_recvs.at[0], across(spot, "core")
    )
    my_rows = pl.ds(pl.multiple_of(core * side, 32), side)
    slab_far = remote(
        slab_sibling.at[my_rows],
        slab_region,
        slab_sends.at[1],
        slab_recvs.at[1],
        chip_device((me + blocks) % chips, core, cols),
    )

    def slab_peer(step):
        other = me // blocks * blocks + (block + step) % blocks
        ref = gathered.at[block, my_rows]
        return remote(
            ref, ref, slab_sends.at[1 + step], slab_recvs.at[1 + step], chip_device(other, core, cols)
        )

    slab_last = remote(
        gathered.at[:, my_rows],
        gathered.at[:, my_rows],
        slab_sends.at[1 + blocks],
        slab_recvs.at[1 + blocks],
        across(spot, "core"),
    )

    def slab_start():
        for k, (weight, bias) in enumerate(
            ((kernel_slope, bias_slope), (mixer_slope, offset_slope))
        ):
            whole = weight[...]
            upper, lower = whole[:block_size], whole[block_size:]
            first = k * side
            slab[first : first + block_size, :block_size] = (
                upper[:, :block_size] + lower[:, block_size:]
            )
            slab[first + block_size : first + side, :block_size] = (
                upper[:, block_size:] - lower[:, :block_size]
            )
            slab[first : first + side, block_size:] = jnp.broadcast_to(
                bias[...], (side, slab.shape[1] - block_size)
            )
        slab_core.start()

    def slab_regions():
        slab_core.wait()
        slab_sibling[...] = slab_sibling[...] + slab[...]
        slab_far.start()

    def slab_blocks():
        slab_far.wait()
        gathered[block, my_rows] = slab_region[...] + slab_sibling[my_rows, :]
        for step in range(1, blocks):
            slab_peer(step).start()

    def slab_cores():
        for step in range(1, blocks):
            slab_peer(step).wait()
        slab_last.start()

    partners = (
        across(spot, "core"),
        across(spot, "x"),
        across(spot, "y"),
        device_at({**spot, "z": spot["z"] // 2 * 2 + 1 - spot["z"] % 2}),
        across(spot, "z", 2),
    )
    hops = [
        remote(
            vector_sent.at[k], vector_got.at[k], vector_sends.at[k], vector_recvs.at[k], device
        )
        for k, device in enumerate(partners)
    ]

    def vector_step(k):
        if k > 0:
            hops[k - 1].wait()
            vector_sum[...] = vector_sum[...] + vector_got[k - 1]
        if k < len(hops):
            vector_sent[k] = vector_sum[...]
            hops[k].start()

    regions_seen = []

    def tick(place):
        if place == "sent":
            load_own.wait()
            reduce(1, 0, 0)
            vector_step(0)
        if place == "zonal":
            reduce(1, 0, 1)
            reduce(1, 1, 0)
            reduce(0, 0, 0)
            vector_step(1)
        if place == "turned":
            reduce(0, 0, 1)
            reduce(0, 1, 0)
            reduce(1, 1, 1)
            reduce(1, 2, 0)
            vector_step(2)
        if place == "halfway":
            reduce(0, 1, 1)
            share(0, 0)
            reduce(1, 2, 1)
            reduce(1, 3, 0)
            vector_step(3)
        if place == "modes":
            slab_start()
            share(0, 1)
            reduce(1, 3, 1)
            share(1, 0)
            vector_step(4)
        if place == "returned":
            share(0, 2)
            share(1, 1)
            vector_step(5)
        if place == "back":
            slab_regions()
        if place == "columns":
            load_tokens.wait()
            slab_blocks()
            share(0, 3)
            share(1, 2)
            share(1, 3)
            slab_cores()
        if place == "region":
            regions_seen.append(place)
            if len(regions_seen) == 1:
                share(0, 4)

    tables = (to_columns, to_modes, ahead, behind)
    filter_pass(sizes, me, core, produce, middle, consume, tables, work, sems, tick)
    late_core = remote(late, late_got, late_sends.at[0], late_recvs.at[0], across(spot, "core"))
    late_core.start()
    late_core.wait()
    late[...] = late[...] + late_got[...]
    late_all[me] = late[...]

    def late_hop(step):
        other = chip_device((me + step) % chips, core, cols)
        return remote(late, late_all.at[me], late_sends.at[step], late_recvs.at[step], other)

    for step in range(1, chips):
        late_hop(step).start()
    slab_last.wait()
    share(1, 4)
    share(0, 5)
    share(1, 5)
    for step in range(1, chips):
        late_hop(step).wait()
    total = late_all[0]
    for chip in range(1, chips):
        total = total + late_all[chip]
    for k in range(3):
        vector_sum[0:1, k * 256 : (k + 1) * 256] = total[k : k + 1, :]
        vector_sum[1:2, k * 256 : (k + 1) * 256] = total[3 + k : 4 + k, :]
    for region in range(regions):
        leave(region).wait()


def call_filter(body, sizes, outs, cid, operands, scalars, spaces, out_spaces, scratch):
    shapes = [jax.ShapeDtypeStruct(shape, kind) for shape, kind in outs]
    anywhere = pl.BlockSpec(memory_space=pl.ANY)
    scalar = pl.BlockSpec(memory_space=pltpu.SMEM)
    return pl.pallas_call(
        functools.partial(body, sizes),
        out_shape=shapes,
        in_specs=[scalar] * len(scalars)
        + [anywhere if place in spaces else vmem for place in range(len(operands))],
        out_specs=[anywhere if place in out_spaces else vmem for place in range(len(outs))],
        scratch_shapes=[*work_shapes(sizes), *scratch],
        compiler_params=pltpu.CompilerParams(
            collective_id=cid, has_side_effects=True, vmem_limit_bytes=60 * 1024 * 1024
        ),
    )(*scalars, *operands)


def forward_scratch(sizes, kept):
    regions, blocks, block_size, chips, cols, tokens = sizes
    dma = pltpu.SemaphoreType.DMA
    features = blocks * block_size
    return (
        pltpu.VMEM((regions * tokens, features), wide),
        pltpu.VMEM((regions * tokens, features), low),
        dma((regions,)),
        dma((regions,)),
        dma((len(kept), 2)),
        *(pltpu.VMEM((2, *shape[1:]), kind) for shape, kind in kept),
    )


def backward_scratch(sizes, kept):
    regions, blocks, block_size, chips, cols, tokens = sizes
    features = blocks * block_size
    side = 2 * block_size
    dma = pltpu.SemaphoreType.DMA
    return (
        pltpu.VMEM((regions * tokens, features), low),
        pltpu.VMEM((regions * tokens, features), wide),
        dma((regions,)),
        pltpu.VMEM((2, features, features), low),
        dma((2,)),
        pltpu.VMEM((side, side), wide),
        pltpu.VMEM((side, 1), wide),
        pltpu.VMEM((side, side), wide),
        pltpu.VMEM((side, 1), wide),
        *(pltpu.VMEM((2, *shape[1:]), kind) for shape, kind in kept),
        dma((len(kept), 2)),
        pltpu.VMEM((2, features // 2, features), low),
        pltpu.VMEM((2, features // 4, features), low),
        pltpu.VMEM((4, features // 8, features), low),
        pltpu.VMEM((4, features // 16, features), low),
        dma((4, 4)),
        dma((4, 4)),
        dma((4, 7)),
        dma((4, 7)),
        dma((4,)),
        pltpu.VMEM((2 * side, 128), wide),
        pltpu.VMEM((2 * side, 128), wide),
        pltpu.VMEM((side, 128), wide),
        dma((2 + blocks,)),
        dma((2 + blocks,)),
        pltpu.VMEM((5, 16, features), wide),
        pltpu.VMEM((5, 16, features), wide),
        dma((5,)),
        dma((5,)),
        pltpu.VMEM((8, 256), wide),
        pltpu.VMEM((8, 256), wide),
        pltpu.VMEM((chips, 8, 256), wide),
        dma((chips,)),
        dma((chips,)),
    )


def dense_kernel(*refs):
    (
        second_ref,
        up_ref,
        scale_ref,
        returned_ref,
        lift_ref,
        mixed_hbm,
        expand_hbm,
        project_hbm,
        out_hbm,
        mixed_back_hbm,
        own_hbm,
        ready_ref,
        vectors,
        mixed_ref,
        expand_ref,
        project_ref,
        out_ref,
        out_sum,
        back_sum,
        hidden_tile,
        back_tile,
        sent,
        got,
        own,
        halves,
        load_sems,
        weight_sems,
        leave_sems,
        own_sems,
        sent_sem,
        got_sem,
        first_sends,
        first_recvs,
    ) = refs
    tile = expand_ref.shape[2]
    spot = place_of(lax.axis_index("rows"), lax.axis_index("cols"))
    core = spot["core"]
    orders = (("x", "y"), ("y", "x"))
    places = [
        (1 - core) * 2,
        core * 2,
        (1 - core) * 2 + 1,
        core * 2 + 1,
    ]

    def weights(k):
        here = pl.ds(pl.multiple_of(places[k] * tile, tile), tile)
        return [
            pltpu.make_async_copy(project_hbm.at[here], project_ref.at[k], weight_sems.at[0, k]),
            pltpu.make_async_copy(expand_hbm.at[:, here], expand_ref.at[k], weight_sems.at[1, k]),
        ]

    for k in range(4):
        for copy in weights(k):
            copy.start()
    load_mixed = pltpu.make_async_copy(mixed_hbm, mixed_ref, load_sems.at[0])
    load_mixed.start()
    barrier = pltpu.get_barrier_semaphore()
    for axis in ("core", "x", "y"):
        pl.semaphore_signal(barrier, inc=1, device_id=across(spot, axis), device_id_type=MESH)
    count = second_ref.shape[0]
    piece = 512
    vectors[...] = jnp.zeros_like(vectors)

    def start_step(part, carry):
        rows = pl.ds(pl.multiple_of(part * piece, piece), piece)
        out_sum[rows, :] = jnp.broadcast_to(as_row(returned_ref), (piece, out_sum.shape[1]))
        back_sum[rows, :] = jnp.zeros((piece, back_sum.shape[1]), wide)
        return carry + jnp.sum(up_ref[rows, :].astype(wide), 0, keepdims=True)

    vectors[4:5, :] = lax.fori_loop(0, count // piece, start_step, jnp.zeros((1, tile), wide))
    pl.semaphore_wait(barrier, 3)

    def tile_step(k, place, between):
        lift_row = lift_ref[pl.ds(place, 1), :]

        def piece_step(part, carry):
            rows = pl.ds(pl.multiple_of(part * piece, piece), piece)
            pre = dot(second_ref[rows, :], expand_ref[k]) + lift_row
            back = dot_last(up_ref[rows, :], project_ref[k])
            curve = gelu_parts(pre)
            bell = jnp.exp(-0.5 * pre * pre) * (1.0 / math.sqrt(2.0 * math.pi))
            hidden = (pre * curve).astype(low)
            hidden_tile[rows, :] = hidden
            pre_back = (back * (curve + pre * bell)).astype(low)
            back_tile[rows, :] = pre_back
            out_sum[rows, :] += dot(hidden, project_ref[k])
            back_sum[rows, :] += dot_last(pre_back, expand_ref[k])
            return carry + jnp.sum(pre_back.astype(wide), 0, keepdims=True)

        lift = lax.fori_loop(0, count // piece, piece_step, jnp.zeros((1, tile), wide))
        vectors[pl.ds(5 + place, 1), :] = lift
        between()
        return (
            dot_first(hidden_tile[...], up_ref[...]),
            dot_first(second_ref[...], back_tile[...]),
        )

    def swap(j, k):
        return remote(
            sent.at[j, k], got.at[j, k], sent_sem.at[j, k], got_sem.at[j, k], across(spot, "core")
        )

    hops = [
        reduce_steps(
            spot,
            orders[k],
            (own.at[0, k], halves.at[k], ready_ref.at[k]),
            first_sends.at[k],
            first_recvs.at[k],
        )
        for k in range(2)
    ]

    def pair_step(j, carry):
        for copy in weights_at(2 * j):
            copy.wait()
        away = tile_step(2 * j, (1 - core) * 2 + j, lambda: None)
        for k in range(2):
            sent[j, k] = away[k].astype(low)
            swap(j, k).start()

        def forward():
            @pl.when(j == 1)
            def _():
                for hop in hops:
                    hop[0][1]()
                    hop[1][0]()

        for copy in weights_at(2 * j + 1):
            copy.wait()
        home = tile_step(2 * j + 1, core * 2 + j, forward)
        for k in range(2):
            swap(j, k).wait()
            own[j, k] = (home[k] + got[j, k].astype(wide)).astype(low)

        @pl.when(j == 0)
        def _():
            for hop in hops:
                hop[0][0]()

        return carry

    def weights_at(k):
        return [
            pltpu.make_async_copy(project_ref.at[k], project_ref.at[k], weight_sems.at[0, k]),
            pltpu.make_async_copy(expand_ref.at[k], expand_ref.at[k], weight_sems.at[1, k]),
        ]

    lax.fori_loop(0, 2, pair_step, 0)
    keep = pltpu.make_async_copy(own.at[1], own_hbm.at[1], own_sems.at[0])
    keep.start()
    load_mixed.wait()

    def leave(part):
        rows = pl.ds(pl.multiple_of(part * piece, piece), piece)
        return [
            pltpu.make_async_copy(out_ref.at[rows], out_hbm.at[rows], leave_sems.at[0, part]),
            pltpu.make_async_copy(
                back_sum.at[rows], mixed_back_hbm.at[rows], leave_sems.at[1, part]
            ),
        ]

    def end_step(part, carry):
        for quarter in range(4):
            size = piece // 4
            rows = pl.ds(pl.multiple_of(part * piece + quarter * size, size), size)
            mixed = mixed_ref[rows, :]
            out_ref[rows, :] = (out_sum[rows, :] + mixed).astype(low)
            unit, factor = normalise(mixed)
            norm_back = back_sum[rows, :]
            vectors[2:3, :] += jnp.sum(norm_back * unit, 0, keepdims=True)
            vectors[3:4, :] += jnp.sum(norm_back, 0, keepdims=True)
            pull = norm_back * as_row(scale_ref)
            pull = pull - jnp.mean(pull, -1, keepdims=True) - unit * jnp.mean(
                pull * unit, -1, keepdims=True
            )
            back_sum[rows, :] = up_ref[rows, :].astype(wide) + factor * pull
        for copy in leave(part):
            copy.start()
        return carry

    lax.fori_loop(0, count // piece, end_step, 0)
    for hop in hops:
        hop[1][1]()
    keep.wait()
    for part in range(count // piece):
        for copy in leave(part):
            copy.wait()


def call_dense(second_norm, upstream, scale, returned, lift, mixed, expand, project, cid):
    count, features = second_norm.shape
    square = (features, features)
    outs = (
        ((count, features), low),
        ((count, features), wide),
        ((2, 2, *square), low),
        ((2, features // 4, features), low),
        ((16, features), wide),
    )
    shapes = [jax.ShapeDtypeStruct(shape, kind) for shape, kind in outs]
    anywhere = pl.BlockSpec(memory_space=pl.ANY)
    dma = pltpu.SemaphoreType.DMA
    return pl.pallas_call(
        dense_kernel,
        out_shape=shapes,
        in_specs=[vmem] * 5 + [anywhere] * 3,
        out_specs=[anywhere] * 3 + [vmem] * 2,
        scratch_shapes=[
            pltpu.VMEM((count, features), wide),
            pltpu.VMEM((4, *square), low),
            pltpu.VMEM((4, *square), low),
            pltpu.VMEM((count, features), low),
            pltpu.VMEM((count, features), wide),
            pltpu.VMEM((count, features), wide),
            pltpu.VMEM((count, features), low),
            pltpu.VMEM((count, features), low),
            pltpu.VMEM((2, 2, *square), low),
            pltpu.VMEM((2, 2, *square), low),
            pltpu.VMEM((2, 2, *square), low),
            pltpu.VMEM((2, features // 2, features), low),
            dma((1,)),
            dma((2, 4)),
            dma((2, count // 512)),
            dma((1,)),
            dma((2, 2)),
            dma((2, 2)),
            dma((2, 2)),
            dma((2, 2)),
        ],
        compiler_params=pltpu.CompilerParams(
            collective_id=cid, has_side_effects=True, vmem_limit_bytes=60 * 1024 * 1024
        ),
    )(second_norm, upstream, scale, returned, lift, mixed, expand, project)


def shards(
    tokens,
    region_sizes,
    region_starts,
    entry_gain,
    entry_shift,
    spectral_kernel,
    spectral_bias,
    spectral_mixer,
    spectral_offset,
    exit_scale,
    exit_center,
    dense_expand,
    dense_lift,
    dense_project,
    dense_return,
    cotangent,
):
    regions, rows_here, cols_here, features = tokens.shape
    row_devices = lax.axis_size("rows")
    cols = lax.axis_size("cols")
    blocks, block_size = spectral_kernel.shape[1:3]
    chips = row_devices // 2 * cols
    fits = (
        row_devices % 2 == 0
        and chips == regions * blocks
        and cols == 2
        and cols_here == 64
        and rows_here == 8
        and block_size == 96
        and blocks == 8
        and regions == 2
        and dense_expand.shape == (features, 4 * features)
    )
    if not fits:
        return shards_general(
            tokens,
            region_sizes,
            region_starts,
            entry_gain,
            entry_shift,
            spectral_kernel,
            spectral_bias,
            spectral_mixer,
            spectral_offset,
            exit_scale,
            exit_center,
            dense_expand,
            dense_lift,
            dense_project,
            dense_return,
            cotangent,
        )
    height = rows_here * row_devices
    width = cols_here * cols
    patches = rows_here * cols_here
    count = regions * patches
    sizes = (regions, blocks, block_size, chips, cols, patches)
    block = ((lax.axis_index("rows") // 2) * cols + lax.axis_index("cols")) % blocks

    def own(weight):
        return lax.dynamic_index_in_dim(weight, block, 1, False)

    def square(weight):
        real, imaginary = weight[0], weight[1]
        return jnp.concatenate(
            [
                jnp.concatenate([real, imaginary], 1),
                jnp.concatenate([-imaginary, real], 1),
            ],
            0,
        )

    side = 2 * block_size
    weights = jnp.stack([square(own(spectral_kernel)), square(own(spectral_mixer))])
    biases = jnp.stack(
        [own(spectral_bias).reshape(side), own(spectral_offset).reshape(side)], 1
    )
    to_modes, to_columns, ahead, behind, eye = task_tables(height, width, rows_here, cols_here)
    flat_tokens = tokens.reshape(count, features)
    upstream = cotangent.reshape(count, features)
    steps = width // 4 // 4
    shape = (steps, side, 4 * 128)
    kept = ((shape, low), (shape, wide), (shape, low), (shape, wide))
    scalars = (region_sizes, region_starts)
    mixed, second_norm, *stream = call_filter(
        forward_kernel,
        sizes,
        (((count, features), wide), ((count, features), low), *kept),
        1,
        (
            flat_tokens,
            entry_gain,
            entry_shift,
            exit_scale,
            exit_center,
            weights,
            biases,
            to_modes,
            to_columns,
            ahead,
            behind,
            eye,
        ),
        scalars,
        (),
        range(6),
        forward_scratch(sizes, kept),
    )
    output, mixed_back, own_tiles, ready, part_sums = call_dense(
        second_norm,
        upstream,
        exit_scale,
        dense_return,
        dense_lift.reshape(-1, features),
        mixed,
        dense_expand,
        dense_project,
        3,
    )
    slope, project_sum, expand_sum, gathered, sums = call_filter(
        backward_kernel,
        sizes,
        (
            ((count, features), wide),
            (dense_project.shape, low),
            (dense_expand.shape, low),
            ((blocks, 2 * side, 128), wide),
            ((16, features), wide),
        ),
        2,
        (
            flat_tokens,
            mixed_back,
            entry_gain,
            weights,
            to_modes.T,
            to_columns.T,
            ahead,
            behind,
            eye,
            *stream,
            own_tiles,
            ready,
            part_sums,
        ),
        scalars,
        (0, 9, 10, 11, 12, 13),
        range(3),
        backward_scratch(sizes, kept),
    )
    weights = gathered[:, :, :block_size].reshape(blocks, 2, 2, block_size, block_size)
    weights = weights.transpose(1, 2, 0, 3, 4)
    biases = gathered[:, :, block_size].reshape(blocks, 2, 2, block_size).transpose(1, 2, 0, 3)
    return (
        output.reshape(tokens.shape),
        slope.reshape(tokens.shape),
        sums[0],
        sums[1],
        weights[0],
        biases[0],
        weights[1],
        biases[1],
        sums[2],
        sums[3],
        expand_sum.astype(wide),
        sums[5:9].reshape(-1),
        project_sum.astype(wide),
        sums[4],
    )


def solution(mesh):
    placed = (
        P(None, "rows", "cols", None),
        P(),
        P(),
        P(),
        P(),
        P(),
        P(),
        P(),
        P(),
        P(),
        P(),
        P(),
        P(),
        P(),
        P(),
        P(None, "rows", "cols", None),
    )
    return jax.shard_map(
        shards,
        mesh=mesh,
        in_specs=placed,
        out_specs=(
            P(None, "rows", "cols", None),
            P(None, "rows", "cols", None),
            P(),
            P(),
            P(),
            P(),
            P(),
            P(),
            P(),
            P(),
            P(),
            P(),
            P(),
            P(),
        ),
        check_vma=False,
    )
```

```python
import functools
import math

import jax
import jax.numpy as jnp
import ml_dtypes
import numpy as np
from jax import lax
from jax.experimental import pallas as pl
from jax.experimental.pallas import tpu as pltpu
from jax.sharding import PartitionSpec as P

shrink_width = 0.01
norm_eps = 1e-06
highest = lax.Precision.HIGHEST


def tables(height, width, modes):
    column = jnp.arange(width, dtype=jnp.int32)
    frequency = jnp.arange(modes, dtype=jnp.int32)
    turns = column[:, None] * frequency[None, :] % width
    angle = turns.astype(jnp.float32) * (2.0 * math.pi / width)
    cosine = jnp.cos(angle)
    sine = jnp.sin(angle)
    scale = 1.0 / math.sqrt(width)
    forward_zonal = jnp.stack([cosine, -sine], 1) * scale
    factor = jnp.where(frequency == 0, 1.0, 2.0).astype(jnp.float32)
    inverse_zonal = jnp.stack([cosine.T * factor[:, None], -sine.T * factor[:, None]], 0) * scale
    latitude = jnp.arange(height, dtype=jnp.int32)
    meridian_turns = latitude[:, None] * latitude[None, :] % height
    meridian_angle = meridian_turns.astype(jnp.float32) * (2.0 * math.pi / height)
    meridian_cos = jnp.cos(meridian_angle) / math.sqrt(height)
    meridian_sin = jnp.sin(meridian_angle) / math.sqrt(height)
    meridian_table = jnp.stack(
        [jnp.stack([meridian_cos, meridian_sin], -1), jnp.stack([-meridian_sin, meridian_cos], -1)],
        1,
    )
    forward_low = forward_zonal.astype(jnp.bfloat16)
    inverse_low = inverse_zonal.astype(jnp.bfloat16)
    meridian_low = meridian_table.astype(jnp.bfloat16)
    meridian_wide = meridian_low.astype(jnp.float32)
    return (forward_low, inverse_low, meridian_low, meridian_wide)


def layer_norm(value, gain, shift):
    centre = jnp.mean(value, -1, keepdims=True)
    centred = value - centre
    spread = jnp.mean(centred * centred, -1, keepdims=True)
    return centred * lax.rsqrt(spread + norm_eps) * gain + shift


def gelu_exact(value):
    return jax.nn.gelu(value, approximate=False)


def shrink(value):
    return value - shrink_width * jnp.tanh(value / shrink_width)


def block_layout(spectrum, blocks, block_size):
    leading = spectrum.shape[:3]
    parts = spectrum.reshape(leading + (2, blocks, block_size))
    parts = jnp.moveaxis(parts, 3, 4)
    return parts.reshape((-1, blocks, 2 * block_size))


def spectral_layout(modes_flat, leading, blocks, block_size):
    parts = modes_flat.reshape(leading + (blocks, 2, block_size))
    parts = jnp.moveaxis(parts, 4, 3)
    return parts.reshape(leading + (2, blocks * block_size))


def complex_matrix(weight):
    real = weight[0]
    imaginary = weight[1]
    upper = jnp.concatenate([real, imaginary], 2)
    lower = jnp.concatenate([-imaginary, real], 2)
    return jnp.concatenate([upper, lower], 1)


def matrix_gradient(whole, block_size):
    upper = whole[:, :block_size]
    lower = whole[:, block_size:]
    real = upper[:, :, :block_size] + lower[:, :, block_size:]
    imaginary = upper[:, :, block_size:] - lower[:, :, :block_size]
    return jnp.stack([real, imaginary], 0)


def bias_rows(bias):
    return jnp.moveaxis(bias, 0, 1).reshape(bias.shape[1], 2 * bias.shape[2])


def bias_gradient(summed, block_size):
    return jnp.moveaxis(summed.reshape(summed.shape[0], 2, block_size), 1, 0)


def advance(tokens, mask, weights, grids, layout):
    (
        entry_gain,
        entry_shift,
        spectral_kernel,
        spectral_bias,
        spectral_mixer,
        spectral_offset,
        exit_scale,
        exit_center,
        dense_expand,
        dense_lift,
        dense_project,
        dense_return,
    ) = weights
    forward_zonal, inverse_zonal, meridian_table, meridian_wide = grids
    blocks, block_size, first_block = layout
    residual = tokens.astype(jnp.float32)
    normed = layer_norm(residual, entry_gain, entry_shift)
    sent = (mask * normed).astype(jnp.bfloat16)
    by_channel = lax.all_to_all(sent, "cols", split_axis=3, concat_axis=2, tiled=True)
    zonal = jnp.einsum(
        "rhwc,wpk->rhkpc", by_channel, forward_zonal, preferred_element_type=jnp.float32
    )
    by_mode = lax.all_to_all(
        zonal.astype(jnp.bfloat16), "rows", split_axis=2, concat_axis=1, tiled=True
    )
    spectrum = jnp.einsum(
        "kphq,rhmqc->rkmpc", meridian_table, by_mode, preferred_element_type=jnp.float32
    ).astype(jnp.bfloat16)
    leading = spectrum.shape[:3]
    modes_flat = block_layout(spectrum, blocks, block_size)
    kernel_matrix = complex_matrix(
        lax.dynamic_slice_in_dim(spectral_kernel, first_block, blocks, 1)
    )
    mixer_matrix = complex_matrix(lax.dynamic_slice_in_dim(spectral_mixer, first_block, blocks, 1))
    kernel_bias = bias_rows(lax.dynamic_slice_in_dim(spectral_bias, first_block, blocks, 1))
    mixer_bias = bias_rows(lax.dynamic_slice_in_dim(spectral_offset, first_block, blocks, 1))
    first_pre = (
        jnp.einsum("nbx,bxy->nby", modes_flat, kernel_matrix, preferred_element_type=jnp.float32)
        + kernel_bias
    )
    first_act = gelu_exact(first_pre).astype(jnp.bfloat16)
    second_pre = (
        jnp.einsum("nbx,bxy->nby", first_act, mixer_matrix, preferred_element_type=jnp.float32)
        + mixer_bias
    )
    shrunk = spectral_layout(shrink(second_pre), leading, blocks, block_size)
    back_meridian = jnp.einsum(
        "kphq,rkmpc->rhmqc", meridian_wide, shrunk, precision=highest
    ).astype(jnp.bfloat16)
    by_row = lax.all_to_all(back_meridian, "rows", split_axis=1, concat_axis=2, tiled=True)
    filtered = jnp.einsum(
        "rhkpc,pkw->rhwc", by_row, inverse_zonal, preferred_element_type=jnp.float32
    ).astype(jnp.bfloat16)
    by_token = lax.all_to_all(filtered, "cols", split_axis=2, concat_axis=3, tiled=True)
    mixed = residual + mask * by_token.astype(jnp.float32) + normed
    features = mixed.shape[-1]
    second_norm = (
        layer_norm(mixed, exit_scale, exit_center).astype(jnp.bfloat16).reshape(-1, features)
    )
    hidden_pre = jnp.dot(second_norm, dense_expand, preferred_element_type=jnp.float32) + dense_lift
    hidden = gelu_exact(hidden_pre).astype(jnp.bfloat16)
    output = mixed + (
        jnp.dot(hidden, dense_project, preferred_element_type=jnp.float32) + dense_return
    ).reshape(mixed.shape)
    kept = (
        residual,
        modes_flat,
        first_pre,
        first_act,
        second_pre,
        mixed,
        second_norm,
        hidden_pre,
        hidden,
        kernel_matrix,
        mixer_matrix,
        leading,
    )
    return (output, kept)


def retreat(cotangent, mask, kept, weights, grids, layout):
    (
        entry_gain,
        entry_shift,
        spectral_kernel,
        spectral_bias,
        spectral_mixer,
        spectral_offset,
        exit_scale,
        exit_center,
        dense_expand,
        dense_lift,
        dense_project,
        dense_return,
    ) = weights
    forward_zonal, inverse_zonal, meridian_table, meridian_wide = grids
    blocks, block_size, first_block = layout
    (
        residual,
        modes_flat,
        first_pre,
        first_act,
        second_pre,
        mixed,
        second_norm,
        hidden_pre,
        hidden,
        kernel_matrix,
        mixer_matrix,
        leading,
    ) = kept
    features = mixed.shape[-1]
    upstream = cotangent.reshape(-1, features)
    gradient_project = jnp.einsum("tf,tc->fc", hidden, upstream, preferred_element_type=jnp.float32)
    gradient_return = jnp.sum(upstream.astype(jnp.float32), 0)
    outer = (gradient_project, gradient_return)
    hidden_back = jnp.einsum(
        "tc,fc->tf", upstream, dense_project, preferred_element_type=jnp.float32
    )
    hidden_pull = jax.vjp(gelu_exact, hidden_pre)[1]
    pre_back = hidden_pull(hidden_back)[0].astype(jnp.bfloat16)
    gradient_expand = jnp.einsum(
        "tc,tf->cf", second_norm, pre_back, preferred_element_type=jnp.float32
    )
    gradient_lift = jnp.sum(pre_back.astype(jnp.float32), 0)
    norm_back = jnp.einsum(
        "tf,cf->tc", pre_back, dense_expand, preferred_element_type=jnp.float32
    ).reshape(mixed.shape)
    exit_pull = jax.vjp(layer_norm, mixed, exit_scale, exit_center)[1]
    mixed_part, gradient_scale, gradient_center = exit_pull(norm_back)
    inner = (gradient_expand, gradient_lift, gradient_scale, gradient_center)
    mixed_back = cotangent.astype(jnp.float32) + mixed_part
    filter_back = (mask * mixed_back).astype(jnp.bfloat16)
    channel_back = lax.all_to_all(filter_back, "cols", split_axis=3, concat_axis=2, tiled=True)
    zonal_back = jnp.einsum(
        "rhwc,pkw->rhkpc", channel_back, inverse_zonal, preferred_element_type=jnp.float32
    ).astype(jnp.bfloat16)
    meridian_back = lax.all_to_all(zonal_back, "rows", split_axis=2, concat_axis=1, tiled=True)
    shrunk_back = jnp.einsum(
        "kphq,rhmqc->rkmpc", meridian_table, meridian_back, preferred_element_type=jnp.float32
    )
    shrink_pull = jax.vjp(shrink, second_pre)[1]
    second_back = shrink_pull(block_layout(shrunk_back, blocks, block_size))[0].astype(jnp.bfloat16)
    mixer_whole = jnp.einsum(
        "nbx,nby->bxy", first_act, second_back, preferred_element_type=jnp.float32
    )
    offset_rows = jnp.sum(second_back.astype(jnp.float32), 0)
    activation_back = jnp.einsum(
        "nby,bxy->nbx", second_back, mixer_matrix, preferred_element_type=jnp.float32
    )
    first_pull = jax.vjp(gelu_exact, first_pre)[1]
    first_back = first_pull(activation_back)[0].astype(jnp.bfloat16)
    kernel_whole = jnp.einsum(
        "nbx,nby->bxy", modes_flat, first_back, preferred_element_type=jnp.float32
    )
    kernel_rows = jnp.sum(first_back.astype(jnp.float32), 0)
    spectrum_back = spectral_layout(
        jnp.einsum("nby,bxy->nbx", first_back, kernel_matrix, preferred_element_type=jnp.float32),
        leading,
        blocks,
        block_size,
    )
    modes_back = jnp.einsum(
        "kphq,rkmpc->rhmqc", meridian_wide, spectrum_back, precision=highest
    ).astype(jnp.bfloat16)
    row_back = lax.all_to_all(modes_back, "rows", split_axis=1, concat_axis=2, tiled=True)
    sent_back = jnp.einsum(
        "rhkpc,wpk->rhwc", row_back, forward_zonal, preferred_element_type=jnp.float32
    ).astype(jnp.bfloat16)
    token_back = lax.all_to_all(sent_back, "cols", split_axis=2, concat_axis=3, tiled=True)
    normed_back = mixed_back + mask * token_back.astype(jnp.float32)
    entry_pull = jax.vjp(layer_norm, residual, entry_gain, entry_shift)[1]
    residual_part, gradient_gain, gradient_shift = entry_pull(normed_back)
    gradient_tokens = mixed_back + residual_part
    shared = (
        gradient_gain,
        gradient_shift,
        inner[2],
        inner[3],
        inner[0],
        inner[1],
        outer[0],
        outer[1],
    )
    local_blocks = (
        matrix_gradient(kernel_whole, block_size),
        bias_gradient(kernel_rows, block_size),
        matrix_gradient(mixer_whole, block_size),
        bias_gradient(offset_rows, block_size),
    )
    return (gradient_tokens, shared, local_blocks)


def shards_general(
    tokens,
    region_sizes,
    region_starts,
    entry_gain,
    entry_shift,
    spectral_kernel,
    spectral_bias,
    spectral_mixer,
    spectral_offset,
    exit_scale,
    exit_center,
    dense_expand,
    dense_lift,
    dense_project,
    dense_return,
    cotangent,
):
    rows_here = tokens.shape[1]
    cols_here = tokens.shape[2]
    height = rows_here * lax.axis_size("rows")
    width = cols_here * lax.axis_size("cols")
    grids = tables(height, width, width // 2)
    latitude = lax.axis_index("rows") * rows_here + jnp.arange(rows_here, dtype=jnp.int32)
    longitude = lax.axis_index("cols") * cols_here + jnp.arange(cols_here, dtype=jnp.int32)
    inside_rows = latitude[None, :, None] < region_sizes[:, 0][:, None, None]
    offset = (longitude[None, None, :] - region_starts[:, None, None]) % width
    inside_cols = offset < region_sizes[:, 1][:, None, None]
    mask = jnp.where(inside_rows & inside_cols, 1.0, 0.0).astype(jnp.float32)[..., None]
    block_size = spectral_kernel.shape[2]
    total_blocks = spectral_kernel.shape[1]
    blocks = tokens.shape[3] // lax.axis_size("cols") // block_size
    first_block = lax.axis_index("cols") * blocks
    layout = (blocks, block_size, first_block)
    weights = (
        entry_gain,
        entry_shift,
        spectral_kernel,
        spectral_bias,
        spectral_mixer,
        spectral_offset,
        exit_scale,
        exit_center,
        dense_expand,
        dense_lift,
        dense_project,
        dense_return,
    )
    output, kept = advance(tokens, mask, weights, grids, layout)
    gradient_tokens, shared, local_blocks = retreat(cotangent, mask, kept, weights, grids, layout)
    (
        gain_part,
        shift_part,
        scale_part,
        center_part,
        expand_part,
        lift_part,
        project_part,
        return_part,
    ) = shared
    everywhere = ("rows", "cols")
    project_sum = lax.psum(project_part.astype(jnp.bfloat16), everywhere).astype(jnp.float32)
    expand_sum = lax.psum(expand_part.astype(jnp.bfloat16), everywhere).astype(jnp.float32)
    vectors = (gain_part, shift_part, scale_part, center_part, lift_part, return_part)
    sums = lax.psum(jnp.concatenate(vectors), everywhere)
    ends = [0]
    for vector in vectors:
        ends.append(ends[-1] + vector.shape[0])
    parts = [sums[low:high] for low, high in zip(ends[:-1], ends[1:])]
    summed = (*parts[:4], expand_sum, parts[4], project_sum, parts[5])
    kernel_local, bias_local, mixer_local, offset_local = local_blocks
    kernel_full = lax.dynamic_update_slice_in_dim(
        jnp.zeros((2, total_blocks, block_size, block_size), jnp.float32),
        kernel_local,
        first_block,
        1,
    )
    bias_full = lax.dynamic_update_slice_in_dim(
        jnp.zeros((2, total_blocks, block_size), jnp.float32), bias_local, first_block, 1
    )
    mixer_full = lax.dynamic_update_slice_in_dim(
        jnp.zeros((2, total_blocks, block_size, block_size), jnp.float32),
        mixer_local,
        first_block,
        1,
    )
    offset_full = lax.dynamic_update_slice_in_dim(
        jnp.zeros((2, total_blocks, block_size), jnp.float32), offset_local, first_block, 1
    )
    block_totals = lax.psum((kernel_full, bias_full, mixer_full, offset_full), ("rows", "cols"))
    return (
        output.astype(jnp.bfloat16),
        gradient_tokens,
        summed[0],
        summed[1],
        block_totals[0],
        block_totals[1],
        block_totals[2],
        block_totals[3],
        summed[2],
        summed[3],
        summed[4],
        summed[5],
        summed[6],
        summed[7],
    )


MESH = pl.DeviceIdType.MESH
wide = jnp.float32
low = jnp.bfloat16
by_last = (((1,), (1,)), ((), ()))
by_first = (((0,), (0,)), ((), ()))
vmem = pl.BlockSpec(memory_space=pltpu.VMEM)


def dot(a, b):
    return jnp.dot(a, b, preferred_element_type=wide)


def dot_last(a, b):
    return lax.dot_general(a, b, by_last, preferred_element_type=wide)


def dot_first(a, b):
    return lax.dot_general(a, b, by_first, preferred_element_type=wide)


def task_tables(height, width, rows_here, cols_here):
    modes = width // 2
    near = modes // 2
    column = np.arange(width)
    frequency = np.arange(modes)
    angle = (column[:, None] * frequency[None, :] % width).astype(np.float32) * np.float32(
        2.0 * math.pi / width
    )
    scale = np.float32(1.0 / math.sqrt(width))
    zonal = np.stack([np.cos(angle), -np.sin(angle)], 1) * scale
    factor = np.where(frequency == 0, 1.0, 2.0).astype(np.float32)
    inverse = (
        np.stack([np.cos(angle).T * factor[:, None], -np.sin(angle).T * factor[:, None]], 0) * scale
    )
    latitude = np.arange(height)
    turn = (latitude[:, None] * latitude[None, :] % height).astype(np.float32) * np.float32(
        2.0 * math.pi / height
    )
    cosine = np.cos(turn) / np.float32(math.sqrt(height))
    sine = np.sin(turn) / np.float32(math.sqrt(height))
    meridian = np.stack([np.stack([cosine, sine], -1), np.stack([-sine, cosine], -1)], 1)
    halves = width // cols_here
    split_f = zonal.reshape(halves, cols_here, 2, 2, near)
    to_modes = np.zeros((halves, 2, cols_here, 2, 2, 2, near), np.float32)
    split_g = inverse.reshape(2, 2, near, halves, cols_here)
    to_columns = np.zeros((2, 2, 2, near, halves, 2, cols_here), np.float32)
    for i in range(2):
        to_modes[:, i, :, :, i] = split_f.transpose(0, 1, 3, 2, 4)
        to_columns[:, i, :, :, :, i] = split_g.transpose(1, 0, 2, 3, 4)
    side = halves * 2 * cols_here
    to_modes = to_modes.reshape(side, side)
    to_columns = to_columns.reshape(side, side)
    pairs = rows_here // 2
    senders = height // rows_here
    order = np.zeros((height // 2, 2), np.int64)
    for core in range(2):
        for chip in range(senders // 2):
            for pair in range(pairs):
                for i in range(2):
                    order[(core * (senders // 2) + chip) * pairs + pair, i] = (
                        (chip * 2 + core) * rows_here + pair * 2 + i
                    )
    placed = meridian[:, :, order]
    ahead = np.zeros((2, 2, 2, height // 2, 2, 2, height), np.float32)
    for c in range(2):
        ahead[:, :, c, :, c] = placed.transpose(3, 4, 2, 1, 0)
    ahead = ahead.reshape(2, 2 * height, 4 * height)
    behind = ahead.reshape(4 * height, 4 * height).T
    return tuple(
        np.asarray(item, ml_dtypes.bfloat16)
        for item in (to_modes, to_columns, ahead, behind, np.eye(256, dtype=np.float32))
    )


def chip_device(chip, core, cols):
    return ((chip // cols) * 2 + core, chip % cols)


def swap_bits(value, mask, bits):
    out = 0
    for k in range(bits):
        bit = (value // (1 << k)) % 2
        if (mask >> k) & 1:
            bit = 1 - bit
        out = out + bit * (1 << k)
    return out


def greet(chips, cols):
    row = lax.axis_index("rows")
    core = row % 2
    me = (row // 2) * cols + lax.axis_index("cols")
    barrier = pltpu.get_barrier_semaphore()
    for step in range(1, chips):
        other = (me + step) % chips
        pl.semaphore_signal(
            barrier, inc=1, device_id=chip_device(other, core, cols), device_id_type=MESH
        )
    pl.semaphore_signal(
        barrier, inc=1, device_id=chip_device(me, 1 - core, cols), device_id_type=MESH
    )
    pl.semaphore_wait(barrier, chips)
    return me, core


def send_piece(src, dst, send_sem, recv_sem, target, me, core, cols):
    @pl.when(target == me)
    def _():
        pltpu.make_async_copy(src, dst, recv_sem).start()

    @pl.when(target != me)
    def _():
        pltpu.make_async_remote_copy(
            src_ref=src,
            dst_ref=dst,
            send_sem=send_sem,
            recv_sem=recv_sem,
            device_id=chip_device(target, core, cols),
            device_id_type=MESH,
        ).start()


def await_piece(ref, sem):
    pltpu.make_async_copy(ref, ref, sem).wait()


def to_feature_rows(out_ref, region, place, piece, eye):
    features = piece.shape[1]
    for low_end in range(0, features, 256):
        turned = dot_last(eye, piece[:, low_end : low_end + 256])
        out_ref[region, low_end : low_end + 256, place] = turned.astype(low)


def modes_first(block, group, half):
    columns = []
    for m in range(group):
        rows = block[m * half : (m + 1) * half]
        height = block.shape[1] // 4
        columns.append(
            jnp.concatenate(
                [
                    rows[:, (c * 2 + p) * height : (c * 2 + p + 1) * height]
                    for p in range(2)
                    for c in range(2)
                ],
                0,
            )
        )
    return jnp.concatenate(columns, 1)


def modes_last(block, group, half):
    height = block.shape[1] // group
    rows = []
    for m in range(group):
        part = block[:, m * height : (m + 1) * height]
        rows.append(
            jnp.concatenate(
                [
                    part[(p * 2 + c) * half : (p * 2 + c + 1) * half]
                    for c in range(2)
                    for p in range(2)
                ],
                1,
            )
        )
    return jnp.concatenate(rows, 0)


def filter_pass(sizes, me, core, produce, middle, consume, tables, work, sems, tick):
    regions, blocks, block_size, chips, cols, tokens = sizes
    table_in, table_out, ahead, behind = tables
    sent, got, zonal, zonal_got, tall, flat, back, sibling, leaving, coming = work
    send_a, recv_a, send_b, recv_b, send_c, recv_c, send_d, recv_d = sems
    lanes = 128
    senders = chips // cols
    pairs = tokens // lanes
    half = block_size // 2
    points = senders * pairs
    group = 4
    bits = (blocks - 1).bit_length()
    home = me // blocks
    tick("start")
    for turn in range(regions):
        region = (home + 1 + turn) % regions
        produce(region)
        for step in range(blocks - 1, -1, -1):
            target = region * blocks + swap_bits(me % blocks, step, bits)
            src = sent.at[region, pl.ds(pl.multiple_of(target % blocks * block_size, 32), block_size)]
            place = turn * blocks + step
            send_piece(src, got.at[me], send_a.at[place], recv_a.at[me], target, me, core, cols)
    tick("sent")

    def zonal_step(index, carry):
        tick("arrival", index)
        chip = (index + home * senders // regions) % senders
        for col in range(cols):
            await_piece(got.at[chip * cols + col], recv_a.at[chip * cols + col])
        for pair in range(pairs):
            x = jnp.concatenate(
                [got[chip * cols + col, :, pair * lanes : (pair + 1) * lanes] for col in range(cols)], 1
            )
            y = dot(x, table_in[...]).astype(low)
            for part in range(2):
                zonal[part, chip * pairs + pair] = y[:, part * lanes : (part + 1) * lanes]
        return carry

    lax.fori_loop(0, senders, zonal_step, 0)
    swap = pltpu.make_async_remote_copy(
        src_ref=zonal.at[1 - core],
        dst_ref=zonal_got,
        send_sem=send_b,
        recv_sem=recv_b,
        device_id=chip_device(me, 1 - core, cols),
        device_id_type=MESH,
    )
    swap.start()
    tick("zonal")

    def widen(source, first):
        def step(point, carry):
            row = pl.multiple_of((first + point) * block_size, 32)
            tall[pl.ds(row, block_size), :] = source(point).astype(wide)
            return carry

        lax.fori_loop(0, points, step, 0)

    widen(lambda point: zonal[core, point], core * points)
    swap.wait()
    widen(lambda point: zonal_got[point], (1 - core) * points)
    modes = lanes // 4

    def turn_step(c, carry):
        x = jnp.concatenate(
            [tall[pl.ds(c + half * side, 2 * points, stride=block_size), :] for side in range(2)], 0
        )
        y = jnp.transpose(x)
        for i in range(4):
            flat[i, pl.ds(c, modes, stride=half), :] = y[i * modes : (i + 1) * modes]
        return carry

    lax.fori_loop(0, half, turn_step, 0, unroll=4)
    tick("turned")

    def mode_step(step, carry):
        rows = pl.ds(pl.multiple_of(step * group * half, 64), group * half)
        spectrum = 0.0
        for i in range(2):
            x = jnp.concatenate([flat[i * 2, rows, :], flat[i * 2 + 1, rows, :]], 1).astype(low)
            spectrum = spectrum + dot(x, ahead[i])
        out = modes_last(middle(step, modes_first(spectrum, group, half)), group, half)
        high = out.astype(low)
        rest = (out - high.astype(wide)).astype(low)
        y = (dot(high, behind[...]) + dot(rest, behind[...])).astype(low).astype(wide)
        for i in range(4):
            flat[i, rows, :] = y[:, i * lanes : (i + 1) * lanes]
        tick("mode", step)
        return carry

    lax.fori_loop(0, modes // group, mode_step, 0)
    tick("modes")

    def return_step(c, carry):
        x = jnp.concatenate([flat[i, pl.ds(c, modes, stride=half), :] for i in range(4)], 0)
        y = jnp.transpose(x)
        for side in range(2):
            tall[pl.ds(c + half * side, 2 * points, stride=block_size), :] = y[
                side * 2 * points : (side + 1) * 2 * points
            ]
        return carry

    lax.fori_loop(0, half, return_step, 0, unroll=4)
    tick("returned")

    def narrow(store, first):
        def step(point, carry):
            row = pl.multiple_of((first + point) * block_size, 32)
            store(point, tall[pl.ds(row, block_size), :].astype(low))
            return carry

        lax.fori_loop(0, points, step, 0)

    def to_sibling(point, value):
        back[point] = value

    def to_self(point, value):
        sibling[core, point] = value

    narrow(to_sibling, (1 - core) * points)
    swap_back = pltpu.make_async_remote_copy(
        src_ref=back,
        dst_ref=sibling.at[core],
        send_sem=send_c,
        recv_sem=recv_c,
        device_id=chip_device(me, 1 - core, cols),
        device_id_type=MESH,
    )
    swap_back.start()
    tick("back")
    narrow(to_self, core * points)
    swap_back.wait_send()
    await_piece(sibling.at[1 - core], recv_c)

    def column_step(index, carry):
        chip = (index + (home + 1) * senders // regions) % senders
        for pair in range(pairs):
            point = chip * pairs + pair
            x = jnp.concatenate([sibling[0, point], sibling[1, point]], 1)
            y = dot(x, table_out[...]).astype(low)
            for col in range(cols):
                leaving[chip * cols + col, :, pair * lanes : (pair + 1) * lanes] = y[
                    :, col * lanes : (col + 1) * lanes
                ]
        for col in range(cols):
            target = chip * cols + col
            dst = coming.at[
                me // blocks, pl.ds(pl.multiple_of(me % blocks * block_size, 32), block_size)
            ]
            send_piece(
                leaving.at[target], dst, send_d.at[target], recv_d.at[me], target, me, core, cols
            )
        return carry

    lax.fori_loop(0, senders, column_step, 0)
    tick("columns")
    for turn in range(regions):
        region = (home + turn) % regions

        def arrive(block, carry, region=region):
            ref = coming.at[region, pl.ds(pl.multiple_of(block * block_size, 32), block_size)]
            await_piece(ref, recv_d.at[region * blocks + block])
            return carry

        lax.fori_loop(0, blocks, arrive, 0)
        consume(region)
        tick("region")

    for place in range(regions * blocks):
        turn, step = place // blocks, place % blocks
        target = (home + 1 + turn) % regions * blocks + swap_bits(me % blocks, step, bits)

        @pl.when(target != me)
        def _():
            await_piece(got.at[0], send_a.at[place])

        @pl.when(place != me)
        def _():
            await_piece(leaving.at[0], send_d.at[place])


def work_shapes(sizes):
    regions, blocks, block_size, chips, cols, tokens = sizes
    lanes = 128
    features = blocks * block_size
    points = (chips // cols) * (tokens // lanes)
    rows = (lanes // 4) * (block_size // 2)
    return [
        pltpu.VMEM((regions, features, tokens), low),
        pltpu.VMEM((chips, block_size, tokens), low),
        pltpu.VMEM((2, points, block_size, lanes), low),
        pltpu.VMEM((points, block_size, lanes), low),
        pltpu.VMEM((2 * points * block_size, lanes), wide),
        pltpu.VMEM((4, rows, lanes), wide),
        pltpu.VMEM((points, block_size, lanes), low),
        pltpu.VMEM((2, points, block_size, lanes), low),
        pltpu.VMEM((chips, block_size, tokens), low),
        pltpu.VMEM((regions, features, tokens), low),
        pltpu.SemaphoreType.DMA((chips,)),
        pltpu.SemaphoreType.DMA((chips,)),
        pltpu.SemaphoreType.DMA,
        pltpu.SemaphoreType.DMA,
        pltpu.SemaphoreType.DMA,
        pltpu.SemaphoreType.DMA,
        pltpu.SemaphoreType.DMA((chips,)),
        pltpu.SemaphoreType.DMA((chips,)),
    ]


def normalise(value):
    centre = jnp.mean(value, -1, keepdims=True)
    centred = value - centre
    spread = jnp.mean(centred * centred, -1, keepdims=True)
    factor = lax.rsqrt(spread + norm_eps)
    return centred * factor, factor


def gelu_parts(value):
    curve = 0.5 * (1.0 + lax.erf(value * (1.0 / math.sqrt(2.0))))
    return curve


def gelu_slope(value):
    bell = jnp.exp(-0.5 * value * value) * (1.0 / math.sqrt(2.0 * math.pi))
    return gelu_parts(value) + value * bell


def inside_region(sizes_ref, starts_ref, region, first, shape, width):
    rows, rows_here, cols_here = shape
    index = first + lax.broadcasted_iota(jnp.int32, (rows, 1), 0)
    bits = cols_here.bit_length() - 1
    latitude = lax.axis_index("rows") * rows_here + lax.shift_right_logical(index, bits)
    longitude = lax.axis_index("cols") * cols_here + (index & (cols_here - 1))
    offset = longitude - starts_ref[region]
    offset = jnp.where(offset < 0, offset + width, offset)
    near = jnp.where(latitude < sizes_ref[region, 0], 1.0, 0.0)
    return jnp.where(offset < sizes_ref[region, 1], near, 0.0)


def as_row(ref):
    return ref[...].reshape(1, ref.shape[0])


def field_rows(coming, region, place, eye):
    return jnp.concatenate(
        [
            dot_last(eye, coming[region, first : first + 256, place])
            for first in range(0, coming.shape[1], 256)
        ],
        1,
    )


def forward_kernel(sizes, *refs):
    (
        region_sizes,
        region_starts,
        tokens_ref,
        gain_ref,
        shift_ref,
        scale_ref,
        center_ref,
        weights_ref,
        biases_ref,
        to_modes,
        to_columns,
        ahead,
        behind,
        eye,
        mixed_hbm,
        second_hbm,
        *kept_hbm,
    ) = refs[:20]
    work, sems = refs[20:30], refs[30:38]
    mixed, second, mixed_sems, second_sems, kept_sems, *kept = refs[38:]
    regions, blocks, block_size, chips, cols, tokens = sizes
    me, core = greet(chips, cols)
    sent, coming = work[0], work[-1]
    piece = 128
    steps = kept_hbm[0].shape[0]
    cols_here = 128 // cols
    gain, shift, scale, center = (
        as_row(ref) for ref in (gain_ref, shift_ref, scale_ref, center_ref)
    )

    def inside(region, first, rows):
        shape = (rows, tokens // cols_here, cols_here)
        return inside_region(region_sizes, region_starts, region, first, shape, 128)

    def produce(region):
        def step(part, carry):
            rows = pl.ds(pl.multiple_of(region * tokens + part * piece, piece), piece)
            unit, factor = normalise(tokens_ref[rows, :].astype(wide))
            values = (inside(region, part * piece, piece) * (unit * gain + shift)).astype(low)
            place = pl.ds(pl.multiple_of(part * piece, piece), piece)
            to_feature_rows(sent, region, place, values, eye[...])
            return carry

        lax.fori_loop(0, tokens // piece, step, 0)

    def keep(step):
        slot = step % 2
        return [
            pltpu.make_async_copy(ref.at[slot], hbm.at[step], kept_sems.at[k, slot])
            for k, (ref, hbm) in enumerate(zip(kept, kept_hbm))
        ]

    def middle(step, spectrum):
        slot = step % 2

        @pl.when(step >= 2)
        def _():
            for copy in keep(step - 2):
                copy.wait()

        spectrum_kept, first_kept, act_kept, second_kept = kept
        spectrum = spectrum.astype(low)
        spectrum_kept[slot] = spectrum
        first = dot_first(weights_ref[0], spectrum) + biases_ref[:, 0:1]
        first_kept[slot] = first
        act = (first * gelu_parts(first)).astype(low)
        act_kept[slot] = act
        second_pre = dot_first(weights_ref[1], act) + biases_ref[:, 1:2]
        second_kept[slot] = second_pre
        for copy in keep(step):
            copy.start()
        return second_pre - shrink_width * jnp.tanh(second_pre / shrink_width)

    def leave(region):
        rows = pl.ds(pl.multiple_of(region * tokens, tokens), tokens)
        return [
            pltpu.make_async_copy(mixed.at[rows], mixed_hbm.at[rows], mixed_sems.at[region]),
            pltpu.make_async_copy(second.at[rows], second_hbm.at[rows], second_sems.at[region]),
        ]

    def consume(region):
        def step(part, carry):
            rows = pl.ds(pl.multiple_of(region * tokens + part * 256, 256), 256)
            place = pl.ds(pl.multiple_of(part * 256, 256), 256)
            fields = field_rows(coming, region, place, eye[...])
            residual = tokens_ref[rows, :].astype(wide)
            unit, factor = normalise(residual)
            value = residual + inside(region, part * 256, 256) * fields + (unit * gain + shift)
            mixed[rows, :] = value
            unit, factor = normalise(value)
            second[rows, :] = (unit * scale + center).astype(low)
            return carry

        lax.fori_loop(0, tokens // 256, step, 0)
        for copy in leave(region):
            copy.start()

    tables = (to_modes, to_columns, ahead, behind)
    filter_pass(
        sizes, me, core, produce, middle, consume, tables, work, sems, lambda place, step=0: None
    )
    for step in (steps - 2, steps - 1):
        for copy in keep(step):
            copy.wait()
    for region in range(regions):
        for copy in leave(region):
            copy.wait()


def place_of(row, col):
    return {"core": row % 2, "x": (row // 2) % 2, "z": row // 4, "y": col}


def device_at(spot):
    return (spot["z"] * 4 + spot["x"] * 2 + spot["core"], spot["y"])


def across(spot, axis, step=1):
    size = 4 if axis == "z" else 2
    return device_at({**spot, axis: (spot[axis] + step) % size})


def remote(src, dst, send_sem, recv_sem, device):
    return pltpu.make_async_remote_copy(
        src_ref=src,
        dst_ref=dst,
        send_sem=send_sem,
        recv_sem=recv_sem,
        device_id=device,
        device_id_type=MESH,
    )


def add_rows(out_ref, out_row, terms, rows):
    step = [size for size in (96, 64, 48, 32) if rows % size == 0][0]

    def add(part, carry):
        total = 0.0
        for ref, row in terms:
            here = pl.ds(pl.multiple_of(row + part * step, 16), step)
            total = total + ref[here, :].astype(wide)
        there = pl.ds(pl.multiple_of(out_row + part * step, 16), step)
        out_ref[there, :] = total.astype(low)
        return carry

    lax.fori_loop(0, rows // step, add, 0)


def row_part(ref, row, rows):
    return ref.at[pl.ds(pl.multiple_of(row, 16), rows)]


def facing(spot, axis):
    if axis == "near":
        z = spot["z"] // 2 * 2 + 1 - spot["z"] % 2
        return spot["z"] % 2, device_at({**spot, "z": z})
    if axis == "far":
        return spot["z"] // 2, across(spot, "z", 2)
    return spot[axis], across(spot, axis)


def reduce_steps(spot, axes, buffers, sends, recvs):
    steps = []
    for k, axis in enumerate(axes):
        bit, device = facing(spot, axis)
        source, target = buffers[k], buffers[k + 1]
        rows = target.shape[0]
        hop = remote(
            row_part(source, (1 - bit) * rows, rows), target, sends.at[k], recvs.at[k], device
        )

        def finish(hop=hop, source=source, target=target, rows=rows, bit=bit):
            hop.wait()
            add_rows(target, 0, ((target, 0), (source, bit * rows)), rows)

        steps.append((hop.start, finish))
    return steps


def share_steps(spot, axes, piece, total, sends, recvs, own_sem):
    offsets, rows, bits, devices = [0], [total.shape[0]], [], []
    for axis in axes:
        bit, device = facing(spot, axis)
        bits.append(bit)
        devices.append(device)
        rows.append(rows[-1] // 2)
        offsets.append(offsets[-1] + bit * rows[-1])
    last = len(axes) - 1
    hops = []
    for k in range(last, -1, -1):
        place = row_part(total, offsets[k + 1], rows[k + 1])
        source = piece if k == last else place
        hops.append(remote(source, place, sends.at[k], recvs.at[k], devices[k]))
    keep = pltpu.make_async_copy(piece, row_part(total, offsets[-1], rows[-1]), own_sem)
    ready = (
        (offsets[2], rows[2]),
        (offsets[1] + (1 - bits[1]) * rows[2], rows[2]),
        ((1 - bits[0]) * rows[1], rows[1]),
    )
    cores = []
    for k, (offset, size) in enumerate(ready):
        place = row_part(total, offset, size)
        cores.append(
            remote(place, place, sends.at[4 + k], recvs.at[4 + k], across(spot, "core"))
        )

    def begin():
        keep.start()
        hops[0].start()

    def second():
        keep.wait()
        hops[0].wait()
        hops[1].start()

    def third():
        hops[1].wait()
        hops[2].start()
        cores[0].start()

    def fourth():
        hops[2].wait()
        hops[3].start()
        cores[1].start()

    def fifth():
        hops[3].wait()
        cores[2].start()

    def finish():
        for core in cores:
            core.wait()

    return begin, second, third, fourth, fifth, finish


def backward_kernel(sizes, *refs):
    (
        region_sizes,
        region_starts,
        tokens_hbm,
        mixed_back_ref,
        gain_ref,
        weights_ref,
        to_modes,
        to_columns,
        ahead,
        behind,
        eye,
        spectrum_hbm,
        first_hbm,
        act_hbm,
        pre_hbm,
        project_hbm,
        expand_hbm,
        project_piece,
        expand_piece,
        project_ready,
        expand_ready,
        sums_ref,
        slope_hbm,
        project_total,
        expand_total,
        gathered,
        gathered_bias,
        vector_sum,
    ) = refs[:28]
    work, sems = refs[28:38], refs[38:46]
    (
        tokens_ref,
        slope,
        slope_sems,
        project_own,
        expand_own,
        load_sems,
        kernel_slope,
        bias_slope,
        mixer_slope,
        offset_slope,
        spectrum_slots,
        first_slots,
        act_slots,
        pre_slots,
        slot_sems,
        project_halves,
        expand_halves,
        project_quarters,
        expand_quarters,
        project_eighths,
        expand_eighths,
        project_pieces,
        expand_pieces,
        reduce_sends,
        reduce_recvs,
        share_sends,
        share_recvs,
        own_sems,
        slab,
        slab_bias,
        slab_got,
        slab_bias_got,
        slab_region,
        slab_bias_region,
        slab_sends,
        slab_recvs,
        vector_sent,
        vector_got,
        vector_sends,
        vector_recvs,
        late,
        late_got,
        late_all,
        late_sends,
        late_recvs,
    ) = refs[46:]
    regions, blocks, block_size, chips, cols, tokens = sizes
    steps = spectrum_hbm.shape[0]
    slots = (spectrum_slots, first_slots, act_slots, pre_slots)
    streams = (spectrum_hbm, first_hbm, act_hbm, pre_hbm)

    def fetch(step, slot):
        return [
            pltpu.make_async_copy(hbm.at[step], ref.at[slot], slot_sems.at[k, slot])
            for k, (hbm, ref) in enumerate(zip(streams, slots))
        ]

    own = (project_own, expand_own)
    load_own = [
        pltpu.make_async_copy(hbm, own[k], load_sems.at[1 + k])
        for k, hbm in enumerate((project_hbm, expand_hbm))
    ]
    load_tokens = pltpu.make_async_copy(tokens_hbm, tokens_ref, load_sems.at[0])
    for copy in load_own:
        copy.start()
    for copy in fetch(0, 0):
        copy.start()
    load_tokens.start()
    me, core = greet(chips, cols)
    spot = place_of(lax.axis_index("rows"), lax.axis_index("cols"))
    block = me % blocks
    sent, coming = work[0], work[-1]
    piece = 128
    cols_here = 128 // cols
    late[...] = jnp.zeros_like(late)
    vector_sum[...] = sums_ref[...]
    for ref in (kernel_slope, bias_slope, mixer_slope, offset_slope):
        ref[...] = jnp.zeros_like(ref)
    reducing, sharing = [], []
    pairs = 3
    tile = project_own.shape[0]
    own_pieces = (
        (project_piece, expand_piece),
        (project_pieces.at[0], expand_pieces.at[0]),
        (project_pieces.at[1], expand_pieces.at[1]),
    )
    chains = (
        ((project_piece,), (expand_piece,)),
        (
            (project_ready, project_eighths.at[0], own_pieces[1][0]),
            (expand_ready, expand_eighths.at[0], own_pieces[1][1]),
        ),
        (
            (
                project_own,
                project_halves,
                project_quarters,
                project_eighths.at[1],
                own_pieces[2][0],
            ),
            (expand_own, expand_halves, expand_quarters, expand_eighths.at[1], own_pieces[2][1]),
        ),
    )
    for j in range(pairs):
        place = pl.multiple_of((core * pairs + j) * tile, tile)
        totals = (project_total.at[pl.ds(place, tile)], expand_total.at[:, pl.ds(place, tile)])
        for k in range(2):
            axes = (("x", "y"), ("y", "x"))[k] + ("near", "far")
            buffers = chains[j][k]
            reducing.append(
                reduce_steps(
                    spot,
                    axes[5 - len(buffers) :],
                    buffers,
                    reduce_sends.at[j, k],
                    reduce_recvs.at[j, k],
                )
            )
            sharing.append(
                share_steps(
                    spot,
                    axes,
                    own_pieces[j][k],
                    totals[k],
                    share_sends.at[j, k],
                    share_recvs.at[j, k],
                    own_sems.at[j, k],
                )
            )

    def reduce(j, step, finish):
        for steps_of in reducing[2 * j : 2 * j + 2]:
            steps_of[step][finish]()

    def share(j, step):
        for steps_of in sharing[2 * j : 2 * j + 2]:
            steps_of[step]()

    def inside(region, first, rows):
        shape = (rows, tokens // cols_here, cols_here)
        return inside_region(region_sizes, region_starts, region, first, shape, 128)

    def produce(region):
        def step(part, carry):
            rows = pl.ds(pl.multiple_of(region * tokens + part * piece, piece), piece)
            place = pl.ds(pl.multiple_of(part * piece, piece), piece)
            values = (inside(region, part * piece, piece) * mixed_back_ref[rows, :]).astype(low)
            to_feature_rows(sent, region, place, values, eye[...])
            return carry

        lax.fori_loop(0, tokens // piece, step, 0)

    def middle(step, shrunk_back):
        slot = step % 2
        for copy in fetch(step, slot):
            copy.wait()

        @pl.when(step + 1 < steps)
        def _():
            for copy in fetch(step + 1, 1 - slot):
                copy.start()

        level = jnp.tanh(pre_slots[slot] / shrink_width)
        second = (shrunk_back * (level * level)).astype(low)
        ones = jnp.ones((8, second.shape[1]), low)
        offset_slope[...] += dot_last(ones, second)
        mixer_slope[...] += dot_last(act_slots[slot], second)
        first = (dot(weights_ref[1], second) * gelu_slope(first_slots[slot])).astype(low)
        bias_slope[...] += dot_last(ones, first)
        kernel_slope[...] += dot_last(spectrum_slots[slot], first)
        return dot(weights_ref[0], first)

    def leave(region):
        rows = pl.ds(pl.multiple_of(region * tokens, tokens), tokens)
        return pltpu.make_async_copy(slope.at[rows], slope_hbm.at[rows], slope_sems.at[region])

    def consume(region):
        def step(part, carry):
            rows = pl.ds(pl.multiple_of(region * tokens + part * 256, 256), 256)
            place = pl.ds(pl.multiple_of(part * 256, 256), 256)
            fields = field_rows(coming, region, place, eye[...])
            unit, factor = normalise(tokens_ref[rows, :].astype(wide))
            mixed_back = mixed_back_ref[rows, :]
            normed_back = mixed_back + inside(region, part * 256, 256) * fields
            gains = jnp.sum(normed_back * unit, 0, keepdims=True)
            shifts = jnp.sum(normed_back, 0, keepdims=True)
            for k in range(3):
                late[k : k + 1, :] += gains[:, k * 256 : (k + 1) * 256]
                late[3 + k : 4 + k, :] += shifts[:, k * 256 : (k + 1) * 256]
            pull = normed_back * as_row(gain_ref)
            pull = pull - jnp.mean(pull, -1, keepdims=True) - unit * jnp.mean(
                pull * unit, -1, keepdims=True
            )
            slope[rows, :] = mixed_back + factor * pull
            return carry

        lax.fori_loop(0, tokens // 256, step, 0)
        leave(region).start()

    def slab_hops(place, mine, theirs, device):
        return [
            remote(src, dst, slab_sends.at[k, place], slab_recvs.at[k, place], device)
            for k, (src, dst) in enumerate(zip(mine, theirs))
        ]

    slab_core = slab_hops(
        0, (slab, slab_bias), (slab_got, slab_bias_got), across(spot, "core")
    )
    slab_far = slab_hops(
        1,
        (slab_got.at[core], slab_bias_got.at[core]),
        (slab_region, slab_bias_region),
        chip_device((me + blocks) % chips, core, cols),
    )
    here = (gathered.at[core, :, block], gathered_bias.at[core, block])

    def slab_peer(step):
        other = me // blocks * blocks + (block + step) % blocks
        return slab_hops(1 + step, here, here, chip_device(other, core, cols))

    everything = (gathered.at[core], gathered_bias.at[core])
    slab_last = slab_hops(1 + blocks, everything, everything, across(spot, "core"))

    def slab_start():
        for k, (weight, bias) in enumerate(
            ((kernel_slope, bias_slope), (mixer_slope, offset_slope))
        ):
            whole = weight[...]
            upper, lower = whole[:block_size], whole[block_size:]
            slab[k, 0] = upper[:, :block_size] + lower[:, block_size:]
            slab[k, 1] = upper[:, block_size:] - lower[:, :block_size]
            slab_bias[k] = bias[...]
        for hop in slab_core:
            hop.start()

    def slab_regions():
        for hop in slab_core:
            hop.wait()
        slab_got[...] = slab_got[...] + slab[...]
        slab_bias_got[...] = slab_bias_got[...] + slab_bias[...]
        for hop in slab_far:
            hop.start()

    def slab_blocks():
        for hop in slab_far:
            hop.wait()
        gathered[core, :, block] = slab_region[...] + slab_got[core]
        gathered_bias[core, block] = slab_bias_region[...] + slab_bias_got[core]
        for step in range(1, blocks):
            for hop in slab_peer(step):
                hop.start()

    def slab_cores():
        for step in range(1, blocks):
            for hop in slab_peer(step):
                hop.wait()
        for hop in slab_last:
            hop.start()

    partners = (
        across(spot, "core"),
        across(spot, "x"),
        across(spot, "y"),
        device_at({**spot, "z": spot["z"] // 2 * 2 + 1 - spot["z"] % 2}),
        across(spot, "z", 2),
    )
    hops = [
        remote(
            vector_sent.at[k], vector_got.at[k], vector_sends.at[k], vector_recvs.at[k], device
        )
        for k, device in enumerate(partners)
    ]

    def vector_step(k):
        if k > 0:
            hops[k - 1].wait()
            vector_sum[...] = vector_sum[...] + vector_got[k - 1]
        if k < len(hops):
            vector_sent[k] = vector_sum[...]
            hops[k].start()

    regions_seen = []

    def tick(place, step=0):
        if place == "arrival":

            @pl.when(step == 4)
            def _():
                reduce(2, 0, 1)
                reduce(2, 1, 0)

        if place == "mode":

            @pl.when(step == 3)
            def _():
                share(0, 3)
                reduce(2, 2, 1)
                reduce(2, 3, 0)
                share(1, 1)

            @pl.when(step == 5)
            def _():
                reduce(2, 3, 1)

        if place == "start":
            for copy in load_own:
                copy.wait()
            reduce(2, 0, 0)
            reduce(1, 0, 0)
            vector_step(0)
        if place == "sent":
            reduce(1, 0, 1)
            share(0, 0)
            vector_step(1)
        if place == "zonal":
            share(0, 1)
            reduce(1, 1, 0)
            reduce(2, 1, 1)
            reduce(2, 2, 0)
            vector_step(2)
        if place == "turned":
            share(0, 2)
            reduce(1, 1, 1)
            share(1, 0)
            vector_step(3)
        if place == "modes":
            slab_start()
            share(1, 2)
            share(2, 0)
            vector_step(4)
        if place == "returned":
            share(0, 4)
            share(1, 3)
            share(2, 1)
            vector_step(5)
        if place == "back":
            slab_regions()
        if place == "columns":
            load_tokens.wait()
            slab_blocks()
            share(2, 2)
            share(1, 4)
            share(2, 3)
            slab_cores()
        if place == "region":
            regions_seen.append(place)
            if len(regions_seen) == 1:
                share(2, 4)

    tables = (to_columns, to_modes, ahead, behind)
    filter_pass(sizes, me, core, produce, middle, consume, tables, work, sems, tick)
    late_core = remote(late, late_got, late_sends.at[0], late_recvs.at[0], across(spot, "core"))
    late_core.start()
    late_core.wait()
    late[...] = late[...] + late_got[...]
    late_all[me] = late[...]

    def late_hop(step):
        other = chip_device((me + step) % chips, core, cols)
        return remote(late, late_all.at[me], late_sends.at[step], late_recvs.at[step], other)

    for step in range(1, chips):
        late_hop(step).start()
    for hop in slab_last:
        hop.wait()
    share(0, 5)
    share(1, 5)
    share(2, 5)
    for step in range(1, chips):
        late_hop(step).wait()
    total = late_all[0]
    for chip in range(1, chips):
        total = total + late_all[chip]
    for k in range(3):
        vector_sum[0:1, k * 256 : (k + 1) * 256] = total[k : k + 1, :]
        vector_sum[1:2, k * 256 : (k + 1) * 256] = total[3 + k : 4 + k, :]
    for region in range(regions):
        leave(region).wait()


def call_filter(body, sizes, outs, cid, operands, scalars, spaces, out_spaces, scratch):
    shapes = [jax.ShapeDtypeStruct(shape, kind) for shape, kind in outs]
    anywhere = pl.BlockSpec(memory_space=pl.ANY)
    scalar = pl.BlockSpec(memory_space=pltpu.SMEM)
    return pl.pallas_call(
        functools.partial(body, sizes),
        out_shape=shapes,
        in_specs=[scalar] * len(scalars)
        + [anywhere if place in spaces else vmem for place in range(len(operands))],
        out_specs=[anywhere if place in out_spaces else vmem for place in range(len(outs))],
        scratch_shapes=[*work_shapes(sizes), *scratch],
        compiler_params=pltpu.CompilerParams(
            collective_id=cid, has_side_effects=True, vmem_limit_bytes=60 * 1024 * 1024
        ),
    )(*scalars, *operands)


def forward_scratch(sizes, kept):
    regions, blocks, block_size, chips, cols, tokens = sizes
    dma = pltpu.SemaphoreType.DMA
    features = blocks * block_size
    return (
        pltpu.VMEM((regions * tokens, features), wide),
        pltpu.VMEM((regions * tokens, features), low),
        dma((regions,)),
        dma((regions,)),
        dma((len(kept), 2)),
        *(pltpu.VMEM((2, *shape[1:]), kind) for shape, kind in kept),
    )


def backward_scratch(sizes, kept, tile, pairs):
    regions, blocks, block_size, chips, cols, tokens = sizes
    features = blocks * block_size
    side = 2 * block_size
    dma = pltpu.SemaphoreType.DMA
    return (
        pltpu.VMEM((regions * tokens, features), low),
        pltpu.VMEM((regions * tokens, features), wide),
        dma((regions,)),
        pltpu.VMEM((tile, features), low),
        pltpu.VMEM((features, tile), low),
        dma((3,)),
        pltpu.VMEM((side, side), wide),
        pltpu.VMEM((8, side), wide),
        pltpu.VMEM((side, side), wide),
        pltpu.VMEM((8, side), wide),
        *(pltpu.VMEM((2, *shape[1:]), kind) for shape, kind in kept),
        dma((len(kept), 2)),
        pltpu.VMEM((tile // 2, features), low),
        pltpu.VMEM((features // 2, tile), low),
        pltpu.VMEM((tile // 4, features), low),
        pltpu.VMEM((features // 4, tile), low),
        pltpu.VMEM((2, tile // 8, features), low),
        pltpu.VMEM((2, features // 8, tile), low),
        pltpu.VMEM((2, tile // 16, features), low),
        pltpu.VMEM((2, features // 16, tile), low),
        dma((pairs, 2, 4)),
        dma((pairs, 2, 4)),
        dma((pairs, 2, 7)),
        dma((pairs, 2, 7)),
        dma((pairs, 2)),
        pltpu.VMEM((2, 2, block_size, block_size), wide),
        pltpu.VMEM((2, 8, side), wide),
        pltpu.VMEM((2, 2, block_size, block_size), wide),
        pltpu.VMEM((2, 8, side), wide),
        pltpu.VMEM((2, block_size, block_size), wide),
        pltpu.VMEM((8, side), wide),
        dma((2, 2 + blocks)),
        dma((2, 2 + blocks)),
        pltpu.VMEM((5, 16, features), wide),
        pltpu.VMEM((5, 16, features), wide),
        dma((5,)),
        dma((5,)),
        pltpu.VMEM((8, 256), wide),
        pltpu.VMEM((8, 256), wide),
        pltpu.VMEM((chips, 8, 256), wide),
        dma((chips,)),
        dma((chips,)),
    )


def dense_kernel(*refs):
    (
        second_ref,
        up_ref,
        scale_ref,
        returned_ref,
        lift_ref,
        mixed_hbm,
        expand_hbm,
        project_hbm,
        out_hbm,
        mixed_back_hbm,
        project_hbm_own,
        expand_hbm_own,
        project_piece,
        expand_piece,
        project_ready,
        expand_ready,
        vectors,
        mixed_ref,
        expand_ref,
        project_ref,
        out_ref,
        out_sum,
        back_sum,
        hidden_tile,
        back_tile,
        project_sent,
        expand_sent,
        project_got,
        expand_got,
        project_own,
        expand_own,
        project_halves,
        expand_halves,
        project_quarters,
        expand_quarters,
        project_eighths,
        expand_eighths,
        load_sems,
        weight_sems,
        leave_sems,
        own_sems,
        sent_sem,
        got_sem,
        first_sends,
        first_recvs,
    ) = refs
    tile = expand_ref.shape[2]
    pairs = project_own.shape[0]
    spot = place_of(lax.axis_index("rows"), lax.axis_index("cols"))
    core = spot["core"]
    orders = (("x", "y"), ("y", "x"))
    sent = (project_sent, expand_sent)
    got = (project_got, expand_got)
    own = (project_own, expand_own)
    halves = (project_halves, expand_halves)
    quarters = (project_quarters, expand_quarters)
    eighths = (project_eighths, expand_eighths)
    piece0 = (project_piece, expand_piece)
    ready = (project_ready, expand_ready)
    places = []
    for j in range(pairs):
        places += [(1 - core) * pairs + j, core * pairs + j]

    def weights(k):
        here = pl.ds(pl.multiple_of(places[k] * tile, tile), tile)
        return [
            pltpu.make_async_copy(project_hbm.at[here], project_ref.at[k], weight_sems.at[0, k]),
            pltpu.make_async_copy(expand_hbm.at[:, here], expand_ref.at[k], weight_sems.at[1, k]),
        ]

    for k in range(2 * pairs):
        for copy in weights(k):
            copy.start()
    load_mixed = pltpu.make_async_copy(mixed_hbm, mixed_ref, load_sems.at[0])
    load_mixed.start()
    barrier = pltpu.get_barrier_semaphore()
    for axis in ("core", "x", "y", "near", "far"):
        device = facing(spot, axis)[1]
        pl.semaphore_signal(barrier, inc=1, device_id=device, device_id_type=MESH)
    count = second_ref.shape[0]
    piece = 512
    vectors[...] = jnp.zeros_like(vectors)

    def start_step(part, carry):
        rows = pl.ds(pl.multiple_of(part * piece, piece), piece)
        out_sum[rows, :] = jnp.broadcast_to(as_row(returned_ref), (piece, out_sum.shape[1]))
        back_sum[rows, :] = jnp.zeros((piece, back_sum.shape[1]), wide)
        return carry + jnp.sum(up_ref[rows, :].astype(wide), 0, keepdims=True)

    vectors[4:5, :] = lax.fori_loop(
        0, count // piece, start_step, jnp.zeros((1, up_ref.shape[1]), wide)
    )
    pl.semaphore_wait(barrier, 5)

    def tile_step(k, place, between):
        lift_row = lift_ref[pl.ds(pl.multiple_of(place * tile, tile), tile)].reshape(1, tile)

        def piece_step(part, carry):
            rows = pl.ds(pl.multiple_of(part * piece, piece), piece)
            pre = dot(second_ref[rows, :], expand_ref[k]) + lift_row
            back = dot_last(up_ref[rows, :], project_ref[k])
            curve = gelu_parts(pre)
            bell = jnp.exp(-0.5 * pre * pre) * (1.0 / math.sqrt(2.0 * math.pi))
            hidden = (pre * curve).astype(low)
            hidden_tile[rows, :] = hidden
            pre_back = (back * (curve + pre * bell)).astype(low)
            back_tile[rows, :] = pre_back
            out_sum[rows, :] += dot(hidden, project_ref[k])
            back_sum[rows, :] += dot_last(pre_back, expand_ref[k])
            return carry + jnp.sum(pre_back.astype(wide), 0, keepdims=True)

        lift = lax.fori_loop(0, count // piece, piece_step, jnp.zeros((1, tile), wide))
        vectors[pl.ds(5 + place, 1), 0:tile] = lift
        between()
        return (
            dot_first(hidden_tile[...], up_ref[...]),
            dot_first(second_ref[...], back_tile[...]),
        )

    def swap(j, k):
        return remote(
            sent[k].at[j], got[k].at[j], sent_sem.at[j, k], got_sem.at[j, k], across(spot, "core")
        )

    chains = []
    for pair in range(2):
        for k in range(2):
            buffers = (own[k].at[pair], halves[k].at[pair])
            if pair == 0:
                buffers += (quarters[k], eighths[k], piece0[k])
            else:
                buffers += (ready[k],)
            chains.append(
                reduce_steps(
                    spot,
                    (orders[k] + ("near", "far"))[: len(buffers) - 1],
                    buffers,
                    first_sends.at[pair, k],
                    first_recvs.at[pair, k],
                )
            )

    def begin(pair, step):
        for chain in chains[pair * 2 : pair * 2 + 2]:
            chain[step][0]()

    def finish(pair, step):
        for chain in chains[pair * 2 : pair * 2 + 2]:
            chain[step][1]()

    def pair_step(j, carry):
        for copy in weights_at(2 * j):
            copy.wait()

        def away_between():
            @pl.when(j == 2)
            def _():
                finish(0, 1)
                begin(0, 2)

        away = tile_step(2 * j, (1 - core) * pairs + j, away_between)
        for k in range(2):
            sent[k][j] = away[k].astype(low)
            swap(j, k).start()
        for copy in weights_at(2 * j + 1):
            copy.wait()

        def home_between():
            @pl.when(j == 1)
            def _():
                finish(0, 0)
                begin(0, 1)

            @pl.when(j == 2)
            def _():
                finish(0, 2)
                begin(0, 3)
                finish(1, 0)
                begin(1, 1)

        home = tile_step(2 * j + 1, core * pairs + j, home_between)
        for k in range(2):
            swap(j, k).wait()
            own[k][j] = (home[k] + got[k][j].astype(wide)).astype(low)

        @pl.when(j == 0)
        def _():
            begin(0, 0)

        @pl.when(j == 1)
        def _():
            begin(1, 0)

        return carry

    def weights_at(k):
        return [
            pltpu.make_async_copy(project_ref.at[k], project_ref.at[k], weight_sems.at[0, k]),
            pltpu.make_async_copy(expand_ref.at[k], expand_ref.at[k], weight_sems.at[1, k]),
        ]

    lax.fori_loop(0, pairs, pair_step, 0)
    keeps = [
        pltpu.make_async_copy(own[k].at[pairs - 1], hbm, own_sems.at[k])
        for k, hbm in enumerate((project_hbm_own, expand_hbm_own))
    ]
    for keep in keeps:
        keep.start()
    load_mixed.wait()

    def leave(part):
        rows = pl.ds(pl.multiple_of(part * piece, piece), piece)
        return [
            pltpu.make_async_copy(out_ref.at[rows], out_hbm.at[rows], leave_sems.at[0, part]),
            pltpu.make_async_copy(
                back_sum.at[rows], mixed_back_hbm.at[rows], leave_sems.at[1, part]
            ),
        ]

    def end_step(part, carry):
        for quarter in range(4):
            size = piece // 4
            rows = pl.ds(pl.multiple_of(part * piece + quarter * size, size), size)
            mixed = mixed_ref[rows, :]
            out_ref[rows, :] = (out_sum[rows, :] + mixed).astype(low)
            unit, factor = normalise(mixed)
            norm_back = back_sum[rows, :]
            vectors[2:3, :] += jnp.sum(norm_back * unit, 0, keepdims=True)
            vectors[3:4, :] += jnp.sum(norm_back, 0, keepdims=True)
            pull = norm_back * as_row(scale_ref)
            pull = pull - jnp.mean(pull, -1, keepdims=True) - unit * jnp.mean(
                pull * unit, -1, keepdims=True
            )
            back_sum[rows, :] = up_ref[rows, :].astype(wide) + factor * pull
        for copy in leave(part):
            copy.start()
        return carry

    lax.fori_loop(0, count // piece, end_step, 0)
    finish(0, 3)
    finish(1, 1)
    for keep in keeps:
        keep.wait()
    for part in range(count // piece):
        for copy in leave(part):
            copy.wait()


def call_dense(second_norm, upstream, scale, returned, lift, mixed, expand, project, cid):
    count, features = second_norm.shape
    tile = 512
    pairs = expand.shape[1] // tile // 2
    tall, broad = (tile, features), (features, tile)
    outs = (
        ((count, features), low),
        ((count, features), wide),
        (tall, low),
        (broad, low),
        ((tile // 16, features), low),
        ((features // 16, tile), low),
        ((tile // 4, features), low),
        ((features // 4, tile), low),
        ((16, features), wide),
    )
    shapes = [jax.ShapeDtypeStruct(shape, kind) for shape, kind in outs]
    anywhere = pl.BlockSpec(memory_space=pl.ANY)
    dma = pltpu.SemaphoreType.DMA
    return pl.pallas_call(
        dense_kernel,
        out_shape=shapes,
        in_specs=[vmem] * 5 + [anywhere] * 3,
        out_specs=[anywhere] * 4 + [vmem] * 5,
        scratch_shapes=[
            pltpu.VMEM((count, features), wide),
            pltpu.VMEM((2 * pairs, *broad), low),
            pltpu.VMEM((2 * pairs, *tall), low),
            pltpu.VMEM((count, features), low),
            pltpu.VMEM((count, features), wide),
            pltpu.VMEM((count, features), wide),
            pltpu.VMEM((count, tile), low),
            pltpu.VMEM((count, tile), low),
            *(pltpu.VMEM((pairs, *shape), low) for shape in (tall, broad) * 3),
            pltpu.VMEM((pairs - 1, tile // 2, features), low),
            pltpu.VMEM((pairs - 1, features // 2, tile), low),
            pltpu.VMEM((tile // 4, features), low),
            pltpu.VMEM((features // 4, tile), low),
            pltpu.VMEM((tile // 8, features), low),
            pltpu.VMEM((features // 8, tile), low),
            dma((1,)),
            dma((2, 2 * pairs)),
            dma((2, count // 512)),
            dma((2,)),
            dma((pairs, 2)),
            dma((pairs, 2)),
            dma((pairs - 1, 2, 4)),
            dma((pairs - 1, 2, 4)),
        ],
        compiler_params=pltpu.CompilerParams(
            collective_id=cid, has_side_effects=True, vmem_limit_bytes=60 * 1024 * 1024
        ),
    )(second_norm, upstream, scale, returned, lift, mixed, expand, project)


def shards(
    tokens,
    region_sizes,
    region_starts,
    entry_gain,
    entry_shift,
    spectral_kernel,
    spectral_bias,
    spectral_mixer,
    spectral_offset,
    exit_scale,
    exit_center,
    dense_expand,
    dense_lift,
    dense_project,
    dense_return,
    cotangent,
):
    regions, rows_here, cols_here, features = tokens.shape
    row_devices = lax.axis_size("rows")
    cols = lax.axis_size("cols")
    blocks, block_size = spectral_kernel.shape[1:3]
    chips = row_devices // 2 * cols
    fits = (
        row_devices % 2 == 0
        and chips == regions * blocks
        and cols == 2
        and cols_here == 64
        and rows_here == 8
        and block_size == 96
        and blocks == 8
        and regions == 2
        and dense_expand.shape == (features, 4 * features)
    )
    if not fits:
        return shards_general(
            tokens,
            region_sizes,
            region_starts,
            entry_gain,
            entry_shift,
            spectral_kernel,
            spectral_bias,
            spectral_mixer,
            spectral_offset,
            exit_scale,
            exit_center,
            dense_expand,
            dense_lift,
            dense_project,
            dense_return,
            cotangent,
        )
    height = rows_here * row_devices
    width = cols_here * cols
    patches = rows_here * cols_here
    count = regions * patches
    sizes = (regions, blocks, block_size, chips, cols, patches)
    block = ((lax.axis_index("rows") // 2) * cols + lax.axis_index("cols")) % blocks

    def own(weight):
        return lax.dynamic_index_in_dim(weight, block, 1, False)

    def square(weight):
        real, imaginary = weight[0], weight[1]
        return jnp.concatenate(
            [
                jnp.concatenate([real, imaginary], 1),
                jnp.concatenate([-imaginary, real], 1),
            ],
            0,
        )

    side = 2 * block_size
    weights = jnp.stack([square(own(spectral_kernel)), square(own(spectral_mixer))])
    biases = jnp.stack(
        [own(spectral_bias).reshape(side), own(spectral_offset).reshape(side)], 1
    )
    to_modes, to_columns, ahead, behind, eye = task_tables(height, width, rows_here, cols_here)
    flat_tokens = tokens.reshape(count, features)
    upstream = cotangent.reshape(count, features)
    steps = width // 4 // 4
    shape = (steps, side, 4 * 128)
    kept = ((shape, low), (shape, wide), (shape, low), (shape, wide))
    scalars = (region_sizes, region_starts)
    mixed, second_norm, *stream = call_filter(
        forward_kernel,
        sizes,
        (((count, features), wide), ((count, features), low), *kept),
        1,
        (
            flat_tokens,
            entry_gain,
            entry_shift,
            exit_scale,
            exit_center,
            weights,
            biases,
            to_modes,
            to_columns,
            ahead,
            behind,
            eye,
        ),
        scalars,
        (),
        range(6),
        forward_scratch(sizes, kept),
    )
    output, mixed_back, *tiles, part_sums = call_dense(
        second_norm,
        upstream,
        exit_scale,
        dense_return,
        dense_lift,
        mixed,
        dense_expand,
        dense_project,
        3,
    )
    slope, project_sum, expand_sum, gathered, gathered_bias, sums = call_filter(
        backward_kernel,
        sizes,
        (
            ((count, features), wide),
            (dense_project.shape, low),
            (dense_expand.shape, low),
            ((2, 2, blocks, block_size, block_size), wide),
            ((2, blocks, 8, side), wide),
            ((16, features), wide),
        ),
        2,
        (
            flat_tokens,
            mixed_back,
            entry_gain,
            weights,
            to_modes.T,
            to_columns.T,
            ahead,
            behind,
            eye,
            *stream,
            *tiles,
            part_sums,
        ),
        scalars,
        (0, 9, 10, 11, 12, 13, 14),
        range(3),
        backward_scratch(sizes, kept, tiles[0].shape[0], 3),
    )
    biases = gathered_bias[:, :, 0].reshape(2, blocks, 2, block_size).swapaxes(1, 2)
    return (
        output.reshape(tokens.shape),
        slope.reshape(tokens.shape),
        sums[0],
        sums[1],
        gathered[0],
        biases[0],
        gathered[1],
        biases[1],
        sums[2],
        sums[3],
        expand_sum.astype(wide),
        sums[5 : 5 + dense_lift.shape[0] // tiles[0].shape[0], : tiles[0].shape[0]].reshape(-1),
        project_sum.astype(wide),
        sums[4],
    )


def solution(mesh):
    placed = (
        P(None, "rows", "cols", None),
        P(),
        P(),
        P(),
        P(),
        P(),
        P(),
        P(),
        P(),
        P(),
        P(),
        P(),
        P(),
        P(),
        P(),
        P(None, "rows", "cols", None),
    )
    return jax.shard_map(
        shards,
        mesh=mesh,
        in_specs=placed,
        out_specs=(
            P(None, "rows", "cols", None),
            P(None, "rows", "cols", None),
            P(),
            P(),
            P(),
            P(),
            P(),
            P(),
            P(),
            P(),
            P(),
            P(),
            P(),
            P(),
        ),
        check_vma=False,
    )
```

```python
import functools
import math

import jax
import jax.numpy as jnp
import ml_dtypes
import numpy as np
from jax import lax
from jax.experimental import pallas as pl
from jax.experimental.pallas import tpu as pltpu
from jax.sharding import PartitionSpec as P

shrink_width = 0.01
norm_eps = 1e-06
highest = lax.Precision.HIGHEST


def tables(height, width, modes):
    column = jnp.arange(width, dtype=jnp.int32)
    frequency = jnp.arange(modes, dtype=jnp.int32)
    turns = column[:, None] * frequency[None, :] % width
    angle = turns.astype(jnp.float32) * (2.0 * math.pi / width)
    cosine = jnp.cos(angle)
    sine = jnp.sin(angle)
    scale = 1.0 / math.sqrt(width)
    forward_zonal = jnp.stack([cosine, -sine], 1) * scale
    factor = jnp.where(frequency == 0, 1.0, 2.0).astype(jnp.float32)
    inverse_zonal = jnp.stack([cosine.T * factor[:, None], -sine.T * factor[:, None]], 0) * scale
    latitude = jnp.arange(height, dtype=jnp.int32)
    meridian_turns = latitude[:, None] * latitude[None, :] % height
    meridian_angle = meridian_turns.astype(jnp.float32) * (2.0 * math.pi / height)
    meridian_cos = jnp.cos(meridian_angle) / math.sqrt(height)
    meridian_sin = jnp.sin(meridian_angle) / math.sqrt(height)
    meridian_table = jnp.stack(
        [jnp.stack([meridian_cos, meridian_sin], -1), jnp.stack([-meridian_sin, meridian_cos], -1)],
        1,
    )
    forward_low = forward_zonal.astype(jnp.bfloat16)
    inverse_low = inverse_zonal.astype(jnp.bfloat16)
    meridian_low = meridian_table.astype(jnp.bfloat16)
    meridian_wide = meridian_low.astype(jnp.float32)
    return (forward_low, inverse_low, meridian_low, meridian_wide)


def layer_norm(value, gain, shift):
    centre = jnp.mean(value, -1, keepdims=True)
    centred = value - centre
    spread = jnp.mean(centred * centred, -1, keepdims=True)
    return centred * lax.rsqrt(spread + norm_eps) * gain + shift


def gelu_exact(value):
    return jax.nn.gelu(value, approximate=False)


def shrink(value):
    return value - shrink_width * jnp.tanh(value / shrink_width)


def block_layout(spectrum, blocks, block_size):
    leading = spectrum.shape[:3]
    parts = spectrum.reshape(leading + (2, blocks, block_size))
    parts = jnp.moveaxis(parts, 3, 4)
    return parts.reshape((-1, blocks, 2 * block_size))


def spectral_layout(modes_flat, leading, blocks, block_size):
    parts = modes_flat.reshape(leading + (blocks, 2, block_size))
    parts = jnp.moveaxis(parts, 4, 3)
    return parts.reshape(leading + (2, blocks * block_size))


def complex_matrix(weight):
    real = weight[0]
    imaginary = weight[1]
    upper = jnp.concatenate([real, imaginary], 2)
    lower = jnp.concatenate([-imaginary, real], 2)
    return jnp.concatenate([upper, lower], 1)


def matrix_gradient(whole, block_size):
    upper = whole[:, :block_size]
    lower = whole[:, block_size:]
    real = upper[:, :, :block_size] + lower[:, :, block_size:]
    imaginary = upper[:, :, block_size:] - lower[:, :, :block_size]
    return jnp.stack([real, imaginary], 0)


def bias_rows(bias):
    return jnp.moveaxis(bias, 0, 1).reshape(bias.shape[1], 2 * bias.shape[2])


def bias_gradient(summed, block_size):
    return jnp.moveaxis(summed.reshape(summed.shape[0], 2, block_size), 1, 0)


def advance(tokens, mask, weights, grids, layout):
    (
        entry_gain,
        entry_shift,
        spectral_kernel,
        spectral_bias,
        spectral_mixer,
        spectral_offset,
        exit_scale,
        exit_center,
        dense_expand,
        dense_lift,
        dense_project,
        dense_return,
    ) = weights
    forward_zonal, inverse_zonal, meridian_table, meridian_wide = grids
    blocks, block_size, first_block = layout
    residual = tokens.astype(jnp.float32)
    normed = layer_norm(residual, entry_gain, entry_shift)
    sent = (mask * normed).astype(jnp.bfloat16)
    by_channel = lax.all_to_all(sent, "cols", split_axis=3, concat_axis=2, tiled=True)
    zonal = jnp.einsum(
        "rhwc,wpk->rhkpc", by_channel, forward_zonal, preferred_element_type=jnp.float32
    )
    by_mode = lax.all_to_all(
        zonal.astype(jnp.bfloat16), "rows", split_axis=2, concat_axis=1, tiled=True
    )
    spectrum = jnp.einsum(
        "kphq,rhmqc->rkmpc", meridian_table, by_mode, preferred_element_type=jnp.float32
    ).astype(jnp.bfloat16)
    leading = spectrum.shape[:3]
    modes_flat = block_layout(spectrum, blocks, block_size)
    kernel_matrix = complex_matrix(
        lax.dynamic_slice_in_dim(spectral_kernel, first_block, blocks, 1)
    )
    mixer_matrix = complex_matrix(lax.dynamic_slice_in_dim(spectral_mixer, first_block, blocks, 1))
    kernel_bias = bias_rows(lax.dynamic_slice_in_dim(spectral_bias, first_block, blocks, 1))
    mixer_bias = bias_rows(lax.dynamic_slice_in_dim(spectral_offset, first_block, blocks, 1))
    first_pre = (
        jnp.einsum("nbx,bxy->nby", modes_flat, kernel_matrix, preferred_element_type=jnp.float32)
        + kernel_bias
    )
    first_act = gelu_exact(first_pre).astype(jnp.bfloat16)
    second_pre = (
        jnp.einsum("nbx,bxy->nby", first_act, mixer_matrix, preferred_element_type=jnp.float32)
        + mixer_bias
    )
    shrunk = spectral_layout(shrink(second_pre), leading, blocks, block_size)
    back_meridian = jnp.einsum(
        "kphq,rkmpc->rhmqc", meridian_wide, shrunk, precision=highest
    ).astype(jnp.bfloat16)
    by_row = lax.all_to_all(back_meridian, "rows", split_axis=1, concat_axis=2, tiled=True)
    filtered = jnp.einsum(
        "rhkpc,pkw->rhwc", by_row, inverse_zonal, preferred_element_type=jnp.float32
    ).astype(jnp.bfloat16)
    by_token = lax.all_to_all(filtered, "cols", split_axis=2, concat_axis=3, tiled=True)
    mixed = residual + mask * by_token.astype(jnp.float32) + normed
    features = mixed.shape[-1]
    second_norm = (
        layer_norm(mixed, exit_scale, exit_center).astype(jnp.bfloat16).reshape(-1, features)
    )
    hidden_pre = jnp.dot(second_norm, dense_expand, preferred_element_type=jnp.float32) + dense_lift
    hidden = gelu_exact(hidden_pre).astype(jnp.bfloat16)
    output = mixed + (
        jnp.dot(hidden, dense_project, preferred_element_type=jnp.float32) + dense_return
    ).reshape(mixed.shape)
    kept = (
        residual,
        modes_flat,
        first_pre,
        first_act,
        second_pre,
        mixed,
        second_norm,
        hidden_pre,
        hidden,
        kernel_matrix,
        mixer_matrix,
        leading,
    )
    return (output, kept)


def retreat(cotangent, mask, kept, weights, grids, layout):
    (
        entry_gain,
        entry_shift,
        spectral_kernel,
        spectral_bias,
        spectral_mixer,
        spectral_offset,
        exit_scale,
        exit_center,
        dense_expand,
        dense_lift,
        dense_project,
        dense_return,
    ) = weights
    forward_zonal, inverse_zonal, meridian_table, meridian_wide = grids
    blocks, block_size, first_block = layout
    (
        residual,
        modes_flat,
        first_pre,
        first_act,
        second_pre,
        mixed,
        second_norm,
        hidden_pre,
        hidden,
        kernel_matrix,
        mixer_matrix,
        leading,
    ) = kept
    features = mixed.shape[-1]
    upstream = cotangent.reshape(-1, features)
    gradient_project = jnp.einsum("tf,tc->fc", hidden, upstream, preferred_element_type=jnp.float32)
    gradient_return = jnp.sum(upstream.astype(jnp.float32), 0)
    outer = (gradient_project, gradient_return)
    hidden_back = jnp.einsum(
        "tc,fc->tf", upstream, dense_project, preferred_element_type=jnp.float32
    )
    hidden_pull = jax.vjp(gelu_exact, hidden_pre)[1]
    pre_back = hidden_pull(hidden_back)[0].astype(jnp.bfloat16)
    gradient_expand = jnp.einsum(
        "tc,tf->cf", second_norm, pre_back, preferred_element_type=jnp.float32
    )
    gradient_lift = jnp.sum(pre_back.astype(jnp.float32), 0)
    norm_back = jnp.einsum(
        "tf,cf->tc", pre_back, dense_expand, preferred_element_type=jnp.float32
    ).reshape(mixed.shape)
    exit_pull = jax.vjp(layer_norm, mixed, exit_scale, exit_center)[1]
    mixed_part, gradient_scale, gradient_center = exit_pull(norm_back)
    inner = (gradient_expand, gradient_lift, gradient_scale, gradient_center)
    mixed_back = cotangent.astype(jnp.float32) + mixed_part
    filter_back = (mask * mixed_back).astype(jnp.bfloat16)
    channel_back = lax.all_to_all(filter_back, "cols", split_axis=3, concat_axis=2, tiled=True)
    zonal_back = jnp.einsum(
        "rhwc,pkw->rhkpc", channel_back, inverse_zonal, preferred_element_type=jnp.float32
    ).astype(jnp.bfloat16)
    meridian_back = lax.all_to_all(zonal_back, "rows", split_axis=2, concat_axis=1, tiled=True)
    shrunk_back = jnp.einsum(
        "kphq,rhmqc->rkmpc", meridian_table, meridian_back, preferred_element_type=jnp.float32
    )
    shrink_pull = jax.vjp(shrink, second_pre)[1]
    second_back = shrink_pull(block_layout(shrunk_back, blocks, block_size))[0].astype(jnp.bfloat16)
    mixer_whole = jnp.einsum(
        "nbx,nby->bxy", first_act, second_back, preferred_element_type=jnp.float32
    )
    offset_rows = jnp.sum(second_back.astype(jnp.float32), 0)
    activation_back = jnp.einsum(
        "nby,bxy->nbx", second_back, mixer_matrix, preferred_element_type=jnp.float32
    )
    first_pull = jax.vjp(gelu_exact, first_pre)[1]
    first_back = first_pull(activation_back)[0].astype(jnp.bfloat16)
    kernel_whole = jnp.einsum(
        "nbx,nby->bxy", modes_flat, first_back, preferred_element_type=jnp.float32
    )
    kernel_rows = jnp.sum(first_back.astype(jnp.float32), 0)
    spectrum_back = spectral_layout(
        jnp.einsum("nby,bxy->nbx", first_back, kernel_matrix, preferred_element_type=jnp.float32),
        leading,
        blocks,
        block_size,
    )
    modes_back = jnp.einsum(
        "kphq,rkmpc->rhmqc", meridian_wide, spectrum_back, precision=highest
    ).astype(jnp.bfloat16)
    row_back = lax.all_to_all(modes_back, "rows", split_axis=1, concat_axis=2, tiled=True)
    sent_back = jnp.einsum(
        "rhkpc,wpk->rhwc", row_back, forward_zonal, preferred_element_type=jnp.float32
    ).astype(jnp.bfloat16)
    token_back = lax.all_to_all(sent_back, "cols", split_axis=2, concat_axis=3, tiled=True)
    normed_back = mixed_back + mask * token_back.astype(jnp.float32)
    entry_pull = jax.vjp(layer_norm, residual, entry_gain, entry_shift)[1]
    residual_part, gradient_gain, gradient_shift = entry_pull(normed_back)
    gradient_tokens = mixed_back + residual_part
    shared = (
        gradient_gain,
        gradient_shift,
        inner[2],
        inner[3],
        inner[0],
        inner[1],
        outer[0],
        outer[1],
    )
    local_blocks = (
        matrix_gradient(kernel_whole, block_size),
        bias_gradient(kernel_rows, block_size),
        matrix_gradient(mixer_whole, block_size),
        bias_gradient(offset_rows, block_size),
    )
    return (gradient_tokens, shared, local_blocks)


def shards_general(
    tokens,
    region_sizes,
    region_starts,
    entry_gain,
    entry_shift,
    spectral_kernel,
    spectral_bias,
    spectral_mixer,
    spectral_offset,
    exit_scale,
    exit_center,
    dense_expand,
    dense_lift,
    dense_project,
    dense_return,
    cotangent,
):
    rows_here = tokens.shape[1]
    cols_here = tokens.shape[2]
    height = rows_here * lax.axis_size("rows")
    width = cols_here * lax.axis_size("cols")
    grids = tables(height, width, width // 2)
    latitude = lax.axis_index("rows") * rows_here + jnp.arange(rows_here, dtype=jnp.int32)
    longitude = lax.axis_index("cols") * cols_here + jnp.arange(cols_here, dtype=jnp.int32)
    inside_rows = latitude[None, :, None] < region_sizes[:, 0][:, None, None]
    offset = (longitude[None, None, :] - region_starts[:, None, None]) % width
    inside_cols = offset < region_sizes[:, 1][:, None, None]
    mask = jnp.where(inside_rows & inside_cols, 1.0, 0.0).astype(jnp.float32)[..., None]
    block_size = spectral_kernel.shape[2]
    total_blocks = spectral_kernel.shape[1]
    blocks = tokens.shape[3] // lax.axis_size("cols") // block_size
    first_block = lax.axis_index("cols") * blocks
    layout = (blocks, block_size, first_block)
    weights = (
        entry_gain,
        entry_shift,
        spectral_kernel,
        spectral_bias,
        spectral_mixer,
        spectral_offset,
        exit_scale,
        exit_center,
        dense_expand,
        dense_lift,
        dense_project,
        dense_return,
    )
    output, kept = advance(tokens, mask, weights, grids, layout)
    gradient_tokens, shared, local_blocks = retreat(cotangent, mask, kept, weights, grids, layout)
    (
        gain_part,
        shift_part,
        scale_part,
        center_part,
        expand_part,
        lift_part,
        project_part,
        return_part,
    ) = shared
    everywhere = ("rows", "cols")
    project_sum = lax.psum(project_part.astype(jnp.bfloat16), everywhere).astype(jnp.float32)
    expand_sum = lax.psum(expand_part.astype(jnp.bfloat16), everywhere).astype(jnp.float32)
    vectors = (gain_part, shift_part, scale_part, center_part, lift_part, return_part)
    sums = lax.psum(jnp.concatenate(vectors), everywhere)
    ends = [0]
    for vector in vectors:
        ends.append(ends[-1] + vector.shape[0])
    parts = [sums[low:high] for low, high in zip(ends[:-1], ends[1:])]
    summed = (*parts[:4], expand_sum, parts[4], project_sum, parts[5])
    kernel_local, bias_local, mixer_local, offset_local = local_blocks
    kernel_full = lax.dynamic_update_slice_in_dim(
        jnp.zeros((2, total_blocks, block_size, block_size), jnp.float32),
        kernel_local,
        first_block,
        1,
    )
    bias_full = lax.dynamic_update_slice_in_dim(
        jnp.zeros((2, total_blocks, block_size), jnp.float32), bias_local, first_block, 1
    )
    mixer_full = lax.dynamic_update_slice_in_dim(
        jnp.zeros((2, total_blocks, block_size, block_size), jnp.float32),
        mixer_local,
        first_block,
        1,
    )
    offset_full = lax.dynamic_update_slice_in_dim(
        jnp.zeros((2, total_blocks, block_size), jnp.float32), offset_local, first_block, 1
    )
    block_totals = lax.psum((kernel_full, bias_full, mixer_full, offset_full), ("rows", "cols"))
    return (
        output.astype(jnp.bfloat16),
        gradient_tokens,
        summed[0],
        summed[1],
        block_totals[0],
        block_totals[1],
        block_totals[2],
        block_totals[3],
        summed[2],
        summed[3],
        summed[4],
        summed[5],
        summed[6],
        summed[7],
    )


MESH = pl.DeviceIdType.MESH
wide = jnp.float32
low = jnp.bfloat16
by_last = (((1,), (1,)), ((), ()))
by_first = (((0,), (0,)), ((), ()))
vmem = pl.BlockSpec(memory_space=pltpu.VMEM)


def dot(a, b):
    return jnp.dot(a, b, preferred_element_type=wide)


def dot_last(a, b):
    return lax.dot_general(a, b, by_last, preferred_element_type=wide)


def dot_first(a, b):
    return lax.dot_general(a, b, by_first, preferred_element_type=wide)


def task_tables(height, width, rows_here, cols_here):
    modes = width // 2
    near = modes // 2
    column = np.arange(width)
    frequency = np.arange(modes)
    angle = (column[:, None] * frequency[None, :] % width).astype(np.float32) * np.float32(
        2.0 * math.pi / width
    )
    scale = np.float32(1.0 / math.sqrt(width))
    zonal = np.stack([np.cos(angle), -np.sin(angle)], 1) * scale
    factor = np.where(frequency == 0, 1.0, 2.0).astype(np.float32)
    inverse = (
        np.stack([np.cos(angle).T * factor[:, None], -np.sin(angle).T * factor[:, None]], 0) * scale
    )
    latitude = np.arange(height)
    turn = (latitude[:, None] * latitude[None, :] % height).astype(np.float32) * np.float32(
        2.0 * math.pi / height
    )
    cosine = np.cos(turn) / np.float32(math.sqrt(height))
    sine = np.sin(turn) / np.float32(math.sqrt(height))
    meridian = np.stack([np.stack([cosine, sine], -1), np.stack([-sine, cosine], -1)], 1)
    halves = width // cols_here
    split_f = zonal.reshape(halves, cols_here, 2, 2, near)
    to_modes = np.zeros((halves, 2, cols_here, 2, 2, 2, near), np.float32)
    split_g = inverse.reshape(2, 2, near, halves, cols_here)
    to_columns = np.zeros((2, 2, 2, near, halves, 2, cols_here), np.float32)
    for i in range(2):
        to_modes[:, i, :, :, i] = split_f.transpose(0, 1, 3, 2, 4)
        to_columns[:, i, :, :, :, i] = split_g.transpose(1, 0, 2, 3, 4)
    side = halves * 2 * cols_here
    to_modes = to_modes.reshape(side, side)
    to_columns = to_columns.reshape(side, side)
    pairs = rows_here // 2
    senders = height // rows_here
    order = np.zeros((height // 2, 2), np.int64)
    for core in range(2):
        for chip in range(senders // 2):
            for pair in range(pairs):
                for i in range(2):
                    order[(core * (senders // 2) + chip) * pairs + pair, i] = (
                        (chip * 2 + core) * rows_here + pair * 2 + i
                    )
    placed = meridian[:, :, order]
    ahead = np.zeros((2, 2, 2, height // 2, 2, 2, height), np.float32)
    for c in range(2):
        ahead[:, :, c, :, c] = placed.transpose(3, 4, 2, 1, 0)
    ahead = ahead.reshape(2, 2 * height, 4 * height)
    behind = ahead.reshape(4 * height, 4 * height).T
    return tuple(
        np.asarray(item, ml_dtypes.bfloat16)
        for item in (to_modes, to_columns, ahead, behind, np.eye(256, dtype=np.float32))
    )


def chip_device(chip, core, cols):
    return ((chip // cols) * 2 + core, chip % cols)


def swap_bits(value, mask, bits):
    out = 0
    for k in range(bits):
        bit = (value // (1 << k)) % 2
        if (mask >> k) & 1:
            bit = 1 - bit
        out = out + bit * (1 << k)
    return out


def greet(chips, cols):
    row = lax.axis_index("rows")
    core = row % 2
    me = (row // 2) * cols + lax.axis_index("cols")
    barrier = pltpu.get_barrier_semaphore()
    for step in range(1, chips):
        other = (me + step) % chips
        pl.semaphore_signal(
            barrier, inc=1, device_id=chip_device(other, core, cols), device_id_type=MESH
        )
    pl.semaphore_signal(
        barrier, inc=1, device_id=chip_device(me, 1 - core, cols), device_id_type=MESH
    )
    pl.semaphore_wait(barrier, chips)
    return me, core


def send_piece(src, dst, send_sem, recv_sem, target, me, core, cols):
    @pl.when(target == me)
    def _():
        pltpu.make_async_copy(src, dst, recv_sem).start()

    @pl.when(target != me)
    def _():
        pltpu.make_async_remote_copy(
            src_ref=src,
            dst_ref=dst,
            send_sem=send_sem,
            recv_sem=recv_sem,
            device_id=chip_device(target, core, cols),
            device_id_type=MESH,
        ).start()


def await_piece(ref, sem):
    pltpu.make_async_copy(ref, ref, sem).wait()


def to_feature_rows(out_ref, region, place, piece, eye):
    features = piece.shape[1]
    for low_end in range(0, features, 256):
        turned = dot_last(eye, piece[:, low_end : low_end + 256])
        out_ref[region, low_end : low_end + 256, place] = turned.astype(low)


def modes_first(block, group, half):
    columns = []
    for m in range(group):
        rows = block[m * half : (m + 1) * half]
        height = block.shape[1] // 4
        columns.append(
            jnp.concatenate(
                [
                    rows[:, (c * 2 + p) * height : (c * 2 + p + 1) * height]
                    for p in range(2)
                    for c in range(2)
                ],
                0,
            )
        )
    return jnp.concatenate(columns, 1)


def modes_last(block, group, half):
    height = block.shape[1] // group
    rows = []
    for m in range(group):
        part = block[:, m * height : (m + 1) * height]
        rows.append(
            jnp.concatenate(
                [
                    part[(p * 2 + c) * half : (p * 2 + c + 1) * half]
                    for c in range(2)
                    for p in range(2)
                ],
                1,
            )
        )
    return jnp.concatenate(rows, 0)


def filter_pass(sizes, me, core, produce, middle, consume, tables, work, sems, tick):
    regions, blocks, block_size, chips, cols, tokens = sizes
    table_in, table_out, ahead, behind = tables
    sent, got, zonal, zonal_got, tall, flat, back, sibling, leaving, coming = work
    send_a, recv_a, send_b, recv_b, send_c, recv_c, send_d, recv_d = sems
    lanes = 128
    senders = chips // cols
    pairs = tokens // lanes
    half = block_size // 2
    points = senders * pairs
    group = 4
    bits = (blocks - 1).bit_length()
    home = me // blocks
    tick("start")
    for turn in range(regions):
        region = (home + 1 + turn) % regions
        produce(region)
        for step in range(blocks - 1, -1, -1):
            target = region * blocks + swap_bits(me % blocks, step, bits)
            src = sent.at[region, pl.ds(pl.multiple_of(target % blocks * block_size, 32), block_size)]
            place = turn * blocks + step
            send_piece(src, got.at[me], send_a.at[place], recv_a.at[me], target, me, core, cols)
    tick("sent")

    def zonal_step(index, carry):
        tick("arrival", index)
        chip = (index + home * senders // regions) % senders
        for col in range(cols):
            await_piece(got.at[chip * cols + col], recv_a.at[chip * cols + col])
        for pair in range(pairs):
            x = jnp.concatenate(
                [got[chip * cols + col, :, pair * lanes : (pair + 1) * lanes] for col in range(cols)], 1
            )
            y = dot(x, table_in[...]).astype(low)
            for part in range(2):
                zonal[part, chip * pairs + pair] = y[:, part * lanes : (part + 1) * lanes]
        return carry

    lax.fori_loop(0, senders, zonal_step, 0)
    swap = pltpu.make_async_remote_copy(
        src_ref=zonal.at[1 - core],
        dst_ref=zonal_got,
        send_sem=send_b,
        recv_sem=recv_b,
        device_id=chip_device(me, 1 - core, cols),
        device_id_type=MESH,
    )
    swap.start()
    tick("zonal")

    def widen(source, first):
        def step(point, carry):
            row = pl.multiple_of((first + point) * block_size, 32)
            tall[pl.ds(row, block_size), :] = source(point).astype(wide)
            return carry

        lax.fori_loop(0, points, step, 0)

    widen(lambda point: zonal[core, point], core * points)
    swap.wait()
    widen(lambda point: zonal_got[point], (1 - core) * points)
    modes = lanes // 4

    def turn_step(c, carry):
        x = jnp.concatenate(
            [tall[pl.ds(c + half * side, 2 * points, stride=block_size), :] for side in range(2)], 0
        )
        y = jnp.transpose(x)
        for i in range(4):
            flat[i, pl.ds(c, modes, stride=half), :] = y[i * modes : (i + 1) * modes]
        return carry

    lax.fori_loop(0, half, turn_step, 0, unroll=4)
    tick("turned")

    def mode_step(step, carry):
        rows = pl.ds(pl.multiple_of(step * group * half, 64), group * half)
        spectrum = 0.0
        for i in range(2):
            x = jnp.concatenate([flat[i * 2, rows, :], flat[i * 2 + 1, rows, :]], 1).astype(low)
            spectrum = spectrum + dot(x, ahead[i])
        out = modes_last(middle(step, modes_first(spectrum, group, half)), group, half)
        high = out.astype(low)
        rest = (out - high.astype(wide)).astype(low)
        y = (dot(high, behind[...]) + dot(rest, behind[...])).astype(low).astype(wide)
        for i in range(4):
            flat[i, rows, :] = y[:, i * lanes : (i + 1) * lanes]
        tick("mode", step)
        return carry

    lax.fori_loop(0, modes // group, mode_step, 0)
    tick("modes")

    def return_step(c, carry):
        x = jnp.concatenate([flat[i, pl.ds(c, modes, stride=half), :] for i in range(4)], 0)
        y = jnp.transpose(x)
        for side in range(2):
            tall[pl.ds(c + half * side, 2 * points, stride=block_size), :] = y[
                side * 2 * points : (side + 1) * 2 * points
            ]
        return carry

    lax.fori_loop(0, half, return_step, 0, unroll=4)
    tick("returned")

    def narrow(store, first):
        def step(point, carry):
            row = pl.multiple_of((first + point) * block_size, 32)
            store(point, tall[pl.ds(row, block_size), :].astype(low))
            return carry

        lax.fori_loop(0, points, step, 0)

    def to_sibling(point, value):
        back[point] = value

    def to_self(point, value):
        sibling[core, point] = value

    narrow(to_sibling, (1 - core) * points)
    swap_back = pltpu.make_async_remote_copy(
        src_ref=back,
        dst_ref=sibling.at[core],
        send_sem=send_c,
        recv_sem=recv_c,
        device_id=chip_device(me, 1 - core, cols),
        device_id_type=MESH,
    )
    swap_back.start()
    tick("back")
    narrow(to_self, core * points)
    swap_back.wait_send()
    await_piece(sibling.at[1 - core], recv_c)

    def column_step(index, carry):
        chip = (index + (home + 1) * senders // regions) % senders
        for pair in range(pairs):
            point = chip * pairs + pair
            x = jnp.concatenate([sibling[0, point], sibling[1, point]], 1)
            y = dot(x, table_out[...]).astype(low)
            for col in range(cols):
                leaving[chip * cols + col, :, pair * lanes : (pair + 1) * lanes] = y[
                    :, col * lanes : (col + 1) * lanes
                ]
        for col in range(cols):
            target = chip * cols + col
            dst = coming.at[
                me // blocks, pl.ds(pl.multiple_of(me % blocks * block_size, 32), block_size)
            ]
            send_piece(
                leaving.at[target], dst, send_d.at[target], recv_d.at[me], target, me, core, cols
            )
        return carry

    lax.fori_loop(0, senders, column_step, 0)
    tick("columns")
    for turn in range(regions):
        region = (home + turn) % regions

        def arrive(block, carry, region=region):
            ref = coming.at[region, pl.ds(pl.multiple_of(block * block_size, 32), block_size)]
            await_piece(ref, recv_d.at[region * blocks + block])
            return carry

        lax.fori_loop(0, blocks, arrive, 0)
        consume(region)
        tick("region")

    for place in range(regions * blocks):
        turn, step = place // blocks, place % blocks
        target = (home + 1 + turn) % regions * blocks + swap_bits(me % blocks, step, bits)

        @pl.when(target != me)
        def _():
            await_piece(got.at[0], send_a.at[place])

        @pl.when(place != me)
        def _():
            await_piece(leaving.at[0], send_d.at[place])


def work_shapes(sizes):
    regions, blocks, block_size, chips, cols, tokens = sizes
    lanes = 128
    features = blocks * block_size
    points = (chips // cols) * (tokens // lanes)
    rows = (lanes // 4) * (block_size // 2)
    return [
        pltpu.VMEM((regions, features, tokens), low),
        pltpu.VMEM((chips, block_size, tokens), low),
        pltpu.VMEM((2, points, block_size, lanes), low),
        pltpu.VMEM((points, block_size, lanes), low),
        pltpu.VMEM((2 * points * block_size, lanes), wide),
        pltpu.VMEM((4, rows, lanes), wide),
        pltpu.VMEM((points, block_size, lanes), low),
        pltpu.VMEM((2, points, block_size, lanes), low),
        pltpu.VMEM((chips, block_size, tokens), low),
        pltpu.VMEM((regions, features, tokens), low),
        pltpu.SemaphoreType.DMA((chips,)),
        pltpu.SemaphoreType.DMA((chips,)),
        pltpu.SemaphoreType.DMA,
        pltpu.SemaphoreType.DMA,
        pltpu.SemaphoreType.DMA,
        pltpu.SemaphoreType.DMA,
        pltpu.SemaphoreType.DMA((chips,)),
        pltpu.SemaphoreType.DMA((chips,)),
    ]


def normalise(value):
    centre = jnp.mean(value, -1, keepdims=True)
    centred = value - centre
    spread = jnp.mean(centred * centred, -1, keepdims=True)
    factor = lax.rsqrt(spread + norm_eps)
    return centred * factor, factor


def gelu_parts(value):
    curve = 0.5 * (1.0 + lax.erf(value * (1.0 / math.sqrt(2.0))))
    return curve


def gelu_bell(value):
    return jnp.exp(-0.5 * value * value) * (1.0 / math.sqrt(2.0 * math.pi))


def inside_region(sizes_ref, starts_ref, region, first, shape, width):
    rows, rows_here, cols_here = shape
    index = first + lax.broadcasted_iota(jnp.int32, (rows, 1), 0)
    bits = cols_here.bit_length() - 1
    latitude = lax.axis_index("rows") * rows_here + lax.shift_right_logical(index, bits)
    longitude = lax.axis_index("cols") * cols_here + (index & (cols_here - 1))
    offset = longitude - starts_ref[region]
    offset = jnp.where(offset < 0, offset + width, offset)
    near = jnp.where(latitude < sizes_ref[region, 0], 1.0, 0.0)
    return jnp.where(offset < sizes_ref[region, 1], near, 0.0)


def as_row(ref):
    return ref[...].reshape(1, ref.shape[0])


def field_rows(coming, region, place, eye):
    return jnp.concatenate(
        [
            dot_last(eye, coming[region, first : first + 256, place])
            for first in range(0, coming.shape[1], 256)
        ],
        1,
    )


def forward_kernel(sizes, *refs):
    (
        region_sizes,
        region_starts,
        tokens_ref,
        gain_ref,
        shift_ref,
        scale_ref,
        center_ref,
        weights_ref,
        biases_ref,
        to_modes,
        to_columns,
        ahead,
        behind,
        eye,
        up_hbm,
        project_hbm,
        mixed_hbm,
        second_hbm,
        *kept_hbm,
        hidden_back_hbm,
    ) = refs[:23]
    work, sems = refs[23:33], refs[33:41]
    (
        mixed,
        second,
        mixed_sems,
        second_sems,
        kept_sems,
        up_ref,
        project_ref,
        hidden_back,
        load_sems,
        back_sems,
        *kept,
    ) = refs[41:]
    loads = [
        pltpu.make_async_copy(up_hbm, up_ref, load_sems.at[0]),
        pltpu.make_async_copy(project_hbm, project_ref, load_sems.at[1]),
    ]
    for copy in loads:
        copy.start()
    regions, blocks, block_size, chips, cols, tokens = sizes
    me, core = greet(chips, cols)
    sent, coming = work[0], work[-1]
    piece = 128
    steps = kept_hbm[0].shape[0]
    cols_here = 128 // cols
    gain, shift, scale, center = (
        as_row(ref) for ref in (gain_ref, shift_ref, scale_ref, center_ref)
    )

    def inside(region, first, rows):
        shape = (rows, tokens // cols_here, cols_here)
        return inside_region(region_sizes, region_starts, region, first, shape, 128)

    def produce(region):
        def step(part, carry):
            rows = pl.ds(pl.multiple_of(region * tokens + part * piece, piece), piece)
            unit, factor = normalise(tokens_ref[rows, :].astype(wide))
            values = (inside(region, part * piece, piece) * (unit * gain + shift)).astype(low)
            place = pl.ds(pl.multiple_of(part * piece, piece), piece)
            to_feature_rows(sent, region, place, values, eye[...])
            return carry

        lax.fori_loop(0, tokens // piece, step, 0)

    def keep(step):
        slot = step % 2
        return [
            pltpu.make_async_copy(ref.at[slot], hbm.at[step], kept_sems.at[k, slot])
            for k, (ref, hbm) in enumerate(zip(kept, kept_hbm))
        ]

    def middle(step, spectrum):
        slot = step % 2

        @pl.when(step >= 2)
        def _():
            for copy in keep(step - 2):
                copy.wait()

        spectrum_kept, first_kept, act_kept, second_kept = kept
        spectrum = spectrum.astype(low)
        spectrum_kept[slot] = spectrum
        first = dot_first(weights_ref[0], spectrum) + biases_ref[:, 0:1]
        curve = gelu_parts(first)
        first_kept[slot] = curve + first * gelu_bell(first)
        act = (first * curve).astype(low)
        act_kept[slot] = act
        second_pre = dot_first(weights_ref[1], act) + biases_ref[:, 1:2]
        level = jnp.tanh(second_pre / shrink_width)
        second_kept[slot] = level * level
        for copy in keep(step):
            copy.start()
        return second_pre - shrink_width * level

    def leave(region):
        rows = pl.ds(pl.multiple_of(region * tokens, tokens), tokens)
        return [
            pltpu.make_async_copy(mixed.at[rows], mixed_hbm.at[rows], mixed_sems.at[region]),
            pltpu.make_async_copy(second.at[rows], second_hbm.at[rows], second_sems.at[region]),
        ]

    def consume(region):
        def step(part, carry):
            rows = pl.ds(pl.multiple_of(region * tokens + part * 256, 256), 256)
            place = pl.ds(pl.multiple_of(part * 256, 256), 256)
            fields = field_rows(coming, region, place, eye[...])
            residual = tokens_ref[rows, :].astype(wide)
            unit, factor = normalise(residual)
            value = residual + inside(region, part * 256, 256) * fields + (unit * gain + shift)
            mixed[rows, :] = value
            unit, factor = normalise(value)
            second[rows, :] = (unit * scale + center).astype(low)
            return carry

        lax.fori_loop(0, tokens // 256, step, 0)
        for copy in leave(region):
            copy.start()

    tiles, count, tile = hidden_back.shape

    def leave_back(k):
        return pltpu.make_async_copy(hidden_back.at[k], hidden_back_hbm.at[k], back_sems.at[k])

    def tick(place, step=0):
        if place == "sent":
            for copy in loads:
                copy.wait()

            def tile_step(k, carry):
                here = pl.ds(pl.multiple_of(k * tile, tile), tile)
                for first in range(0, count, 256):
                    rows = slice(first, first + 256)
                    hidden_back[k, rows, :] = dot_last(up_ref[rows, :], project_ref[here, :]).astype(low)
                leave_back(k).start()
                return carry

            lax.fori_loop(0, tiles, tile_step, 0)

    tables = (to_modes, to_columns, ahead, behind)
    filter_pass(sizes, me, core, produce, middle, consume, tables, work, sems, tick)
    for k in range(tiles):
        leave_back(k).wait()
    for step in (steps - 2, steps - 1):
        for copy in keep(step):
            copy.wait()
    for region in range(regions):
        for copy in leave(region):
            copy.wait()


def place_of(row, col):
    return {"core": row % 2, "x": (row // 2) % 2, "z": row // 4, "y": col}


def device_at(spot):
    return (spot["z"] * 4 + spot["x"] * 2 + spot["core"], spot["y"])


def across(spot, axis, step=1):
    size = 4 if axis == "z" else 2
    return device_at({**spot, axis: (spot[axis] + step) % size})


def remote(src, dst, send_sem, recv_sem, device):
    return pltpu.make_async_remote_copy(
        src_ref=src,
        dst_ref=dst,
        send_sem=send_sem,
        recv_sem=recv_sem,
        device_id=device,
        device_id_type=MESH,
    )


def add_rows(out_ref, out_row, terms, rows):
    step = [size for size in (96, 64, 48, 32) if rows % size == 0][0]

    def add(part, carry):
        total = 0.0
        for ref, row in terms:
            here = pl.ds(pl.multiple_of(row + part * step, 16), step)
            total = total + ref[here, :].astype(wide)
        there = pl.ds(pl.multiple_of(out_row + part * step, 16), step)
        out_ref[there, :] = total.astype(low)
        return carry

    lax.fori_loop(0, rows // step, add, 0)


def row_part(ref, row, rows):
    return ref.at[pl.ds(pl.multiple_of(row, 16), rows)]


def facing(spot, axis):
    if axis == "near":
        z = spot["z"] // 2 * 2 + 1 - spot["z"] % 2
        return spot["z"] % 2, device_at({**spot, "z": z})
    if axis == "far":
        return spot["z"] // 2, across(spot, "z", 2)
    return spot[axis], across(spot, axis)


def reduce_steps(spot, axes, buffers, sends, recvs):
    steps = []
    for k, axis in enumerate(axes):
        bit, device = facing(spot, axis)
        source, target = buffers[k], buffers[k + 1]
        rows = target.shape[0]
        hop = remote(
            row_part(source, (1 - bit) * rows, rows), target, sends.at[k], recvs.at[k], device
        )

        def finish(hop=hop, source=source, target=target, rows=rows, bit=bit):
            hop.wait()
            add_rows(target, 0, ((target, 0), (source, bit * rows)), rows)

        steps.append((hop.start, finish))
    return steps


def share_steps(spot, axes, piece, total, sends, recvs, own_sem):
    offsets, rows, bits, devices = [0], [total.shape[0]], [], []
    for axis in axes:
        bit, device = facing(spot, axis)
        bits.append(bit)
        devices.append(device)
        rows.append(rows[-1] // 2)
        offsets.append(offsets[-1] + bit * rows[-1])
    last = len(axes) - 1
    hops = []
    for k in range(last, -1, -1):
        place = row_part(total, offsets[k + 1], rows[k + 1])
        source = piece if k == last else place
        hops.append(remote(source, place, sends.at[k], recvs.at[k], devices[k]))
    keep = pltpu.make_async_copy(piece, row_part(total, offsets[-1], rows[-1]), own_sem)
    ready = (
        (offsets[2], rows[2]),
        (offsets[1] + (1 - bits[1]) * rows[2], rows[2]),
        ((1 - bits[0]) * rows[1], rows[1]),
    )
    cores = []
    for k, (offset, size) in enumerate(ready):
        place = row_part(total, offset, size)
        cores.append(
            remote(place, place, sends.at[4 + k], recvs.at[4 + k], across(spot, "core"))
        )

    def begin():
        keep.start()
        hops[0].start()

    def second():
        keep.wait()
        hops[0].wait()
        hops[1].start()

    def third():
        hops[1].wait()
        hops[2].start()
        cores[0].start()

    def fourth():
        hops[2].wait()
        hops[3].start()
        cores[1].start()

    def fifth():
        hops[3].wait()
        cores[2].start()

    def finish():
        for core in cores:
            core.wait()

    return begin, second, third, fourth, fifth, finish


def backward_kernel(sizes, *refs):
    (
        region_sizes,
        region_starts,
        tokens_hbm,
        mixed_back_ref,
        gain_ref,
        weights_ref,
        to_modes,
        to_columns,
        ahead,
        behind,
        eye,
        spectrum_hbm,
        first_hbm,
        act_hbm,
        pre_hbm,
        project_hbm,
        expand_hbm,
        project_piece,
        expand_piece,
        project_ready,
        expand_ready,
        sums_ref,
        slope_hbm,
        project_total,
        expand_total,
        gathered,
        gathered_bias,
        vector_sum,
    ) = refs[:28]
    work, sems = refs[28:38], refs[38:46]
    (
        tokens_ref,
        slope,
        slope_sems,
        project_own,
        expand_own,
        load_sems,
        kernel_slope,
        bias_slope,
        mixer_slope,
        offset_slope,
        spectrum_slots,
        first_slots,
        act_slots,
        pre_slots,
        slot_sems,
        project_halves,
        expand_halves,
        project_quarters,
        expand_quarters,
        project_eighths,
        expand_eighths,
        project_pieces,
        expand_pieces,
        reduce_sends,
        reduce_recvs,
        share_sends,
        share_recvs,
        own_sems,
        slab,
        slab_bias,
        slab_got,
        slab_bias_got,
        slab_region,
        slab_bias_region,
        slab_sends,
        slab_recvs,
        vector_sent,
        vector_got,
        vector_sends,
        vector_recvs,
        late,
        late_got,
        late_all,
        late_sends,
        late_recvs,
    ) = refs[46:]
    regions, blocks, block_size, chips, cols, tokens = sizes
    steps = spectrum_hbm.shape[0]
    slots = (spectrum_slots, first_slots, act_slots, pre_slots)
    streams = (spectrum_hbm, first_hbm, act_hbm, pre_hbm)

    def fetch(step, slot):
        return [
            pltpu.make_async_copy(hbm.at[step], ref.at[slot], slot_sems.at[k, slot])
            for k, (hbm, ref) in enumerate(zip(streams, slots))
        ]

    own = (project_own, expand_own)
    load_own = [
        pltpu.make_async_copy(hbm, own[k], load_sems.at[1 + k])
        for k, hbm in enumerate((project_hbm, expand_hbm))
    ]
    load_tokens = pltpu.make_async_copy(tokens_hbm, tokens_ref, load_sems.at[0])
    for copy in load_own:
        copy.start()
    for copy in fetch(0, 0):
        copy.start()
    load_tokens.start()
    me, core = greet(chips, cols)
    spot = place_of(lax.axis_index("rows"), lax.axis_index("cols"))
    block = me % blocks
    sent, coming = work[0], work[-1]
    piece = 128
    cols_here = 128 // cols
    late[...] = jnp.zeros_like(late)
    vector_sum[...] = sums_ref[...]
    for ref in (kernel_slope, bias_slope, mixer_slope, offset_slope):
        ref[...] = jnp.zeros_like(ref)
    reducing, sharing = [], []
    pairs = 3
    tile = project_own.shape[0]
    own_pieces = (
        (project_piece, expand_piece),
        (project_pieces.at[0], expand_pieces.at[0]),
        (project_pieces.at[1], expand_pieces.at[1]),
    )
    chains = (
        ((project_piece,), (expand_piece,)),
        (
            (project_ready, project_eighths.at[0], own_pieces[1][0]),
            (expand_ready, expand_eighths.at[0], own_pieces[1][1]),
        ),
        (
            (
                project_own,
                project_halves,
                project_quarters,
                project_eighths.at[1],
                own_pieces[2][0],
            ),
            (expand_own, expand_halves, expand_quarters, expand_eighths.at[1], own_pieces[2][1]),
        ),
    )
    for j in range(pairs):
        place = pl.multiple_of((core * pairs + j) * tile, tile)
        totals = (project_total.at[pl.ds(place, tile)], expand_total.at[:, pl.ds(place, tile)])
        for k in range(2):
            axes = (("x", "y"), ("y", "x"))[k] + ("near", "far")
            buffers = chains[j][k]
            reducing.append(
                reduce_steps(
                    spot,
                    axes[5 - len(buffers) :],
                    buffers,
                    reduce_sends.at[j, k],
                    reduce_recvs.at[j, k],
                )
            )
            sharing.append(
                share_steps(
                    spot,
                    axes,
                    own_pieces[j][k],
                    totals[k],
                    share_sends.at[j, k],
                    share_recvs.at[j, k],
                    own_sems.at[j, k],
                )
            )

    def reduce(j, step, finish):
        for steps_of in reducing[2 * j : 2 * j + 2]:
            steps_of[step][finish]()

    def share(j, step):
        for steps_of in sharing[2 * j : 2 * j + 2]:
            steps_of[step]()

    def inside(region, first, rows):
        shape = (rows, tokens // cols_here, cols_here)
        return inside_region(region_sizes, region_starts, region, first, shape, 128)

    def produce(region):
        def step(part, carry):
            rows = pl.ds(pl.multiple_of(region * tokens + part * piece, piece), piece)
            place = pl.ds(pl.multiple_of(part * piece, piece), piece)
            values = (inside(region, part * piece, piece) * mixed_back_ref[rows, :]).astype(low)
            to_feature_rows(sent, region, place, values, eye[...])
            return carry

        lax.fori_loop(0, tokens // piece, step, 0)

    def middle(step, shrunk_back):
        slot = step % 2
        for copy in fetch(step, slot):
            copy.wait()

        @pl.when(step + 1 < steps)
        def _():
            for copy in fetch(step + 1, 1 - slot):
                copy.start()

        second = (shrunk_back * pre_slots[slot]).astype(low)
        ones = jnp.ones((8, second.shape[1]), low)
        offset_slope[...] += dot_last(ones, second)
        mixer_slope[...] += dot_last(act_slots[slot], second)
        first = (dot(weights_ref[1], second) * first_slots[slot]).astype(low)
        bias_slope[...] += dot_last(ones, first)
        kernel_slope[...] += dot_last(spectrum_slots[slot], first)
        return dot(weights_ref[0], first)

    def leave(region):
        rows = pl.ds(pl.multiple_of(region * tokens, tokens), tokens)
        return pltpu.make_async_copy(slope.at[rows], slope_hbm.at[rows], slope_sems.at[region])

    def consume(region):
        def step(part, carry):
            rows = pl.ds(pl.multiple_of(region * tokens + part * 256, 256), 256)
            place = pl.ds(pl.multiple_of(part * 256, 256), 256)
            fields = field_rows(coming, region, place, eye[...])
            unit, factor = normalise(tokens_ref[rows, :].astype(wide))
            mixed_back = mixed_back_ref[rows, :]
            normed_back = mixed_back + inside(region, part * 256, 256) * fields
            gains = jnp.sum(normed_back * unit, 0, keepdims=True)
            shifts = jnp.sum(normed_back, 0, keepdims=True)
            for k in range(3):
                late[k : k + 1, :] += gains[:, k * 256 : (k + 1) * 256]
                late[3 + k : 4 + k, :] += shifts[:, k * 256 : (k + 1) * 256]
            pull = normed_back * as_row(gain_ref)
            pull = pull - jnp.mean(pull, -1, keepdims=True) - unit * jnp.mean(
                pull * unit, -1, keepdims=True
            )
            slope[rows, :] = mixed_back + factor * pull
            return carry

        lax.fori_loop(0, tokens // 256, step, 0)
        leave(region).start()

    def slab_hops(place, mine, theirs, device):
        return [
            remote(src, dst, slab_sends.at[k, place], slab_recvs.at[k, place], device)
            for k, (src, dst) in enumerate(zip(mine, theirs))
        ]

    slab_core = slab_hops(
        0, (slab, slab_bias), (slab_got, slab_bias_got), across(spot, "core")
    )
    slab_far = slab_hops(
        1,
        (slab_got.at[core], slab_bias_got.at[core]),
        (slab_region, slab_bias_region),
        chip_device((me + blocks) % chips, core, cols),
    )
    here = (gathered.at[core, :, block], gathered_bias.at[core, block])

    def slab_peer(step):
        other = me // blocks * blocks + (block + step) % blocks
        return slab_hops(1 + step, here, here, chip_device(other, core, cols))

    everything = (gathered.at[core], gathered_bias.at[core])
    slab_last = slab_hops(1 + blocks, everything, everything, across(spot, "core"))

    def slab_start():
        for k, (weight, bias) in enumerate(
            ((kernel_slope, bias_slope), (mixer_slope, offset_slope))
        ):
            whole = weight[...]
            upper, lower = whole[:block_size], whole[block_size:]
            slab[k, 0] = upper[:, :block_size] + lower[:, block_size:]
            slab[k, 1] = upper[:, block_size:] - lower[:, :block_size]
            slab_bias[k] = bias[...]
        for hop in slab_core:
            hop.start()

    def slab_regions():
        for hop in slab_core:
            hop.wait()
        slab_got[...] = slab_got[...] + slab[...]
        slab_bias_got[...] = slab_bias_got[...] + slab_bias[...]
        for hop in slab_far:
            hop.start()

    def slab_blocks():
        for hop in slab_far:
            hop.wait()
        gathered[core, :, block] = slab_region[...] + slab_got[core]
        gathered_bias[core, block] = slab_bias_region[...] + slab_bias_got[core]
        for step in range(1, blocks):
            for hop in slab_peer(step):
                hop.start()

    def slab_cores():
        for step in range(1, blocks):
            for hop in slab_peer(step):
                hop.wait()
        for hop in slab_last:
            hop.start()

    partners = (
        across(spot, "core"),
        across(spot, "x"),
        across(spot, "y"),
        device_at({**spot, "z": spot["z"] // 2 * 2 + 1 - spot["z"] % 2}),
        across(spot, "z", 2),
    )
    hops = [
        remote(
            vector_sent.at[k], vector_got.at[k], vector_sends.at[k], vector_recvs.at[k], device
        )
        for k, device in enumerate(partners)
    ]

    def vector_step(k):
        if k > 0:
            hops[k - 1].wait()
            vector_sum[...] = vector_sum[...] + vector_got[k - 1]
        if k < len(hops):
            vector_sent[k] = vector_sum[...]
            hops[k].start()

    regions_seen = []

    def tick(place, step=0):
        if place == "arrival":

            @pl.when(step == 4)
            def _():
                reduce(2, 0, 1)
                reduce(2, 1, 0)

        if place == "mode":

            @pl.when(step == 3)
            def _():
                share(0, 3)
                reduce(2, 2, 1)
                reduce(2, 3, 0)
                share(1, 1)

            @pl.when(step == 5)
            def _():
                reduce(2, 3, 1)

        if place == "start":
            for copy in load_own:
                copy.wait()
            reduce(2, 0, 0)
            reduce(1, 0, 0)
            vector_step(0)
        if place == "sent":
            reduce(1, 0, 1)
            share(0, 0)
            vector_step(1)
        if place == "zonal":
            share(0, 1)
            reduce(1, 1, 0)
            reduce(2, 1, 1)
            reduce(2, 2, 0)
            vector_step(2)
        if place == "turned":
            share(0, 2)
            reduce(1, 1, 1)
            share(1, 0)
            vector_step(3)
        if place == "modes":
            slab_start()
            share(1, 2)
            share(2, 0)
            vector_step(4)
        if place == "returned":
            share(0, 4)
            share(1, 3)
            share(2, 1)
            vector_step(5)
        if place == "back":
            slab_regions()
        if place == "columns":
            load_tokens.wait()
            slab_blocks()
            share(2, 2)
            share(1, 4)
            share(2, 3)
            slab_cores()
        if place == "region":
            regions_seen.append(place)
            if len(regions_seen) == 1:
                share(2, 4)

    tables = (to_columns, to_modes, ahead, behind)
    filter_pass(sizes, me, core, produce, middle, consume, tables, work, sems, tick)
    late_core = remote(late, late_got, late_sends.at[0], late_recvs.at[0], across(spot, "core"))
    late_core.start()
    late_core.wait()
    late[...] = late[...] + late_got[...]
    late_all[me] = late[...]

    def late_hop(step):
        other = chip_device((me + step) % chips, core, cols)
        return remote(late, late_all.at[me], late_sends.at[step], late_recvs.at[step], other)

    for step in range(1, chips):
        late_hop(step).start()
    for hop in slab_last:
        hop.wait()
    share(0, 5)
    share(1, 5)
    share(2, 5)
    for step in range(1, chips):
        late_hop(step).wait()
    total = late_all[0]
    for chip in range(1, chips):
        total = total + late_all[chip]
    for k in range(3):
        vector_sum[0:1, k * 256 : (k + 1) * 256] = total[k : k + 1, :]
        vector_sum[1:2, k * 256 : (k + 1) * 256] = total[3 + k : 4 + k, :]
    for region in range(regions):
        leave(region).wait()


def call_filter(body, sizes, outs, cid, operands, scalars, spaces, out_spaces, scratch):
    shapes = [jax.ShapeDtypeStruct(shape, kind) for shape, kind in outs]
    anywhere = pl.BlockSpec(memory_space=pl.ANY)
    scalar = pl.BlockSpec(memory_space=pltpu.SMEM)
    return pl.pallas_call(
        functools.partial(body, sizes),
        out_shape=shapes,
        in_specs=[scalar] * len(scalars)
        + [anywhere if place in spaces else vmem for place in range(len(operands))],
        out_specs=[anywhere if place in out_spaces else vmem for place in range(len(outs))],
        scratch_shapes=[*work_shapes(sizes), *scratch],
        compiler_params=pltpu.CompilerParams(
            collective_id=cid, has_side_effects=True, vmem_limit_bytes=60 * 1024 * 1024
        ),
    )(*scalars, *operands)


def forward_scratch(sizes, kept, hidden, tile):
    regions, blocks, block_size, chips, cols, tokens = sizes
    dma = pltpu.SemaphoreType.DMA
    features = blocks * block_size
    return (
        pltpu.VMEM((regions * tokens, features), wide),
        pltpu.VMEM((regions * tokens, features), low),
        dma((regions,)),
        dma((regions,)),
        dma((len(kept), 2)),
        pltpu.VMEM((regions * tokens, features), low),
        pltpu.VMEM((hidden, features), low),
        pltpu.VMEM((hidden // tile, regions * tokens, tile), low),
        dma((2,)),
        dma((hidden // tile,)),
        *(pltpu.VMEM((2, *shape[1:]), kind) for shape, kind in kept),
    )


def backward_scratch(sizes, kept, tile, pairs):
    regions, blocks, block_size, chips, cols, tokens = sizes
    features = blocks * block_size
    side = 2 * block_size
    dma = pltpu.SemaphoreType.DMA
    return (
        pltpu.VMEM((regions * tokens, features), low),
        pltpu.VMEM((regions * tokens, features), wide),
        dma((regions,)),
        pltpu.VMEM((tile, features), low),
        pltpu.VMEM((features, tile), low),
        dma((3,)),
        pltpu.VMEM((side, side), wide),
        pltpu.VMEM((8, side), wide),
        pltpu.VMEM((side, side), wide),
        pltpu.VMEM((8, side), wide),
        *(pltpu.VMEM((2, *shape[1:]), kind) for shape, kind in kept),
        dma((len(kept), 2)),
        pltpu.VMEM((tile // 2, features), low),
        pltpu.VMEM((features // 2, tile), low),
        pltpu.VMEM((tile // 4, features), low),
        pltpu.VMEM((features // 4, tile), low),
        pltpu.VMEM((2, tile // 8, features), low),
        pltpu.VMEM((2, features // 8, tile), low),
        pltpu.VMEM((2, tile // 16, features), low),
        pltpu.VMEM((2, features // 16, tile), low),
        dma((pairs, 2, 4)),
        dma((pairs, 2, 4)),
        dma((pairs, 2, 7)),
        dma((pairs, 2, 7)),
        dma((pairs, 2)),
        pltpu.VMEM((2, 2, block_size, block_size), wide),
        pltpu.VMEM((2, 8, side), wide),
        pltpu.VMEM((2, 2, block_size, block_size), wide),
        pltpu.VMEM((2, 8, side), wide),
        pltpu.VMEM((2, block_size, block_size), wide),
        pltpu.VMEM((8, side), wide),
        dma((2, 2 + blocks)),
        dma((2, 2 + blocks)),
        pltpu.VMEM((5, 16, features), wide),
        pltpu.VMEM((5, 16, features), wide),
        dma((5,)),
        dma((5,)),
        pltpu.VMEM((8, 256), wide),
        pltpu.VMEM((8, 256), wide),
        pltpu.VMEM((chips, 8, 256), wide),
        dma((chips,)),
        dma((chips,)),
    )


def finish_kernel(*refs):
    (
        project,
        expand,
        slope,
        output,
        gathered,
        gathered_bias,
        sums,
        output_out,
        slope_out,
        gain,
        shift,
        kernel,
        bias,
        mixer,
        offset,
        scale,
        center,
        expand_out,
        lift,
        project_out,
        returned,
        project_low,
        expand_low,
        project_wide,
        expand_wide,
        slope_held,
        output_held,
        load_sems,
        store_sems,
        pass_sems,
    ) = refs
    parts = load_sems.shape[1]
    whole = ((project, project_low, project_wide, project_out), (expand, expand_low, expand_wide, expand_out))

    def rows_of(ref, part):
        size = ref.shape[0] // parts
        return ref.at[pl.ds(part * size, size)]

    def load(k, part):
        source, narrow, broad, target = whole[k]
        return pltpu.make_async_copy(
            rows_of(source, part), rows_of(narrow, part), load_sems.at[k, part]
        )

    def store(k, part):
        source, narrow, broad, target = whole[k]
        return pltpu.make_async_copy(
            rows_of(broad, part), rows_of(target, part), store_sems.at[k, part]
        )

    for part in range(parts):
        for k in range(2):
            load(k, part).start()
    passes = [
        [
            pltpu.make_async_copy(source, held, pass_sems.at[0, k]),
            pltpu.make_async_copy(held, target, pass_sems.at[1, k]),
        ]
        for k, (source, held, target) in enumerate(
            ((slope, slope_held, slope_out), (output, output_held, output_out))
        )
    ]
    for copy in passes:
        copy[0].start()
    kernel[...] = gathered[0]
    mixer[...] = gathered[1]
    side = bias.shape[2]
    for b in range(bias.shape[1]):
        for i in range(2):
            bias[i, b : b + 1, :] = gathered_bias[0, b, 0:1, i * side : (i + 1) * side]
            offset[i, b : b + 1, :] = gathered_bias[1, b, 0:1, i * side : (i + 1) * side]
    for k, ref in enumerate((gain, shift, scale, center, returned)):
        ref[...] = sums[k : k + 1, :].reshape(ref.shape)
    tile = lift.shape[0] // 6
    for k in range(6):
        lift[k * tile : (k + 1) * tile] = sums[5 + k : 6 + k, :tile].reshape(tile)
    for copy in passes:
        copy[0].wait()
        copy[1].start()
    for part in range(parts):
        for k in range(2):
            load(k, part).wait()
            source, narrow, broad, target = whole[k]
            rows_of(broad, part)[...] = rows_of(narrow, part)[...].astype(wide)
            store(k, part).start()
    for part in range(parts):
        for k in range(2):
            store(k, part).wait()
    for copy in passes:
        copy[1].wait()


def call_finish(project, expand, slope, output, gathered, gathered_bias, sums):
    hidden, features = project.shape
    line = jax.ShapeDtypeStruct((features,), wide)
    weight = jax.ShapeDtypeStruct(gathered.shape[1:], wide)
    bias = jax.ShapeDtypeStruct(gathered.shape[1:4], wide)
    shapes = [
        jax.ShapeDtypeStruct(output.shape, low),
        jax.ShapeDtypeStruct(slope.shape, wide),
        line,
        line,
        weight,
        bias,
        weight,
        bias,
        line,
        line,
        jax.ShapeDtypeStruct(expand.shape, wide),
        jax.ShapeDtypeStruct((hidden,), wide),
        jax.ShapeDtypeStruct(project.shape, wide),
        line,
    ]
    anywhere = pl.BlockSpec(memory_space=pl.ANY)
    dma = pltpu.SemaphoreType.DMA
    parts = 8
    return pl.pallas_call(
        finish_kernel,
        out_shape=shapes,
        in_specs=[anywhere] * 4 + [vmem] * 3,
        out_specs=[anywhere if k in (0, 1, 10, 12) else vmem for k in range(len(shapes))],
        scratch_shapes=[
            pltpu.VMEM(project.shape, low),
            pltpu.VMEM(expand.shape, low),
            pltpu.VMEM(project.shape, wide),
            pltpu.VMEM(expand.shape, wide),
            pltpu.VMEM(slope.shape, wide),
            pltpu.VMEM(output.shape, low),
            dma((2, parts)),
            dma((2, parts)),
            dma((2, 2)),
        ],
        compiler_params=pltpu.CompilerParams(vmem_limit_bytes=60 * 1024 * 1024),
    )(project, expand, slope, output, gathered, gathered_bias, sums)


def dense_kernel(*refs):
    (
        second_ref,
        up_ref,
        scale_ref,
        returned_ref,
        lift_ref,
        mixed_hbm,
        expand_hbm,
        project_hbm,
        hidden_back_hbm,
        out_hbm,
        mixed_back_hbm,
        project_hbm_own,
        expand_hbm_own,
        project_piece,
        expand_piece,
        project_ready,
        expand_ready,
        vectors,
        mixed_ref,
        expand_ref,
        project_ref,
        hidden_back,
        out_ref,
        out_sum,
        back_sum,
        hidden_tile,
        back_tile,
        project_sent,
        expand_sent,
        project_got,
        expand_got,
        project_own,
        expand_own,
        project_halves,
        expand_halves,
        project_quarters,
        expand_quarters,
        project_eighths,
        expand_eighths,
        load_sems,
        weight_sems,
        leave_sems,
        own_sems,
        sent_sem,
        got_sem,
        first_sends,
        first_recvs,
    ) = refs
    tile = expand_ref.shape[2]
    pairs = project_own.shape[0]
    spot = place_of(lax.axis_index("rows"), lax.axis_index("cols"))
    core = spot["core"]
    orders = (("x", "y"), ("y", "x"))
    sent = (project_sent, expand_sent)
    got = (project_got, expand_got)
    own = (project_own, expand_own)
    halves = (project_halves, expand_halves)
    quarters = (project_quarters, expand_quarters)
    eighths = (project_eighths, expand_eighths)
    piece0 = (project_piece, expand_piece)
    ready = (project_ready, expand_ready)
    places = []
    for j in range(pairs):
        places += [(1 - core) * pairs + j, core * pairs + j]

    def weights(k):
        here = pl.ds(pl.multiple_of(places[k] * tile, tile), tile)
        return [
            pltpu.make_async_copy(project_hbm.at[here], project_ref.at[k], weight_sems.at[0, k]),
            pltpu.make_async_copy(expand_hbm.at[:, here], expand_ref.at[k], weight_sems.at[1, k]),
            pltpu.make_async_copy(
                hidden_back_hbm.at[places[k]], hidden_back.at[k], weight_sems.at[2, k]
            ),
        ]

    for k in range(2 * pairs):
        for copy in weights(k):
            copy.start()
    load_mixed = pltpu.make_async_copy(mixed_hbm, mixed_ref, load_sems.at[0])
    load_mixed.start()
    barrier = pltpu.get_barrier_semaphore()
    for axis in ("core", "x", "y", "near", "far"):
        device = facing(spot, axis)[1]
        pl.semaphore_signal(barrier, inc=1, device_id=device, device_id_type=MESH)
    count = second_ref.shape[0]
    piece = 1024
    vectors[...] = jnp.zeros_like(vectors)

    def start_step(part, carry):
        rows = pl.ds(pl.multiple_of(part * piece, piece), piece)
        out_sum[rows, :] = jnp.broadcast_to(as_row(returned_ref), (piece, out_sum.shape[1]))
        back_sum[rows, :] = jnp.zeros((piece, back_sum.shape[1]), wide)
        return carry + jnp.sum(up_ref[rows, :].astype(wide), 0, keepdims=True)

    vectors[4:5, :] = lax.fori_loop(
        0, count // piece, start_step, jnp.zeros((1, up_ref.shape[1]), wide)
    )
    pl.semaphore_wait(barrier, 5)

    def tile_step(k, place, between):
        lift_row = lift_ref[pl.ds(pl.multiple_of(place * tile, tile), tile)].reshape(1, tile)

        def piece_step(part, carry):
            rows = pl.ds(pl.multiple_of(part * piece, piece), piece)
            pre = dot(second_ref[rows, :], expand_ref[k]) + lift_row
            back = hidden_back[k, rows, :].astype(wide)
            curve = gelu_parts(pre)
            bell = gelu_bell(pre)
            hidden = (pre * curve).astype(low)
            hidden_tile[rows, :] = hidden
            pre_back = (back * (curve + pre * bell)).astype(low)
            back_tile[rows, :] = pre_back
            out_sum[rows, :] += dot(hidden, project_ref[k])
            back_sum[rows, :] += dot_last(pre_back, expand_ref[k])
            return carry + jnp.sum(pre_back.astype(wide), 0, keepdims=True)

        lift = lax.fori_loop(0, count // piece, piece_step, jnp.zeros((1, tile), wide))
        vectors[pl.ds(5 + place, 1), 0:tile] = lift
        between()
        return (
            dot_first(hidden_tile[...], up_ref[...]),
            dot_first(second_ref[...], back_tile[...]),
        )

    def swap(j, k):
        return remote(
            sent[k].at[j], got[k].at[j], sent_sem.at[j, k], got_sem.at[j, k], across(spot, "core")
        )

    chains = []
    for pair in range(2):
        for k in range(2):
            buffers = (own[k].at[pair], halves[k].at[pair])
            if pair == 0:
                buffers += (quarters[k], eighths[k], piece0[k])
            else:
                buffers += (ready[k],)
            chains.append(
                reduce_steps(
                    spot,
                    (orders[k] + ("near", "far"))[: len(buffers) - 1],
                    buffers,
                    first_sends.at[pair, k],
                    first_recvs.at[pair, k],
                )
            )

    def begin(pair, step):
        for chain in chains[pair * 2 : pair * 2 + 2]:
            chain[step][0]()

    def finish(pair, step):
        for chain in chains[pair * 2 : pair * 2 + 2]:
            chain[step][1]()

    def pair_step(j, carry):
        for copy in weights_at(2 * j):
            copy.wait()

        def away_between():
            @pl.when(j == 2)
            def _():
                finish(0, 1)
                begin(0, 2)

        away = tile_step(2 * j, (1 - core) * pairs + j, away_between)
        for k in range(2):
            sent[k][j] = away[k].astype(low)
            swap(j, k).start()
        for copy in weights_at(2 * j + 1):
            copy.wait()

        def home_between():
            @pl.when(j == 1)
            def _():
                finish(0, 0)
                begin(0, 1)

            @pl.when(j == 2)
            def _():
                finish(0, 2)
                begin(0, 3)
                finish(1, 0)
                begin(1, 1)

        home = tile_step(2 * j + 1, core * pairs + j, home_between)
        for k in range(2):
            swap(j, k).wait()
            own[k][j] = (home[k] + got[k][j].astype(wide)).astype(low)

        @pl.when(j == 0)
        def _():
            begin(0, 0)

        @pl.when(j == 1)
        def _():
            begin(1, 0)

        return carry

    def weights_at(k):
        return [
            pltpu.make_async_copy(project_ref.at[k], project_ref.at[k], weight_sems.at[0, k]),
            pltpu.make_async_copy(expand_ref.at[k], expand_ref.at[k], weight_sems.at[1, k]),
            pltpu.make_async_copy(hidden_back.at[k], hidden_back.at[k], weight_sems.at[2, k]),
        ]

    lax.fori_loop(0, pairs, pair_step, 0)
    keeps = [
        pltpu.make_async_copy(own[k].at[pairs - 1], hbm, own_sems.at[k])
        for k, hbm in enumerate((project_hbm_own, expand_hbm_own))
    ]
    for keep in keeps:
        keep.start()
    load_mixed.wait()

    def leave(part):
        rows = pl.ds(pl.multiple_of(part * piece, piece), piece)
        return [
            pltpu.make_async_copy(out_ref.at[rows], out_hbm.at[rows], leave_sems.at[0, part]),
            pltpu.make_async_copy(
                back_sum.at[rows], mixed_back_hbm.at[rows], leave_sems.at[1, part]
            ),
        ]

    def end_step(part, carry):
        for quarter in range(4):
            size = piece // 4
            rows = pl.ds(pl.multiple_of(part * piece + quarter * size, size), size)
            mixed = mixed_ref[rows, :]
            out_ref[rows, :] = (out_sum[rows, :] + mixed).astype(low)
            unit, factor = normalise(mixed)
            norm_back = back_sum[rows, :]
            vectors[2:3, :] += jnp.sum(norm_back * unit, 0, keepdims=True)
            vectors[3:4, :] += jnp.sum(norm_back, 0, keepdims=True)
            pull = norm_back * as_row(scale_ref)
            pull = pull - jnp.mean(pull, -1, keepdims=True) - unit * jnp.mean(
                pull * unit, -1, keepdims=True
            )
            back_sum[rows, :] = up_ref[rows, :].astype(wide) + factor * pull
        for copy in leave(part):
            copy.start()
        return carry

    lax.fori_loop(0, count // piece, end_step, 0)
    finish(0, 3)
    finish(1, 1)
    for keep in keeps:
        keep.wait()
    for part in range(count // piece):
        for copy in leave(part):
            copy.wait()


def call_dense(second_norm, upstream, scale, returned, lift, mixed, expand, project, hidden_back, cid):
    count, features = second_norm.shape
    tile = hidden_back.shape[2]
    pairs = expand.shape[1] // tile // 2
    tall, broad = (tile, features), (features, tile)
    outs = (
        ((count, features), low),
        ((count, features), wide),
        (tall, low),
        (broad, low),
        ((tile // 16, features), low),
        ((features // 16, tile), low),
        ((tile // 4, features), low),
        ((features // 4, tile), low),
        ((16, features), wide),
    )
    shapes = [jax.ShapeDtypeStruct(shape, kind) for shape, kind in outs]
    anywhere = pl.BlockSpec(memory_space=pl.ANY)
    dma = pltpu.SemaphoreType.DMA
    return pl.pallas_call(
        dense_kernel,
        out_shape=shapes,
        in_specs=[vmem] * 5 + [anywhere] * 4,
        out_specs=[anywhere] * 4 + [vmem] * 5,
        scratch_shapes=[
            pltpu.VMEM((count, features), wide),
            pltpu.VMEM((2 * pairs, *broad), low),
            pltpu.VMEM((2 * pairs, *tall), low),
            pltpu.VMEM(hidden_back.shape, low),
            pltpu.VMEM((count, features), low),
            pltpu.VMEM((count, features), wide),
            pltpu.VMEM((count, features), wide),
            pltpu.VMEM((count, tile), low),
            pltpu.VMEM((count, tile), low),
            *(pltpu.VMEM((pairs, *shape), low) for shape in (tall, broad) * 3),
            pltpu.VMEM((pairs - 1, tile // 2, features), low),
            pltpu.VMEM((pairs - 1, features // 2, tile), low),
            pltpu.VMEM((tile // 4, features), low),
            pltpu.VMEM((features // 4, tile), low),
            pltpu.VMEM((tile // 8, features), low),
            pltpu.VMEM((features // 8, tile), low),
            dma((1,)),
            dma((3, 2 * pairs)),
            dma((2, count // 512)),
            dma((2,)),
            dma((pairs, 2)),
            dma((pairs, 2)),
            dma((pairs - 1, 2, 4)),
            dma((pairs - 1, 2, 4)),
        ],
        compiler_params=pltpu.CompilerParams(
            collective_id=cid, has_side_effects=True, vmem_limit_bytes=60 * 1024 * 1024
        ),
    )(second_norm, upstream, scale, returned, lift, mixed, expand, project, hidden_back)


def shards(
    tokens,
    region_sizes,
    region_starts,
    entry_gain,
    entry_shift,
    spectral_kernel,
    spectral_bias,
    spectral_mixer,
    spectral_offset,
    exit_scale,
    exit_center,
    dense_expand,
    dense_lift,
    dense_project,
    dense_return,
    cotangent,
):
    regions, rows_here, cols_here, features = tokens.shape
    row_devices = lax.axis_size("rows")
    cols = lax.axis_size("cols")
    blocks, block_size = spectral_kernel.shape[1:3]
    chips = row_devices // 2 * cols
    fits = (
        row_devices % 2 == 0
        and chips == regions * blocks
        and cols == 2
        and cols_here == 64
        and rows_here == 8
        and block_size == 96
        and blocks == 8
        and regions == 2
        and dense_expand.shape == (features, 4 * features)
    )
    if not fits:
        return shards_general(
            tokens,
            region_sizes,
            region_starts,
            entry_gain,
            entry_shift,
            spectral_kernel,
            spectral_bias,
            spectral_mixer,
            spectral_offset,
            exit_scale,
            exit_center,
            dense_expand,
            dense_lift,
            dense_project,
            dense_return,
            cotangent,
        )
    height = rows_here * row_devices
    width = cols_here * cols
    patches = rows_here * cols_here
    count = regions * patches
    sizes = (regions, blocks, block_size, chips, cols, patches)
    block = ((lax.axis_index("rows") // 2) * cols + lax.axis_index("cols")) % blocks

    def own(weight):
        return lax.dynamic_index_in_dim(weight, block, 1, False)

    def square(weight):
        real, imaginary = weight[0], weight[1]
        return jnp.concatenate(
            [
                jnp.concatenate([real, imaginary], 1),
                jnp.concatenate([-imaginary, real], 1),
            ],
            0,
        )

    side = 2 * block_size
    weights = jnp.stack([square(own(spectral_kernel)), square(own(spectral_mixer))])
    biases = jnp.stack(
        [own(spectral_bias).reshape(side), own(spectral_offset).reshape(side)], 1
    )
    to_modes, to_columns, ahead, behind, eye = task_tables(height, width, rows_here, cols_here)
    flat_tokens = tokens.reshape(count, features)
    upstream = cotangent.reshape(count, features)
    steps = width // 4 // 4
    shape = (steps, side, 4 * 128)
    kept = ((shape, low), (shape, wide), (shape, low), (shape, wide))
    scalars = (region_sizes, region_starts)
    hidden, tile = dense_lift.shape[0], 512
    mixed, second_norm, *stream, hidden_back = call_filter(
        forward_kernel,
        sizes,
        (
            ((count, features), wide),
            ((count, features), low),
            *kept,
            ((hidden // tile, count, tile), low),
        ),
        1,
        (
            flat_tokens,
            entry_gain,
            entry_shift,
            exit_scale,
            exit_center,
            weights,
            biases,
            to_modes,
            to_columns,
            ahead,
            behind,
            eye,
            upstream,
            dense_project,
        ),
        scalars,
        (12, 13),
        range(7),
        forward_scratch(sizes, kept, hidden, tile),
    )
    output, mixed_back, *tiles, part_sums = call_dense(
        second_norm,
        upstream,
        exit_scale,
        dense_return,
        dense_lift,
        mixed,
        dense_expand,
        dense_project,
        hidden_back,
        3,
    )
    slope, project_sum, expand_sum, gathered, gathered_bias, sums = call_filter(
        backward_kernel,
        sizes,
        (
            ((count, features), wide),
            (dense_project.shape, low),
            (dense_expand.shape, low),
            ((2, 2, blocks, block_size, block_size), wide),
            ((2, blocks, 8, side), wide),
            ((16, features), wide),
        ),
        2,
        (
            flat_tokens,
            mixed_back,
            entry_gain,
            weights,
            to_modes.T,
            to_columns.T,
            ahead,
            behind,
            eye,
            *stream,
            *tiles,
            part_sums,
        ),
        scalars,
        (0, 9, 10, 11, 12, 13, 14),
        range(3),
        backward_scratch(sizes, kept, tiles[0].shape[0], 3),
    )
    return tuple(
        call_finish(
            project_sum,
            expand_sum,
            slope.reshape(tokens.shape),
            output.reshape(tokens.shape),
            gathered,
            gathered_bias,
            sums,
        )
    )


def solution(mesh):
    placed = (
        P(None, "rows", "cols", None),
        P(),
        P(),
        P(),
        P(),
        P(),
        P(),
        P(),
        P(),
        P(),
        P(),
        P(),
        P(),
        P(),
        P(),
        P(None, "rows", "cols", None),
    )
    return jax.shard_map(
        shards,
        mesh=mesh,
        in_specs=placed,
        out_specs=(
            P(None, "rows", "cols", None),
            P(None, "rows", "cols", None),
            P(),
            P(),
            P(),
            P(),
            P(),
            P(),
            P(),
            P(),
            P(),
            P(),
            P(),
            P(),
        ),
        check_vma=False,
    )
```

```python
import functools
import math

import jax
import jax.numpy as jnp
import ml_dtypes
import numpy as np
from jax import lax
from jax.experimental import pallas as pl
from jax.experimental.pallas import tpu as pltpu
from jax.sharding import PartitionSpec as P

shrink_width = 0.01
norm_eps = 1e-06
highest = lax.Precision.HIGHEST


def tables(height, width, modes):
    column = jnp.arange(width, dtype=jnp.int32)
    frequency = jnp.arange(modes, dtype=jnp.int32)
    turns = column[:, None] * frequency[None, :] % width
    angle = turns.astype(jnp.float32) * (2.0 * math.pi / width)
    cosine = jnp.cos(angle)
    sine = jnp.sin(angle)
    scale = 1.0 / math.sqrt(width)
    forward_zonal = jnp.stack([cosine, -sine], 1) * scale
    factor = jnp.where(frequency == 0, 1.0, 2.0).astype(jnp.float32)
    inverse_zonal = jnp.stack([cosine.T * factor[:, None], -sine.T * factor[:, None]], 0) * scale
    latitude = jnp.arange(height, dtype=jnp.int32)
    meridian_turns = latitude[:, None] * latitude[None, :] % height
    meridian_angle = meridian_turns.astype(jnp.float32) * (2.0 * math.pi / height)
    meridian_cos = jnp.cos(meridian_angle) / math.sqrt(height)
    meridian_sin = jnp.sin(meridian_angle) / math.sqrt(height)
    meridian_table = jnp.stack(
        [jnp.stack([meridian_cos, meridian_sin], -1), jnp.stack([-meridian_sin, meridian_cos], -1)],
        1,
    )
    forward_low = forward_zonal.astype(jnp.bfloat16)
    inverse_low = inverse_zonal.astype(jnp.bfloat16)
    meridian_low = meridian_table.astype(jnp.bfloat16)
    meridian_wide = meridian_low.astype(jnp.float32)
    return (forward_low, inverse_low, meridian_low, meridian_wide)


def layer_norm(value, gain, shift):
    centre = jnp.mean(value, -1, keepdims=True)
    centred = value - centre
    spread = jnp.mean(centred * centred, -1, keepdims=True)
    return centred * lax.rsqrt(spread + norm_eps) * gain + shift


def gelu_exact(value):
    return jax.nn.gelu(value, approximate=False)


def shrink(value):
    return value - shrink_width * jnp.tanh(value / shrink_width)


def block_layout(spectrum, blocks, block_size):
    leading = spectrum.shape[:3]
    parts = spectrum.reshape(leading + (2, blocks, block_size))
    parts = jnp.moveaxis(parts, 3, 4)
    return parts.reshape((-1, blocks, 2 * block_size))


def spectral_layout(modes_flat, leading, blocks, block_size):
    parts = modes_flat.reshape(leading + (blocks, 2, block_size))
    parts = jnp.moveaxis(parts, 4, 3)
    return parts.reshape(leading + (2, blocks * block_size))


def complex_matrix(weight):
    real = weight[0]
    imaginary = weight[1]
    upper = jnp.concatenate([real, imaginary], 2)
    lower = jnp.concatenate([-imaginary, real], 2)
    return jnp.concatenate([upper, lower], 1)


def matrix_gradient(whole, block_size):
    upper = whole[:, :block_size]
    lower = whole[:, block_size:]
    real = upper[:, :, :block_size] + lower[:, :, block_size:]
    imaginary = upper[:, :, block_size:] - lower[:, :, :block_size]
    return jnp.stack([real, imaginary], 0)


def bias_rows(bias):
    return jnp.moveaxis(bias, 0, 1).reshape(bias.shape[1], 2 * bias.shape[2])


def bias_gradient(summed, block_size):
    return jnp.moveaxis(summed.reshape(summed.shape[0], 2, block_size), 1, 0)


def advance(tokens, mask, weights, grids, layout):
    (
        entry_gain,
        entry_shift,
        spectral_kernel,
        spectral_bias,
        spectral_mixer,
        spectral_offset,
        exit_scale,
        exit_center,
        dense_expand,
        dense_lift,
        dense_project,
        dense_return,
    ) = weights
    forward_zonal, inverse_zonal, meridian_table, meridian_wide = grids
    blocks, block_size, first_block = layout
    residual = tokens.astype(jnp.float32)
    normed = layer_norm(residual, entry_gain, entry_shift)
    sent = (mask * normed).astype(jnp.bfloat16)
    by_channel = lax.all_to_all(sent, "cols", split_axis=3, concat_axis=2, tiled=True)
    zonal = jnp.einsum(
        "rhwc,wpk->rhkpc", by_channel, forward_zonal, preferred_element_type=jnp.float32
    )
    by_mode = lax.all_to_all(
        zonal.astype(jnp.bfloat16), "rows", split_axis=2, concat_axis=1, tiled=True
    )
    spectrum = jnp.einsum(
        "kphq,rhmqc->rkmpc", meridian_table, by_mode, preferred_element_type=jnp.float32
    ).astype(jnp.bfloat16)
    leading = spectrum.shape[:3]
    modes_flat = block_layout(spectrum, blocks, block_size)
    kernel_matrix = complex_matrix(
        lax.dynamic_slice_in_dim(spectral_kernel, first_block, blocks, 1)
    )
    mixer_matrix = complex_matrix(lax.dynamic_slice_in_dim(spectral_mixer, first_block, blocks, 1))
    kernel_bias = bias_rows(lax.dynamic_slice_in_dim(spectral_bias, first_block, blocks, 1))
    mixer_bias = bias_rows(lax.dynamic_slice_in_dim(spectral_offset, first_block, blocks, 1))
    first_pre = (
        jnp.einsum("nbx,bxy->nby", modes_flat, kernel_matrix, preferred_element_type=jnp.float32)
        + kernel_bias
    )
    first_act = gelu_exact(first_pre).astype(jnp.bfloat16)
    second_pre = (
        jnp.einsum("nbx,bxy->nby", first_act, mixer_matrix, preferred_element_type=jnp.float32)
        + mixer_bias
    )
    shrunk = spectral_layout(shrink(second_pre), leading, blocks, block_size)
    back_meridian = jnp.einsum(
        "kphq,rkmpc->rhmqc", meridian_wide, shrunk, precision=highest
    ).astype(jnp.bfloat16)
    by_row = lax.all_to_all(back_meridian, "rows", split_axis=1, concat_axis=2, tiled=True)
    filtered = jnp.einsum(
        "rhkpc,pkw->rhwc", by_row, inverse_zonal, preferred_element_type=jnp.float32
    ).astype(jnp.bfloat16)
    by_token = lax.all_to_all(filtered, "cols", split_axis=2, concat_axis=3, tiled=True)
    mixed = residual + mask * by_token.astype(jnp.float32) + normed
    features = mixed.shape[-1]
    second_norm = (
        layer_norm(mixed, exit_scale, exit_center).astype(jnp.bfloat16).reshape(-1, features)
    )
    hidden_pre = jnp.dot(second_norm, dense_expand, preferred_element_type=jnp.float32) + dense_lift
    hidden = gelu_exact(hidden_pre).astype(jnp.bfloat16)
    output = mixed + (
        jnp.dot(hidden, dense_project, preferred_element_type=jnp.float32) + dense_return
    ).reshape(mixed.shape)
    kept = (
        residual,
        modes_flat,
        first_pre,
        first_act,
        second_pre,
        mixed,
        second_norm,
        hidden_pre,
        hidden,
        kernel_matrix,
        mixer_matrix,
        leading,
    )
    return (output, kept)


def retreat(cotangent, mask, kept, weights, grids, layout):
    (
        entry_gain,
        entry_shift,
        spectral_kernel,
        spectral_bias,
        spectral_mixer,
        spectral_offset,
        exit_scale,
        exit_center,
        dense_expand,
        dense_lift,
        dense_project,
        dense_return,
    ) = weights
    forward_zonal, inverse_zonal, meridian_table, meridian_wide = grids
    blocks, block_size, first_block = layout
    (
        residual,
        modes_flat,
        first_pre,
        first_act,
        second_pre,
        mixed,
        second_norm,
        hidden_pre,
        hidden,
        kernel_matrix,
        mixer_matrix,
        leading,
    ) = kept
    features = mixed.shape[-1]
    upstream = cotangent.reshape(-1, features)
    gradient_project = jnp.einsum("tf,tc->fc", hidden, upstream, preferred_element_type=jnp.float32)
    gradient_return = jnp.sum(upstream.astype(jnp.float32), 0)
    outer = (gradient_project, gradient_return)
    hidden_back = jnp.einsum(
        "tc,fc->tf", upstream, dense_project, preferred_element_type=jnp.float32
    )
    hidden_pull = jax.vjp(gelu_exact, hidden_pre)[1]
    pre_back = hidden_pull(hidden_back)[0].astype(jnp.bfloat16)
    gradient_expand = jnp.einsum(
        "tc,tf->cf", second_norm, pre_back, preferred_element_type=jnp.float32
    )
    gradient_lift = jnp.sum(pre_back.astype(jnp.float32), 0)
    norm_back = jnp.einsum(
        "tf,cf->tc", pre_back, dense_expand, preferred_element_type=jnp.float32
    ).reshape(mixed.shape)
    exit_pull = jax.vjp(layer_norm, mixed, exit_scale, exit_center)[1]
    mixed_part, gradient_scale, gradient_center = exit_pull(norm_back)
    inner = (gradient_expand, gradient_lift, gradient_scale, gradient_center)
    mixed_back = cotangent.astype(jnp.float32) + mixed_part
    filter_back = (mask * mixed_back).astype(jnp.bfloat16)
    channel_back = lax.all_to_all(filter_back, "cols", split_axis=3, concat_axis=2, tiled=True)
    zonal_back = jnp.einsum(
        "rhwc,pkw->rhkpc", channel_back, inverse_zonal, preferred_element_type=jnp.float32
    ).astype(jnp.bfloat16)
    meridian_back = lax.all_to_all(zonal_back, "rows", split_axis=2, concat_axis=1, tiled=True)
    shrunk_back = jnp.einsum(
        "kphq,rhmqc->rkmpc", meridian_table, meridian_back, preferred_element_type=jnp.float32
    )
    shrink_pull = jax.vjp(shrink, second_pre)[1]
    second_back = shrink_pull(block_layout(shrunk_back, blocks, block_size))[0].astype(jnp.bfloat16)
    mixer_whole = jnp.einsum(
        "nbx,nby->bxy", first_act, second_back, preferred_element_type=jnp.float32
    )
    offset_rows = jnp.sum(second_back.astype(jnp.float32), 0)
    activation_back = jnp.einsum(
        "nby,bxy->nbx", second_back, mixer_matrix, preferred_element_type=jnp.float32
    )
    first_pull = jax.vjp(gelu_exact, first_pre)[1]
    first_back = first_pull(activation_back)[0].astype(jnp.bfloat16)
    kernel_whole = jnp.einsum(
        "nbx,nby->bxy", modes_flat, first_back, preferred_element_type=jnp.float32
    )
    kernel_rows = jnp.sum(first_back.astype(jnp.float32), 0)
    spectrum_back = spectral_layout(
        jnp.einsum("nby,bxy->nbx", first_back, kernel_matrix, preferred_element_type=jnp.float32),
        leading,
        blocks,
        block_size,
    )
    modes_back = jnp.einsum(
        "kphq,rkmpc->rhmqc", meridian_wide, spectrum_back, precision=highest
    ).astype(jnp.bfloat16)
    row_back = lax.all_to_all(modes_back, "rows", split_axis=1, concat_axis=2, tiled=True)
    sent_back = jnp.einsum(
        "rhkpc,wpk->rhwc", row_back, forward_zonal, preferred_element_type=jnp.float32
    ).astype(jnp.bfloat16)
    token_back = lax.all_to_all(sent_back, "cols", split_axis=2, concat_axis=3, tiled=True)
    normed_back = mixed_back + mask * token_back.astype(jnp.float32)
    entry_pull = jax.vjp(layer_norm, residual, entry_gain, entry_shift)[1]
    residual_part, gradient_gain, gradient_shift = entry_pull(normed_back)
    gradient_tokens = mixed_back + residual_part
    shared = (
        gradient_gain,
        gradient_shift,
        inner[2],
        inner[3],
        inner[0],
        inner[1],
        outer[0],
        outer[1],
    )
    local_blocks = (
        matrix_gradient(kernel_whole, block_size),
        bias_gradient(kernel_rows, block_size),
        matrix_gradient(mixer_whole, block_size),
        bias_gradient(offset_rows, block_size),
    )
    return (gradient_tokens, shared, local_blocks)


def shards_general(
    tokens,
    region_sizes,
    region_starts,
    entry_gain,
    entry_shift,
    spectral_kernel,
    spectral_bias,
    spectral_mixer,
    spectral_offset,
    exit_scale,
    exit_center,
    dense_expand,
    dense_lift,
    dense_project,
    dense_return,
    cotangent,
):
    rows_here = tokens.shape[1]
    cols_here = tokens.shape[2]
    height = rows_here * lax.axis_size("rows")
    width = cols_here * lax.axis_size("cols")
    grids = tables(height, width, width // 2)
    latitude = lax.axis_index("rows") * rows_here + jnp.arange(rows_here, dtype=jnp.int32)
    longitude = lax.axis_index("cols") * cols_here + jnp.arange(cols_here, dtype=jnp.int32)
    inside_rows = latitude[None, :, None] < region_sizes[:, 0][:, None, None]
    offset = (longitude[None, None, :] - region_starts[:, None, None]) % width
    inside_cols = offset < region_sizes[:, 1][:, None, None]
    mask = jnp.where(inside_rows & inside_cols, 1.0, 0.0).astype(jnp.float32)[..., None]
    block_size = spectral_kernel.shape[2]
    total_blocks = spectral_kernel.shape[1]
    blocks = tokens.shape[3] // lax.axis_size("cols") // block_size
    first_block = lax.axis_index("cols") * blocks
    layout = (blocks, block_size, first_block)
    weights = (
        entry_gain,
        entry_shift,
        spectral_kernel,
        spectral_bias,
        spectral_mixer,
        spectral_offset,
        exit_scale,
        exit_center,
        dense_expand,
        dense_lift,
        dense_project,
        dense_return,
    )
    output, kept = advance(tokens, mask, weights, grids, layout)
    gradient_tokens, shared, local_blocks = retreat(cotangent, mask, kept, weights, grids, layout)
    (
        gain_part,
        shift_part,
        scale_part,
        center_part,
        expand_part,
        lift_part,
        project_part,
        return_part,
    ) = shared
    everywhere = ("rows", "cols")
    project_sum = lax.psum(project_part.astype(jnp.bfloat16), everywhere).astype(jnp.float32)
    expand_sum = lax.psum(expand_part.astype(jnp.bfloat16), everywhere).astype(jnp.float32)
    vectors = (gain_part, shift_part, scale_part, center_part, lift_part, return_part)
    sums = lax.psum(jnp.concatenate(vectors), everywhere)
    ends = [0]
    for vector in vectors:
        ends.append(ends[-1] + vector.shape[0])
    parts = [sums[low:high] for low, high in zip(ends[:-1], ends[1:])]
    summed = (*parts[:4], expand_sum, parts[4], project_sum, parts[5])
    kernel_local, bias_local, mixer_local, offset_local = local_blocks
    kernel_full = lax.dynamic_update_slice_in_dim(
        jnp.zeros((2, total_blocks, block_size, block_size), jnp.float32),
        kernel_local,
        first_block,
        1,
    )
    bias_full = lax.dynamic_update_slice_in_dim(
        jnp.zeros((2, total_blocks, block_size), jnp.float32), bias_local, first_block, 1
    )
    mixer_full = lax.dynamic_update_slice_in_dim(
        jnp.zeros((2, total_blocks, block_size, block_size), jnp.float32),
        mixer_local,
        first_block,
        1,
    )
    offset_full = lax.dynamic_update_slice_in_dim(
        jnp.zeros((2, total_blocks, block_size), jnp.float32), offset_local, first_block, 1
    )
    block_totals = lax.psum((kernel_full, bias_full, mixer_full, offset_full), ("rows", "cols"))
    return (
        output.astype(jnp.bfloat16),
        gradient_tokens,
        summed[0],
        summed[1],
        block_totals[0],
        block_totals[1],
        block_totals[2],
        block_totals[3],
        summed[2],
        summed[3],
        summed[4],
        summed[5],
        summed[6],
        summed[7],
    )


MESH = pl.DeviceIdType.MESH
wide = jnp.float32
low = jnp.bfloat16
by_last = (((1,), (1,)), ((), ()))
by_first = (((0,), (0,)), ((), ()))
vmem = pl.BlockSpec(memory_space=pltpu.VMEM)


def dot(a, b):
    return jnp.dot(a, b, preferred_element_type=wide)


def dot_last(a, b):
    return lax.dot_general(a, b, by_last, preferred_element_type=wide)


def dot_first(a, b):
    return lax.dot_general(a, b, by_first, preferred_element_type=wide)


def task_tables(height, width, rows_here, cols_here):
    modes = width // 2
    near = modes // 2
    column = np.arange(width)
    frequency = np.arange(modes)
    angle = (column[:, None] * frequency[None, :] % width).astype(np.float32) * np.float32(
        2.0 * math.pi / width
    )
    scale = np.float32(1.0 / math.sqrt(width))
    zonal = np.stack([np.cos(angle), -np.sin(angle)], 1) * scale
    factor = np.where(frequency == 0, 1.0, 2.0).astype(np.float32)
    inverse = (
        np.stack([np.cos(angle).T * factor[:, None], -np.sin(angle).T * factor[:, None]], 0) * scale
    )
    latitude = np.arange(height)
    turn = (latitude[:, None] * latitude[None, :] % height).astype(np.float32) * np.float32(
        2.0 * math.pi / height
    )
    cosine = np.cos(turn) / np.float32(math.sqrt(height))
    sine = np.sin(turn) / np.float32(math.sqrt(height))
    meridian = np.stack([np.stack([cosine, sine], -1), np.stack([-sine, cosine], -1)], 1)
    halves = width // cols_here
    split_f = zonal.reshape(halves, cols_here, 2, 2, near)
    to_modes = np.zeros((halves, 2, cols_here, 2, 2, 2, near), np.float32)
    split_g = inverse.reshape(2, 2, near, halves, cols_here)
    to_columns = np.zeros((2, 2, 2, near, halves, 2, cols_here), np.float32)
    for i in range(2):
        to_modes[:, i, :, :, i] = split_f.transpose(0, 1, 3, 2, 4)
        to_columns[:, i, :, :, :, i] = split_g.transpose(1, 0, 2, 3, 4)
    side = halves * 2 * cols_here
    to_modes = to_modes.reshape(side, side)
    to_columns = to_columns.reshape(side, side)
    pairs = rows_here // 2
    senders = height // rows_here
    order = np.zeros((height // 2, 2), np.int64)
    for core in range(2):
        for chip in range(senders // 2):
            for pair in range(pairs):
                for i in range(2):
                    order[(core * (senders // 2) + chip) * pairs + pair, i] = (
                        (chip * 2 + core) * rows_here + pair * 2 + i
                    )
    placed = meridian[:, :, order]
    ahead = np.zeros((2, 2, 2, height // 2, 2, 2, height), np.float32)
    for c in range(2):
        ahead[:, :, c, :, c] = placed.transpose(3, 4, 2, 1, 0)
    ahead = ahead.reshape(2, 2 * height, 4 * height)
    behind = ahead.reshape(4 * height, 4 * height).T
    return tuple(
        np.asarray(item, ml_dtypes.bfloat16)
        for item in (to_modes, to_columns, ahead, behind, np.eye(256, dtype=np.float32))
    )


def chip_device(chip, core, cols):
    return ((chip // cols) * 2 + core, chip % cols)


def swap_bits(value, mask, bits):
    out = 0
    for k in range(bits):
        bit = (value // (1 << k)) % 2
        if (mask >> k) & 1:
            bit = 1 - bit
        out = out + bit * (1 << k)
    return out


def cross(value, mask, bits):
    out = 0
    for k in range(bits):
        out = out + (value // (1 << k) + mask // (1 << k)) % 2 * (1 << k)
    return out


def greet(chips, cols):
    row = lax.axis_index("rows")
    core = row % 2
    me = (row // 2) * cols + lax.axis_index("cols")
    barrier = pltpu.get_barrier_semaphore()
    for step in range(1, chips):
        other = (me + step) % chips
        pl.semaphore_signal(
            barrier, inc=1, device_id=chip_device(other, core, cols), device_id_type=MESH
        )
    pl.semaphore_signal(
        barrier, inc=1, device_id=chip_device(me, 1 - core, cols), device_id_type=MESH
    )
    pl.semaphore_wait(barrier, chips)
    return me, core


def send_piece(src, dst, send_sem, recv_sem, target, me, core, cols):
    @pl.when(target == me)
    def _():
        pltpu.make_async_copy(src, dst, recv_sem).start()

    @pl.when(target != me)
    def _():
        pltpu.make_async_remote_copy(
            src_ref=src,
            dst_ref=dst,
            send_sem=send_sem,
            recv_sem=recv_sem,
            device_id=chip_device(target, core, cols),
            device_id_type=MESH,
        ).start()


def await_piece(ref, sem):
    pltpu.make_async_copy(ref, ref, sem).wait()


def to_feature_rows(out_ref, region, place, piece, eye):
    features = piece.shape[1]
    for low_end in range(0, features, 256):
        turned = dot_last(eye, piece[:, low_end : low_end + 256])
        out_ref[region, low_end : low_end + 256, place] = turned.astype(low)


def modes_first(block, group, half):
    columns = []
    for m in range(group):
        rows = block[m * half : (m + 1) * half]
        height = block.shape[1] // 4
        columns.append(
            jnp.concatenate(
                [
                    rows[:, (c * 2 + p) * height : (c * 2 + p + 1) * height]
                    for p in range(2)
                    for c in range(2)
                ],
                0,
            )
        )
    return jnp.concatenate(columns, 1)


def modes_last(block, group, half):
    height = block.shape[1] // group
    rows = []
    for m in range(group):
        part = block[:, m * height : (m + 1) * height]
        rows.append(
            jnp.concatenate(
                [
                    part[(p * 2 + c) * half : (p * 2 + c + 1) * half]
                    for c in range(2)
                    for p in range(2)
                ],
                1,
            )
        )
    return jnp.concatenate(rows, 0)


def filter_pass(sizes, me, core, produce, middle, consume, tables, work, sems, tick):
    regions, blocks, block_size, chips, cols, tokens = sizes
    table_in, table_out, ahead, behind = tables
    sent, got, zonal, zonal_got, tall, flat, back, sibling, leaving, coming = work
    send_a, recv_a, send_b, recv_b, send_c, recv_c, send_d, recv_d = sems
    lanes = 128
    senders = chips // cols
    pairs = tokens // lanes
    half = block_size // 2
    points = senders * pairs
    group = 4
    bits = (blocks - 1).bit_length()
    home = me // blocks
    tick("start")
    for turn in range(regions):
        region = (home + 1 + turn) % regions
        produce(region)
        for step in range(blocks - 1, -1, -1):
            target = region * blocks + swap_bits(me % blocks, step, bits)
            src = sent.at[region, pl.ds(pl.multiple_of(target % blocks * block_size, 32), block_size)]
            place = turn * blocks + step
            send_piece(src, got.at[me], send_a.at[place], recv_a.at[me], target, me, core, cols)
    tick("sent")

    middle_point = points // 2

    def swap_half(k, first):
        place = pl.ds(pl.multiple_of(first, middle_point), middle_point)
        return pltpu.make_async_remote_copy(
            src_ref=zonal.at[1 - core, place],
            dst_ref=zonal_got.at[place],
            send_sem=send_b.at[k],
            recv_sem=recv_b.at[k],
            device_id=chip_device(me, 1 - core, cols),
            device_id_type=MESH,
        )

    swaps = [
        swap_half(0, home * middle_point),
        swap_half(1, (1 - home) * middle_point),
    ]

    def zonal_step(index, carry):
        tick("arrival", index)
        chip = cross(me // cols, index, senders.bit_length() - 1)
        for col in range(cols):
            await_piece(got.at[chip * cols + col], recv_a.at[chip * cols + col])
        for pair in range(pairs):
            x = jnp.concatenate(
                [got[chip * cols + col, :, pair * lanes : (pair + 1) * lanes] for col in range(cols)], 1
            )
            y = dot(x, table_in[...]).astype(low)
            for part in range(2):
                zonal[part, chip * pairs + pair] = y[:, part * lanes : (part + 1) * lanes]

        @pl.when(index == senders // 2 - 1)
        def _():
            swaps[0].start()

        return carry

    lax.fori_loop(0, senders, zonal_step, 0)
    swaps[1].start()
    tick("zonal")

    def widen(source, first):
        def step(point, carry):
            row = pl.multiple_of((first + point) * block_size, 32)
            tall[pl.ds(row, block_size), :] = source(point).astype(wide)
            return carry

        lax.fori_loop(0, points, step, 0)

    widen(lambda point: zonal[core, point], core * points)
    for swap in swaps:
        swap.wait()
    widen(lambda point: zonal_got[point], (1 - core) * points)
    modes = lanes // 4

    def turn_step(c, carry):
        x = jnp.concatenate(
            [tall[pl.ds(c + half * side, 2 * points, stride=block_size), :] for side in range(2)], 0
        )
        y = jnp.transpose(x)
        for i in range(4):
            flat[i, pl.ds(c, modes, stride=half), :] = y[i * modes : (i + 1) * modes]
        return carry

    lax.fori_loop(0, half, turn_step, 0, unroll=4)
    tick("turned")

    def mode_step(step, carry):
        rows = pl.ds(pl.multiple_of(step * group * half, 64), group * half)
        spectrum = 0.0
        for i in range(2):
            x = jnp.concatenate([flat[i * 2, rows, :], flat[i * 2 + 1, rows, :]], 1).astype(low)
            spectrum = spectrum + dot(x, ahead[i])
        out = modes_last(middle(step, modes_first(spectrum, group, half)), group, half)
        high = out.astype(low)
        rest = (out - high.astype(wide)).astype(low)
        y = (dot(high, behind[...]) + dot(rest, behind[...])).astype(low).astype(wide)
        for i in range(4):
            flat[i, rows, :] = y[:, i * lanes : (i + 1) * lanes]
        tick("mode", step)
        return carry

    lax.fori_loop(0, modes // group, mode_step, 0)
    tick("modes")

    def return_step(c, carry):
        x = jnp.concatenate([flat[i, pl.ds(c, modes, stride=half), :] for i in range(4)], 0)
        y = jnp.transpose(x)
        for side in range(2):
            tall[pl.ds(c + half * side, 2 * points, stride=block_size), :] = y[
                side * 2 * points : (side + 1) * 2 * points
            ]
        return carry

    lax.fori_loop(0, half, return_step, 0, unroll=4)
    tick("returned")

    def narrow(store, first):
        def step(point, carry):
            row = pl.multiple_of((first + point) * block_size, 32)
            store(point, tall[pl.ds(row, block_size), :].astype(low))
            return carry

        lax.fori_loop(0, points, step, 0)

    def to_sibling(point, value):
        back[point] = value

    def to_self(point, value):
        sibling[core, point] = value

    narrow(to_sibling, (1 - core) * points)
    swap_back = pltpu.make_async_remote_copy(
        src_ref=back,
        dst_ref=sibling.at[core],
        send_sem=send_c,
        recv_sem=recv_c,
        device_id=chip_device(me, 1 - core, cols),
        device_id_type=MESH,
    )
    swap_back.start()
    tick("back")
    narrow(to_self, core * points)
    swap_back.wait_send()
    await_piece(sibling.at[1 - core], recv_c)

    def column_step(index, carry):
        chip = cross(me // cols, senders - 1 - index, senders.bit_length() - 1)
        for pair in range(pairs):
            point = chip * pairs + pair
            x = jnp.concatenate([sibling[0, point], sibling[1, point]], 1)
            y = dot(x, table_out[...]).astype(low)
            for col in range(cols):
                leaving[chip * cols + col, :, pair * lanes : (pair + 1) * lanes] = y[
                    :, col * lanes : (col + 1) * lanes
                ]
        for turn in range(cols):
            target = chip * cols + (me + turn + 1) % cols
            dst = coming.at[
                me // blocks, pl.ds(pl.multiple_of(me % blocks * block_size, 32), block_size)
            ]
            send_piece(
                leaving.at[target], dst, send_d.at[target], recv_d.at[me], target, me, core, cols
            )
        return carry

    lax.fori_loop(0, senders, column_step, 0)
    tick("columns")
    for turn in range(regions):
        region = (home + turn) % regions

        def arrive(block, carry, region=region):
            ref = coming.at[region, pl.ds(pl.multiple_of(block * block_size, 32), block_size)]
            await_piece(ref, recv_d.at[region * blocks + block])
            return carry

        lax.fori_loop(0, blocks, arrive, 0)
        consume(region)
        tick("region")

    for place in range(regions * blocks):
        turn, step = place // blocks, place % blocks
        target = (home + 1 + turn) % regions * blocks + swap_bits(me % blocks, step, bits)

        @pl.when(target != me)
        def _():
            await_piece(got.at[0], send_a.at[place])

        @pl.when(place != me)
        def _():
            await_piece(leaving.at[0], send_d.at[place])


def work_shapes(sizes):
    regions, blocks, block_size, chips, cols, tokens = sizes
    lanes = 128
    features = blocks * block_size
    points = (chips // cols) * (tokens // lanes)
    rows = (lanes // 4) * (block_size // 2)
    return [
        pltpu.VMEM((regions, features, tokens), low),
        pltpu.VMEM((chips, block_size, tokens), low),
        pltpu.VMEM((2, points, block_size, lanes), low),
        pltpu.VMEM((points, block_size, lanes), low),
        pltpu.VMEM((2 * points * block_size, lanes), wide),
        pltpu.VMEM((4, rows, lanes), wide),
        pltpu.VMEM((points, block_size, lanes), low),
        pltpu.VMEM((2, points, block_size, lanes), low),
        pltpu.VMEM((chips, block_size, tokens), low),
        pltpu.VMEM((regions, features, tokens), low),
        pltpu.SemaphoreType.DMA((chips,)),
        pltpu.SemaphoreType.DMA((chips,)),
        pltpu.SemaphoreType.DMA((2,)),
        pltpu.SemaphoreType.DMA((2,)),
        pltpu.SemaphoreType.DMA,
        pltpu.SemaphoreType.DMA,
        pltpu.SemaphoreType.DMA((chips,)),
        pltpu.SemaphoreType.DMA((chips,)),
    ]


def normalise(value):
    centre = jnp.mean(value, -1, keepdims=True)
    centred = value - centre
    spread = jnp.mean(centred * centred, -1, keepdims=True)
    factor = lax.rsqrt(spread + norm_eps)
    return centred * factor, factor


def gelu_parts(value):
    curve = 0.5 * (1.0 + lax.erf(value * (1.0 / math.sqrt(2.0))))
    return curve


def gelu_bell(value):
    return jnp.exp(-0.5 * value * value) * (1.0 / math.sqrt(2.0 * math.pi))


def inside_region(sizes_ref, starts_ref, region, first, shape, width):
    rows, rows_here, cols_here = shape
    index = first + lax.broadcasted_iota(jnp.int32, (rows, 1), 0)
    bits = cols_here.bit_length() - 1
    latitude = lax.axis_index("rows") * rows_here + lax.shift_right_logical(index, bits)
    longitude = lax.axis_index("cols") * cols_here + (index & (cols_here - 1))
    offset = longitude - starts_ref[region]
    offset = jnp.where(offset < 0, offset + width, offset)
    near = jnp.where(latitude < sizes_ref[region, 0], 1.0, 0.0)
    return jnp.where(offset < sizes_ref[region, 1], near, 0.0)


def as_row(ref):
    return ref[...].reshape(1, ref.shape[0])


def field_rows(coming, region, place, eye):
    return jnp.concatenate(
        [
            dot_last(eye, coming[region, first : first + 256, place])
            for first in range(0, coming.shape[1], 256)
        ],
        1,
    )


def forward_kernel(sizes, *refs):
    (
        region_sizes,
        region_starts,
        tokens_ref,
        gain_ref,
        shift_ref,
        scale_ref,
        center_ref,
        weights_ref,
        biases_ref,
        to_modes,
        to_columns,
        ahead,
        behind,
        eye,
        up_hbm,
        project_hbm,
        mixed_hbm,
        second_hbm,
        *kept_hbm,
        hidden_back_hbm,
    ) = refs[:23]
    work, sems = refs[23:33], refs[33:41]
    (
        mixed,
        second,
        mixed_sems,
        second_sems,
        kept_sems,
        up_ref,
        project_ref,
        hidden_back,
        load_sems,
        back_sems,
        *kept,
    ) = refs[41:]
    loads = [
        pltpu.make_async_copy(up_hbm, up_ref, load_sems.at[0]),
        pltpu.make_async_copy(project_hbm, project_ref, load_sems.at[1]),
    ]
    for copy in loads:
        copy.start()
    regions, blocks, block_size, chips, cols, tokens = sizes
    me, core = greet(chips, cols)
    sent, coming = work[0], work[-1]
    piece = 128
    steps = kept_hbm[0].shape[0]
    cols_here = 128 // cols
    gain, shift, scale, center = (
        as_row(ref) for ref in (gain_ref, shift_ref, scale_ref, center_ref)
    )

    def inside(region, first, rows):
        shape = (rows, tokens // cols_here, cols_here)
        return inside_region(region_sizes, region_starts, region, first, shape, 128)

    def produce(region):
        def step(part, carry):
            rows = pl.ds(pl.multiple_of(region * tokens + part * piece, piece), piece)
            unit, factor = normalise(tokens_ref[rows, :].astype(wide))
            values = (inside(region, part * piece, piece) * (unit * gain + shift)).astype(low)
            place = pl.ds(pl.multiple_of(part * piece, piece), piece)
            to_feature_rows(sent, region, place, values, eye[...])
            return carry

        lax.fori_loop(0, tokens // piece, step, 0)

    def keep(step):
        slot = step % 2
        return [
            pltpu.make_async_copy(ref.at[slot], hbm.at[step], kept_sems.at[k, slot])
            for k, (ref, hbm) in enumerate(zip(kept, kept_hbm))
        ]

    def middle(step, spectrum):
        slot = step % 2

        @pl.when(step >= 2)
        def _():
            for copy in keep(step - 2):
                copy.wait()

        spectrum_kept, first_kept, act_kept, second_kept = kept
        spectrum = spectrum.astype(low)
        spectrum_kept[slot] = spectrum
        first = dot_first(weights_ref[0], spectrum) + biases_ref[:, 0:1]
        curve = gelu_parts(first)
        first_kept[slot] = curve + first * gelu_bell(first)
        act = (first * curve).astype(low)
        act_kept[slot] = act
        second_pre = dot_first(weights_ref[1], act) + biases_ref[:, 1:2]
        level = jnp.tanh(second_pre / shrink_width)
        second_kept[slot] = level * level
        for copy in keep(step):
            copy.start()
        return second_pre - shrink_width * level

    def leave(region):
        rows = pl.ds(pl.multiple_of(region * tokens, tokens), tokens)
        return [
            pltpu.make_async_copy(mixed.at[rows], mixed_hbm.at[rows], mixed_sems.at[region]),
            pltpu.make_async_copy(second.at[rows], second_hbm.at[rows], second_sems.at[region]),
        ]

    def consume(region):
        def step(part, carry):
            rows = pl.ds(pl.multiple_of(region * tokens + part * 256, 256), 256)
            place = pl.ds(pl.multiple_of(part * 256, 256), 256)
            fields = field_rows(coming, region, place, eye[...])
            residual = tokens_ref[rows, :].astype(wide)
            unit, factor = normalise(residual)
            value = residual + inside(region, part * 256, 256) * fields + (unit * gain + shift)
            mixed[rows, :] = value
            unit, factor = normalise(value)
            second[rows, :] = (unit * scale + center).astype(low)
            return carry

        lax.fori_loop(0, tokens // 256, step, 0)
        for copy in leave(region):
            copy.start()

    tiles, count, tile = hidden_back.shape

    def leave_back(k):
        return pltpu.make_async_copy(hidden_back.at[k], hidden_back_hbm.at[k], back_sems.at[k])

    def tick(place, step=0):
        if place == "sent":
            for copy in loads:
                copy.wait()

            def tile_step(k, carry):
                here = pl.ds(pl.multiple_of(k * tile, tile), tile)
                for first in range(0, count, 256):
                    rows = slice(first, first + 256)
                    hidden_back[k, rows, :] = dot_last(up_ref[rows, :], project_ref[here, :]).astype(low)
                leave_back(k).start()
                return carry

            lax.fori_loop(0, tiles, tile_step, 0)

    tables = (to_modes, to_columns, ahead, behind)
    filter_pass(sizes, me, core, produce, middle, consume, tables, work, sems, tick)
    for k in range(tiles):
        leave_back(k).wait()
    for step in (steps - 2, steps - 1):
        for copy in keep(step):
            copy.wait()
    for region in range(regions):
        for copy in leave(region):
            copy.wait()


def place_of(row, col):
    return {"core": row % 2, "x": (row // 2) % 2, "z": row // 4, "y": col}


def device_at(spot):
    return (spot["z"] * 4 + spot["x"] * 2 + spot["core"], spot["y"])


def across(spot, axis, step=1):
    size = 4 if axis == "z" else 2
    return device_at({**spot, axis: (spot[axis] + step) % size})


def remote(src, dst, send_sem, recv_sem, device):
    return pltpu.make_async_remote_copy(
        src_ref=src,
        dst_ref=dst,
        send_sem=send_sem,
        recv_sem=recv_sem,
        device_id=device,
        device_id_type=MESH,
    )


def add_rows(out_ref, out_row, terms, rows):
    step = [size for size in (96, 64, 48, 32) if rows % size == 0][0]

    def add(part, carry):
        total = 0.0
        for ref, row in terms:
            here = pl.ds(pl.multiple_of(row + part * step, 16), step)
            total = total + ref[here, :].astype(wide)
        there = pl.ds(pl.multiple_of(out_row + part * step, 16), step)
        out_ref[there, :] = total.astype(low)
        return carry

    lax.fori_loop(0, rows // step, add, 0)


def row_part(ref, row, rows):
    return ref.at[pl.ds(pl.multiple_of(row, 16), rows)]


def facing(spot, axis):
    if axis == "near":
        z = spot["z"] // 2 * 2 + 1 - spot["z"] % 2
        return spot["z"] % 2, device_at({**spot, "z": z})
    if axis == "far":
        return spot["z"] // 2, across(spot, "z", 2)
    return spot[axis], across(spot, axis)


def reduce_steps(spot, axes, buffers, sends, recvs):
    steps = []
    for k, axis in enumerate(axes):
        bit, device = facing(spot, axis)
        source, target = buffers[k], buffers[k + 1]
        rows = target.shape[0]
        hop = remote(
            row_part(source, (1 - bit) * rows, rows), target, sends.at[k], recvs.at[k], device
        )

        def finish(hop=hop, source=source, target=target, rows=rows, bit=bit):
            hop.wait()
            add_rows(target, 0, ((target, 0), (source, bit * rows)), rows)

        steps.append((hop.start, finish))
    return steps


def share_steps(spot, axes, piece, total, sends, recvs, own_sem):
    offsets, rows, bits, devices = [0], [total.shape[0]], [], []
    for axis in axes:
        bit, device = facing(spot, axis)
        bits.append(bit)
        devices.append(device)
        rows.append(rows[-1] // 2)
        offsets.append(offsets[-1] + bit * rows[-1])
    last = len(axes) - 1
    hops = []
    for k in range(last, -1, -1):
        place = row_part(total, offsets[k + 1], rows[k + 1])
        source = piece if k == last else place
        hops.append(remote(source, place, sends.at[k], recvs.at[k], devices[k]))
    keep = pltpu.make_async_copy(piece, row_part(total, offsets[-1], rows[-1]), own_sem)
    ready = (
        (offsets[2], rows[2]),
        (offsets[1] + (1 - bits[1]) * rows[2], rows[2]),
        ((1 - bits[0]) * rows[1], rows[1]),
    )
    cores = []
    for k, (offset, size) in enumerate(ready):
        place = row_part(total, offset, size)
        cores.append(
            remote(place, place, sends.at[4 + k], recvs.at[4 + k], across(spot, "core"))
        )

    def begin():
        keep.start()
        hops[0].start()

    def second():
        keep.wait()
        hops[0].wait()
        hops[1].start()

    def third():
        hops[1].wait()
        hops[2].start()
        cores[0].start()

    def fourth():
        hops[2].wait()
        hops[3].start()
        cores[1].start()

    def fifth():
        hops[3].wait()
        cores[2].start()

    def finish():
        for core in cores:
            core.wait()

    return begin, second, third, fourth, fifth, finish


def backward_kernel(sizes, *refs):
    (
        region_sizes,
        region_starts,
        tokens_hbm,
        mixed_back_ref,
        gain_ref,
        weights_ref,
        to_modes,
        to_columns,
        ahead,
        behind,
        eye,
        spectrum_hbm,
        first_hbm,
        act_hbm,
        pre_hbm,
        project_hbm,
        expand_hbm,
        project_piece,
        expand_piece,
        project_ready,
        expand_ready,
        sums_ref,
        slope_hbm,
        project_total,
        expand_total,
        gathered,
        gathered_bias,
        vector_sum,
    ) = refs[:28]
    work, sems = refs[28:38], refs[38:46]
    (
        tokens_ref,
        slope,
        slope_sems,
        project_own,
        expand_own,
        load_sems,
        kernel_slope,
        bias_slope,
        mixer_slope,
        offset_slope,
        spectrum_slots,
        first_slots,
        act_slots,
        pre_slots,
        slot_sems,
        project_halves,
        expand_halves,
        project_quarters,
        expand_quarters,
        project_eighths,
        expand_eighths,
        project_pieces,
        expand_pieces,
        reduce_sends,
        reduce_recvs,
        share_sends,
        share_recvs,
        own_sems,
        slab,
        slab_bias,
        slab_got,
        slab_bias_got,
        slab_region,
        slab_bias_region,
        slab_sends,
        slab_recvs,
        vector_sent,
        vector_got,
        vector_sends,
        vector_recvs,
        late,
        late_got,
        late_all,
        late_sends,
        late_recvs,
    ) = refs[46:]
    regions, blocks, block_size, chips, cols, tokens = sizes
    steps = spectrum_hbm.shape[0]
    slots = (spectrum_slots, first_slots, act_slots, pre_slots)
    streams = (spectrum_hbm, first_hbm, act_hbm, pre_hbm)

    def fetch(step, slot):
        return [
            pltpu.make_async_copy(hbm.at[step], ref.at[slot], slot_sems.at[k, slot])
            for k, (hbm, ref) in enumerate(zip(streams, slots))
        ]

    own = (project_own, expand_own)
    load_own = [
        pltpu.make_async_copy(hbm, own[k], load_sems.at[1 + k])
        for k, hbm in enumerate((project_hbm, expand_hbm))
    ]
    load_tokens = pltpu.make_async_copy(tokens_hbm, tokens_ref, load_sems.at[0])
    for copy in load_own:
        copy.start()
    for copy in fetch(0, 0):
        copy.start()
    load_tokens.start()
    me, core = greet(chips, cols)
    spot = place_of(lax.axis_index("rows"), lax.axis_index("cols"))
    block = me % blocks
    sent, coming = work[0], work[-1]
    piece = 128
    cols_here = 128 // cols
    late[...] = jnp.zeros_like(late)
    vector_sum[...] = sums_ref[...]
    for ref in (kernel_slope, bias_slope, mixer_slope, offset_slope):
        ref[...] = jnp.zeros_like(ref)
    reducing, sharing = [], []
    pairs = 3
    tile = project_own.shape[0]
    own_pieces = (
        (project_piece, expand_piece),
        (project_pieces.at[0], expand_pieces.at[0]),
        (project_pieces.at[1], expand_pieces.at[1]),
    )
    chains = (
        ((project_piece,), (expand_piece,)),
        (
            (project_ready, project_eighths.at[0], own_pieces[1][0]),
            (expand_ready, expand_eighths.at[0], own_pieces[1][1]),
        ),
        (
            (
                project_own,
                project_halves,
                project_quarters,
                project_eighths.at[1],
                own_pieces[2][0],
            ),
            (expand_own, expand_halves, expand_quarters, expand_eighths.at[1], own_pieces[2][1]),
        ),
    )
    for j in range(pairs):
        place = pl.multiple_of((core * pairs + j) * tile, tile)
        totals = (project_total.at[pl.ds(place, tile)], expand_total.at[:, pl.ds(place, tile)])
        for k in range(2):
            axes = (("x", "y"), ("y", "x"))[k] + ("near", "far")
            buffers = chains[j][k]
            reducing.append(
                reduce_steps(
                    spot,
                    axes[5 - len(buffers) :],
                    buffers,
                    reduce_sends.at[j, k],
                    reduce_recvs.at[j, k],
                )
            )
            sharing.append(
                share_steps(
                    spot,
                    axes,
                    own_pieces[j][k],
                    totals[k],
                    share_sends.at[j, k],
                    share_recvs.at[j, k],
                    own_sems.at[j, k],
                )
            )

    def reduce(j, step, finish):
        for steps_of in reducing[2 * j : 2 * j + 2]:
            steps_of[step][finish]()

    def share(j, step):
        for steps_of in sharing[2 * j : 2 * j + 2]:
            steps_of[step]()

    def inside(region, first, rows):
        shape = (rows, tokens // cols_here, cols_here)
        return inside_region(region_sizes, region_starts, region, first, shape, 128)

    def produce(region):
        def step(part, carry):
            rows = pl.ds(pl.multiple_of(region * tokens + part * piece, piece), piece)
            place = pl.ds(pl.multiple_of(part * piece, piece), piece)
            values = (inside(region, part * piece, piece) * mixed_back_ref[rows, :]).astype(low)
            to_feature_rows(sent, region, place, values, eye[...])
            return carry

        lax.fori_loop(0, tokens // piece, step, 0)

    def middle(step, shrunk_back):
        slot = step % 2
        for copy in fetch(step, slot):
            copy.wait()

        @pl.when(step + 1 < steps)
        def _():
            for copy in fetch(step + 1, 1 - slot):
                copy.start()

        second = (shrunk_back * pre_slots[slot]).astype(low)
        ones = jnp.ones((8, second.shape[1]), low)
        offset_slope[...] += dot_last(ones, second)
        mixer_slope[...] += dot_last(act_slots[slot], second)
        first = (dot(weights_ref[1], second) * first_slots[slot]).astype(low)
        bias_slope[...] += dot_last(ones, first)
        kernel_slope[...] += dot_last(spectrum_slots[slot], first)
        return dot(weights_ref[0], first)

    def leave(region):
        rows = pl.ds(pl.multiple_of(region * tokens, tokens), tokens)
        return pltpu.make_async_copy(slope.at[rows], slope_hbm.at[rows], slope_sems.at[region])

    def consume(region):
        def step(part, carry):
            rows = pl.ds(pl.multiple_of(region * tokens + part * 256, 256), 256)
            place = pl.ds(pl.multiple_of(part * 256, 256), 256)
            fields = field_rows(coming, region, place, eye[...])
            unit, factor = normalise(tokens_ref[rows, :].astype(wide))
            mixed_back = mixed_back_ref[rows, :]
            normed_back = mixed_back + inside(region, part * 256, 256) * fields
            gains = jnp.sum(normed_back * unit, 0, keepdims=True)
            shifts = jnp.sum(normed_back, 0, keepdims=True)
            for k in range(3):
                late[k : k + 1, :] += gains[:, k * 256 : (k + 1) * 256]
                late[3 + k : 4 + k, :] += shifts[:, k * 256 : (k + 1) * 256]
            pull = normed_back * as_row(gain_ref)
            pull = pull - jnp.mean(pull, -1, keepdims=True) - unit * jnp.mean(
                pull * unit, -1, keepdims=True
            )
            slope[rows, :] = mixed_back + factor * pull
            return carry

        lax.fori_loop(0, tokens // 256, step, 0)
        leave(region).start()

    def slab_hops(place, mine, theirs, device):
        return [
            remote(src, dst, slab_sends.at[k, place], slab_recvs.at[k, place], device)
            for k, (src, dst) in enumerate(zip(mine, theirs))
        ]

    slab_core = slab_hops(
        0, (slab, slab_bias), (slab_got, slab_bias_got), across(spot, "core")
    )
    slab_far = slab_hops(
        1,
        (slab_got.at[core], slab_bias_got.at[core]),
        (slab_region, slab_bias_region),
        chip_device((me + blocks) % chips, core, cols),
    )
    here = (gathered.at[core, :, block], gathered_bias.at[core, block])

    def slab_peer(step):
        other = me // blocks * blocks + (block + step) % blocks
        return slab_hops(1 + step, here, here, chip_device(other, core, cols))

    everything = (gathered.at[core], gathered_bias.at[core])
    slab_last = slab_hops(1 + blocks, everything, everything, across(spot, "core"))

    def slab_start():
        for k, (weight, bias) in enumerate(
            ((kernel_slope, bias_slope), (mixer_slope, offset_slope))
        ):
            whole = weight[...]
            upper, lower = whole[:block_size], whole[block_size:]
            slab[k, 0] = upper[:, :block_size] + lower[:, block_size:]
            slab[k, 1] = upper[:, block_size:] - lower[:, :block_size]
            slab_bias[k] = bias[...]
        for hop in slab_core:
            hop.start()

    def slab_regions():
        for hop in slab_core:
            hop.wait()
        slab_got[...] = slab_got[...] + slab[...]
        slab_bias_got[...] = slab_bias_got[...] + slab_bias[...]
        for hop in slab_far:
            hop.start()

    def slab_blocks():
        for hop in slab_far:
            hop.wait()
        gathered[core, :, block] = slab_region[...] + slab_got[core]
        gathered_bias[core, block] = slab_bias_region[...] + slab_bias_got[core]
        for step in range(1, blocks):
            for hop in slab_peer(step):
                hop.start()

    def slab_cores():
        for step in range(1, blocks):
            for hop in slab_peer(step):
                hop.wait()
        for hop in slab_last:
            hop.start()

    partners = (
        across(spot, "core"),
        across(spot, "x"),
        across(spot, "y"),
        device_at({**spot, "z": spot["z"] // 2 * 2 + 1 - spot["z"] % 2}),
        across(spot, "z", 2),
    )
    hops = [
        remote(
            vector_sent.at[k], vector_got.at[k], vector_sends.at[k], vector_recvs.at[k], device
        )
        for k, device in enumerate(partners)
    ]

    def vector_step(k):
        if k > 0:
            hops[k - 1].wait()
            vector_sum[...] = vector_sum[...] + vector_got[k - 1]
        if k < len(hops):
            vector_sent[k] = vector_sum[...]
            hops[k].start()

    regions_seen = []

    def tick(place, step=0):
        if place == "arrival":

            @pl.when(step == 4)
            def _():
                reduce(2, 0, 1)
                reduce(2, 1, 0)

        if place == "mode":

            @pl.when(step == 3)
            def _():
                share(0, 3)
                reduce(2, 2, 1)
                reduce(2, 3, 0)
                share(1, 1)

            @pl.when(step == 5)
            def _():
                reduce(2, 3, 1)

        if place == "start":
            for copy in load_own:
                copy.wait()
            reduce(2, 0, 0)
            reduce(1, 0, 0)
            vector_step(0)
        if place == "sent":
            reduce(1, 0, 1)
            share(0, 0)
            vector_step(1)
        if place == "zonal":
            share(0, 1)
            reduce(1, 1, 0)
            reduce(2, 1, 1)
            reduce(2, 2, 0)
            vector_step(2)
        if place == "turned":
            share(0, 2)
            reduce(1, 1, 1)
            share(1, 0)
            vector_step(3)
        if place == "modes":
            slab_start()
            share(1, 2)
            share(2, 0)
            vector_step(4)
        if place == "returned":
            share(0, 4)
            share(1, 3)
            share(2, 1)
            vector_step(5)
        if place == "back":
            slab_regions()
        if place == "columns":
            load_tokens.wait()
            slab_blocks()
            share(2, 2)
            share(1, 4)
            share(2, 3)
            slab_cores()
        if place == "region":
            regions_seen.append(place)
            if len(regions_seen) == 1:
                share(2, 4)

    tables = (to_columns, to_modes, ahead, behind)
    filter_pass(sizes, me, core, produce, middle, consume, tables, work, sems, tick)
    late_core = remote(late, late_got, late_sends.at[0], late_recvs.at[0], across(spot, "core"))
    late_core.start()
    late_core.wait()
    late[...] = late[...] + late_got[...]
    late_all[me] = late[...]

    def late_hop(step):
        other = chip_device((me + step) % chips, core, cols)
        return remote(late, late_all.at[me], late_sends.at[step], late_recvs.at[step], other)

    for step in range(1, chips):
        late_hop(step).start()
    for hop in slab_last:
        hop.wait()
    share(0, 5)
    share(1, 5)
    share(2, 5)
    for step in range(1, chips):
        late_hop(step).wait()
    total = late_all[0]
    for chip in range(1, chips):
        total = total + late_all[chip]
    for k in range(3):
        vector_sum[0:1, k * 256 : (k + 1) * 256] = total[k : k + 1, :]
        vector_sum[1:2, k * 256 : (k + 1) * 256] = total[3 + k : 4 + k, :]
    for region in range(regions):
        leave(region).wait()


def call_filter(body, sizes, outs, cid, operands, scalars, spaces, out_spaces, scratch):
    shapes = [jax.ShapeDtypeStruct(shape, kind) for shape, kind in outs]
    anywhere = pl.BlockSpec(memory_space=pl.ANY)
    scalar = pl.BlockSpec(memory_space=pltpu.SMEM)
    return pl.pallas_call(
        functools.partial(body, sizes),
        out_shape=shapes,
        in_specs=[scalar] * len(scalars)
        + [anywhere if place in spaces else vmem for place in range(len(operands))],
        out_specs=[anywhere if place in out_spaces else vmem for place in range(len(outs))],
        scratch_shapes=[*work_shapes(sizes), *scratch],
        compiler_params=pltpu.CompilerParams(
            collective_id=cid, has_side_effects=True, vmem_limit_bytes=60 * 1024 * 1024
        ),
    )(*scalars, *operands)


def forward_scratch(sizes, kept, hidden, tile):
    regions, blocks, block_size, chips, cols, tokens = sizes
    dma = pltpu.SemaphoreType.DMA
    features = blocks * block_size
    return (
        pltpu.VMEM((regions * tokens, features), wide),
        pltpu.VMEM((regions * tokens, features), low),
        dma((regions,)),
        dma((regions,)),
        dma((len(kept), 2)),
        pltpu.VMEM((regions * tokens, features), low),
        pltpu.VMEM((hidden, features), low),
        pltpu.VMEM((hidden // tile, regions * tokens, tile), low),
        dma((2,)),
        dma((hidden // tile,)),
        *(pltpu.VMEM((2, *shape[1:]), kind) for shape, kind in kept),
    )


def backward_scratch(sizes, kept, tile, pairs):
    regions, blocks, block_size, chips, cols, tokens = sizes
    features = blocks * block_size
    side = 2 * block_size
    dma = pltpu.SemaphoreType.DMA
    return (
        pltpu.VMEM((regions * tokens, features), low),
        pltpu.VMEM((regions * tokens, features), wide),
        dma((regions,)),
        pltpu.VMEM((tile, features), low),
        pltpu.VMEM((features, tile), low),
        dma((3,)),
        pltpu.VMEM((side, side), wide),
        pltpu.VMEM((8, side), wide),
        pltpu.VMEM((side, side), wide),
        pltpu.VMEM((8, side), wide),
        *(pltpu.VMEM((2, *shape[1:]), kind) for shape, kind in kept),
        dma((len(kept), 2)),
        pltpu.VMEM((tile // 2, features), low),
        pltpu.VMEM((features // 2, tile), low),
        pltpu.VMEM((tile // 4, features), low),
        pltpu.VMEM((features // 4, tile), low),
        pltpu.VMEM((2, tile // 8, features), low),
        pltpu.VMEM((2, features // 8, tile), low),
        pltpu.VMEM((2, tile // 16, features), low),
        pltpu.VMEM((2, features // 16, tile), low),
        dma((pairs, 2, 4)),
        dma((pairs, 2, 4)),
        dma((pairs, 2, 7)),
        dma((pairs, 2, 7)),
        dma((pairs, 2)),
        pltpu.VMEM((2, 2, block_size, block_size), wide),
        pltpu.VMEM((2, 8, side), wide),
        pltpu.VMEM((2, 2, block_size, block_size), wide),
        pltpu.VMEM((2, 8, side), wide),
        pltpu.VMEM((2, block_size, block_size), wide),
        pltpu.VMEM((8, side), wide),
        dma((2, 2 + blocks)),
        dma((2, 2 + blocks)),
        pltpu.VMEM((5, 16, features), wide),
        pltpu.VMEM((5, 16, features), wide),
        dma((5,)),
        dma((5,)),
        pltpu.VMEM((8, 256), wide),
        pltpu.VMEM((8, 256), wide),
        pltpu.VMEM((chips, 8, 256), wide),
        dma((chips,)),
        dma((chips,)),
    )


def finish_kernel(*refs):
    (
        project,
        expand,
        slope,
        output,
        gathered,
        gathered_bias,
        sums,
        output_out,
        slope_out,
        gain,
        shift,
        kernel,
        bias,
        mixer,
        offset,
        scale,
        center,
        expand_out,
        lift,
        project_out,
        returned,
        project_low,
        expand_low,
        project_wide,
        expand_wide,
        slope_held,
        output_held,
        load_sems,
        store_sems,
        pass_sems,
    ) = refs
    parts = load_sems.shape[1]
    whole = ((project, project_low, project_wide, project_out), (expand, expand_low, expand_wide, expand_out))

    def rows_of(ref, part):
        size = ref.shape[0] // parts
        return ref.at[pl.ds(part * size, size)]

    def load(k, part):
        source, narrow, broad, target = whole[k]
        return pltpu.make_async_copy(
            rows_of(source, part), rows_of(narrow, part), load_sems.at[k, part]
        )

    def store(k, part):
        source, narrow, broad, target = whole[k]
        return pltpu.make_async_copy(
            rows_of(broad, part), rows_of(target, part), store_sems.at[k, part]
        )

    for part in range(parts):
        for k in range(2):
            load(k, part).start()
    passes = [
        [
            pltpu.make_async_copy(source, held, pass_sems.at[0, k]),
            pltpu.make_async_copy(held, target, pass_sems.at[1, k]),
        ]
        for k, (source, held, target) in enumerate(
            ((slope, slope_held, slope_out), (output, output_held, output_out))
        )
    ]
    for copy in passes:
        copy[0].start()
    kernel[...] = gathered[0]
    mixer[...] = gathered[1]
    side = bias.shape[2]
    for b in range(bias.shape[1]):
        for i in range(2):
            bias[i, b : b + 1, :] = gathered_bias[0, b, 0:1, i * side : (i + 1) * side]
            offset[i, b : b + 1, :] = gathered_bias[1, b, 0:1, i * side : (i + 1) * side]
    for k, ref in enumerate((gain, shift, scale, center, returned)):
        ref[...] = sums[k : k + 1, :].reshape(ref.shape)
    tile = lift.shape[0] // 6
    for k in range(6):
        lift[k * tile : (k + 1) * tile] = sums[5 + k : 6 + k, :tile].reshape(tile)
    for copy in passes:
        copy[0].wait()
        copy[1].start()
    for part in range(parts):
        for k in range(2):
            load(k, part).wait()
            source, narrow, broad, target = whole[k]
            rows_of(broad, part)[...] = rows_of(narrow, part)[...].astype(wide)
            store(k, part).start()
    for part in range(parts):
        for k in range(2):
            store(k, part).wait()
    for copy in passes:
        copy[1].wait()


def call_finish(project, expand, slope, output, gathered, gathered_bias, sums):
    hidden, features = project.shape
    line = jax.ShapeDtypeStruct((features,), wide)
    weight = jax.ShapeDtypeStruct(gathered.shape[1:], wide)
    bias = jax.ShapeDtypeStruct(gathered.shape[1:4], wide)
    shapes = [
        jax.ShapeDtypeStruct(output.shape, low),
        jax.ShapeDtypeStruct(slope.shape, wide),
        line,
        line,
        weight,
        bias,
        weight,
        bias,
        line,
        line,
        jax.ShapeDtypeStruct(expand.shape, wide),
        jax.ShapeDtypeStruct((hidden,), wide),
        jax.ShapeDtypeStruct(project.shape, wide),
        line,
    ]
    anywhere = pl.BlockSpec(memory_space=pl.ANY)
    dma = pltpu.SemaphoreType.DMA
    parts = 8
    return pl.pallas_call(
        finish_kernel,
        out_shape=shapes,
        in_specs=[anywhere] * 4 + [vmem] * 3,
        out_specs=[anywhere if k in (0, 1, 10, 12) else vmem for k in range(len(shapes))],
        scratch_shapes=[
            pltpu.VMEM(project.shape, low),
            pltpu.VMEM(expand.shape, low),
            pltpu.VMEM(project.shape, wide),
            pltpu.VMEM(expand.shape, wide),
            pltpu.VMEM(slope.shape, wide),
            pltpu.VMEM(output.shape, low),
            dma((2, parts)),
            dma((2, parts)),
            dma((2, 2)),
        ],
        compiler_params=pltpu.CompilerParams(vmem_limit_bytes=60 * 1024 * 1024),
    )(project, expand, slope, output, gathered, gathered_bias, sums)


def dense_kernel(*refs):
    (
        second_ref,
        up_ref,
        scale_ref,
        returned_ref,
        lift_ref,
        mixed_hbm,
        expand_hbm,
        project_hbm,
        hidden_back_hbm,
        out_hbm,
        mixed_back_hbm,
        project_hbm_own,
        expand_hbm_own,
        project_piece,
        expand_piece,
        project_ready,
        expand_ready,
        vectors,
        mixed_ref,
        expand_ref,
        project_ref,
        hidden_back,
        out_ref,
        out_sum,
        back_sum,
        hidden_tile,
        back_tile,
        project_sent,
        expand_sent,
        project_got,
        expand_got,
        project_own,
        expand_own,
        project_halves,
        expand_halves,
        project_quarters,
        expand_quarters,
        project_eighths,
        expand_eighths,
        load_sems,
        weight_sems,
        leave_sems,
        own_sems,
        sent_sem,
        got_sem,
        first_sends,
        first_recvs,
    ) = refs
    tile = expand_ref.shape[2]
    pairs = project_own.shape[0]
    spot = place_of(lax.axis_index("rows"), lax.axis_index("cols"))
    core = spot["core"]
    orders = (("x", "y"), ("y", "x"))
    sent = (project_sent, expand_sent)
    got = (project_got, expand_got)
    own = (project_own, expand_own)
    halves = (project_halves, expand_halves)
    quarters = (project_quarters, expand_quarters)
    eighths = (project_eighths, expand_eighths)
    piece0 = (project_piece, expand_piece)
    ready = (project_ready, expand_ready)
    places = []
    for j in range(pairs):
        places += [(1 - core) * pairs + j, core * pairs + j]

    def weights(k):
        here = pl.ds(pl.multiple_of(places[k] * tile, tile), tile)
        return [
            pltpu.make_async_copy(project_hbm.at[here], project_ref.at[k], weight_sems.at[0, k]),
            pltpu.make_async_copy(expand_hbm.at[:, here], expand_ref.at[k], weight_sems.at[1, k]),
            pltpu.make_async_copy(
                hidden_back_hbm.at[places[k]], hidden_back.at[k], weight_sems.at[2, k]
            ),
        ]

    for k in range(2 * pairs):
        for copy in weights(k):
            copy.start()
    load_mixed = pltpu.make_async_copy(mixed_hbm, mixed_ref, load_sems.at[0])
    load_mixed.start()
    barrier = pltpu.get_barrier_semaphore()
    for axis in ("core", "x", "y", "near", "far"):
        device = facing(spot, axis)[1]
        pl.semaphore_signal(barrier, inc=1, device_id=device, device_id_type=MESH)
    count = second_ref.shape[0]
    piece = 1024
    vectors[...] = jnp.zeros_like(vectors)

    def start_step(part, carry):
        rows = pl.ds(pl.multiple_of(part * piece, piece), piece)
        out_sum[rows, :] = jnp.broadcast_to(as_row(returned_ref), (piece, out_sum.shape[1]))
        back_sum[rows, :] = jnp.zeros((piece, back_sum.shape[1]), wide)
        return carry + jnp.sum(up_ref[rows, :].astype(wide), 0, keepdims=True)

    vectors[4:5, :] = lax.fori_loop(
        0, count // piece, start_step, jnp.zeros((1, up_ref.shape[1]), wide)
    )
    pl.semaphore_wait(barrier, 5)

    def tile_step(k, place, between):
        lift_row = lift_ref[pl.ds(pl.multiple_of(place * tile, tile), tile)].reshape(1, tile)

        def piece_step(part, carry):
            rows = pl.ds(pl.multiple_of(part * piece, piece), piece)
            pre = dot(second_ref[rows, :], expand_ref[k]) + lift_row
            back = hidden_back[k, rows, :].astype(wide)
            curve = gelu_parts(pre)
            bell = gelu_bell(pre)
            hidden = (pre * curve).astype(low)
            hidden_tile[rows, :] = hidden
            pre_back = (back * (curve + pre * bell)).astype(low)
            back_tile[rows, :] = pre_back
            out_sum[rows, :] += dot(hidden, project_ref[k])
            back_sum[rows, :] += dot_last(pre_back, expand_ref[k])
            return carry + jnp.sum(pre_back.astype(wide), 0, keepdims=True)

        lift = lax.fori_loop(0, count // piece, piece_step, jnp.zeros((1, tile), wide))
        vectors[pl.ds(5 + place, 1), 0:tile] = lift
        between()
        return (
            dot_first(hidden_tile[...], up_ref[...]),
            dot_first(second_ref[...], back_tile[...]),
        )

    def swap(j, k):
        return remote(
            sent[k].at[j], got[k].at[j], sent_sem.at[j, k], got_sem.at[j, k], across(spot, "core")
        )

    chains = []
    for pair in range(2):
        for k in range(2):
            buffers = (own[k].at[pair], halves[k].at[pair])
            if pair == 0:
                buffers += (quarters[k], eighths[k], piece0[k])
            else:
                buffers += (ready[k],)
            chains.append(
                reduce_steps(
                    spot,
                    (orders[k] + ("near", "far"))[: len(buffers) - 1],
                    buffers,
                    first_sends.at[pair, k],
                    first_recvs.at[pair, k],
                )
            )

    def begin(pair, step):
        for chain in chains[pair * 2 : pair * 2 + 2]:
            chain[step][0]()

    def finish(pair, step):
        for chain in chains[pair * 2 : pair * 2 + 2]:
            chain[step][1]()

    def pair_step(j, carry):
        for copy in weights_at(2 * j):
            copy.wait()

        def away_between():
            @pl.when(j == 2)
            def _():
                finish(0, 1)
                begin(0, 2)

        away = tile_step(2 * j, (1 - core) * pairs + j, away_between)
        for k in range(2):
            sent[k][j] = away[k].astype(low)
            swap(j, k).start()
        for copy in weights_at(2 * j + 1):
            copy.wait()

        def home_between():
            @pl.when(j == 1)
            def _():
                finish(0, 0)
                begin(0, 1)

            @pl.when(j == 2)
            def _():
                finish(0, 2)
                begin(0, 3)
                finish(1, 0)
                begin(1, 1)

        home = tile_step(2 * j + 1, core * pairs + j, home_between)
        for k in range(2):
            swap(j, k).wait()
            own[k][j] = (home[k] + got[k][j].astype(wide)).astype(low)

        @pl.when(j == 0)
        def _():
            begin(0, 0)

        @pl.when(j == 1)
        def _():
            begin(1, 0)

        return carry

    def weights_at(k):
        return [
            pltpu.make_async_copy(project_ref.at[k], project_ref.at[k], weight_sems.at[0, k]),
            pltpu.make_async_copy(expand_ref.at[k], expand_ref.at[k], weight_sems.at[1, k]),
            pltpu.make_async_copy(hidden_back.at[k], hidden_back.at[k], weight_sems.at[2, k]),
        ]

    lax.fori_loop(0, pairs, pair_step, 0)
    keeps = [
        pltpu.make_async_copy(own[k].at[pairs - 1], hbm, own_sems.at[k])
        for k, hbm in enumerate((project_hbm_own, expand_hbm_own))
    ]
    for keep in keeps:
        keep.start()
    load_mixed.wait()

    def leave(part):
        rows = pl.ds(pl.multiple_of(part * piece, piece), piece)
        return [
            pltpu.make_async_copy(out_ref.at[rows], out_hbm.at[rows], leave_sems.at[0, part]),
            pltpu.make_async_copy(
                back_sum.at[rows], mixed_back_hbm.at[rows], leave_sems.at[1, part]
            ),
        ]

    def end_step(part, carry):
        for quarter in range(4):
            size = piece // 4
            rows = pl.ds(pl.multiple_of(part * piece + quarter * size, size), size)
            mixed = mixed_ref[rows, :]
            out_ref[rows, :] = (out_sum[rows, :] + mixed).astype(low)
            unit, factor = normalise(mixed)
            norm_back = back_sum[rows, :]
            vectors[2:3, :] += jnp.sum(norm_back * unit, 0, keepdims=True)
            vectors[3:4, :] += jnp.sum(norm_back, 0, keepdims=True)
            pull = norm_back * as_row(scale_ref)
            pull = pull - jnp.mean(pull, -1, keepdims=True) - unit * jnp.mean(
                pull * unit, -1, keepdims=True
            )
            back_sum[rows, :] = up_ref[rows, :].astype(wide) + factor * pull
        for copy in leave(part):
            copy.start()
        return carry

    lax.fori_loop(0, count // piece, end_step, 0)
    finish(0, 3)
    finish(1, 1)
    for keep in keeps:
        keep.wait()
    for part in range(count // piece):
        for copy in leave(part):
            copy.wait()


def call_dense(second_norm, upstream, scale, returned, lift, mixed, expand, project, hidden_back, cid):
    count, features = second_norm.shape
    tile = hidden_back.shape[2]
    pairs = expand.shape[1] // tile // 2
    tall, broad = (tile, features), (features, tile)
    outs = (
        ((count, features), low),
        ((count, features), wide),
        (tall, low),
        (broad, low),
        ((tile // 16, features), low),
        ((features // 16, tile), low),
        ((tile // 4, features), low),
        ((features // 4, tile), low),
        ((16, features), wide),
    )
    shapes = [jax.ShapeDtypeStruct(shape, kind) for shape, kind in outs]
    anywhere = pl.BlockSpec(memory_space=pl.ANY)
    dma = pltpu.SemaphoreType.DMA
    return pl.pallas_call(
        dense_kernel,
        out_shape=shapes,
        in_specs=[vmem] * 5 + [anywhere] * 4,
        out_specs=[anywhere] * 4 + [vmem] * 5,
        scratch_shapes=[
            pltpu.VMEM((count, features), wide),
            pltpu.VMEM((2 * pairs, *broad), low),
            pltpu.VMEM((2 * pairs, *tall), low),
            pltpu.VMEM(hidden_back.shape, low),
            pltpu.VMEM((count, features), low),
            pltpu.VMEM((count, features), wide),
            pltpu.VMEM((count, features), wide),
            pltpu.VMEM((count, tile), low),
            pltpu.VMEM((count, tile), low),
            *(pltpu.VMEM((pairs, *shape), low) for shape in (tall, broad) * 3),
            pltpu.VMEM((pairs - 1, tile // 2, features), low),
            pltpu.VMEM((pairs - 1, features // 2, tile), low),
            pltpu.VMEM((tile // 4, features), low),
            pltpu.VMEM((features // 4, tile), low),
            pltpu.VMEM((tile // 8, features), low),
            pltpu.VMEM((features // 8, tile), low),
            dma((1,)),
            dma((3, 2 * pairs)),
            dma((2, count // 512)),
            dma((2,)),
            dma((pairs, 2)),
            dma((pairs, 2)),
            dma((pairs - 1, 2, 4)),
            dma((pairs - 1, 2, 4)),
        ],
        compiler_params=pltpu.CompilerParams(
            collective_id=cid, has_side_effects=True, vmem_limit_bytes=60 * 1024 * 1024
        ),
    )(second_norm, upstream, scale, returned, lift, mixed, expand, project, hidden_back)


def shards(
    tokens,
    region_sizes,
    region_starts,
    entry_gain,
    entry_shift,
    spectral_kernel,
    spectral_bias,
    spectral_mixer,
    spectral_offset,
    exit_scale,
    exit_center,
    dense_expand,
    dense_lift,
    dense_project,
    dense_return,
    cotangent,
):
    regions, rows_here, cols_here, features = tokens.shape
    row_devices = lax.axis_size("rows")
    cols = lax.axis_size("cols")
    blocks, block_size = spectral_kernel.shape[1:3]
    chips = row_devices // 2 * cols
    fits = (
        row_devices % 2 == 0
        and chips == regions * blocks
        and cols == 2
        and cols_here == 64
        and rows_here == 8
        and block_size == 96
        and blocks == 8
        and regions == 2
        and dense_expand.shape == (features, 4 * features)
    )
    if not fits:
        return shards_general(
            tokens,
            region_sizes,
            region_starts,
            entry_gain,
            entry_shift,
            spectral_kernel,
            spectral_bias,
            spectral_mixer,
            spectral_offset,
            exit_scale,
            exit_center,
            dense_expand,
            dense_lift,
            dense_project,
            dense_return,
            cotangent,
        )
    height = rows_here * row_devices
    width = cols_here * cols
    patches = rows_here * cols_here
    count = regions * patches
    sizes = (regions, blocks, block_size, chips, cols, patches)
    block = ((lax.axis_index("rows") // 2) * cols + lax.axis_index("cols")) % blocks

    def own(weight):
        return lax.dynamic_index_in_dim(weight, block, 1, False)

    def square(weight):
        real, imaginary = weight[0], weight[1]
        return jnp.concatenate(
            [
                jnp.concatenate([real, imaginary], 1),
                jnp.concatenate([-imaginary, real], 1),
            ],
            0,
        )

    side = 2 * block_size
    weights = jnp.stack([square(own(spectral_kernel)), square(own(spectral_mixer))])
    biases = jnp.stack(
        [own(spectral_bias).reshape(side), own(spectral_offset).reshape(side)], 1
    )
    to_modes, to_columns, ahead, behind, eye = task_tables(height, width, rows_here, cols_here)
    flat_tokens = tokens.reshape(count, features)
    upstream = cotangent.reshape(count, features)
    steps = width // 4 // 4
    shape = (steps, side, 4 * 128)
    kept = ((shape, low), (shape, wide), (shape, low), (shape, wide))
    scalars = (region_sizes, region_starts)
    hidden, tile = dense_lift.shape[0], 512
    mixed, second_norm, *stream, hidden_back = call_filter(
        forward_kernel,
        sizes,
        (
            ((count, features), wide),
            ((count, features), low),
            *kept,
            ((hidden // tile, count, tile), low),
        ),
        1,
        (
            flat_tokens,
            entry_gain,
            entry_shift,
            exit_scale,
            exit_center,
            weights,
            biases,
            to_modes,
            to_columns,
            ahead,
            behind,
            eye,
            upstream,
            dense_project,
        ),
        scalars,
        (12, 13),
        range(7),
        forward_scratch(sizes, kept, hidden, tile),
    )
    output, mixed_back, *tiles, part_sums = call_dense(
        second_norm,
        upstream,
        exit_scale,
        dense_return,
        dense_lift,
        mixed,
        dense_expand,
        dense_project,
        hidden_back,
        3,
    )
    slope, project_sum, expand_sum, gathered, gathered_bias, sums = call_filter(
        backward_kernel,
        sizes,
        (
            ((count, features), wide),
            (dense_project.shape, low),
            (dense_expand.shape, low),
            ((2, 2, blocks, block_size, block_size), wide),
            ((2, blocks, 8, side), wide),
            ((16, features), wide),
        ),
        2,
        (
            flat_tokens,
            mixed_back,
            entry_gain,
            weights,
            to_modes.T,
            to_columns.T,
            ahead,
            behind,
            eye,
            *stream,
            *tiles,
            part_sums,
        ),
        scalars,
        (0, 9, 10, 11, 12, 13, 14),
        range(3),
        backward_scratch(sizes, kept, tiles[0].shape[0], 3),
    )
    return tuple(
        call_finish(
            project_sum,
            expand_sum,
            slope.reshape(tokens.shape),
            output.reshape(tokens.shape),
            gathered,
            gathered_bias,
            sums,
        )
    )


def solution(mesh):
    placed = (
        P(None, "rows", "cols", None),
        P(),
        P(),
        P(),
        P(),
        P(),
        P(),
        P(),
        P(),
        P(),
        P(),
        P(),
        P(),
        P(),
        P(),
        P(None, "rows", "cols", None),
    )
    return jax.shard_map(
        shards,
        mesh=mesh,
        in_specs=placed,
        out_specs=(
            P(None, "rows", "cols", None),
            P(None, "rows", "cols", None),
            P(),
            P(),
            P(),
            P(),
            P(),
            P(),
            P(),
            P(),
            P(),
            P(),
            P(),
            P(),
        ),
        check_vma=False,
    )
```

```python
import functools
import math

import jax
import jax.numpy as jnp
import ml_dtypes
import numpy as np
from jax import lax
from jax.experimental import pallas as pl
from jax.experimental.pallas import tpu as pltpu
from jax.sharding import PartitionSpec as P

shrink_width = 0.01
norm_eps = 1e-06
highest = lax.Precision.HIGHEST


def tables(height, width, modes):
    column = jnp.arange(width, dtype=jnp.int32)
    frequency = jnp.arange(modes, dtype=jnp.int32)
    turns = column[:, None] * frequency[None, :] % width
    angle = turns.astype(jnp.float32) * (2.0 * math.pi / width)
    cosine = jnp.cos(angle)
    sine = jnp.sin(angle)
    scale = 1.0 / math.sqrt(width)
    forward_zonal = jnp.stack([cosine, -sine], 1) * scale
    factor = jnp.where(frequency == 0, 1.0, 2.0).astype(jnp.float32)
    inverse_zonal = jnp.stack([cosine.T * factor[:, None], -sine.T * factor[:, None]], 0) * scale
    latitude = jnp.arange(height, dtype=jnp.int32)
    meridian_turns = latitude[:, None] * latitude[None, :] % height
    meridian_angle = meridian_turns.astype(jnp.float32) * (2.0 * math.pi / height)
    meridian_cos = jnp.cos(meridian_angle) / math.sqrt(height)
    meridian_sin = jnp.sin(meridian_angle) / math.sqrt(height)
    meridian_table = jnp.stack(
        [jnp.stack([meridian_cos, meridian_sin], -1), jnp.stack([-meridian_sin, meridian_cos], -1)],
        1,
    )
    forward_low = forward_zonal.astype(jnp.bfloat16)
    inverse_low = inverse_zonal.astype(jnp.bfloat16)
    meridian_low = meridian_table.astype(jnp.bfloat16)
    meridian_wide = meridian_low.astype(jnp.float32)
    return (forward_low, inverse_low, meridian_low, meridian_wide)


def layer_norm(value, gain, shift):
    centre = jnp.mean(value, -1, keepdims=True)
    centred = value - centre
    spread = jnp.mean(centred * centred, -1, keepdims=True)
    return centred * lax.rsqrt(spread + norm_eps) * gain + shift


def gelu_exact(value):
    return jax.nn.gelu(value, approximate=False)


def shrink(value):
    return value - shrink_width * jnp.tanh(value / shrink_width)


def block_layout(spectrum, blocks, block_size):
    leading = spectrum.shape[:3]
    parts = spectrum.reshape(leading + (2, blocks, block_size))
    parts = jnp.moveaxis(parts, 3, 4)
    return parts.reshape((-1, blocks, 2 * block_size))


def spectral_layout(modes_flat, leading, blocks, block_size):
    parts = modes_flat.reshape(leading + (blocks, 2, block_size))
    parts = jnp.moveaxis(parts, 4, 3)
    return parts.reshape(leading + (2, blocks * block_size))


def complex_matrix(weight):
    real = weight[0]
    imaginary = weight[1]
    upper = jnp.concatenate([real, imaginary], 2)
    lower = jnp.concatenate([-imaginary, real], 2)
    return jnp.concatenate([upper, lower], 1)


def matrix_gradient(whole, block_size):
    upper = whole[:, :block_size]
    lower = whole[:, block_size:]
    real = upper[:, :, :block_size] + lower[:, :, block_size:]
    imaginary = upper[:, :, block_size:] - lower[:, :, :block_size]
    return jnp.stack([real, imaginary], 0)


def bias_rows(bias):
    return jnp.moveaxis(bias, 0, 1).reshape(bias.shape[1], 2 * bias.shape[2])


def bias_gradient(summed, block_size):
    return jnp.moveaxis(summed.reshape(summed.shape[0], 2, block_size), 1, 0)


def advance(tokens, mask, weights, grids, layout):
    (
        entry_gain,
        entry_shift,
        spectral_kernel,
        spectral_bias,
        spectral_mixer,
        spectral_offset,
        exit_scale,
        exit_center,
        dense_expand,
        dense_lift,
        dense_project,
        dense_return,
    ) = weights
    forward_zonal, inverse_zonal, meridian_table, meridian_wide = grids
    blocks, block_size, first_block = layout
    residual = tokens.astype(jnp.float32)
    normed = layer_norm(residual, entry_gain, entry_shift)
    sent = (mask * normed).astype(jnp.bfloat16)
    by_channel = lax.all_to_all(sent, "cols", split_axis=3, concat_axis=2, tiled=True)
    zonal = jnp.einsum(
        "rhwc,wpk->rhkpc", by_channel, forward_zonal, preferred_element_type=jnp.float32
    )
    by_mode = lax.all_to_all(
        zonal.astype(jnp.bfloat16), "rows", split_axis=2, concat_axis=1, tiled=True
    )
    spectrum = jnp.einsum(
        "kphq,rhmqc->rkmpc", meridian_table, by_mode, preferred_element_type=jnp.float32
    ).astype(jnp.bfloat16)
    leading = spectrum.shape[:3]
    modes_flat = block_layout(spectrum, blocks, block_size)
    kernel_matrix = complex_matrix(
        lax.dynamic_slice_in_dim(spectral_kernel, first_block, blocks, 1)
    )
    mixer_matrix = complex_matrix(lax.dynamic_slice_in_dim(spectral_mixer, first_block, blocks, 1))
    kernel_bias = bias_rows(lax.dynamic_slice_in_dim(spectral_bias, first_block, blocks, 1))
    mixer_bias = bias_rows(lax.dynamic_slice_in_dim(spectral_offset, first_block, blocks, 1))
    first_pre = (
        jnp.einsum("nbx,bxy->nby", modes_flat, kernel_matrix, preferred_element_type=jnp.float32)
        + kernel_bias
    )
    first_act = gelu_exact(first_pre).astype(jnp.bfloat16)
    second_pre = (
        jnp.einsum("nbx,bxy->nby", first_act, mixer_matrix, preferred_element_type=jnp.float32)
        + mixer_bias
    )
    shrunk = spectral_layout(shrink(second_pre), leading, blocks, block_size)
    back_meridian = jnp.einsum(
        "kphq,rkmpc->rhmqc", meridian_wide, shrunk, precision=highest
    ).astype(jnp.bfloat16)
    by_row = lax.all_to_all(back_meridian, "rows", split_axis=1, concat_axis=2, tiled=True)
    filtered = jnp.einsum(
        "rhkpc,pkw->rhwc", by_row, inverse_zonal, preferred_element_type=jnp.float32
    ).astype(jnp.bfloat16)
    by_token = lax.all_to_all(filtered, "cols", split_axis=2, concat_axis=3, tiled=True)
    mixed = residual + mask * by_token.astype(jnp.float32) + normed
    features = mixed.shape[-1]
    second_norm = (
        layer_norm(mixed, exit_scale, exit_center).astype(jnp.bfloat16).reshape(-1, features)
    )
    hidden_pre = jnp.dot(second_norm, dense_expand, preferred_element_type=jnp.float32) + dense_lift
    hidden = gelu_exact(hidden_pre).astype(jnp.bfloat16)
    output = mixed + (
        jnp.dot(hidden, dense_project, preferred_element_type=jnp.float32) + dense_return
    ).reshape(mixed.shape)
    kept = (
        residual,
        modes_flat,
        first_pre,
        first_act,
        second_pre,
        mixed,
        second_norm,
        hidden_pre,
        hidden,
        kernel_matrix,
        mixer_matrix,
        leading,
    )
    return (output, kept)


def retreat(cotangent, mask, kept, weights, grids, layout):
    (
        entry_gain,
        entry_shift,
        spectral_kernel,
        spectral_bias,
        spectral_mixer,
        spectral_offset,
        exit_scale,
        exit_center,
        dense_expand,
        dense_lift,
        dense_project,
        dense_return,
    ) = weights
    forward_zonal, inverse_zonal, meridian_table, meridian_wide = grids
    blocks, block_size, first_block = layout
    (
        residual,
        modes_flat,
        first_pre,
        first_act,
        second_pre,
        mixed,
        second_norm,
        hidden_pre,
        hidden,
        kernel_matrix,
        mixer_matrix,
        leading,
    ) = kept
    features = mixed.shape[-1]
    upstream = cotangent.reshape(-1, features)
    gradient_project = jnp.einsum("tf,tc->fc", hidden, upstream, preferred_element_type=jnp.float32)
    gradient_return = jnp.sum(upstream.astype(jnp.float32), 0)
    outer = (gradient_project, gradient_return)
    hidden_back = jnp.einsum(
        "tc,fc->tf", upstream, dense_project, preferred_element_type=jnp.float32
    )
    hidden_pull = jax.vjp(gelu_exact, hidden_pre)[1]
    pre_back = hidden_pull(hidden_back)[0].astype(jnp.bfloat16)
    gradient_expand = jnp.einsum(
        "tc,tf->cf", second_norm, pre_back, preferred_element_type=jnp.float32
    )
    gradient_lift = jnp.sum(pre_back.astype(jnp.float32), 0)
    norm_back = jnp.einsum(
        "tf,cf->tc", pre_back, dense_expand, preferred_element_type=jnp.float32
    ).reshape(mixed.shape)
    exit_pull = jax.vjp(layer_norm, mixed, exit_scale, exit_center)[1]
    mixed_part, gradient_scale, gradient_center = exit_pull(norm_back)
    inner = (gradient_expand, gradient_lift, gradient_scale, gradient_center)
    mixed_back = cotangent.astype(jnp.float32) + mixed_part
    filter_back = (mask * mixed_back).astype(jnp.bfloat16)
    channel_back = lax.all_to_all(filter_back, "cols", split_axis=3, concat_axis=2, tiled=True)
    zonal_back = jnp.einsum(
        "rhwc,pkw->rhkpc", channel_back, inverse_zonal, preferred_element_type=jnp.float32
    ).astype(jnp.bfloat16)
    meridian_back = lax.all_to_all(zonal_back, "rows", split_axis=2, concat_axis=1, tiled=True)
    shrunk_back = jnp.einsum(
        "kphq,rhmqc->rkmpc", meridian_table, meridian_back, preferred_element_type=jnp.float32
    )
    shrink_pull = jax.vjp(shrink, second_pre)[1]
    second_back = shrink_pull(block_layout(shrunk_back, blocks, block_size))[0].astype(jnp.bfloat16)
    mixer_whole = jnp.einsum(
        "nbx,nby->bxy", first_act, second_back, preferred_element_type=jnp.float32
    )
    offset_rows = jnp.sum(second_back.astype(jnp.float32), 0)
    activation_back = jnp.einsum(
        "nby,bxy->nbx", second_back, mixer_matrix, preferred_element_type=jnp.float32
    )
    first_pull = jax.vjp(gelu_exact, first_pre)[1]
    first_back = first_pull(activation_back)[0].astype(jnp.bfloat16)
    kernel_whole = jnp.einsum(
        "nbx,nby->bxy", modes_flat, first_back, preferred_element_type=jnp.float32
    )
    kernel_rows = jnp.sum(first_back.astype(jnp.float32), 0)
    spectrum_back = spectral_layout(
        jnp.einsum("nby,bxy->nbx", first_back, kernel_matrix, preferred_element_type=jnp.float32),
        leading,
        blocks,
        block_size,
    )
    modes_back = jnp.einsum(
        "kphq,rkmpc->rhmqc", meridian_wide, spectrum_back, precision=highest
    ).astype(jnp.bfloat16)
    row_back = lax.all_to_all(modes_back, "rows", split_axis=1, concat_axis=2, tiled=True)
    sent_back = jnp.einsum(
        "rhkpc,wpk->rhwc", row_back, forward_zonal, preferred_element_type=jnp.float32
    ).astype(jnp.bfloat16)
    token_back = lax.all_to_all(sent_back, "cols", split_axis=2, concat_axis=3, tiled=True)
    normed_back = mixed_back + mask * token_back.astype(jnp.float32)
    entry_pull = jax.vjp(layer_norm, residual, entry_gain, entry_shift)[1]
    residual_part, gradient_gain, gradient_shift = entry_pull(normed_back)
    gradient_tokens = mixed_back + residual_part
    shared = (
        gradient_gain,
        gradient_shift,
        inner[2],
        inner[3],
        inner[0],
        inner[1],
        outer[0],
        outer[1],
    )
    local_blocks = (
        matrix_gradient(kernel_whole, block_size),
        bias_gradient(kernel_rows, block_size),
        matrix_gradient(mixer_whole, block_size),
        bias_gradient(offset_rows, block_size),
    )
    return (gradient_tokens, shared, local_blocks)


def shards_general(
    tokens,
    region_sizes,
    region_starts,
    entry_gain,
    entry_shift,
    spectral_kernel,
    spectral_bias,
    spectral_mixer,
    spectral_offset,
    exit_scale,
    exit_center,
    dense_expand,
    dense_lift,
    dense_project,
    dense_return,
    cotangent,
):
    rows_here = tokens.shape[1]
    cols_here = tokens.shape[2]
    height = rows_here * lax.axis_size("rows")
    width = cols_here * lax.axis_size("cols")
    grids = tables(height, width, width // 2)
    latitude = lax.axis_index("rows") * rows_here + jnp.arange(rows_here, dtype=jnp.int32)
    longitude = lax.axis_index("cols") * cols_here + jnp.arange(cols_here, dtype=jnp.int32)
    inside_rows = latitude[None, :, None] < region_sizes[:, 0][:, None, None]
    offset = (longitude[None, None, :] - region_starts[:, None, None]) % width
    inside_cols = offset < region_sizes[:, 1][:, None, None]
    mask = jnp.where(inside_rows & inside_cols, 1.0, 0.0).astype(jnp.float32)[..., None]
    block_size = spectral_kernel.shape[2]
    total_blocks = spectral_kernel.shape[1]
    blocks = tokens.shape[3] // lax.axis_size("cols") // block_size
    first_block = lax.axis_index("cols") * blocks
    layout = (blocks, block_size, first_block)
    weights = (
        entry_gain,
        entry_shift,
        spectral_kernel,
        spectral_bias,
        spectral_mixer,
        spectral_offset,
        exit_scale,
        exit_center,
        dense_expand,
        dense_lift,
        dense_project,
        dense_return,
    )
    output, kept = advance(tokens, mask, weights, grids, layout)
    gradient_tokens, shared, local_blocks = retreat(cotangent, mask, kept, weights, grids, layout)
    (
        gain_part,
        shift_part,
        scale_part,
        center_part,
        expand_part,
        lift_part,
        project_part,
        return_part,
    ) = shared
    everywhere = ("rows", "cols")
    project_sum = lax.psum(project_part.astype(jnp.bfloat16), everywhere).astype(jnp.float32)
    expand_sum = lax.psum(expand_part.astype(jnp.bfloat16), everywhere).astype(jnp.float32)
    vectors = (gain_part, shift_part, scale_part, center_part, lift_part, return_part)
    sums = lax.psum(jnp.concatenate(vectors), everywhere)
    ends = [0]
    for vector in vectors:
        ends.append(ends[-1] + vector.shape[0])
    parts = [sums[low:high] for low, high in zip(ends[:-1], ends[1:])]
    summed = (*parts[:4], expand_sum, parts[4], project_sum, parts[5])
    kernel_local, bias_local, mixer_local, offset_local = local_blocks
    kernel_full = lax.dynamic_update_slice_in_dim(
        jnp.zeros((2, total_blocks, block_size, block_size), jnp.float32),
        kernel_local,
        first_block,
        1,
    )
    bias_full = lax.dynamic_update_slice_in_dim(
        jnp.zeros((2, total_blocks, block_size), jnp.float32), bias_local, first_block, 1
    )
    mixer_full = lax.dynamic_update_slice_in_dim(
        jnp.zeros((2, total_blocks, block_size, block_size), jnp.float32),
        mixer_local,
        first_block,
        1,
    )
    offset_full = lax.dynamic_update_slice_in_dim(
        jnp.zeros((2, total_blocks, block_size), jnp.float32), offset_local, first_block, 1
    )
    block_totals = lax.psum((kernel_full, bias_full, mixer_full, offset_full), ("rows", "cols"))
    return (
        output.astype(jnp.bfloat16),
        gradient_tokens,
        summed[0],
        summed[1],
        block_totals[0],
        block_totals[1],
        block_totals[2],
        block_totals[3],
        summed[2],
        summed[3],
        summed[4],
        summed[5],
        summed[6],
        summed[7],
    )


MESH = pl.DeviceIdType.MESH
wide = jnp.float32
low = jnp.bfloat16
by_last = (((1,), (1,)), ((), ()))
by_first = (((0,), (0,)), ((), ()))
vmem = pl.BlockSpec(memory_space=pltpu.VMEM)


def dot(a, b):
    return jnp.dot(a, b, preferred_element_type=wide)


def dot_last(a, b):
    return lax.dot_general(a, b, by_last, preferred_element_type=wide)


def dot_first(a, b):
    return lax.dot_general(a, b, by_first, preferred_element_type=wide)


def task_tables(height, width, rows_here, cols_here):
    modes = width // 2
    near = modes // 2
    column = np.arange(width)
    frequency = np.arange(modes)
    angle = (column[:, None] * frequency[None, :] % width).astype(np.float32) * np.float32(
        2.0 * math.pi / width
    )
    scale = np.float32(1.0 / math.sqrt(width))
    zonal = np.stack([np.cos(angle), -np.sin(angle)], 1) * scale
    factor = np.where(frequency == 0, 1.0, 2.0).astype(np.float32)
    inverse = (
        np.stack([np.cos(angle).T * factor[:, None], -np.sin(angle).T * factor[:, None]], 0) * scale
    )
    latitude = np.arange(height)
    turn = (latitude[:, None] * latitude[None, :] % height).astype(np.float32) * np.float32(
        2.0 * math.pi / height
    )
    cosine = np.cos(turn) / np.float32(math.sqrt(height))
    sine = np.sin(turn) / np.float32(math.sqrt(height))
    meridian = np.stack([np.stack([cosine, sine], -1), np.stack([-sine, cosine], -1)], 1)
    halves = width // cols_here
    split_f = zonal.reshape(halves, cols_here, 2, 2, near)
    to_modes = np.zeros((halves, 2, cols_here, 2, 2, 2, near), np.float32)
    split_g = inverse.reshape(2, 2, near, halves, cols_here)
    to_columns = np.zeros((2, 2, 2, near, halves, 2, cols_here), np.float32)
    for i in range(2):
        to_modes[:, i, :, :, i] = split_f.transpose(0, 1, 3, 2, 4)
        to_columns[:, i, :, :, :, i] = split_g.transpose(1, 0, 2, 3, 4)
    side = halves * 2 * cols_here
    to_modes = to_modes.reshape(side, side)
    to_columns = to_columns.reshape(side, side)
    pairs = rows_here // 2
    senders = height // rows_here
    order = np.zeros((height // 2, 2), np.int64)
    for core in range(2):
        for chip in range(senders // 2):
            for pair in range(pairs):
                for i in range(2):
                    order[(core * (senders // 2) + chip) * pairs + pair, i] = (
                        (chip * 2 + core) * rows_here + pair * 2 + i
                    )
    placed = meridian[:, :, order]
    ahead = np.zeros((2, 2, 2, height // 2, 2, 2, height), np.float32)
    for c in range(2):
        ahead[:, :, c, :, c] = placed.transpose(3, 4, 2, 1, 0)
    ahead = ahead.reshape(2, 2 * height, 4 * height)
    behind = ahead.reshape(4 * height, 4 * height).T
    return tuple(
        np.asarray(item, ml_dtypes.bfloat16)
        for item in (to_modes, to_columns, ahead, behind, np.eye(256, dtype=np.float32))
    )


def chip_device(chip, core, cols):
    return ((chip // cols) * 2 + core, chip % cols)


def swap_bits(value, mask, bits):
    out = 0
    for k in range(bits):
        bit = (value // (1 << k)) % 2
        if (mask >> k) & 1:
            bit = 1 - bit
        out = out + bit * (1 << k)
    return out


def cross(value, mask, bits):
    out = 0
    for k in range(bits):
        out = out + (value // (1 << k) + mask // (1 << k)) % 2 * (1 << k)
    return out


def greet(chips, cols):
    row = lax.axis_index("rows")
    core = row % 2
    me = (row // 2) * cols + lax.axis_index("cols")
    barrier = pltpu.get_barrier_semaphore()
    for step in range(1, chips):
        other = (me + step) % chips
        pl.semaphore_signal(
            barrier, inc=1, device_id=chip_device(other, core, cols), device_id_type=MESH
        )
    pl.semaphore_signal(
        barrier, inc=1, device_id=chip_device(me, 1 - core, cols), device_id_type=MESH
    )
    pl.semaphore_wait(barrier, chips)
    return me, core


def send_piece(src, dst, send_sem, recv_sem, target, me, core, cols):
    @pl.when(target == me)
    def _():
        pltpu.make_async_copy(src, dst, recv_sem).start()

    @pl.when(target != me)
    def _():
        pltpu.make_async_remote_copy(
            src_ref=src,
            dst_ref=dst,
            send_sem=send_sem,
            recv_sem=recv_sem,
            device_id=chip_device(target, core, cols),
            device_id_type=MESH,
        ).start()


def await_piece(ref, sem):
    pltpu.make_async_copy(ref, ref, sem).wait()


def to_feature_rows(out_ref, region, place, piece, eye):
    features = piece.shape[1]
    for low_end in range(0, features, 256):
        turned = dot_last(eye, piece[:, low_end : low_end + 256])
        out_ref[region, low_end : low_end + 256, place] = turned.astype(low)


def modes_first(block, group, half):
    columns = []
    for m in range(group):
        rows = block[m * half : (m + 1) * half]
        height = block.shape[1] // 4
        columns.append(
            jnp.concatenate(
                [
                    rows[:, (c * 2 + p) * height : (c * 2 + p + 1) * height]
                    for p in range(2)
                    for c in range(2)
                ],
                0,
            )
        )
    return jnp.concatenate(columns, 1)


def modes_last(block, group, half):
    height = block.shape[1] // group
    rows = []
    for m in range(group):
        part = block[:, m * height : (m + 1) * height]
        rows.append(
            jnp.concatenate(
                [
                    part[(p * 2 + c) * half : (p * 2 + c + 1) * half]
                    for c in range(2)
                    for p in range(2)
                ],
                1,
            )
        )
    return jnp.concatenate(rows, 0)


def filter_pass(sizes, me, core, produce, middle, consume, tables, work, sems, tick):
    regions, blocks, block_size, chips, cols, tokens = sizes
    table_in, table_out, ahead, behind = tables
    sent, got, zonal, zonal_got, tall, flat, back, sibling, leaving, coming = work
    send_a, recv_a, send_b, recv_b, send_c, recv_c, send_d, recv_d = sems
    lanes = 128
    senders = chips // cols
    pairs = tokens // lanes
    half = block_size // 2
    points = senders * pairs
    group = 4
    bits = (blocks - 1).bit_length()
    home = me // blocks
    tick("start")
    for turn in range(regions):
        region = (home + 1 + turn) % regions
        produce(region)
        for step in range(blocks - 1, -1, -1):
            target = region * blocks + swap_bits(me % blocks, step, bits)
            src = sent.at[region, pl.ds(pl.multiple_of(target % blocks * block_size, 32), block_size)]
            place = turn * blocks + step
            send_piece(src, got.at[me], send_a.at[place], recv_a.at[me], target, me, core, cols)
    tick("sent")

    middle_point = points // 2

    def swap_half(k, first):
        place = pl.ds(pl.multiple_of(first, middle_point), middle_point)
        return pltpu.make_async_remote_copy(
            src_ref=zonal.at[1 - core, place],
            dst_ref=zonal_got.at[place],
            send_sem=send_b.at[k],
            recv_sem=recv_b.at[k],
            device_id=chip_device(me, 1 - core, cols),
            device_id_type=MESH,
        )

    swaps = [
        swap_half(0, home * middle_point),
        swap_half(1, (1 - home) * middle_point),
    ]

    def zonal_step(index, carry):
        tick("arrival", index)
        chip = cross(me // cols, index, senders.bit_length() - 1)
        for col in range(cols):
            await_piece(got.at[chip * cols + col], recv_a.at[chip * cols + col])
        x = jnp.concatenate(
            [
                jnp.concatenate(
                    [
                        got[chip * cols + col, :, pair * lanes : (pair + 1) * lanes]
                        for col in range(cols)
                    ],
                    1,
                )
                for pair in range(pairs)
            ],
            0,
        )
        y = dot(x, table_in[...]).astype(low)
        for pair in range(pairs):
            rows = slice(pair * block_size, (pair + 1) * block_size)
            for part in range(2):
                zonal[part, chip * pairs + pair] = y[rows, part * lanes : (part + 1) * lanes]

        @pl.when(index == senders // 2 - 1)
        def _():
            swaps[0].start()

        return carry

    lax.fori_loop(0, senders, zonal_step, 0)
    swaps[1].start()
    tick("zonal")

    def widen(source, first):
        def step(point, carry):
            row = pl.multiple_of((first + point) * block_size, 32)
            tall[pl.ds(row, block_size), :] = source(point).astype(wide)
            return carry

        lax.fori_loop(0, points, step, 0)

    widen(lambda point: zonal[core, point], core * points)
    for swap in swaps:
        swap.wait()
    widen(lambda point: zonal_got[point], (1 - core) * points)
    modes = lanes // 4

    def turn_step(c, carry):
        x = jnp.concatenate(
            [tall[pl.ds(c + half * side, 2 * points, stride=block_size), :] for side in range(2)], 0
        )
        y = jnp.transpose(x)
        for i in range(4):
            flat[i, pl.ds(c, modes, stride=half), :] = y[i * modes : (i + 1) * modes]
        return carry

    lax.fori_loop(0, half, turn_step, 0, unroll=8)
    tick("turned")

    def mode_step(step, carry):
        rows = pl.ds(pl.multiple_of(step * group * half, 64), group * half)
        spectrum = 0.0
        for i in range(2):
            x = jnp.concatenate([flat[i * 2, rows, :], flat[i * 2 + 1, rows, :]], 1).astype(low)
            spectrum = spectrum + dot(x, ahead[i])
        out = modes_last(middle(step, modes_first(spectrum, group, half)), group, half)
        high = out.astype(low)
        rest = (out - high.astype(wide)).astype(low)
        y = (dot(high, behind[...]) + dot(rest, behind[...])).astype(low).astype(wide)
        for i in range(4):
            flat[i, rows, :] = y[:, i * lanes : (i + 1) * lanes]
        tick("mode", step)
        return carry

    lax.fori_loop(0, modes // group, mode_step, 0)
    tick("modes")

    def return_step(c, carry):
        x = jnp.concatenate([flat[i, pl.ds(c, modes, stride=half), :] for i in range(4)], 0)
        y = jnp.transpose(x)
        for side in range(2):
            tall[pl.ds(c + half * side, 2 * points, stride=block_size), :] = y[
                side * 2 * points : (side + 1) * 2 * points
            ]
        return carry

    lax.fori_loop(0, half, return_step, 0, unroll=8)
    tick("returned")

    def narrow(store, first):
        def step(point, carry):
            row = pl.multiple_of((first + point) * block_size, 32)
            store(point, tall[pl.ds(row, block_size), :].astype(low))
            return carry

        lax.fori_loop(0, points, step, 0)

    def to_sibling(point, value):
        back[point] = value

    def to_self(point, value):
        sibling[core, point] = value

    narrow(to_sibling, (1 - core) * points)
    swap_back = pltpu.make_async_remote_copy(
        src_ref=back,
        dst_ref=sibling.at[core],
        send_sem=send_c,
        recv_sem=recv_c,
        device_id=chip_device(me, 1 - core, cols),
        device_id_type=MESH,
    )
    swap_back.start()
    tick("back")
    narrow(to_self, core * points)
    swap_back.wait_send()
    await_piece(sibling.at[1 - core], recv_c)

    def column_step(index, carry):
        chip = cross(me // cols, senders - 1 - index, senders.bit_length() - 1)
        x = jnp.concatenate(
            [
                jnp.concatenate([sibling[part, chip * pairs + pair] for part in range(2)], 1)
                for pair in range(pairs)
            ],
            0,
        )
        y = dot(x, table_out[...]).astype(low)
        for pair in range(pairs):
            rows = slice(pair * block_size, (pair + 1) * block_size)
            for col in range(cols):
                leaving[chip * cols + col, :, pair * lanes : (pair + 1) * lanes] = y[
                    rows, col * lanes : (col + 1) * lanes
                ]
        for turn in range(cols):
            target = chip * cols + (me + turn + 1) % cols
            dst = coming.at[
                me // blocks, pl.ds(pl.multiple_of(me % blocks * block_size, 32), block_size)
            ]
            send_piece(
                leaving.at[target], dst, send_d.at[target], recv_d.at[me], target, me, core, cols
            )
        return carry

    lax.fori_loop(0, senders, column_step, 0)
    tick("columns")
    for turn in range(regions):
        region = (home + turn) % regions

        def arrive(block, carry, region=region):
            ref = coming.at[region, pl.ds(pl.multiple_of(block * block_size, 32), block_size)]
            await_piece(ref, recv_d.at[region * blocks + block])
            return carry

        lax.fori_loop(0, blocks, arrive, 0)
        consume(region)
        tick("region")

    for place in range(regions * blocks):
        turn, step = place // blocks, place % blocks
        target = (home + 1 + turn) % regions * blocks + swap_bits(me % blocks, step, bits)

        @pl.when(target != me)
        def _():
            await_piece(got.at[0], send_a.at[place])

        @pl.when(place != me)
        def _():
            await_piece(leaving.at[0], send_d.at[place])


def work_shapes(sizes):
    regions, blocks, block_size, chips, cols, tokens = sizes
    lanes = 128
    features = blocks * block_size
    points = (chips // cols) * (tokens // lanes)
    rows = (lanes // 4) * (block_size // 2)
    return [
        pltpu.VMEM((regions, features, tokens), low),
        pltpu.VMEM((chips, block_size, tokens), low),
        pltpu.VMEM((2, points, block_size, lanes), low),
        pltpu.VMEM((points, block_size, lanes), low),
        pltpu.VMEM((2 * points * block_size, lanes), wide),
        pltpu.VMEM((4, rows, lanes), wide),
        pltpu.VMEM((points, block_size, lanes), low),
        pltpu.VMEM((2, points, block_size, lanes), low),
        pltpu.VMEM((chips, block_size, tokens), low),
        pltpu.VMEM((regions, features, tokens), low),
        pltpu.SemaphoreType.DMA((chips,)),
        pltpu.SemaphoreType.DMA((chips,)),
        pltpu.SemaphoreType.DMA((2,)),
        pltpu.SemaphoreType.DMA((2,)),
        pltpu.SemaphoreType.DMA,
        pltpu.SemaphoreType.DMA,
        pltpu.SemaphoreType.DMA((chips,)),
        pltpu.SemaphoreType.DMA((chips,)),
    ]


def normalise(value):
    centre = jnp.mean(value, -1, keepdims=True)
    centred = value - centre
    spread = jnp.mean(centred * centred, -1, keepdims=True)
    factor = lax.rsqrt(spread + norm_eps)
    return centred * factor, factor


def gelu_parts(value):
    curve = 0.5 * (1.0 + lax.erf(value * (1.0 / math.sqrt(2.0))))
    return curve


def gelu_bell(value):
    return jnp.exp(-0.5 * value * value) * (1.0 / math.sqrt(2.0 * math.pi))


def inside_region(sizes_ref, starts_ref, region, first, shape, width):
    rows, rows_here, cols_here = shape
    index = first + lax.broadcasted_iota(jnp.int32, (rows, 1), 0)
    bits = cols_here.bit_length() - 1
    latitude = lax.axis_index("rows") * rows_here + lax.shift_right_logical(index, bits)
    longitude = lax.axis_index("cols") * cols_here + (index & (cols_here - 1))
    offset = longitude - starts_ref[region]
    offset = jnp.where(offset < 0, offset + width, offset)
    near = jnp.where(latitude < sizes_ref[region, 0], 1.0, 0.0)
    return jnp.where(offset < sizes_ref[region, 1], near, 0.0)


def as_row(ref):
    return ref[...].reshape(1, ref.shape[0])


def field_rows(coming, region, place, eye):
    return jnp.concatenate(
        [
            dot_last(eye, coming[region, first : first + 256, place])
            for first in range(0, coming.shape[1], 256)
        ],
        1,
    )


def forward_kernel(sizes, *refs):
    (
        region_sizes,
        region_starts,
        tokens_ref,
        gain_ref,
        shift_ref,
        scale_ref,
        center_ref,
        weights_ref,
        biases_ref,
        to_modes,
        to_columns,
        ahead,
        behind,
        eye,
        up_hbm,
        project_hbm,
        mixed_hbm,
        second_hbm,
        *kept_hbm,
        hidden_back_hbm,
    ) = refs[:23]
    work, sems = refs[23:33], refs[33:41]
    (
        mixed,
        second,
        mixed_sems,
        second_sems,
        kept_sems,
        up_ref,
        project_ref,
        hidden_back,
        load_sems,
        back_sems,
        *kept,
    ) = refs[41:]
    loads = [
        pltpu.make_async_copy(up_hbm, up_ref, load_sems.at[0]),
        pltpu.make_async_copy(project_hbm, project_ref, load_sems.at[1]),
    ]
    for copy in loads:
        copy.start()
    regions, blocks, block_size, chips, cols, tokens = sizes
    me, core = greet(chips, cols)
    sent, coming = work[0], work[-1]
    piece = 256
    steps = kept_hbm[0].shape[0]
    cols_here = 128 // cols
    gain, shift, scale, center = (
        as_row(ref) for ref in (gain_ref, shift_ref, scale_ref, center_ref)
    )

    def inside(region, first, rows):
        shape = (rows, tokens // cols_here, cols_here)
        return inside_region(region_sizes, region_starts, region, first, shape, 128)

    def produce(region):
        def step(part, carry):
            rows = pl.ds(pl.multiple_of(region * tokens + part * piece, piece), piece)
            unit, factor = normalise(tokens_ref[rows, :].astype(wide))
            values = (inside(region, part * piece, piece) * (unit * gain + shift)).astype(low)
            place = pl.ds(pl.multiple_of(part * piece, piece), piece)
            to_feature_rows(sent, region, place, values, eye[...])
            return carry

        lax.fori_loop(0, tokens // piece, step, 0)

    def keep(step):
        slot = step % 2
        return [
            pltpu.make_async_copy(ref.at[slot], hbm.at[step], kept_sems.at[k, slot])
            for k, (ref, hbm) in enumerate(zip(kept, kept_hbm))
        ]

    def middle(step, spectrum):
        slot = step % 2

        @pl.when(step >= 2)
        def _():
            for copy in keep(step - 2):
                copy.wait()

        spectrum_kept, first_kept, act_kept, second_kept = kept
        spectrum = spectrum.astype(low)
        spectrum_kept[slot] = spectrum
        first = dot_first(weights_ref[0], spectrum) + biases_ref[:, 0:1]
        curve = gelu_parts(first)
        first_kept[slot] = curve + first * gelu_bell(first)
        act = (first * curve).astype(low)
        act_kept[slot] = act
        second_pre = dot_first(weights_ref[1], act) + biases_ref[:, 1:2]
        level = jnp.tanh(second_pre / shrink_width)
        second_kept[slot] = level * level
        for copy in keep(step):
            copy.start()
        return second_pre - shrink_width * level

    def leave(region):
        rows = pl.ds(pl.multiple_of(region * tokens, tokens), tokens)
        return [
            pltpu.make_async_copy(mixed.at[rows], mixed_hbm.at[rows], mixed_sems.at[region]),
            pltpu.make_async_copy(second.at[rows], second_hbm.at[rows], second_sems.at[region]),
        ]

    def consume(region):
        def step(part, carry):
            rows = pl.ds(pl.multiple_of(region * tokens + part * 256, 256), 256)
            place = pl.ds(pl.multiple_of(part * 256, 256), 256)
            fields = field_rows(coming, region, place, eye[...])
            residual = tokens_ref[rows, :].astype(wide)
            unit, factor = normalise(residual)
            value = residual + inside(region, part * 256, 256) * fields + (unit * gain + shift)
            mixed[rows, :] = value
            unit, factor = normalise(value)
            second[rows, :] = (unit * scale + center).astype(low)
            return carry

        lax.fori_loop(0, tokens // 256, step, 0)
        for copy in leave(region):
            copy.start()

    tiles, count, tile = hidden_back.shape

    def leave_back(k):
        return pltpu.make_async_copy(hidden_back.at[k], hidden_back_hbm.at[k], back_sems.at[k])

    def tick(place, step=0):
        if place == "sent":
            for copy in loads:
                copy.wait()

            def tile_step(k, carry):
                here = pl.ds(pl.multiple_of(k * tile, tile), tile)
                for first in range(0, count, 256):
                    rows = slice(first, first + 256)
                    hidden_back[k, rows, :] = dot_last(up_ref[rows, :], project_ref[here, :]).astype(low)
                leave_back(k).start()
                return carry

            lax.fori_loop(0, tiles, tile_step, 0)

    tables = (to_modes, to_columns, ahead, behind)
    filter_pass(sizes, me, core, produce, middle, consume, tables, work, sems, tick)
    for k in range(tiles):
        leave_back(k).wait()
    for step in (steps - 2, steps - 1):
        for copy in keep(step):
            copy.wait()
    for region in range(regions):
        for copy in leave(region):
            copy.wait()


def place_of(row, col):
    return {"core": row % 2, "x": (row // 2) % 2, "z": row // 4, "y": col}


def device_at(spot):
    return (spot["z"] * 4 + spot["x"] * 2 + spot["core"], spot["y"])


def across(spot, axis, step=1):
    size = 4 if axis == "z" else 2
    return device_at({**spot, axis: (spot[axis] + step) % size})


def remote(src, dst, send_sem, recv_sem, device):
    return pltpu.make_async_remote_copy(
        src_ref=src,
        dst_ref=dst,
        send_sem=send_sem,
        recv_sem=recv_sem,
        device_id=device,
        device_id_type=MESH,
    )


def add_rows(out_ref, out_row, terms, rows):
    step = [size for size in (96, 64, 48, 32) if rows % size == 0][0]

    def add(part, carry):
        total = 0.0
        for ref, row in terms:
            here = pl.ds(pl.multiple_of(row + part * step, 16), step)
            total = total + ref[here, :].astype(wide)
        there = pl.ds(pl.multiple_of(out_row + part * step, 16), step)
        out_ref[there, :] = total.astype(low)
        return carry

    lax.fori_loop(0, rows // step, add, 0)


def row_part(ref, row, rows):
    return ref.at[pl.ds(pl.multiple_of(row, 16), rows)]


def facing(spot, axis):
    if axis == "near":
        z = spot["z"] // 2 * 2 + 1 - spot["z"] % 2
        return spot["z"] % 2, device_at({**spot, "z": z})
    if axis == "far":
        return spot["z"] // 2, across(spot, "z", 2)
    return spot[axis], across(spot, axis)


def reduce_steps(spot, axes, buffers, sends, recvs):
    steps = []
    for k, axis in enumerate(axes):
        bit, device = facing(spot, axis)
        source, target = buffers[k], buffers[k + 1]
        rows = target.shape[0]
        hop = remote(
            row_part(source, (1 - bit) * rows, rows), target, sends.at[k], recvs.at[k], device
        )

        def finish(hop=hop, source=source, target=target, rows=rows, bit=bit):
            hop.wait()
            add_rows(target, 0, ((target, 0), (source, bit * rows)), rows)

        steps.append((hop.start, finish))
    return steps


def share_steps(spot, axes, piece, total, sends, recvs, own_sem):
    offsets, rows, bits, devices = [0], [total.shape[0]], [], []
    for axis in axes:
        bit, device = facing(spot, axis)
        bits.append(bit)
        devices.append(device)
        rows.append(rows[-1] // 2)
        offsets.append(offsets[-1] + bit * rows[-1])
    last = len(axes) - 1
    hops = []
    for k in range(last, -1, -1):
        place = row_part(total, offsets[k + 1], rows[k + 1])
        source = piece if k == last else place
        hops.append(remote(source, place, sends.at[k], recvs.at[k], devices[k]))
    keep = pltpu.make_async_copy(piece, row_part(total, offsets[-1], rows[-1]), own_sem)
    ready = (
        (offsets[2], rows[2]),
        (offsets[1] + (1 - bits[1]) * rows[2], rows[2]),
        ((1 - bits[0]) * rows[1], rows[1]),
    )
    cores = []
    for k, (offset, size) in enumerate(ready):
        place = row_part(total, offset, size)
        cores.append(
            remote(place, place, sends.at[4 + k], recvs.at[4 + k], across(spot, "core"))
        )

    def begin():
        keep.start()
        hops[0].start()

    def second():
        keep.wait()
        hops[0].wait()
        hops[1].start()

    def third():
        hops[1].wait()
        hops[2].start()
        cores[0].start()

    def fourth():
        hops[2].wait()
        hops[3].start()
        cores[1].start()

    def fifth():
        hops[3].wait()
        cores[2].start()

    def finish():
        for core in cores:
            core.wait()

    return begin, second, third, fourth, fifth, finish


def backward_kernel(sizes, *refs):
    (
        region_sizes,
        region_starts,
        tokens_hbm,
        mixed_back_ref,
        gain_ref,
        weights_ref,
        to_modes,
        to_columns,
        ahead,
        behind,
        eye,
        spectrum_hbm,
        first_hbm,
        act_hbm,
        pre_hbm,
        project_hbm,
        expand_hbm,
        project_piece,
        expand_piece,
        project_ready,
        expand_ready,
        sums_ref,
        slope_hbm,
        project_total,
        expand_total,
        gathered,
        gathered_bias,
        vector_sum,
    ) = refs[:28]
    work, sems = refs[28:38], refs[38:46]
    (
        tokens_ref,
        slope,
        slope_sems,
        project_own,
        expand_own,
        load_sems,
        kernel_slope,
        bias_slope,
        mixer_slope,
        offset_slope,
        spectrum_slots,
        first_slots,
        act_slots,
        pre_slots,
        slot_sems,
        project_halves,
        expand_halves,
        project_quarters,
        expand_quarters,
        project_eighths,
        expand_eighths,
        project_pieces,
        expand_pieces,
        reduce_sends,
        reduce_recvs,
        share_sends,
        share_recvs,
        own_sems,
        slab,
        slab_bias,
        slab_got,
        slab_bias_got,
        slab_region,
        slab_bias_region,
        slab_sends,
        slab_recvs,
        vector_sent,
        vector_got,
        vector_sends,
        vector_recvs,
        late,
        late_got,
        late_all,
        late_sends,
        late_recvs,
    ) = refs[46:]
    regions, blocks, block_size, chips, cols, tokens = sizes
    steps = spectrum_hbm.shape[0]
    slots = (spectrum_slots, first_slots, act_slots, pre_slots)
    streams = (spectrum_hbm, first_hbm, act_hbm, pre_hbm)

    def fetch(step, slot):
        return [
            pltpu.make_async_copy(hbm.at[step], ref.at[slot], slot_sems.at[k, slot])
            for k, (hbm, ref) in enumerate(zip(streams, slots))
        ]

    own = (project_own, expand_own)
    load_own = [
        pltpu.make_async_copy(hbm, own[k], load_sems.at[1 + k])
        for k, hbm in enumerate((project_hbm, expand_hbm))
    ]
    load_tokens = pltpu.make_async_copy(tokens_hbm, tokens_ref, load_sems.at[0])
    for copy in load_own:
        copy.start()
    for copy in fetch(0, 0):
        copy.start()
    load_tokens.start()
    me, core = greet(chips, cols)
    spot = place_of(lax.axis_index("rows"), lax.axis_index("cols"))
    block = me % blocks
    sent, coming = work[0], work[-1]
    piece = 256
    cols_here = 128 // cols
    late[...] = jnp.zeros_like(late)
    vector_sum[...] = sums_ref[...]
    for ref in (kernel_slope, bias_slope, mixer_slope, offset_slope):
        ref[...] = jnp.zeros_like(ref)
    reducing, sharing = [], []
    pairs = 3
    tile = project_own.shape[0]
    own_pieces = (
        (project_piece, expand_piece),
        (project_pieces.at[0], expand_pieces.at[0]),
        (project_pieces.at[1], expand_pieces.at[1]),
    )
    chains = (
        ((project_piece,), (expand_piece,)),
        (
            (project_ready, project_eighths.at[0], own_pieces[1][0]),
            (expand_ready, expand_eighths.at[0], own_pieces[1][1]),
        ),
        (
            (
                project_own,
                project_halves,
                project_quarters,
                project_eighths.at[1],
                own_pieces[2][0],
            ),
            (expand_own, expand_halves, expand_quarters, expand_eighths.at[1], own_pieces[2][1]),
        ),
    )
    for j in range(pairs):
        place = pl.multiple_of((core * pairs + j) * tile, tile)
        totals = (project_total.at[pl.ds(place, tile)], expand_total.at[:, pl.ds(place, tile)])
        for k in range(2):
            axes = (("x", "y"), ("y", "x"))[k] + ("near", "far")
            buffers = chains[j][k]
            reducing.append(
                reduce_steps(
                    spot,
                    axes[5 - len(buffers) :],
                    buffers,
                    reduce_sends.at[j, k],
                    reduce_recvs.at[j, k],
                )
            )
            sharing.append(
                share_steps(
                    spot,
                    axes,
                    own_pieces[j][k],
                    totals[k],
                    share_sends.at[j, k],
                    share_recvs.at[j, k],
                    own_sems.at[j, k],
                )
            )

    def reduce(j, step, finish):
        for steps_of in reducing[2 * j : 2 * j + 2]:
            steps_of[step][finish]()

    def share(j, step):
        for steps_of in sharing[2 * j : 2 * j + 2]:
            steps_of[step]()

    def inside(region, first, rows):
        shape = (rows, tokens // cols_here, cols_here)
        return inside_region(region_sizes, region_starts, region, first, shape, 128)

    def produce(region):
        def step(part, carry):
            rows = pl.ds(pl.multiple_of(region * tokens + part * piece, piece), piece)
            place = pl.ds(pl.multiple_of(part * piece, piece), piece)
            values = (inside(region, part * piece, piece) * mixed_back_ref[rows, :]).astype(low)
            to_feature_rows(sent, region, place, values, eye[...])
            return carry

        lax.fori_loop(0, tokens // piece, step, 0)

    def middle(step, shrunk_back):
        slot = step % 2
        for copy in fetch(step, slot):
            copy.wait()

        @pl.when(step + 1 < steps)
        def _():
            for copy in fetch(step + 1, 1 - slot):
                copy.start()

        second = (shrunk_back * pre_slots[slot]).astype(low)
        ones = jnp.ones((8, second.shape[1]), low)
        offset_slope[...] += dot_last(ones, second)
        mixer_slope[...] += dot_last(act_slots[slot], second)
        first = (dot(weights_ref[1], second) * first_slots[slot]).astype(low)
        bias_slope[...] += dot_last(ones, first)
        kernel_slope[...] += dot_last(spectrum_slots[slot], first)
        return dot(weights_ref[0], first)

    def leave(region):
        rows = pl.ds(pl.multiple_of(region * tokens, tokens), tokens)
        return pltpu.make_async_copy(slope.at[rows], slope_hbm.at[rows], slope_sems.at[region])

    def consume(region):
        def step(part, carry):
            rows = pl.ds(pl.multiple_of(region * tokens + part * 256, 256), 256)
            place = pl.ds(pl.multiple_of(part * 256, 256), 256)
            fields = field_rows(coming, region, place, eye[...])
            unit, factor = normalise(tokens_ref[rows, :].astype(wide))
            mixed_back = mixed_back_ref[rows, :]
            normed_back = mixed_back + inside(region, part * 256, 256) * fields
            gains = jnp.sum(normed_back * unit, 0, keepdims=True)
            shifts = jnp.sum(normed_back, 0, keepdims=True)
            for k in range(3):
                late[k : k + 1, :] += gains[:, k * 256 : (k + 1) * 256]
                late[3 + k : 4 + k, :] += shifts[:, k * 256 : (k + 1) * 256]
            pull = normed_back * as_row(gain_ref)
            pull = pull - jnp.mean(pull, -1, keepdims=True) - unit * jnp.mean(
                pull * unit, -1, keepdims=True
            )
            slope[rows, :] = mixed_back + factor * pull
            return carry

        lax.fori_loop(0, tokens // 256, step, 0)
        leave(region).start()

    def slab_hops(place, mine, theirs, device):
        return [
            remote(src, dst, slab_sends.at[k, place], slab_recvs.at[k, place], device)
            for k, (src, dst) in enumerate(zip(mine, theirs))
        ]

    slab_core = slab_hops(
        0, (slab, slab_bias), (slab_got, slab_bias_got), across(spot, "core")
    )
    slab_far = slab_hops(
        1,
        (slab_got.at[core], slab_bias_got.at[core]),
        (slab_region, slab_bias_region),
        chip_device((me + blocks) % chips, core, cols),
    )
    here = (gathered.at[core, :, block], gathered_bias.at[core, block])

    def slab_peer(step):
        other = me // blocks * blocks + (block + step) % blocks
        return slab_hops(1 + step, here, here, chip_device(other, core, cols))

    everything = (gathered.at[core], gathered_bias.at[core])
    slab_last = slab_hops(1 + blocks, everything, everything, across(spot, "core"))

    def slab_start():
        for k, (weight, bias) in enumerate(
            ((kernel_slope, bias_slope), (mixer_slope, offset_slope))
        ):
            whole = weight[...]
            upper, lower = whole[:block_size], whole[block_size:]
            slab[k, 0] = upper[:, :block_size] + lower[:, block_size:]
            slab[k, 1] = upper[:, block_size:] - lower[:, :block_size]
            slab_bias[k] = bias[...]
        for hop in slab_core:
            hop.start()

    def slab_regions():
        for hop in slab_core:
            hop.wait()
        slab_got[...] = slab_got[...] + slab[...]
        slab_bias_got[...] = slab_bias_got[...] + slab_bias[...]
        for hop in slab_far:
            hop.start()

    def slab_blocks():
        for hop in slab_far:
            hop.wait()
        gathered[core, :, block] = slab_region[...] + slab_got[core]
        gathered_bias[core, block] = slab_bias_region[...] + slab_bias_got[core]
        for step in range(1, blocks):
            for hop in slab_peer(step):
                hop.start()

    def slab_cores():
        for step in range(1, blocks):
            for hop in slab_peer(step):
                hop.wait()
        for hop in slab_last:
            hop.start()

    partners = (
        across(spot, "core"),
        across(spot, "x"),
        across(spot, "y"),
        device_at({**spot, "z": spot["z"] // 2 * 2 + 1 - spot["z"] % 2}),
        across(spot, "z", 2),
    )
    hops = [
        remote(
            vector_sent.at[k], vector_got.at[k], vector_sends.at[k], vector_recvs.at[k], device
        )
        for k, device in enumerate(partners)
    ]

    def vector_step(k):
        if k > 0:
            hops[k - 1].wait()
            vector_sum[...] = vector_sum[...] + vector_got[k - 1]
        if k < len(hops):
            vector_sent[k] = vector_sum[...]
            hops[k].start()

    regions_seen = []

    def tick(place, step=0):
        if place == "arrival":

            @pl.when(step == 4)
            def _():
                reduce(2, 0, 1)
                reduce(2, 1, 0)

        if place == "mode":

            @pl.when(step == 3)
            def _():
                share(0, 3)
                reduce(2, 2, 1)
                reduce(2, 3, 0)
                share(1, 1)

            @pl.when(step == 5)
            def _():
                reduce(2, 3, 1)

        if place == "start":
            for copy in load_own:
                copy.wait()
            reduce(2, 0, 0)
            reduce(1, 0, 0)
            vector_step(0)
        if place == "sent":
            reduce(1, 0, 1)
            share(0, 0)
            vector_step(1)
        if place == "zonal":
            share(0, 1)
            reduce(1, 1, 0)
            reduce(2, 1, 1)
            reduce(2, 2, 0)
            vector_step(2)
        if place == "turned":
            share(0, 2)
            reduce(1, 1, 1)
            share(1, 0)
            vector_step(3)
        if place == "modes":
            slab_start()
            share(1, 2)
            share(2, 0)
            vector_step(4)
        if place == "returned":
            share(0, 4)
            share(1, 3)
            share(2, 1)
            vector_step(5)
        if place == "back":
            slab_regions()
        if place == "columns":
            load_tokens.wait()
            slab_blocks()
            share(2, 2)
            share(1, 4)
            share(2, 3)
            slab_cores()
        if place == "region":
            regions_seen.append(place)
            if len(regions_seen) == 1:
                share(2, 4)

    tables = (to_columns, to_modes, ahead, behind)
    filter_pass(sizes, me, core, produce, middle, consume, tables, work, sems, tick)
    late_core = remote(late, late_got, late_sends.at[0], late_recvs.at[0], across(spot, "core"))
    late_core.start()
    late_core.wait()
    late[...] = late[...] + late_got[...]
    late_all[me] = late[...]

    def late_hop(step):
        other = chip_device((me + step) % chips, core, cols)
        return remote(late, late_all.at[me], late_sends.at[step], late_recvs.at[step], other)

    for step in range(1, chips):
        late_hop(step).start()
    for hop in slab_last:
        hop.wait()
    share(0, 5)
    share(1, 5)
    share(2, 5)
    for step in range(1, chips):
        late_hop(step).wait()
    total = late_all[0]
    for chip in range(1, chips):
        total = total + late_all[chip]
    for k in range(3):
        vector_sum[0:1, k * 256 : (k + 1) * 256] = total[k : k + 1, :]
        vector_sum[1:2, k * 256 : (k + 1) * 256] = total[3 + k : 4 + k, :]
    for region in range(regions):
        leave(region).wait()


def call_filter(body, sizes, outs, cid, operands, scalars, spaces, out_spaces, scratch):
    shapes = [jax.ShapeDtypeStruct(shape, kind) for shape, kind in outs]
    anywhere = pl.BlockSpec(memory_space=pl.ANY)
    scalar = pl.BlockSpec(memory_space=pltpu.SMEM)
    return pl.pallas_call(
        functools.partial(body, sizes),
        out_shape=shapes,
        in_specs=[scalar] * len(scalars)
        + [anywhere if place in spaces else vmem for place in range(len(operands))],
        out_specs=[anywhere if place in out_spaces else vmem for place in range(len(outs))],
        scratch_shapes=[*work_shapes(sizes), *scratch],
        compiler_params=pltpu.CompilerParams(
            collective_id=cid, has_side_effects=True, vmem_limit_bytes=60 * 1024 * 1024
        ),
    )(*scalars, *operands)


def forward_scratch(sizes, kept, hidden, tile):
    regions, blocks, block_size, chips, cols, tokens = sizes
    dma = pltpu.SemaphoreType.DMA
    features = blocks * block_size
    return (
        pltpu.VMEM((regions * tokens, features), wide),
        pltpu.VMEM((regions * tokens, features), low),
        dma((regions,)),
        dma((regions,)),
        dma((len(kept), 2)),
        pltpu.VMEM((regions * tokens, features), low),
        pltpu.VMEM((hidden, features), low),
        pltpu.VMEM((hidden // tile, regions * tokens, tile), low),
        dma((2,)),
        dma((hidden // tile,)),
        *(pltpu.VMEM((2, *shape[1:]), kind) for shape, kind in kept),
    )


def backward_scratch(sizes, kept, tile, pairs):
    regions, blocks, block_size, chips, cols, tokens = sizes
    features = blocks * block_size
    side = 2 * block_size
    dma = pltpu.SemaphoreType.DMA
    return (
        pltpu.VMEM((regions * tokens, features), low),
        pltpu.VMEM((regions * tokens, features), wide),
        dma((regions,)),
        pltpu.VMEM((tile, features), low),
        pltpu.VMEM((features, tile), low),
        dma((3,)),
        pltpu.VMEM((side, side), wide),
        pltpu.VMEM((8, side), wide),
        pltpu.VMEM((side, side), wide),
        pltpu.VMEM((8, side), wide),
        *(pltpu.VMEM((2, *shape[1:]), kind) for shape, kind in kept),
        dma((len(kept), 2)),
        pltpu.VMEM((tile // 2, features), low),
        pltpu.VMEM((features // 2, tile), low),
        pltpu.VMEM((tile // 4, features), low),
        pltpu.VMEM((features // 4, tile), low),
        pltpu.VMEM((2, tile // 8, features), low),
        pltpu.VMEM((2, features // 8, tile), low),
        pltpu.VMEM((2, tile // 16, features), low),
        pltpu.VMEM((2, features // 16, tile), low),
        dma((pairs, 2, 4)),
        dma((pairs, 2, 4)),
        dma((pairs, 2, 7)),
        dma((pairs, 2, 7)),
        dma((pairs, 2)),
        pltpu.VMEM((2, 2, block_size, block_size), wide),
        pltpu.VMEM((2, 8, side), wide),
        pltpu.VMEM((2, 2, block_size, block_size), wide),
        pltpu.VMEM((2, 8, side), wide),
        pltpu.VMEM((2, block_size, block_size), wide),
        pltpu.VMEM((8, side), wide),
        dma((2, 2 + blocks)),
        dma((2, 2 + blocks)),
        pltpu.VMEM((5, 16, features), wide),
        pltpu.VMEM((5, 16, features), wide),
        dma((5,)),
        dma((5,)),
        pltpu.VMEM((8, 256), wide),
        pltpu.VMEM((8, 256), wide),
        pltpu.VMEM((chips, 8, 256), wide),
        dma((chips,)),
        dma((chips,)),
    )


def finish_kernel(*refs):
    (
        project,
        expand,
        slope,
        output,
        gathered,
        gathered_bias,
        sums,
        output_out,
        slope_out,
        gain,
        shift,
        kernel,
        bias,
        mixer,
        offset,
        scale,
        center,
        expand_out,
        lift,
        project_out,
        returned,
        project_low,
        expand_low,
        project_wide,
        expand_wide,
        slope_held,
        output_held,
        load_sems,
        store_sems,
        pass_sems,
    ) = refs
    parts = load_sems.shape[1]
    whole = ((project, project_low, project_wide, project_out), (expand, expand_low, expand_wide, expand_out))

    def rows_of(ref, part):
        size = ref.shape[0] // parts
        return ref.at[pl.ds(part * size, size)]

    def load(k, part):
        source, narrow, broad, target = whole[k]
        return pltpu.make_async_copy(
            rows_of(source, part), rows_of(narrow, part), load_sems.at[k, part]
        )

    def store(k, part):
        source, narrow, broad, target = whole[k]
        return pltpu.make_async_copy(
            rows_of(broad, part), rows_of(target, part), store_sems.at[k, part]
        )

    for part in range(parts):
        for k in range(2):
            load(k, part).start()
    passes = [
        [
            pltpu.make_async_copy(source, held, pass_sems.at[0, k]),
            pltpu.make_async_copy(held, target, pass_sems.at[1, k]),
        ]
        for k, (source, held, target) in enumerate(
            ((slope, slope_held, slope_out), (output, output_held, output_out))
        )
    ]
    for copy in passes:
        copy[0].start()
    kernel[...] = gathered[0]
    mixer[...] = gathered[1]
    side = bias.shape[2]
    for b in range(bias.shape[1]):
        for i in range(2):
            bias[i, b : b + 1, :] = gathered_bias[0, b, 0:1, i * side : (i + 1) * side]
            offset[i, b : b + 1, :] = gathered_bias[1, b, 0:1, i * side : (i + 1) * side]
    for k, ref in enumerate((gain, shift, scale, center, returned)):
        ref[...] = sums[k : k + 1, :].reshape(ref.shape)
    tile = lift.shape[0] // 6
    for k in range(6):
        lift[k * tile : (k + 1) * tile] = sums[5 + k : 6 + k, :tile].reshape(tile)
    for copy in passes:
        copy[0].wait()
        copy[1].start()
    for part in range(parts):
        for k in range(2):
            load(k, part).wait()
            source, narrow, broad, target = whole[k]
            rows_of(broad, part)[...] = rows_of(narrow, part)[...].astype(wide)
            store(k, part).start()
    for part in range(parts):
        for k in range(2):
            store(k, part).wait()
    for copy in passes:
        copy[1].wait()


def call_finish(project, expand, slope, output, gathered, gathered_bias, sums):
    hidden, features = project.shape
    line = jax.ShapeDtypeStruct((features,), wide)
    weight = jax.ShapeDtypeStruct(gathered.shape[1:], wide)
    bias = jax.ShapeDtypeStruct(gathered.shape[1:4], wide)
    shapes = [
        jax.ShapeDtypeStruct(output.shape, low),
        jax.ShapeDtypeStruct(slope.shape, wide),
        line,
        line,
        weight,
        bias,
        weight,
        bias,
        line,
        line,
        jax.ShapeDtypeStruct(expand.shape, wide),
        jax.ShapeDtypeStruct((hidden,), wide),
        jax.ShapeDtypeStruct(project.shape, wide),
        line,
    ]
    anywhere = pl.BlockSpec(memory_space=pl.ANY)
    dma = pltpu.SemaphoreType.DMA
    parts = 8
    return pl.pallas_call(
        finish_kernel,
        out_shape=shapes,
        in_specs=[anywhere] * 4 + [vmem] * 3,
        out_specs=[anywhere if k in (0, 1, 10, 12) else vmem for k in range(len(shapes))],
        scratch_shapes=[
            pltpu.VMEM(project.shape, low),
            pltpu.VMEM(expand.shape, low),
            pltpu.VMEM(project.shape, wide),
            pltpu.VMEM(expand.shape, wide),
            pltpu.VMEM(slope.shape, wide),
            pltpu.VMEM(output.shape, low),
            dma((2, parts)),
            dma((2, parts)),
            dma((2, 2)),
        ],
        compiler_params=pltpu.CompilerParams(vmem_limit_bytes=60 * 1024 * 1024),
    )(project, expand, slope, output, gathered, gathered_bias, sums)


def dense_kernel(*refs):
    (
        second_ref,
        up_ref,
        scale_ref,
        returned_ref,
        lift_ref,
        mixed_hbm,
        expand_hbm,
        project_hbm,
        hidden_back_hbm,
        out_hbm,
        mixed_back_hbm,
        project_hbm_own,
        expand_hbm_own,
        project_piece,
        expand_piece,
        project_ready,
        expand_ready,
        vectors,
        mixed_ref,
        expand_ref,
        project_ref,
        hidden_back,
        out_ref,
        out_sum,
        back_sum,
        hidden_tile,
        back_tile,
        project_sent,
        expand_sent,
        project_got,
        expand_got,
        project_own,
        expand_own,
        project_halves,
        expand_halves,
        project_quarters,
        expand_quarters,
        project_eighths,
        expand_eighths,
        load_sems,
        weight_sems,
        leave_sems,
        own_sems,
        sent_sem,
        got_sem,
        first_sends,
        first_recvs,
    ) = refs
    tile = expand_ref.shape[2]
    pairs = project_own.shape[0]
    spot = place_of(lax.axis_index("rows"), lax.axis_index("cols"))
    core = spot["core"]
    orders = (("x", "y"), ("y", "x"))
    sent = (project_sent, expand_sent)
    got = (project_got, expand_got)
    own = (project_own, expand_own)
    halves = (project_halves, expand_halves)
    quarters = (project_quarters, expand_quarters)
    eighths = (project_eighths, expand_eighths)
    piece0 = (project_piece, expand_piece)
    ready = (project_ready, expand_ready)
    places = []
    for j in range(pairs):
        places += [(1 - core) * pairs + j, core * pairs + j]

    def weights(k):
        here = pl.ds(pl.multiple_of(places[k] * tile, tile), tile)
        return [
            pltpu.make_async_copy(project_hbm.at[here], project_ref.at[k], weight_sems.at[0, k]),
            pltpu.make_async_copy(expand_hbm.at[:, here], expand_ref.at[k], weight_sems.at[1, k]),
            pltpu.make_async_copy(
                hidden_back_hbm.at[places[k]], hidden_back.at[k], weight_sems.at[2, k]
            ),
        ]

    for k in range(2 * pairs):
        for copy in weights(k):
            copy.start()
    load_mixed = pltpu.make_async_copy(mixed_hbm, mixed_ref, load_sems.at[0])
    load_mixed.start()
    barrier = pltpu.get_barrier_semaphore()
    for axis in ("core", "x", "y", "near", "far"):
        device = facing(spot, axis)[1]
        pl.semaphore_signal(barrier, inc=1, device_id=device, device_id_type=MESH)
    count = second_ref.shape[0]
    piece = 1024
    vectors[...] = jnp.zeros_like(vectors)

    def start_step(part, carry):
        rows = pl.ds(pl.multiple_of(part * piece, piece), piece)
        out_sum[rows, :] = jnp.broadcast_to(as_row(returned_ref), (piece, out_sum.shape[1]))
        back_sum[rows, :] = jnp.zeros((piece, back_sum.shape[1]), wide)
        return carry + jnp.sum(up_ref[rows, :].astype(wide), 0, keepdims=True)

    vectors[4:5, :] = lax.fori_loop(
        0, count // piece, start_step, jnp.zeros((1, up_ref.shape[1]), wide)
    )
    pl.semaphore_wait(barrier, 5)

    def tile_step(k, place, between):
        lift_row = lift_ref[pl.ds(pl.multiple_of(place * tile, tile), tile)].reshape(1, tile)

        def piece_step(part, carry):
            rows = pl.ds(pl.multiple_of(part * piece, piece), piece)
            pre = dot(second_ref[rows, :], expand_ref[k]) + lift_row
            back = hidden_back[k, rows, :].astype(wide)
            curve = gelu_parts(pre)
            bell = gelu_bell(pre)
            hidden = (pre * curve).astype(low)
            hidden_tile[rows, :] = hidden
            pre_back = (back * (curve + pre * bell)).astype(low)
            back_tile[rows, :] = pre_back
            out_sum[rows, :] += dot(hidden, project_ref[k])
            back_sum[rows, :] += dot_last(pre_back, expand_ref[k])
            return carry + jnp.sum(pre_back.astype(wide), 0, keepdims=True)

        lift = lax.fori_loop(0, count // piece, piece_step, jnp.zeros((1, tile), wide))
        vectors[pl.ds(5 + place, 1), 0:tile] = lift
        between()
        return (
            dot_first(hidden_tile[...], up_ref[...]),
            dot_first(second_ref[...], back_tile[...]),
        )

    def swap(j, k):
        return remote(
            sent[k].at[j], got[k].at[j], sent_sem.at[j, k], got_sem.at[j, k], across(spot, "core")
        )

    chains = []
    for pair in range(2):
        for k in range(2):
            buffers = (own[k].at[pair], halves[k].at[pair])
            if pair == 0:
                buffers += (quarters[k], eighths[k], piece0[k])
            else:
                buffers += (ready[k],)
            chains.append(
                reduce_steps(
                    spot,
                    (orders[k] + ("near", "far"))[: len(buffers) - 1],
                    buffers,
                    first_sends.at[pair, k],
                    first_recvs.at[pair, k],
                )
            )

    def begin(pair, step):
        for chain in chains[pair * 2 : pair * 2 + 2]:
            chain[step][0]()

    def finish(pair, step):
        for chain in chains[pair * 2 : pair * 2 + 2]:
            chain[step][1]()

    def pair_step(j, carry):
        for copy in weights_at(2 * j):
            copy.wait()

        def away_between():
            @pl.when(j == 2)
            def _():
                finish(0, 1)
                begin(0, 2)

        away = tile_step(2 * j, (1 - core) * pairs + j, away_between)
        for k in range(2):
            sent[k][j] = away[k].astype(low)
            swap(j, k).start()
        for copy in weights_at(2 * j + 1):
            copy.wait()

        def home_between():
            @pl.when(j == 1)
            def _():
                finish(0, 0)
                begin(0, 1)

            @pl.when(j == 2)
            def _():
                finish(0, 2)
                begin(0, 3)
                finish(1, 0)
                begin(1, 1)

        home = tile_step(2 * j + 1, core * pairs + j, home_between)
        for k in range(2):
            swap(j, k).wait()
            own[k][j] = (home[k] + got[k][j].astype(wide)).astype(low)

        @pl.when(j == 0)
        def _():
            begin(0, 0)

        @pl.when(j == 1)
        def _():
            begin(1, 0)

        return carry

    def weights_at(k):
        return [
            pltpu.make_async_copy(project_ref.at[k], project_ref.at[k], weight_sems.at[0, k]),
            pltpu.make_async_copy(expand_ref.at[k], expand_ref.at[k], weight_sems.at[1, k]),
            pltpu.make_async_copy(hidden_back.at[k], hidden_back.at[k], weight_sems.at[2, k]),
        ]

    lax.fori_loop(0, pairs, pair_step, 0)
    keeps = [
        pltpu.make_async_copy(own[k].at[pairs - 1], hbm, own_sems.at[k])
        for k, hbm in enumerate((project_hbm_own, expand_hbm_own))
    ]
    for keep in keeps:
        keep.start()
    load_mixed.wait()

    def leave(part):
        rows = pl.ds(pl.multiple_of(part * piece, piece), piece)
        return [
            pltpu.make_async_copy(out_ref.at[rows], out_hbm.at[rows], leave_sems.at[0, part]),
            pltpu.make_async_copy(
                back_sum.at[rows], mixed_back_hbm.at[rows], leave_sems.at[1, part]
            ),
        ]

    def end_step(part, carry):
        for quarter in range(4):
            size = piece // 4
            rows = pl.ds(pl.multiple_of(part * piece + quarter * size, size), size)
            mixed = mixed_ref[rows, :]
            out_ref[rows, :] = (out_sum[rows, :] + mixed).astype(low)
            unit, factor = normalise(mixed)
            norm_back = back_sum[rows, :]
            vectors[2:3, :] += jnp.sum(norm_back * unit, 0, keepdims=True)
            vectors[3:4, :] += jnp.sum(norm_back, 0, keepdims=True)
            pull = norm_back * as_row(scale_ref)
            pull = pull - jnp.mean(pull, -1, keepdims=True) - unit * jnp.mean(
                pull * unit, -1, keepdims=True
            )
            back_sum[rows, :] = up_ref[rows, :].astype(wide) + factor * pull
        for copy in leave(part):
            copy.start()
        return carry

    lax.fori_loop(0, count // piece, end_step, 0)
    finish(0, 3)
    finish(1, 1)
    for keep in keeps:
        keep.wait()
    for part in range(count // piece):
        for copy in leave(part):
            copy.wait()


def call_dense(second_norm, upstream, scale, returned, lift, mixed, expand, project, hidden_back, cid):
    count, features = second_norm.shape
    tile = hidden_back.shape[2]
    pairs = expand.shape[1] // tile // 2
    tall, broad = (tile, features), (features, tile)
    outs = (
        ((count, features), low),
        ((count, features), wide),
        (tall, low),
        (broad, low),
        ((tile // 16, features), low),
        ((features // 16, tile), low),
        ((tile // 4, features), low),
        ((features // 4, tile), low),
        ((16, features), wide),
    )
    shapes = [jax.ShapeDtypeStruct(shape, kind) for shape, kind in outs]
    anywhere = pl.BlockSpec(memory_space=pl.ANY)
    dma = pltpu.SemaphoreType.DMA
    return pl.pallas_call(
        dense_kernel,
        out_shape=shapes,
        in_specs=[vmem] * 5 + [anywhere] * 4,
        out_specs=[anywhere] * 4 + [vmem] * 5,
        scratch_shapes=[
            pltpu.VMEM((count, features), wide),
            pltpu.VMEM((2 * pairs, *broad), low),
            pltpu.VMEM((2 * pairs, *tall), low),
            pltpu.VMEM(hidden_back.shape, low),
            pltpu.VMEM((count, features), low),
            pltpu.VMEM((count, features), wide),
            pltpu.VMEM((count, features), wide),
            pltpu.VMEM((count, tile), low),
            pltpu.VMEM((count, tile), low),
            *(pltpu.VMEM((pairs, *shape), low) for shape in (tall, broad) * 3),
            pltpu.VMEM((pairs - 1, tile // 2, features), low),
            pltpu.VMEM((pairs - 1, features // 2, tile), low),
            pltpu.VMEM((tile // 4, features), low),
            pltpu.VMEM((features // 4, tile), low),
            pltpu.VMEM((tile // 8, features), low),
            pltpu.VMEM((features // 8, tile), low),
            dma((1,)),
            dma((3, 2 * pairs)),
            dma((2, count // 512)),
            dma((2,)),
            dma((pairs, 2)),
            dma((pairs, 2)),
            dma((pairs - 1, 2, 4)),
            dma((pairs - 1, 2, 4)),
        ],
        compiler_params=pltpu.CompilerParams(
            collective_id=cid, has_side_effects=True, vmem_limit_bytes=60 * 1024 * 1024
        ),
    )(second_norm, upstream, scale, returned, lift, mixed, expand, project, hidden_back)


def shards(
    tokens,
    region_sizes,
    region_starts,
    entry_gain,
    entry_shift,
    spectral_kernel,
    spectral_bias,
    spectral_mixer,
    spectral_offset,
    exit_scale,
    exit_center,
    dense_expand,
    dense_lift,
    dense_project,
    dense_return,
    cotangent,
):
    regions, rows_here, cols_here, features = tokens.shape
    row_devices = lax.axis_size("rows")
    cols = lax.axis_size("cols")
    blocks, block_size = spectral_kernel.shape[1:3]
    chips = row_devices // 2 * cols
    fits = (
        row_devices % 2 == 0
        and chips == regions * blocks
        and cols == 2
        and cols_here == 64
        and rows_here == 8
        and block_size == 96
        and blocks == 8
        and regions == 2
        and dense_expand.shape == (features, 4 * features)
    )
    if not fits:
        return shards_general(
            tokens,
            region_sizes,
            region_starts,
            entry_gain,
            entry_shift,
            spectral_kernel,
            spectral_bias,
            spectral_mixer,
            spectral_offset,
            exit_scale,
            exit_center,
            dense_expand,
            dense_lift,
            dense_project,
            dense_return,
            cotangent,
        )
    height = rows_here * row_devices
    width = cols_here * cols
    patches = rows_here * cols_here
    count = regions * patches
    sizes = (regions, blocks, block_size, chips, cols, patches)
    block = ((lax.axis_index("rows") // 2) * cols + lax.axis_index("cols")) % blocks

    def own(weight):
        return lax.dynamic_index_in_dim(weight, block, 1, False)

    def square(weight):
        real, imaginary = weight[0], weight[1]
        return jnp.concatenate(
            [
                jnp.concatenate([real, imaginary], 1),
                jnp.concatenate([-imaginary, real], 1),
            ],
            0,
        )

    side = 2 * block_size
    weights = jnp.stack([square(own(spectral_kernel)), square(own(spectral_mixer))])
    biases = jnp.stack(
        [own(spectral_bias).reshape(side), own(spectral_offset).reshape(side)], 1
    )
    to_modes, to_columns, ahead, behind, eye = task_tables(height, width, rows_here, cols_here)
    flat_tokens = tokens.reshape(count, features)
    upstream = cotangent.reshape(count, features)
    steps = width // 4 // 4
    shape = (steps, side, 4 * 128)
    kept = ((shape, low), (shape, wide), (shape, low), (shape, wide))
    scalars = (region_sizes, region_starts)
    hidden, tile = dense_lift.shape[0], 512
    mixed, second_norm, *stream, hidden_back = call_filter(
        forward_kernel,
        sizes,
        (
            ((count, features), wide),
            ((count, features), low),
            *kept,
            ((hidden // tile, count, tile), low),
        ),
        1,
        (
            flat_tokens,
            entry_gain,
            entry_shift,
            exit_scale,
            exit_center,
            weights,
            biases,
            to_modes,
            to_columns,
            ahead,
            behind,
            eye,
            upstream,
            dense_project,
        ),
        scalars,
        (12, 13),
        range(7),
        forward_scratch(sizes, kept, hidden, tile),
    )
    output, mixed_back, *tiles, part_sums = call_dense(
        second_norm,
        upstream,
        exit_scale,
        dense_return,
        dense_lift,
        mixed,
        dense_expand,
        dense_project,
        hidden_back,
        3,
    )
    slope, project_sum, expand_sum, gathered, gathered_bias, sums = call_filter(
        backward_kernel,
        sizes,
        (
            ((count, features), wide),
            (dense_project.shape, low),
            (dense_expand.shape, low),
            ((2, 2, blocks, block_size, block_size), wide),
            ((2, blocks, 8, side), wide),
            ((16, features), wide),
        ),
        2,
        (
            flat_tokens,
            mixed_back,
            entry_gain,
            weights,
            to_modes.T,
            to_columns.T,
            ahead,
            behind,
            eye,
            *stream,
            *tiles,
            part_sums,
        ),
        scalars,
        (0, 9, 10, 11, 12, 13, 14),
        range(3),
        backward_scratch(sizes, kept, tiles[0].shape[0], 3),
    )
    return tuple(
        call_finish(
            project_sum,
            expand_sum,
            slope.reshape(tokens.shape),
            output.reshape(tokens.shape),
            gathered,
            gathered_bias,
            sums,
        )
    )


def solution(mesh):
    placed = (
        P(None, "rows", "cols", None),
        P(),
        P(),
        P(),
        P(),
        P(),
        P(),
        P(),
        P(),
        P(),
        P(),
        P(),
        P(),
        P(),
        P(),
        P(None, "rows", "cols", None),
    )
    return jax.shard_map(
        shards,
        mesh=mesh,
        in_specs=placed,
        out_specs=(
            P(None, "rows", "cols", None),
            P(None, "rows", "cols", None),
            P(),
            P(),
            P(),
            P(),
            P(),
            P(),
            P(),
            P(),
            P(),
            P(),
            P(),
            P(),
        ),
        check_vma=False,
    )
```
